32 devices in a mesh: dp: 4 (over y, core), zero: 8 (over z, x).
Axes of the slice: x: 2, y: 2, z: 4, core: 2. Of those that a mesh axis runs over, the one named last changes fastest.
Arguments:
- tokens: bfloat16 [32768, 1024], P(('dp', 'zero')), may hold values from -40 to 40
- segments: int32 [32768], P(('dp', 'zero')), may hold values from 0 to 32767, as said below
- cotangent: bfloat16 [32768, 1024], P(('dp', 'zero')), may hold values from -6 to 6
- w_qkv: float32 [1024, 3072], P('zero'), may hold values from -0.1875 to 0.1875
- w_out: float32 [1024, 1024], P('zero'), may hold values from -0.75 to 0.75
- w_up: float32 [1024, 4096], P('zero'), may hold values from -0.1875 to 0.1875
- w_down: float32 [4096, 1024], P('zero'), may hold values from -0.09375 to 0.09375
- vectors: float32 [13, 1024], P(None, 'zero'), may hold values from -0.8 to 1.6
- m_qkv: float32 [1024, 3072], P('zero'), may hold values from -108.6116 to 108.6116
- m_out: float32 [1024, 1024], P('zero'), may hold values from -36.20387 to 36.20387
- m_up: float32 [1024, 4096], P('zero'), may hold values from -72.40774 to 72.40774
- m_down: float32 [4096, 1024], P('zero'), may hold values from -72.40774 to 72.40774
- m_vectors: float32 [13, 1024], P(None, 'zero'), may hold values from -108.6116 to 108.6116
- v_qkv: float32 [1024, 3072], P('zero'), may hold values from 32.768 to 131.072
- v_out: float32 [1024, 1024], P('zero'), may hold values from 2.94912 to 11.79648
- v_up: float32 [1024, 4096], P('zero'), may hold values from 11.79648 to 47.18592
- v_down: float32 [4096, 1024], P('zero'), may hold values from 11.79648 to 47.18592
- v_vectors: float32 [13, 1024], P(None, 'zero'), may hold values from 32.768 to 131.072
Outputs:
- layer_out: bfloat16 [32768, 1024], P(('dp', 'zero'))
- tokens_grad: float32 [32768, 1024], P(('dp', 'zero'))
- first_qkv: float32 [1024, 3072], P('zero')
- first_out: float32 [1024, 1024], P('zero')
- first_up: float32 [1024, 4096], P('zero')
- first_down: float32 [4096, 1024], P('zero')
- first_vectors: float32 [13, 1024], P(None, 'zero')
- second_qkv: float32 [1024, 3072], P('zero')
- second_out: float32 [1024, 1024], P('zero')
- second_up: float32 [1024, 4096], P('zero')
- second_down: float32 [4096, 1024], P('zero')
- second_vectors: float32 [13, 1024], P(None, 'zero')
- new_qkv: float32 [1024, 3072], P('zero')
- new_out: float32 [1024, 1024], P('zero')
- new_up: float32 [1024, 4096], P('zero')
- new_down: float32 [4096, 1024], P('zero')
- new_vectors: float32 [13, 1024], P(None, 'zero')
The draws below stay inside these ranges and needn't reach their ends.
Inputs may be any that keep to these rules, and one draw needn't show every extreme that they name: The rows of one device (1024 rows) hold whole segments: no segment crosses from one device's rows to another's, an id's rows are consecutive, and no id occurs on two devices. In every draw at least one device holds a single segment of 1024 rows.
All inputs are finite; a program needn't handle non-finite values.
Results may differ from the reference program's by a relative error of at most 0.011.
Values may be sent and summed in bfloat16 or wider, within the bound.
No kernel may reach another device: no remote copies, remote signals or barrier semaphores. Data moves between devices by JAX's collectives and lax.ppermute only.
A program may use at most 384 MiB of HBM per device.

```python
import math
import jax
import jax.numpy as jnp
from jax import lax

D = 1024
HEADS = 16
FF = 4096
HEAD_DIM = 64
ROT_DIM = 16
STEP = 10
TOK_DEV = 1024
TOKENS = 32768


def draw_tokens(key, part):
    key = jax.random.fold_in(key, 5)
    key_cols, key_rows, key_base = jax.random.split(key, 3)
    column_scale = jnp.exp(jax.random.uniform(key_cols, (D,), jnp.float32, math.log(0.5), math.log(5.0)))
    row_scale = jnp.exp(jax.random.uniform(key_rows, (TOKENS, 1), jnp.float32, math.log(0.5), math.log(2.0)))
    base = jnp.clip(jax.random.normal(key_base, (TOKENS, D), jnp.float32), -4.0, 4.0)
    return (base * column_scale[None, :] * row_scale).astype(jnp.bfloat16)


def draw_segments(key, part):
    key = jax.random.fold_in(key, 11)
    key_rate, key_marks, key_whole = jax.random.split(key, 3)
    block_count = TOKENS // TOK_DEV
    limits = jax.random.randint(key_rate, (block_count, 1), 4, 128)
    marks = jax.random.randint(key_marks, (block_count, TOK_DEV), 0, 1024) < limits
    whole_block = jax.random.randint(key_whole, (), 0, block_count)
    block_index = jnp.arange(block_count, dtype=jnp.int32)[:, None]
    row_index = jnp.arange(TOK_DEV, dtype=jnp.int32)[None, :]
    marks = marks & (row_index > 0) & (block_index != whole_block)
    local_ids = jnp.cumsum(marks.astype(jnp.int32), axis=1)
    return (local_ids + block_index * TOK_DEV).reshape(-1).astype(jnp.int32)


def draw_vectors(key, part):
    key = jax.random.fold_in(key, 7)
    noise = jnp.clip(jax.random.normal(key, (13, D), jnp.float32), -4.0, 4.0)
    row_index = jnp.arange(13)[:, None]
    gain_rows = (row_index == 0) | (row_index == 2)
    return jnp.where(gain_rows, 1.0 + 0.15 * noise, 0.2 * noise).astype(jnp.float32)


def block_scale(own_key, shape, cuts, smallest, largest):
    def one(axis_at, blocks):
        draws = jax.random.uniform(jax.random.fold_in(jax.random.fold_in(own_key, 6), axis_at), (blocks,), jnp.float32, smallest / len(cuts), largest / len(cuts))
        return jnp.repeat(jnp.exp(draws), shape[axis_at] // blocks).reshape((-1,) + (1,) * (len(shape) - axis_at - 1))

    level = one(*cuts[0])
    for cut in cuts[1:]:
        level = level * one(*cut)
    return level


def gaussian(key, extent, spread, reach, cuts=(), held_as=jnp.bfloat16):
    factor_of = block_scale(key, extent, cuts, -0.22, 0.18) if cuts else 1.0
    array = jax.random.normal(key, extent, jnp.float32) * spread * factor_of
    return jnp.minimum(jnp.maximum(array, -reach), reach).astype(held_as)


def setup_inputs(seed: int = 0) -> dict:
    keys = jax.random.split(jax.random.key(seed), 19)
    return {
        "tokens": draw_tokens(jax.random.fold_in(keys[18], 71), 0),
        "segments": draw_segments(jax.random.fold_in(keys[18], 71), 0),
        "cotangent": gaussian(keys[2], (TOKENS, D), 1.0, 6.0, ((0, 32),)),
        "w_qkv": gaussian(keys[3], (D, 3 * D), D ** -0.5, 0.1875, ((0, 8),), jnp.float32),
        "w_out": gaussian(keys[4], (D, D), (D // 16) ** -0.5, 0.75, ((0, 8),), jnp.float32),
        "w_up": gaussian(keys[5], (D, FF), D ** -0.5, 0.1875, ((0, 8),), jnp.float32),
        "w_down": gaussian(keys[6], (FF, D), FF ** -0.5, 0.09375, ((0, 8),), jnp.float32),
        "vectors": draw_vectors(jax.random.fold_in(keys[18], 71), 0),
        "m_qkv": gaussian(keys[8], (D, 3 * D), (0.11 * TOKENS ** 0.5), 108.6116, ((0, 8),), jnp.float32),
        "m_out": gaussian(keys[9], (D, D), (0.033 * TOKENS ** 0.5), 36.20387, ((0, 8),), jnp.float32),
        "m_up": gaussian(keys[10], (D, FF), (0.066 * TOKENS ** 0.5), 72.40774, ((0, 8),), jnp.float32),
        "m_down": gaussian(keys[11], (FF, D), (0.066 * TOKENS ** 0.5), 72.40774, ((0, 8),), jnp.float32),
        "m_vectors": gaussian(keys[12], (13, D), (0.11 * TOKENS ** 0.5), 108.6116, ((1, 8),), jnp.float32),
        "v_qkv": jnp.clip(jnp.exp(math.log(131.072) - 1.3862944 * jax.random.uniform(keys[13], (D, 3 * D), jnp.float32) ** block_scale(keys[13], (D, 3 * D), ((0, 8),), -0.2, 0.2)), 32.768, 131.072),
        "v_out": jnp.clip(jnp.exp(math.log(11.79648) - 1.3862944 * jax.random.uniform(keys[14], (D, D), jnp.float32) ** block_scale(keys[14], (D, D), ((0, 8),), -0.2, 0.2)), 2.94912, 11.79648),
        "v_up": jnp.clip(jnp.exp(math.log(47.18592) - 1.3862944 * jax.random.uniform(keys[15], (D, FF), jnp.float32) ** block_scale(keys[15], (D, FF), ((0, 8),), -0.2, 0.2)), 11.79648, 47.18592),
        "v_down": jnp.clip(jnp.exp(math.log(47.18592) - 1.3862944 * jax.random.uniform(keys[16], (FF, D), jnp.float32) ** block_scale(keys[16], (FF, D), ((0, 8),), -0.2, 0.2)), 11.79648, 47.18592),
        "v_vectors": jnp.clip(jnp.exp(math.log(131.072) - 1.3862944 * jax.random.uniform(keys[17], (13, D), jnp.float32) ** block_scale(keys[17], (13, D), ((1, 8),), -0.2, 0.2)), 32.768, 131.072),
    }


@jax.custom_vjp
def low(v):
    return lax.optimization_barrier(v.astype(jnp.bfloat16)).astype(jnp.float32)

@jax.custom_vjp
def low_back(v):
    return v

def low_keep(v):
    return (low(v), None)

def low_pass(kept, grad):
    return (grad,)

def back_keep(v):
    return (v, None)

def back_low(kept, grad):
    return (low(grad),)
low.defvjp(low_keep, low_pass)
low_back.defvjp(back_keep, back_low)
EPS_NORM = 1e-05
BETA_ONE = 0.9
BETA_TWO = 0.999
ADAM_EPS = 1e-08
RATE_MATRIX = 0.05
RATE_VECTOR = 0.2
DECAY_MATRIX = 0.1
ROPE_BASE = 10000.0
MASKED = -1e+30

def product(left, right):
    return jnp.dot(left, right, precision=lax.Precision.HIGHEST, preferred_element_type=jnp.float32)

def normalized(inputs):
    row_mean = lax.optimization_barrier(jnp.mean(inputs, axis=-1, keepdims=True))
    centred = inputs - row_mean
    variance = lax.optimization_barrier(jnp.mean(centred * centred, axis=-1, keepdims=True))
    return centred * lax.rsqrt(variance + EPS_NORM)

def rotary_tables(segment_rows):
    row_count = segment_rows.shape[0]
    row_index = jnp.arange(row_count, dtype=jnp.int32)
    earlier = jnp.concatenate([jnp.full((1,), -1, jnp.int32), segment_rows[:-1].astype(jnp.int32)])
    starts = jnp.where(segment_rows != earlier, row_index, 0)
    position = (row_index - lax.cummax(starts, axis=0)).astype(jnp.float32)
    frequency = ROPE_BASE ** (-2.0 * jnp.arange(ROT_DIM // 2, dtype=jnp.float32) / ROT_DIM)
    angles = position[:, None] * frequency[None, :]
    return (jnp.cos(angles), jnp.sin(angles))

def rotate(head_rows, cosine_table, sine_table):
    half_dim = ROT_DIM // 2
    front_half = head_rows[..., :half_dim]
    back_half = head_rows[..., half_dim:ROT_DIM]
    cos_rows = cosine_table[:, None, :]
    sin_rows = sine_table[:, None, :]
    return jnp.concatenate([front_half * cos_rows - back_half * sin_rows, back_half * cos_rows + front_half * sin_rows, head_rows[..., ROT_DIM:]], axis=-1)

def layer_rows(inputs, segment_rows, qkv_w, out_w, up_w, down_w, vector_rows):
    row_count = inputs.shape[0]
    normed = normalized(inputs)
    attn_in = low(normed * vector_rows[0] + vector_rows[1])
    mlp_in = low(normed * vector_rows[2] + vector_rows[3])
    qkv = low_back(product(attn_in, qkv_w) + vector_rows[4:7].reshape(-1))
    cosine_table, sine_table = rotary_tables(segment_rows)
    queries = low(rotate(qkv[:, :D].reshape(row_count, HEADS, HEAD_DIM), cosine_table, sine_table))
    key_rows = low(rotate(qkv[:, D:2 * D].reshape(row_count, HEADS, HEAD_DIM), cosine_table, sine_table))
    values = low(qkv[:, 2 * D:].reshape(row_count, HEADS, HEAD_DIM))
    scores = low_back(jnp.einsum('qhd,khd->hqk', queries, key_rows, precision=lax.Precision.HIGHEST) * HEAD_DIM ** (-0.5))
    row_index = jnp.arange(row_count)
    allowed = (segment_rows[:, None] == segment_rows[None, :]) & (row_index[:, None] >= row_index[None, :])
    scores = jnp.where(allowed[None], scores, MASKED)
    row_max = lax.optimization_barrier(jnp.max(scores, axis=-1, keepdims=True))
    exp_scores = jnp.exp(scores - row_max)
    attn_probs = low(exp_scores / lax.optimization_barrier(jnp.sum(exp_scores, axis=-1, keepdims=True)))
    attended = jnp.einsum('hqk,khd->qhd', attn_probs, values, precision=lax.Precision.HIGHEST).reshape(row_count, D)
    attended = low(low_back(attended))
    attn_branch = product(attended, out_w) + vector_rows[7]
    pre_up = low_back(product(mlp_in, up_w) + vector_rows[8:12].reshape(-1))
    hidden = low(jax.nn.gelu(pre_up, approximate=False))
    return inputs + attn_branch + product(hidden, down_w) + vector_rows[12]

def adam_step(weight, first, second, gradient, rate, decay):
    first_new = BETA_ONE * first + (1.0 - BETA_ONE) * gradient
    second_new = BETA_TWO * second + (1.0 - BETA_TWO) * gradient * gradient
    first_hat = first_new / (1.0 - BETA_ONE ** STEP)
    second_hat = second_new / (1.0 - BETA_TWO ** STEP)
    weight_new = weight - rate * (first_hat / (jnp.sqrt(second_hat) + ADAM_EPS) + decay * weight)
    return (first_new, second_new, weight_new)

def reference(tokens, segments, cotangent, w_qkv, w_out, w_up, w_down, vectors, m_qkv, m_out, m_up, m_down, m_vectors, v_qkv, v_out, v_up, v_down, v_vectors):

    def rounded(weight):
        return weight.astype(jnp.bfloat16).astype(jnp.float32)
    block_count = TOKENS // TOK_DEV
    segment_blocks = segments.reshape(block_count, TOK_DEV)
    checked = jax.checkpoint(layer_rows)

    def forward(inputs, qkv_w, out_w, up_w, down_w, vector_rows):

        def scan_step(scan_carry, block_item):
            return (scan_carry, checked(block_item[0], block_item[1], qkv_w, out_w, up_w, down_w, vector_rows))
        scan_carry, outputs = lax.scan(scan_step, jnp.zeros((), jnp.float32), (inputs.reshape(block_count, TOK_DEV, D), segment_blocks))
        return outputs.reshape(TOKENS, D)
    layer_out, pullback = jax.vjp(forward, tokens.astype(jnp.float32), rounded(w_qkv), rounded(w_out), rounded(w_up), rounded(w_down), rounded(vectors))
    gradients = pullback(cotangent.astype(jnp.float32))
    tokens_grad = gradients[0]
    first_qkv, second_qkv, new_qkv = adam_step(w_qkv, m_qkv, v_qkv, gradients[1], RATE_MATRIX, DECAY_MATRIX)
    first_out, second_out, new_out = adam_step(w_out, m_out, v_out, gradients[2], RATE_MATRIX, DECAY_MATRIX)
    first_up, second_up, new_up = adam_step(w_up, m_up, v_up, gradients[3], RATE_MATRIX, DECAY_MATRIX)
    first_down, second_down, new_down = adam_step(w_down, m_down, v_down, gradients[4], RATE_MATRIX, DECAY_MATRIX)
    first_vectors, second_vectors, new_vectors = adam_step(vectors, m_vectors, v_vectors, gradients[5], RATE_VECTOR, 0.0)
    return (layer_out.astype(jnp.bfloat16), tokens_grad, first_qkv, first_out, first_up, first_down, first_vectors, second_qkv, second_out, second_up, second_down, second_vectors, new_qkv, new_out, new_up, new_down, new_vectors)
```

```python
import functools

import jax
import jax.numpy as jnp
from jax import lax
from jax.experimental import pallas as pl
from jax.experimental.pallas import tpu as pltpu
from jax.sharding import PartitionSpec as P

HEAD_DIM = 64
ROT_DIM = 16
STEP = 10
EPS_NORM = 1e-05
BETA_ONE = 0.9
BETA_TWO = 0.999
ADAM_EPS = 1e-08
RATE_MATRIX = 0.05
RATE_VECTOR = 0.2
DECAY_MATRIX = 0.1
ROPE_BASE = 10000.0
INV_ROOT_TWO = 0.7071067811865476
INV_ROOT_TAU = 0.3989422804014327
MASKED = -1e30
LANES = 128
AXES = ("dp", "zero")
F32 = jnp.float32
BF16 = jnp.bfloat16
VMEM_LIMIT = 58 * 1024 * 1024


def spec(block, index, single=False):
    if single:
        return pl.BlockSpec(block, index, pipeline_mode=pl.Buffered(1))
    return pl.BlockSpec(block, index)


def whole(shape):
    return spec(shape, lambda *_: (0,) * len(shape), single=True)


def scalars():
    return pl.BlockSpec(memory_space=pltpu.SMEM)


def kernel_call(body, grid, in_specs, out_specs, out_shape, flops, moved, scratch=(), name=None):
    return pl.pallas_call(
        body,
        grid=grid,
        in_specs=in_specs,
        out_specs=out_specs,
        out_shape=out_shape,
        scratch_shapes=list(scratch),
        cost_estimate=pl.CostEstimate(flops=int(flops), bytes_accessed=int(moved), transcendentals=0),
        compiler_params=pltpu.CompilerParams(
            vmem_limit_bytes=VMEM_LIMIT, dimension_semantics=("arbitrary",) * len(grid)
        ),
        name=name,
    )


def nn(left, right):
    return lax.dot_general(left, right, (((1,), (0,)), ((), ())), preferred_element_type=F32)


def nt(left, right):
    return lax.dot_general(left, right, (((1,), (1,)), ((), ())), preferred_element_type=F32)


def tn(left, right):
    return lax.dot_general(left, right, (((0,), (0,)), ((), ())), preferred_element_type=F32)


def offset_of(place):
    return 2 * (place % 4) + place // 4


def low_lanes():
    return lax.broadcasted_iota(jnp.int32, (1, LANES), 1) < HEAD_DIM


def pick_parity(core, tile_a, tile_b):
    low = low_lanes()
    even = jnp.where(low, tile_a, pltpu.roll(tile_b, HEAD_DIM, 1))
    odd = jnp.where(low, pltpu.roll(tile_a, HEAD_DIM, 1), tile_b)
    return jnp.where(core == 0, even, odd)


def prep_attn_body(ids, w_qkv, w_out, vec, out):
    core = ids[1]
    for part in range(3):
        for tile in range(4):
            base = part * 1024 + tile * 256
            out[part * 128 : (part + 1) * 128, tile * 128 : (tile + 1) * 128] = pick_parity(
                core, w_qkv[:, base : base + 128], w_qkv[:, base + 128 : base + 256]
            ).astype(BF16)
    rows = w_out[pl.ds(pl.multiple_of(core * 64, 64), 64), :].astype(BF16)
    out[384:448, :] = rows[:, :512]
    out[448:512, :] = rows[:, 512:]
    out[512:528, :] = vec[...].astype(BF16)


def prep_mlp_body(ids, w_up, w_down, out_a, out_b):
    core = ids[1]
    for part, out in enumerate((out_a, out_b)):
        for owner in range(8):
            start = pl.multiple_of(owner * 512 + core * 256 + part * 128, 128)
            out[0:128, owner * 128 : (owner + 1) * 128] = w_up[:, pl.ds(start, 128)].astype(BF16)
        out[128:256, :] = w_down[pl.ds(pl.multiple_of(core * 256 + part * 128, 128), 128), :].astype(BF16)


def join_attn_body(ids, *refs):
    pieces, (w_qkv, w_out, vec, bias) = refs[:8], refs[8:]
    me, core = ids[0], ids[1]
    for place, piece in enumerate(pieces):
        owner = jnp.bitwise_xor(me, offset_of(place))
        at = pl.ds(pl.multiple_of(owner * 128, 128), 128)
        at_half = pl.ds(pl.multiple_of(owner * 64, 64), 64)
        for part in range(3):
            w_qkv[at, part * 512 : (part + 1) * 512] = piece[part * 128 : (part + 1) * 128, :]
        w_out[at_half, 0:512] = piece[384:448, :]
        w_out[at_half, 512:1024] = piece[448:512, :]
        vec[:, at] = piece[512:528, 0:128].astype(F32)
    for part in range(3):
        for tile in range(4):
            base = tile * 256
            row = slice(4 + part, 5 + part)
            bias[:, part * 512 + tile * 128 : part * 512 + (tile + 1) * 128] = pick_parity(
                core, vec[row, base : base + 128], vec[row, base + 128 : base + 256]
            )


def normalize(inputs):
    centred = inputs - jnp.mean(inputs, axis=-1, keepdims=True)
    variance = jnp.mean(centred * centred, axis=-1, keepdims=True)
    inv_std = lax.rsqrt(variance + EPS_NORM)
    return centred * inv_std, inv_std


def norm_body(tok, dy, vec, attn_in, mlp_in, attn_t, mlp_t, dy_t, dy_sum):
    normed, _ = normalize(tok[...].astype(F32))
    attn = (normed * vec[0:1, :] + vec[1:2, :]).astype(BF16)
    mlp = (normed * vec[2:3, :] + vec[3:4, :]).astype(BF16)
    attn_in[...] = attn
    mlp_in[...] = mlp
    attn_t[...] = attn.T
    mlp_t[...] = mlp.T
    grad = dy[...]
    dy_t[...] = grad.T

    @pl.when(pl.program_id(0) == 0)
    def _():
        dy_sum[...] = jnp.zeros_like(dy_sum)

    dy_sum[0:1, :] += jnp.sum(grad.astype(F32), axis=0, keepdims=True)


def qkv_body(attn_in, dy, w_qkv, w_out, bias, cos, sin_lo, sin_hi, q, k, v, d_att):
    rows = attn_in[...]
    for part, out in enumerate((q, k, v)):
        cols = slice(part * 512, (part + 1) * 512)
        acc = nn(rows, w_qkv[:, cols]) + bias[:, cols]
        if part == 2:
            out[...] = acc.astype(BF16)
            continue
        for tile in range(4):
            x = acc[:, tile * 128 : (tile + 1) * 128]
            x = x * cos[...] + pltpu.roll(x, 8, 1) * sin_hi[...] + pltpu.roll(x, 120, 1) * sin_lo[...]
            if part == 0:
                x = x * HEAD_DIM ** (-0.5)
            out[:, tile * 128 : (tile + 1) * 128] = x.astype(BF16)
    d_att[...] = nt(dy[...], w_out[...]).astype(BF16)


ATTN_ROWS = 256


def attn_body(q, k, v, d_att, seg_col, seg_row, cos, sin_lo, sin_hi, att, grad, dq_acc, dk_acc, dv_acc):
    row_count = q.shape[0]
    low = low_lanes()
    dk_acc[...] = jnp.zeros_like(dk_acc)
    dv_acc[...] = jnp.zeros_like(dv_acc)
    step = ATTN_ROWS
    causal = lax.broadcasted_iota(jnp.int32, (step, step), 0) >= lax.broadcasted_iota(
        jnp.int32, (step, step), 1
    )
    for first in range(0, row_count, step):
        rows = slice(first, first + step)
        ids = seg_col[rows, :]
        ranges = [(0, first), (first, first + step)] if first else [(0, step)]
        outs = []
        dqs = []
        for half in range(2):
            lanes = low if half == 0 else jnp.logical_not(low)
            q_h = jnp.where(lanes, q[rows, :], jnp.zeros((), BF16))
            da_h = jnp.where(lanes, d_att[rows, :], jnp.zeros((), BF16))
            scores = []
            for begin, end in ranges:
                allowed = ids == seg_row[0, :, begin:end]
                if begin == first:
                    allowed = allowed & causal
                scores.append(jnp.where(allowed, nt(q_h, k[begin:end, :]), MASKED))
            top = functools.reduce(jnp.maximum, [jnp.max(s, axis=-1, keepdims=True) for s in scores])
            scores = [jnp.exp(s - top) for s in scores]
            total = functools.reduce(jnp.add, [jnp.sum(s, axis=-1, keepdims=True) for s in scores])
            inv = 1.0 / total
            probs = [s * inv for s in scores]
            low_probs = [p.astype(BF16) for p in probs]
            outs.append(
                functools.reduce(jnp.add, [nn(p, v[b:e, :]) for p, (b, e) in zip(low_probs, ranges)])
            )
            grad_probs = [nt(da_h, v[b:e, :]) for b, e in ranges]
            delta = functools.reduce(
                jnp.add, [jnp.sum(g * p, axis=-1, keepdims=True) for g, p in zip(grad_probs, probs)]
            )
            grad_scores = [(p * (g - delta)).astype(BF16) for g, p in zip(grad_probs, probs)]
            dqs.append(
                functools.reduce(jnp.add, [nn(g, k[b:e, :]) for g, (b, e) in zip(grad_scores, ranges)])
            )
            for g, p, (b, e) in zip(grad_scores, low_probs, ranges):
                dk_acc[b:e, :] += tn(g, q_h)
                dv_acc[b:e, :] += tn(p, da_h)
        att[rows, :] = jnp.where(low, outs[0], outs[1]).astype(BF16)
        dq_acc[rows, :] = jnp.where(low, dqs[0], dqs[1]) * HEAD_DIM ** (-0.5)
    for part, acc in enumerate((dq_acc, dk_acc)):
        x = acc[...]
        x = x * cos[...] - pltpu.roll(x, 8, 1) * sin_hi[...] - pltpu.roll(x, 120, 1) * sin_lo[...]
        grad[part] = x.astype(BF16)
    grad[2] = dv_acc[...].astype(BF16)


def attn_weights_body(ids, attn_t, dy_t, grad, att, out_a, out_b, bias, result):
    me = ids[0]
    step = pl.program_id(0)

    @pl.when(step < 3)
    def _():
        rhs = grad[0]
        result[...] = nn(attn_t[...], rhs).astype(BF16)
        cols = pl.ds(pl.multiple_of(step * 512, 512), 512)
        bias[0:1, cols] = jnp.sum(rhs.astype(F32), axis=0, keepdims=True)
        for place in range(8):
            out = out_a if place < 4 else out_b
            owner = jnp.bitwise_xor(me, offset_of(place))
            out[place % 4, 0:128, cols] = result[pl.ds(pl.multiple_of(owner * 128, 128), 128), :]

    @pl.when(step == 3)
    def _():
        result[...] = nn(dy_t[...], att[...]).astype(BF16)
        for place in range(8):
            out = out_a if place < 4 else out_b
            out[place % 4, 128:192, 1024:1536] = jnp.zeros((64, 512), BF16)
        flipped = result[...].T
        result[0:512, :] = flipped[:, 0:512]
        result[512:1024, :] = flipped[:, 512:1024]
        for place in range(8):
            out = out_a if place < 4 else out_b
            owner = jnp.bitwise_xor(me, offset_of(place))
            base = pl.multiple_of(owner * 64, 64)
            out[place % 4, 128:192, 0:512] = result[pl.ds(base, 64), :]
            out[place % 4, 128:192, 512:1024] = result[pl.ds(pl.multiple_of(base + 512, 64), 64), :]


def attn_back_body(grad, att, w_qkv, w_out, tok, vec, out, scaled, sums):
    normed, _ = normalize(tok[...].astype(F32))
    upstream = nt(grad[0], w_qkv[:, 0:512]) + nt(grad[1], w_qkv[:, 512:1024]) + nt(grad[2], w_qkv[:, 1024:1536])
    out[...] = nn(att[...], w_out[...])
    scaled[...] = upstream * vec[0:1, :]

    @pl.when(pl.program_id(0) == 0)
    def _():
        sums[...] = jnp.zeros_like(sums)

    sums[0:1, :] += jnp.sum(upstream * normed, axis=0, keepdims=True)
    sums[1:2, :] += jnp.sum(upstream, axis=0, keepdims=True)


def mlp_body(part, steps, ids, *refs):
    pieces = refs[:8]
    if part == 0:
        (vec, mlp_in, dy, mlp_t, dy_t, out_in, out_a, out_b, out, back, bias_up) = refs[8:19]
        w_up, w_down, hidden, grad_pre, bias, result = refs[19:]
    else:
        (vec, mlp_in, dy, mlp_t, dy_t, out_in, back_in, scaled_in, tok) = refs[8:17]
        (out_a, out_b, out, scaled, bias_up, sums) = refs[17:23]
        w_up, w_down, hidden, grad_pre, bias, result = refs[23:]
    me, core = ids[0], ids[1]
    step = pl.program_id(0)

    @pl.when(step == 0)
    def _():
        for place, piece in enumerate(pieces):
            owner = jnp.bitwise_xor(me, offset_of(place))
            at = pl.ds(pl.multiple_of(owner * 128, 128), 128)
            w_up[at, :] = piece[0:128, :]
            w_down[at, :] = piece[128:256, :]
        for owner in range(8):
            start = pl.multiple_of((owner % 2) * 512 + core * 256 + part * 128, 128)
            row = 8 + owner // 2
            bias[0:1, owner * 128 : (owner + 1) * 128] = vec[row : row + 1, pl.ds(start, 128)]
        bias_up[...] = jnp.zeros_like(bias_up)
        if part:
            sums[...] = jnp.zeros_like(sums)

    rows = mlp_in[...]
    grads = dy[...]
    count = rows.shape[0]
    at = pl.ds(pl.multiple_of(step * count, count), count)
    for col in range(0, 1024, 256):
        cols = slice(col, col + 256)
        pre = nn(rows, w_up[:, cols]) + bias[0:1, cols]
        grad_hidden = nt(grads, w_down[cols, :])
        cdf = 0.5 + 0.5 * lax.erf(pre * INV_ROOT_TWO)
        pdf = jnp.exp(-0.5 * pre * pre) * INV_ROOT_TAU
        hidden[at, cols] = (pre * cdf).astype(BF16)
        gp = (grad_hidden * (cdf + pre * pdf)).astype(BF16)
        grad_pre[at, cols] = gp
        bias_up[0:1, cols] += jnp.sum(gp.astype(F32), axis=0, keepdims=True)
    out[...] = out_in[...] + nn(hidden[at, :], w_down[...])
    upstream = nt(grad_pre[at, :], w_up[...])
    if part == 0:
        back[...] = upstream
    else:
        upstream = back_in[...] + upstream
        scaled[...] = scaled_in[...] + upstream * vec[2:3, :]
        normed, _ = normalize(tok[...].astype(F32))
        sums[0:1, :] += jnp.sum(upstream * normed, axis=0, keepdims=True)
        sums[1:2, :] += jnp.sum(upstream, axis=0, keepdims=True)

    @pl.when(step == steps - 1)
    def _():
        for col in range(0, 1024, 512):
            cols = slice(col, col + 512)
            result[...] = nn(mlp_t[...], grad_pre[:, cols]).astype(BF16)
            for place in range(8):
                out_ref = out_a if place < 4 else out_b
                owner = jnp.bitwise_xor(me, offset_of(place))
                out_ref[place % 4, 0:128, cols] = result[pl.ds(pl.multiple_of(owner * 128, 128), 128), :]
        for col in range(0, 1024, 512):
            cols = slice(col, col + 512)
            flipped = nn(dy_t[...], hidden[:, cols]).astype(BF16).T
            w_down[cols, :] = flipped
        for place in range(8):
            out_ref = out_a if place < 4 else out_b
            owner = jnp.bitwise_xor(me, offset_of(place))
            out_ref[place % 4, 128:256, :] = w_down[pl.ds(pl.multiple_of(owner * 128, 128), 128), :]


def final_body(tok, dy, vec, out_own, out_other, scaled_own, scaled_other, out, grad):
    inputs = tok[...].astype(F32)
    normed, inv_std = normalize(inputs)
    branches = out_own[...] + out_other[...].astype(F32)
    out[...] = (inputs + branches + (vec[7:8, :] + vec[12:13, :])).astype(BF16)
    scaled = scaled_own[...] + scaled_other[...].astype(F32)
    grad[...] = dy[...].astype(F32) + inv_std * (
        scaled
        - jnp.mean(scaled, axis=-1, keepdims=True)
        - normed * jnp.mean(scaled * normed, axis=-1, keepdims=True)
    )


def adam_math(weight, first, second, gradient, rate, decay):
    first_new = BETA_ONE * first + (1.0 - BETA_ONE) * gradient
    second_new = BETA_TWO * second + (1.0 - BETA_TWO) * gradient * gradient
    first_hat = first_new / (1.0 - BETA_ONE**STEP)
    second_hat = second_new / (1.0 - BETA_TWO**STEP)
    weight_new = weight - rate * (first_hat / (jnp.sqrt(second_hat) + ADAM_EPS) + decay * weight)
    return (first_new, second_new, weight_new)


def adam_store(refs, at, gradient):
    w, m, v, m_out, v_out, w_out = refs
    first, second, weight = adam_math(w[at], m[at], v[at], gradient, RATE_MATRIX, DECAY_MATRIX)
    m_out[at] = first
    v_out[at] = second
    w_out[at] = weight


def parities(core, own, other):
    return jnp.where(core == 0, own, other), jnp.where(core == 0, other, own)


def adam_attn_body(ids, own, other, own_out, other_out, *refs):
    core = ids[1]
    step = pl.program_id(0)
    low = low_lanes()

    @pl.when(step < 3)
    def _():
        qkv_refs = refs[0:3] + refs[6:9]
        for tile in range(4):
            cols = slice(tile * 128, (tile + 1) * 128)
            even, odd = parities(core, own[:, cols].astype(F32), other[:, cols].astype(F32))
            first = jnp.where(low, even, pltpu.roll(odd, HEAD_DIM, 1))
            second = jnp.where(low, pltpu.roll(even, HEAD_DIM, 1), odd)
            adam_store(qkv_refs, (slice(None), slice(tile * 256, tile * 256 + 128)), first)
            adam_store(qkv_refs, (slice(None), slice(tile * 256 + 128, tile * 256 + 256)), second)

    @pl.when(step == 0)
    def _():
        out_refs = refs[3:6] + refs[9:12]
        even, odd = parities(core, own_out[:, 0:1024].astype(F32), other_out[:, 0:1024].astype(F32))
        adam_store(out_refs, (slice(0, 64), slice(None)), even)
        adam_store(out_refs, (slice(64, 128), slice(None)), odd)


def adam_mlp_body(ids, own_a, other_a, own_b, other_b, *refs):
    core = ids[1]
    step = pl.program_id(0)
    up_refs = refs[0:3] + refs[6:9]
    down_refs = refs[3:6] + refs[9:12]
    for half in range(2):
        cols = pl.ds(pl.multiple_of(step * 256 + half * 128, 128), 128)
        for part, (own, other) in enumerate(((own_a, other_a), (own_b, other_b))):
            even, odd = parities(core, own[0:128, cols].astype(F32), other[0:128, cols].astype(F32))
            for parity, grad in enumerate((even, odd)):
                base = half * 512 + parity * 256 + part * 128
                adam_store(up_refs, (slice(None), slice(base, base + 128)), grad)
    cols = pl.ds(pl.multiple_of(step * 256, 256), 256)
    for part, (own, other) in enumerate(((own_a, other_a), (own_b, other_b))):
        even, odd = parities(core, own[128:256, cols].astype(F32), other[128:256, cols].astype(F32))
        for parity, grad in enumerate((even, odd)):
            base = parity * 256 + part * 128
            adam_store(down_refs, (slice(base, base + 128), slice(None)), grad)


def rotary_tables(segments):
    row_count = segments.shape[0]
    row_index = jnp.arange(row_count, dtype=jnp.int32)
    earlier = jnp.concatenate([jnp.full((1,), -1, jnp.int32), segments[:-1]])
    starts = jnp.where(segments != earlier, row_index, 0)
    position = (row_index - lax.cummax(starts, axis=0)).astype(F32)
    half_dim = ROT_DIM // 2
    dims = jnp.arange(LANES, dtype=jnp.int32) % HEAD_DIM
    frequency = ROPE_BASE ** (-2.0 * (dims % half_dim).astype(F32) / ROT_DIM)
    turned = dims < ROT_DIM
    angles = position[:, None] * jnp.where(turned, frequency, 0.0)[None, :]
    cosine, sine = jnp.cos(angles), jnp.sin(angles)
    front = (dims < half_dim)[None, :]
    return cosine, jnp.where(front, -sine, 0.0), jnp.where(front, 0.0, sine)


def on_device(
    sizes,
    tokens,
    segments,
    cotangent,
    w_qkv,
    w_out,
    w_up,
    w_down,
    vectors,
    m_qkv,
    m_out,
    m_up,
    m_down,
    m_vectors,
    v_qkv,
    v_out,
    v_up,
    v_down,
    v_vectors,
):
    copies, owners = sizes
    me = lax.axis_index("zero")
    core = lax.axis_index("dp") % 2
    ids = jnp.stack([me, core]).astype(jnp.int32)

    def swap(value, dp_bits, zero_bits):
        pairs = [
            (d * owners + z, (d ^ dp_bits) * owners + (z ^ zero_bits))
            for d in range(copies)
            for z in range(owners)
        ]
        return lax.ppermute(value, AXES, pairs)

    def after(value, *others):
        return lax.optimization_barrier((value,) + others)[0]

    def gather(own):
        near = [own] + [swap(own, 0, 2 * k) for k in (1, 2, 3)]
        far = [swap(piece, 0, 1) for piece in near]
        return near + far

    def reduce(blocks_near, blocks_far):
        arrived = swap(blocks_far, 0, 1)
        parts = [
            (blocks_near[k].astype(F32) + arrived[k].astype(F32)).astype(BF16) for k in range(4)
        ]
        total = parts[0].astype(F32)
        for k in (1, 2, 3):
            total = total + swap(parts[k], 0, 2 * k).astype(F32)
        total = total.astype(BF16)
        bit = 2
        while bit < copies:
            total = (total.astype(F32) + swap(total, bit, 0).astype(F32)).astype(BF16)
            bit *= 2
        return total, swap(total, 1, 0)

    T, width = tokens.shape
    rows = 2 * T
    sds = jax.ShapeDtypeStruct

    with jax.named_scope("prep"):
        own_attn = kernel_call(
            prep_attn_body,
            (1,),
            [scalars(), whole((128, 3072)), whole((128, 1024)), whole((16, 512))],
            whole((528, 512)),
            sds((528, 512), BF16),
            0,
            3e6,
            name="prep_attn",
        )(ids, w_qkv, w_out, jnp.pad(vectors, ((0, 3), (0, 384))))
        own_mlp = kernel_call(
            prep_mlp_body,
            (1,),
            [scalars(), whole((128, 4096)), whole((512, 1024))],
            [whole((256, 1024))] * 2,
            [sds((256, 1024), BF16)] * 2,
            0,
            5e6,
            name="prep_mlp",
        )(ids, w_up, w_down)

    with jax.named_scope("gather"):
        attn_pieces = gather(own_attn)
        tok_other = swap(tokens, 1, 0)
        dy_other = swap(cotangent, 1, 0)
        seg_other = swap(segments, 1, 0)
        mlp_pieces = [gather(after(own_mlp[0], *attn_pieces[1:4]))]
        mlp_pieces.append(gather(after(own_mlp[1], *mlp_pieces[0][1:4])))

    with jax.named_scope("rows"):
        tok = jnp.concatenate([tokens, tok_other], axis=0)
        dy = jnp.concatenate([cotangent, dy_other], axis=0)
        tables = [
            jnp.concatenate(pair, axis=0)
            for pair in zip(rotary_tables(segments), rotary_tables(seg_other))
        ]
        seg_row = jnp.stack([segments, seg_other])[:, None, :]
        seg_col = jnp.concatenate([segments, seg_other])[:, None]

    with jax.named_scope("join"):
        full_qkv, full_out, vec, bias_qkv = kernel_call(
            join_attn_body,
            (1,),
            [scalars()] + [whole((528, 512))] * 8,
            [whole((1024, 1536)), whole((512, 1024)), whole((16, 1024)), whole((1, 1536))],
            [sds((1024, 1536), BF16), sds((512, 1024), BF16), sds((16, 1024), F32), sds((1, 1536), F32)],
            0,
            9e6,
            name="join_attn",
        )(ids, *attn_pieces)

    row_block = lambda n, c=width: spec((n, c), lambda i: (i, 0))
    col_block = lambda n: spec((width, n), lambda i: (0, i))
    with jax.named_scope("norm"):
        attn_in, mlp_in, attn_t, mlp_t, dy_t, dy_sum = kernel_call(
            norm_body,
            (rows // 256,),
            [row_block(256), row_block(256), whole((16, width))],
            [row_block(256), row_block(256), col_block(256), col_block(256), col_block(256), whole((8, width))],
            [sds((rows, width), BF16)] * 2 + [sds((width, rows), BF16)] * 3 + [sds((8, width), F32)],
            0,
            30e6,
            name="norm",
        )(tok, dy, vec)

    with jax.named_scope("qkv"):
        q, k, v, d_att = kernel_call(
            qkv_body,
            (rows // 512,),
            [row_block(512), row_block(512), whole((1024, 1536)), whole((512, 1024)), whole((1, 1536))]
            + [row_block(512, 128)] * 3,
            [row_block(512, 512)] * 4,
            [sds((rows, 512), BF16)] * 4,
            2 * rows * 1024 * 2048,
            25e6,
            name="qkv",
        )(attn_in, dy, full_qkv, full_out, bias_qkv, *tables)

    with jax.named_scope("attention"):
        head_block = spec((T, 128), lambda h, m: (h, m))
        att, grad_qkv = kernel_call(
            attn_body,
            (2, 4),
            [head_block] * 4
            + [spec((T, 1), lambda h, m: (h, 0)), spec((1, 1, T), lambda h, m: (h, 0, 0))]
            + [spec((T, 128), lambda h, m: (h, 0))] * 3,
            [head_block, spec((3, T, 128), lambda h, m: (0, h, m))],
            [sds((rows, 512), BF16), sds((3, rows, 512), BF16)],
            60e9,
            20e6,
            scratch=[pltpu.VMEM((T, 128), F32)] * 3,
            name="attention",
        )(q, k, v, d_att, seg_col, seg_row, *tables)

    with jax.named_scope("attn_weights"):
        grad_near, grad_far, bias_sum = kernel_call(
            attn_weights_body,
            (4,),
            [
                scalars(),
                whole((width, rows)),
                whole((width, rows)),
                spec((1, rows, 512), lambda n: (jnp.minimum(n, 2), 0, 0)),
                whole((rows, 512)),
            ],
            [whole((4, 192, 1536))] * 2 + [whole((8, 1536))],
            [sds((4, 192, 1536), BF16)] * 2 + [sds((8, 1536), F32)],
            2 * rows * 1024 * 2048,
            25e6,
            scratch=[pltpu.VMEM((1024, 512), BF16)],
            name="attn_weights",
        )(ids, attn_t, dy_t, grad_qkv, att)
        attn_total = reduce(grad_near, grad_far)

    with jax.named_scope("attn_back"):
        branch, scaled, attn_sums = kernel_call(
            attn_back_body,
            (rows // 512,),
            [spec((3, 512, 512), lambda i: (0, i, 0)), row_block(512, 512), whole((1024, 1536)), whole((512, 1024))]
            + [row_block(512), whole((16, width))],
            [row_block(512), row_block(512), whole((8, width))],
            [sds((rows, width), F32)] * 2 + [sds((8, width), F32)],
            2 * rows * 1024 * 2048,
            35e6,
            name="attn_back",
        )(grad_qkv, att, full_qkv, full_out, tok, vec)

    mlp_totals = []
    bias_ups = []
    back = None
    mlp_sums = None
    steps = rows // 256
    for part in range(2):
        with jax.named_scope("mlp"):
            ins = [ids] + mlp_pieces[part] + [vec, mlp_in, dy, mlp_t, dy_t, branch]
            in_specs = (
                [scalars()]
                + [whole((256, 1024))] * 8
                + [whole((16, width)), row_block(256), row_block(256), whole((width, rows)), whole((width, rows))]
                + [row_block(256)]
            )
            out_specs = [whole((4, 256, 1024))] * 2 + [row_block(256)] * 2 + [whole((8, 1024))]
            out_shape = (
                [sds((4, 256, 1024), BF16)] * 2 + [sds((rows, width), F32)] * 2 + [sds((8, 1024), F32)]
            )
            if part:
                ins += [back, scaled, tok]
                in_specs += [row_block(256)] * 3
                out_specs.append(whole((8, width)))
                out_shape.append(sds((8, width), F32))
            results = kernel_call(
                functools.partial(mlp_body, part, steps),
                (steps,),
                in_specs,
                out_specs,
                out_shape,
                2 * rows * 1024 * 1024 * 6,
                60e6,
                scratch=[pltpu.VMEM((1024, 1024), BF16)] * 2
                + [pltpu.VMEM((rows, 1024), BF16)] * 2
                + [pltpu.VMEM((8, 1024), F32), pltpu.VMEM((1024, 512), BF16)],
                name="mlp",
            )(*ins)
            mlp_totals.append(reduce(results[0], results[1]))
            branch = results[2]
            bias_ups.append(results[4][0])
            if part:
                scaled, mlp_sums = results[3], results[5]
            else:
                back = results[3]

    with jax.named_scope("vectors"):
        is_core = jnp.arange(2) == core
        grad_bias = jnp.where(core == 0, dy_sum[0:1], 0.0)
        grad_bias_qkv = jnp.where(
            is_core[None, None, :, None], bias_sum[0].reshape(3, 8, 1, 64), 0.0
        ).reshape(3, width)
        grad_bias_up = jnp.where(
            is_core[None, :, None, None],
            jnp.swapaxes(jnp.stack(bias_ups).reshape(2, 8, 128), 0, 1)[:, None],
            0.0,
        ).reshape(4, width)
        grad_vectors = jnp.concatenate(
            [attn_sums[0:2], mlp_sums[0:2], grad_bias_qkv, grad_bias, grad_bias_up, grad_bias], axis=0
        )
        share = lax.dynamic_slice_in_dim(lax.psum(grad_vectors, AXES), me * 128, 128, 1)
        first_vectors, second_vectors, new_vectors = adam_math(
            vectors, m_vectors, v_vectors, share, RATE_VECTOR, 0.0
        )

    with jax.named_scope("final"):
        out_other = swap(branch[T:].astype(BF16), 1, 0)
        scaled_other = swap(scaled[T:].astype(BF16), 1, 0)
        layer_out, tokens_grad = kernel_call(
            final_body,
            (T // 256,),
            [row_block(256), row_block(256), whole((16, width))] + [row_block(256)] * 4,
            [row_block(256)] * 2,
            [sds((T, width), BF16), sds((T, width), F32)],
            0,
            26e6,
            name="final",
        )(tokens, cotangent, vec, branch, out_other, scaled, scaled_other)

    with jax.named_scope("adam"):
        own, other = attn_total
        third = lambda n: (0, jnp.minimum(n, 2))
        wide = [spec((128, 1024), third)] * 3 + [whole((128, 1024))] * 3
        updated_attn = kernel_call(
            adam_attn_body,
            (3,),
            [scalars()]
            + [spec((128, 512), third)] * 2
            + [spec((64, 1536), lambda n: (2, 0), single=True)] * 2
            + wide,
            wide,
            [sds((128, 3072), F32)] * 3 + [sds((128, 1024), F32)] * 3,
            0,
            13e6,
            name="adam_attn",
        )(ids, own, other, own, other, w_qkv, m_qkv, v_qkv, w_out, m_out, v_out)
        wide = [spec((128, 1024), lambda n: (0, n))] * 3 + [spec((512, 256), lambda n: (0, n))] * 3
        updated_mlp = kernel_call(
            adam_mlp_body,
            (4,),
            [scalars()] + [whole((256, 1024))] * 4 + wide,
            wide,
            [sds((128, 4096), F32)] * 3 + [sds((512, 1024), F32)] * 3,
            0,
            27e6,
            name="adam_mlp",
        )(ids, *mlp_totals[0], *mlp_totals[1], w_up, m_up, v_up, w_down, m_down, v_down)
    first_qkv, second_qkv, new_qkv, first_out, second_out, new_out = updated_attn
    first_up, second_up, new_up, first_down, second_down, new_down = updated_mlp
    return (
        layer_out,
        tokens_grad,
        first_qkv,
        first_out,
        first_up,
        first_down,
        first_vectors,
        second_qkv,
        second_out,
        second_up,
        second_down,
        second_vectors,
        new_qkv,
        new_out,
        new_up,
        new_down,
        new_vectors,
    )


def solution(mesh):
    rows, owned, spread = P(AXES, None), P("zero", None), P(None, "zero")
    state = (owned, owned, owned, owned, spread)
    return jax.shard_map(
        functools.partial(on_device, (mesh.shape["dp"], mesh.shape["zero"])),
        mesh=mesh,
        in_specs=(rows, P(AXES), rows) + state * 3,
        out_specs=(rows, rows) + state * 3,
        check_vma=False,
    )
```

```python
import functools

import jax
import jax.numpy as jnp
from jax import lax
from jax.experimental import pallas as pl
from jax.experimental.pallas import tpu as pltpu
from jax.sharding import PartitionSpec as P

HEAD_DIM = 64
ROT_DIM = 16
STEP = 10
EPS_NORM = 1e-05
BETA_ONE = 0.9
BETA_TWO = 0.999
ADAM_EPS = 1e-08
RATE_MATRIX = 0.05
RATE_VECTOR = 0.2
DECAY_MATRIX = 0.1
ROPE_BASE = 10000.0
INV_ROOT_TWO = 0.7071067811865476
INV_ROOT_TAU = 0.3989422804014327
MASKED = -1e30
LANES = 128
AXES = ("dp", "zero")
F32 = jnp.float32
BF16 = jnp.bfloat16
VMEM_LIMIT = 58 * 1024 * 1024


def spec(block, index, single=False):
    if single:
        return pl.BlockSpec(block, index, pipeline_mode=pl.Buffered(1))
    return pl.BlockSpec(block, index)


def whole(shape):
    return spec(shape, lambda *_: (0,) * len(shape), single=True)


def scalars():
    return pl.BlockSpec(memory_space=pltpu.SMEM)


def kernel_call(body, grid, in_specs, out_specs, out_shape, flops, moved, scratch=(), name=None):
    return pl.pallas_call(
        body,
        grid=grid,
        in_specs=in_specs,
        out_specs=out_specs,
        out_shape=out_shape,
        scratch_shapes=list(scratch),
        cost_estimate=pl.CostEstimate(flops=int(flops), bytes_accessed=int(moved), transcendentals=0),
        compiler_params=pltpu.CompilerParams(
            vmem_limit_bytes=VMEM_LIMIT, dimension_semantics=("arbitrary",) * len(grid)
        ),
        name=name,
    )


def nn(left, right):
    return lax.dot_general(left, right, (((1,), (0,)), ((), ())), preferred_element_type=F32)


def nt(left, right):
    return lax.dot_general(left, right, (((1,), (1,)), ((), ())), preferred_element_type=F32)


def tn(left, right):
    return lax.dot_general(left, right, (((0,), (0,)), ((), ())), preferred_element_type=F32)


def piece_owner(ids, place):
    step = place % 4
    if step > 1:
        step = 2 + ids[2] if step == 2 else 3 - ids[2]
    return jnp.bitwise_xor(ids[0], 2 * step + place // 4)


SLOTS = ((0, 0), (1, 0), (2, 0), (2, 1), (0, 1), (1, 1), (3, 0), (3, 1))


def slot_owner(ids, slot):
    step, side = SLOTS[slot]
    if step > 1:
        step = 2 + ids[2] if step == 2 else 3 - ids[2]
    return jnp.bitwise_xor(ids[0], 2 * step + side)


def slot_ref(outs, slot):
    return (outs[0], slot) if slot < 4 else (outs[1], slot - 4) if slot < 6 else (outs[2], slot - 6)


def low_lanes():
    return lax.broadcasted_iota(jnp.int32, (1, LANES), 1) < HEAD_DIM


def pick_parity(core, tile_a, tile_b):
    low = low_lanes()
    even = jnp.where(low, tile_a, pltpu.roll(tile_b, HEAD_DIM, 1))
    odd = jnp.where(low, pltpu.roll(tile_a, HEAD_DIM, 1), tile_b)
    return jnp.where(core == 0, even, odd)


def prep_attn_body(ids, w_qkv, w_out, out_a, out_b):
    core = ids[1]
    for part in range(3):
        for tile in range(4):
            base = part * 1024 + tile * 256
            out = out_a if tile < 2 else out_b
            at = part * 256 + (tile % 2) * 128
            out[:, at : at + 128] = pick_parity(
                core, w_qkv[:, base : base + 128], w_qkv[:, base + 128 : base + 256]
            ).astype(BF16)
    rows = w_out[pl.ds(pl.multiple_of(core * 64, 64), 64), :].astype(BF16)
    for panel in range(4):
        at = 768 + 256 * (panel // 2)
        base = (panel % 2) * 64
        out_a[base : base + 64, at : at + 256] = rows[:, 256 * panel : 256 * panel + 256]


def prep_mlp_body(ids, w_up, w_down, out_a, out_b):
    core = ids[1]
    for part, out in enumerate((out_a, out_b)):
        for owner in range(8):
            start = pl.multiple_of(owner * 512 + part * 256 + core * 128, 128)
            out[0:128, owner * 128 : (owner + 1) * 128] = w_up[:, pl.ds(start, 128)].astype(BF16)
        out[128:256, :] = w_down[pl.ds(pl.multiple_of(part * 256 + core * 128, 128), 128), :].astype(BF16)


def join_vec_body(ids, pieces, vec, bias):
    for step in range(8):
        owner = jnp.bitwise_xor(ids[0], 2 * (step & 3) + step // 4)
        vec[:, pl.ds(pl.multiple_of(owner * 128, 128), 128)] = pieces[step].astype(F32)
    for part in range(3):
        for tile in range(4):
            base = tile * 256
            row = slice(4 + part, 5 + part)
            at = (tile // 2) * 768 + part * 256 + (tile % 2) * 128
            bias[:, at : at + 128] = pick_parity(
                ids[1], vec[row, base : base + 128], vec[row, base + 128 : base + 256]
            )


def normalize(inputs):
    centred = inputs - jnp.mean(inputs, axis=-1, keepdims=True)
    variance = jnp.mean(centred * centred, axis=-1, keepdims=True)
    inv_std = lax.rsqrt(variance + EPS_NORM)
    return centred * inv_std, inv_std


def norm_body(steps, tok_own, tok_other, dy_own, dy_other, vec, attn_in, mlp_in, dy, attn_t, mlp_t, dy_t, dy_sum):
    first = pl.program_id(0) < steps // 2
    normed, _ = normalize(jnp.where(first, tok_own[...], tok_other[...]).astype(F32))
    attn = (normed * vec[0:1, :] + vec[1:2, :]).astype(BF16)
    mlp = (normed * vec[2:3, :] + vec[3:4, :]).astype(BF16)
    attn_in[...] = attn
    mlp_in[...] = mlp
    attn_t[...] = attn.T
    mlp_t[...] = mlp.T
    grad = jnp.where(first, dy_own[...], dy_other[...])
    dy[...] = grad
    dy_t[...] = grad.T

    @pl.when(pl.program_id(0) == 0)
    def _():
        dy_sum[...] = jnp.zeros_like(dy_sum)

    dy_sum[0:1, :] += jnp.sum(grad.astype(F32), axis=0, keepdims=True)


def turned(x, cos, sin_lo, sin_hi, sign):
    return x * cos[...] + sign * (pltpu.roll(x, 8, 1) * sin_hi[...] + pltpu.roll(x, 120, 1) * sin_lo[...])


def project(group, attn_in, dy, w_qkv, w_out, bias, tables, outs):
    rows = attn_in[...]
    for part, out in enumerate(outs[:3]):
        cols = slice(part * 256, (part + 1) * 256)
        at = group * 768 + part * 256
        acc = nn(rows, w_qkv[:, cols]) + bias[:, at : at + 256]
        if part == 2:
            out[...] = acc.astype(BF16)
            continue
        for tile in range(2):
            x = turned(acc[:, tile * 128 : (tile + 1) * 128], *tables, 1.0)
            if part == 0:
                x = x * HEAD_DIM ** (-0.5)
            out[:, tile * 128 : (tile + 1) * 128] = x.astype(BF16)
    outs[3][...] = nt(dy[...], w_out[group * 256 : group * 256 + 256, :]).astype(BF16)


def qkv_first_body(ids, *refs):
    pieces, (attn_in, dy, bias, cos, sin_lo, sin_hi, q, k, v, d_att, w_qkv, w_out) = refs[:8], refs[8:]

    @pl.when(pl.program_id(0) == 0)
    def _():
        for place, piece in enumerate(pieces):
            owner = piece_owner(ids, place)
            w_qkv[pl.ds(pl.multiple_of(owner * 128, 128), 128), :] = piece[:, 0:768]
            for panel in range(4):
                at = 768 + 256 * (panel // 2)
                base = (panel % 2) * 64
                w_out[pl.ds(pl.multiple_of(owner * 64, 64), 64), 256 * panel : 256 * panel + 256] = piece[
                    base : base + 64, at : at + 256
                ]

    project(0, attn_in, dy, w_qkv, w_out, bias, (cos, sin_lo, sin_hi), (q, k, v, d_att))


def qkv_second_body(attn_in, dy, w_qkv, w_out, bias, cos, sin_lo, sin_hi, q, k, v, d_att):
    project(1, attn_in, dy, w_qkv, w_out, bias, (cos, sin_lo, sin_hi), (q, k, v, d_att))


ATTN_ROWS = 256


def attn_body(q, k, v, d_att, seg_col, seg_row, cos, sin_lo, sin_hi, att, grad, dq_acc, dk_acc, dv_acc):
    row_count = q.shape[0]
    low = low_lanes()
    dk_acc[...] = jnp.zeros_like(dk_acc)
    dv_acc[...] = jnp.zeros_like(dv_acc)
    step = ATTN_ROWS
    causal = lax.broadcasted_iota(jnp.int32, (step, step), 0) >= lax.broadcasted_iota(
        jnp.int32, (step, step), 1
    )
    for first in range(0, row_count, step):
        rows = slice(first, first + step)
        ids = seg_col[rows, :]
        ranges = [(0, first), (first, first + step)] if first else [(0, step)]
        outs = []
        dqs = []
        for half in range(2):
            lanes = low if half == 0 else jnp.logical_not(low)
            q_h = jnp.where(lanes, q[rows, :], jnp.zeros((), BF16))
            da_h = jnp.where(lanes, d_att[rows, :], jnp.zeros((), BF16))
            scores = []
            for begin, end in ranges:
                allowed = ids == seg_row[0, :, begin:end]
                if begin == first:
                    allowed = allowed & causal
                scores.append(jnp.where(allowed, nt(q_h, k[begin:end, :]), MASKED))
            top = functools.reduce(jnp.maximum, [jnp.max(s, axis=-1, keepdims=True) for s in scores])
            scores = [jnp.exp(s - top) for s in scores]
            total = functools.reduce(jnp.add, [jnp.sum(s, axis=-1, keepdims=True) for s in scores])
            inv = 1.0 / total
            probs = [s * inv for s in scores]
            low_probs = [p.astype(BF16) for p in probs]
            outs.append(
                functools.reduce(jnp.add, [nn(p, v[b:e, :]) for p, (b, e) in zip(low_probs, ranges)])
            )
            grad_probs = [nt(da_h, v[b:e, :]) for b, e in ranges]
            delta = functools.reduce(
                jnp.add, [jnp.sum(g * p, axis=-1, keepdims=True) for g, p in zip(grad_probs, probs)]
            )
            grad_scores = [(p * (g - delta)).astype(BF16) for g, p in zip(grad_probs, probs)]
            dqs.append(
                functools.reduce(jnp.add, [nn(g, k[b:e, :]) for g, (b, e) in zip(grad_scores, ranges)])
            )
            for g, p, (b, e) in zip(grad_scores, low_probs, ranges):
                dk_acc[b:e, :] += tn(g, q_h)
                dv_acc[b:e, :] += tn(p, da_h)
        att[rows, :] = jnp.where(low, outs[0], outs[1]).astype(BF16)
        dq_acc[rows, :] = jnp.where(low, dqs[0], dqs[1]) * HEAD_DIM ** (-0.5)
    for part, acc in enumerate((dq_acc, dk_acc)):
        x = acc[...]
        grad[part] = turned(x, cos, sin_lo, sin_hi, -1.0).astype(BF16)
    grad[2] = dv_acc[...].astype(BF16)


def attn_weights_body(last, ids, attn_t, grad, *refs):
    if last:
        dy_t, att_a, att_b, keep, send_x, send_y, bias, result, flipped = refs
    else:
        keep, send_x, send_y, bias, result = refs
    step = pl.program_id(0)
    outs = (keep, send_x, send_y)

    @pl.when(step < 3)
    def _():
        rhs = grad[0]
        result[...] = nn(attn_t[...], rhs).astype(BF16)
        cols = pl.ds(pl.multiple_of(step * 256, 256), 256)
        bias[0:1, cols] = jnp.sum(rhs.astype(F32), axis=0, keepdims=True)
        for slot in range(8):
            out, at = slot_ref(outs, slot)
            base = pl.multiple_of(slot_owner(ids, slot) * 128, 128)
            out[at, 0:128, cols] = result[pl.ds(base, 128), :]

    if not last:
        return

    @pl.when(step == 3)
    def _():
        flipped[0:256, :] = nn(dy_t[...], att_a[...]).astype(BF16).T
        flipped[256:512, :] = nn(dy_t[...], att_b[...]).astype(BF16).T
        for slot in range(8):
            out, at = slot_ref(outs, slot)
            rows = pl.ds(pl.multiple_of(slot_owner(ids, slot) * 64, 64), 64)
            for panel in range(4):
                col = 768 + 256 * (panel // 2)
                base = (panel % 2) * 64
                out[at, base : base + 64, col : col + 256] = flipped[rows, 256 * panel : 256 * panel + 256]


def mlp_body(part, steps, ids, *refs):
    count = 1 if part else 8
    pieces = refs[:count]
    vec, mlp_in, dy, mlp_t, dy_t, keep, send_x, send_y, hidden_out, grad_out, bias_up, w_up, w_down = refs[count:-5]
    hidden, grad_pre, bias, result, flipped = refs[-5:]
    outs = (keep, send_x, send_y)
    core = ids[1]
    step = pl.program_id(0)

    @pl.when(step == 0)
    def _():
        for owner in range(8):
            start = pl.multiple_of((owner % 2) * 512 + part * 256 + core * 128, 128)
            row = 8 + owner // 2
            bias[0:1, owner * 128 : (owner + 1) * 128] = vec[row : row + 1, pl.ds(start, 128)]
        bias_up[...] = jnp.zeros_like(bias_up)
        for place in range(8):
            if part:
                piece, at = pieces[0].at[place], slice(place * 128, place * 128 + 128)
            else:
                piece = pieces[place]
                at = pl.ds(pl.multiple_of(piece_owner(ids, place) * 128, 128), 128)
            w_up[at, :] = piece[0:128, :]
            w_down[at, :] = piece[128:256, :]

    rows = mlp_in[...]
    grads = dy[...]
    count = rows.shape[0]
    at = pl.ds(pl.multiple_of(step * count, count), count)
    for col in range(0, 1024, 256):
        cols = slice(col, col + 256)
        pre = nn(rows, w_up[:, cols]) + bias[0:1, cols]
        grad_hidden = nt(grads, w_down[cols, :])
        cdf = 0.5 + 0.5 * lax.erf(pre * INV_ROOT_TWO)
        pdf = jnp.exp(-0.5 * pre * pre) * INV_ROOT_TAU
        act = (pre * cdf).astype(BF16)
        hidden[at, cols] = act
        hidden_out[:, cols] = act
        gp = (grad_hidden * (cdf + pre * pdf)).astype(BF16)
        grad_pre[at, cols] = gp
        grad_out[:, cols] = gp
        bias_up[0:1, cols] += jnp.sum(gp.astype(F32), axis=0, keepdims=True)

    @pl.when(step == steps - 1)
    def _():
        for col in range(0, 1024, 512):
            cols = slice(col, col + 512)
            result[...] = nn(mlp_t[...], grad_pre[:, cols]).astype(BF16)
            for slot in range(8):
                out, place = slot_ref(outs, slot)
                base = pl.multiple_of(slot_owner(ids, slot) * 128, 128)
                out[place, 0:128, cols] = result[pl.ds(base, 128), :]
        for col in range(0, 1024, 512):
            cols = slice(col, col + 512)
            flipped[cols, :] = nn(dy_t[...], hidden[:, cols]).astype(BF16).T
        for slot in range(8):
            out, place = slot_ref(outs, slot)
            base = pl.multiple_of(slot_owner(ids, slot) * 128, 128)
            out[place, 128:256, :] = flipped[pl.ds(base, 128), :]


def back_body(own, grad_a, grad_b, att_a, att_b, hid_a, hid_b, gp_a, gp_b, wq_a, wq_b, w_out, up_a, up_b, down_a, down_b, tok, vec, *refs):
    if own:
        dy, out_other, scaled_other, out, result, sums = refs
    else:
        out, result, sums = refs
    inputs = tok[...].astype(F32)
    normed, inv_std = normalize(inputs)
    branch = nn(att_a[...], w_out[0:256, :]) + nn(att_b[...], w_out[256:512, :])
    back_mlp = None
    for hid, gp, up, down in ((hid_a, gp_a, up_a, down_a), (hid_b, gp_b, up_b, down_b)):
        branch = branch + nn(hid[...], down[...])
        term = nt(gp[...], up[...])
        back_mlp = term if back_mlp is None else back_mlp + term
    back_attn = None
    for grad, w in ((grad_a, wq_a), (grad_b, wq_b)):
        for part in range(3):
            term = nt(grad[part], w[:, part * 256 : part * 256 + 256])
            back_attn = term if back_attn is None else back_attn + term
    scaled = back_attn * vec[0:1, :] + back_mlp * vec[2:3, :]

    @pl.when(pl.program_id(0) == 0)
    def _():
        sums[...] = jnp.zeros_like(sums)

    for row, value in enumerate((back_attn * normed, back_attn, back_mlp * normed, back_mlp)):
        sums[row : row + 1, :] += jnp.sum(value, axis=0, keepdims=True)
    if not own:
        out[...] = branch.astype(BF16)
        result[...] = scaled.astype(BF16)
        return
    branch = branch + out_other[...].astype(F32)
    out[...] = (inputs + branch + (vec[7:8, :] + vec[12:13, :])).astype(BF16)
    scaled = scaled + scaled_other[...].astype(F32)
    result[...] = dy[...].astype(F32) + inv_std * (
        scaled
        - jnp.mean(scaled, axis=-1, keepdims=True)
        - normed * jnp.mean(scaled * normed, axis=-1, keepdims=True)
    )


def adam_math(weight, first, second, gradient, rate, decay):
    first_new = BETA_ONE * first + (1.0 - BETA_ONE) * gradient
    second_new = BETA_TWO * second + (1.0 - BETA_TWO) * gradient * gradient
    first_hat = first_new / (1.0 - BETA_ONE**STEP)
    second_hat = second_new / (1.0 - BETA_TWO**STEP)
    weight_new = weight - rate * (first_hat / (jnp.sqrt(second_hat) + ADAM_EPS) + decay * weight)
    return (first_new, second_new, weight_new)


def adam_store(refs, at, gradient):
    w, m, v, m_out, v_out, w_out = refs
    first, second, weight = adam_math(w[at], m[at], v[at], gradient, RATE_MATRIX, DECAY_MATRIX)
    m_out[at] = first
    v_out[at] = second
    w_out[at] = weight


def parities(core, own, other):
    return jnp.where(core == 0, own, other), jnp.where(core == 0, other, own)


def adam_attn_body(ids, own_a, other_a, own_b, other_b, own_out, other_out, *refs):
    core = ids[1]
    low = low_lanes()
    qkv_refs = refs[0:3] + refs[6:9]
    for tile in range(4):
        own, other = (own_a, other_a) if tile < 2 else (own_b, other_b)
        cols = slice((tile % 2) * 128, (tile % 2) * 128 + 128)
        even, odd = parities(core, own[:, cols].astype(F32), other[:, cols].astype(F32))
        first = jnp.where(low, even, pltpu.roll(odd, HEAD_DIM, 1))
        second = jnp.where(low, pltpu.roll(even, HEAD_DIM, 1), odd)
        adam_store(qkv_refs, (slice(None), slice(tile * 256, tile * 256 + 128)), first)
        adam_store(qkv_refs, (slice(None), slice(tile * 256 + 128, tile * 256 + 256)), second)

    @pl.when(pl.program_id(0) == 0)
    def _():
        out_refs = refs[3:6] + refs[9:12]
        for panel in range(4):
            rows = slice((panel % 2) * 64, (panel % 2) * 64 + 64)
            cols = slice(256 * (panel // 2), 256 * (panel // 2) + 256)
            span = slice(panel * 256, panel * 256 + 256)
            even, odd = parities(core, own_out[rows, cols].astype(F32), other_out[rows, cols].astype(F32))
            adam_store(out_refs, (slice(0, 64), span), even)
            adam_store(out_refs, (slice(64, 128), span), odd)


def adam_mlp_body(ids, own, other, *refs):
    core = ids[1]
    up_refs = refs[0:3] + refs[-6:-3]
    down_refs = refs[3:6] + refs[-3:]
    cols = pl.ds(pl.multiple_of(pl.program_id(0) * 128, 128), 128)
    for base, refs_of in ((0, up_refs), (128, down_refs)):
        rows = slice(base, base + 128)
        for parity, grad in enumerate(
            parities(core, own[rows, cols].astype(F32), other[rows, cols].astype(F32))
        ):
            span = slice(parity * 128, (parity + 1) * 128)
            adam_store(refs_of, (slice(None), span) if base == 0 else (span, slice(None)), grad)


def rotary_tables(segments):
    row_count = segments.shape[0]
    row_index = jnp.arange(row_count, dtype=jnp.int32)
    earlier = jnp.concatenate([jnp.full((1,), -1, jnp.int32), segments[:-1]])
    starts = jnp.where(segments != earlier, row_index, 0)
    position = (row_index - lax.cummax(starts, axis=0)).astype(F32)
    half_dim = ROT_DIM // 2
    dims = jnp.arange(LANES, dtype=jnp.int32) % HEAD_DIM
    frequency = ROPE_BASE ** (-2.0 * (dims % half_dim).astype(F32) / ROT_DIM)
    turned = dims < ROT_DIM
    angles = position[:, None] * jnp.where(turned, frequency, 0.0)[None, :]
    cosine, sine = jnp.cos(angles), jnp.sin(angles)
    front = (dims < half_dim)[None, :]
    return cosine, jnp.where(front, -sine, 0.0), jnp.where(front, 0.0, sine)


def on_device(
    sizes,
    tokens,
    segments,
    cotangent,
    w_qkv,
    w_out,
    w_up,
    w_down,
    vectors,
    m_qkv,
    m_out,
    m_up,
    m_down,
    m_vectors,
    v_qkv,
    v_out,
    v_up,
    v_down,
    v_vectors,
):
    copies, owners = sizes
    me = lax.axis_index("zero")
    plane = lax.axis_index("dp")
    core = plane % 2
    ids = jnp.stack([me, core, (plane // 2) % 2]).astype(jnp.int32)

    def move(value, target):
        pairs = []
        for d in range(copies):
            for z in range(owners):
                to_d, to_z = target(d, z)
                pairs.append((d * owners + z, to_d * owners + to_z))
        return lax.ppermute(value, AXES, pairs)

    def swap(value, dp_bits, zero_bits):
        return move(value, lambda d, z: (d ^ dp_bits, z ^ zero_bits))

    def swap_far(value):
        return move(value, lambda d, z: (d, z ^ (6 if d & 2 else 4)))

    def sync(*values):
        return lax.optimization_barrier(values)

    def gather_first(own):
        return [own, swap(own, 0, 2), swap_far(own), swap(own, 0, 1)]

    def gather_second(got):
        own, next_z, far_z, across = got
        return got + [swap(next_z, 0, 1), swap(far_z, 0, 1), swap(far_z, 2, 0)]

    def gather_third(got):
        own, next_z, far_z, across, next_across, far_across, rest_z = got
        return [own, next_z, far_z, rest_z, across, next_across, far_across, swap(far_across, 2, 0)]

    def add(*terms):
        return functools.reduce(jnp.add, [t.astype(F32) for t in terms])

    def reduce_first(keep, send_x, send_y):
        return keep, swap(send_x, 0, 1), swap(send_y, 2, 0)

    def reduce_second(state):
        keep, got_x, got_y = state
        far = add(keep[3], got_y[1]).astype(BF16)
        near = add(keep[1], got_x[1]).astype(BF16)
        return keep, got_x, got_y, far, near, swap(far, 0, 1), swap(near, 0, 2)

    def reduce_third(state):
        keep, got_x, got_y, _, _, got_far, got_near = state
        far = add(keep[2], got_y[0], got_far).astype(BF16)
        return add(keep[0], got_x[0], got_near), far, swap_far(far)

    def reduce_fourth(state):
        total = (state[0] + state[2].astype(F32)).astype(BF16)
        bit = 2
        while bit < copies:
            total = add(total, swap(total, bit, 0)).astype(BF16)
            bit *= 2
        return total, swap(total, 1, 0)

    T, width = tokens.shape
    rows = 2 * T
    sds = jax.ShapeDtypeStruct
    row_block = lambda n, c=width: spec((n, c), lambda i: (i, 0))
    col_block = lambda n: spec((width, n), lambda i: (0, i))

    def block_call(body, grid, ins, outs, flops, moved, scratch=(), name=None):
        return kernel_call(
            body,
            grid,
            [place for _, place in ins],
            [place for _, place in outs],
            [shape for shape, _ in outs],
            flops,
            moved,
            scratch=scratch,
            name=name,
        )(*[value for value, _ in ins])

    def const(value):
        return value, whole(value.shape)

    def kept(shape, dtype):
        return sds(shape, dtype), whole(shape)

    with jax.named_scope("exchange"):
        tok_other = swap(tokens, 1, 0)
        dy_other = swap(cotangent, 1, 0)
        seg_other = swap(segments, 1, 0)
        vec_pieces = jnp.pad(vectors, ((0, 3), (0, 0))).astype(BF16)[None]

    with jax.named_scope("prep"):
        own_a, own_q = block_call(
            prep_attn_body,
            (1,),
            [(ids, scalars()), const(w_qkv), const(w_out)],
            [kept((128, 1280), BF16), kept((128, 768), BF16)],
            0,
            3e6,
            name="prep_attn",
        )
        own_mlp = block_call(
            prep_mlp_body,
            (1,),
            [(ids, scalars()), const(w_up), const(w_down)],
            [kept((256, 1024), BF16)] * 2,
            0,
            5e6,
            name="prep_mlp",
        )

    with jax.named_scope("gather"):
        attn_pieces = gather_first(own_a)
        for bits in (2, 4, 1):
            vec_pieces = jnp.concatenate([vec_pieces, swap(vec_pieces, 0, bits)], axis=0)

    with jax.named_scope("rows"):
        tables = [
            jnp.concatenate(pair, axis=0)
            for pair in zip(rotary_tables(segments), rotary_tables(seg_other))
        ]
        seg_row = jnp.stack([segments, seg_other])[:, None, :]
        seg_col = jnp.concatenate([segments, seg_other])[:, None]

    attn_pieces, own_mlp, vec_pieces, tok_other, dy_other = sync(
        attn_pieces, own_mlp, vec_pieces, tok_other, dy_other
    )

    steps = rows // 256
    with jax.named_scope("gather"):
        attn_pieces = gather_second(attn_pieces)
        mlp_pieces = gather_first(own_mlp[0])

    with jax.named_scope("norm"):
        vec, bias_qkv = block_call(
            join_vec_body,
            (1,),
            [(ids, scalars()), const(vec_pieces)],
            [kept((16, 1024), F32), kept((1, 1536), F32)],
            0,
            1e5,
            name="join_vec",
        )
        first_half = spec((256, width), lambda i: (jnp.minimum(i, steps // 2 - 1), 0))
        second_half = spec((256, width), lambda i: (jnp.maximum(i - steps // 2, 0), 0))
        normed = block_call(
            functools.partial(norm_body, steps),
            (steps,),
            [(tokens, first_half), (tok_other, second_half), (cotangent, first_half), (dy_other, second_half)]
            + [const(vec)],
            [(sds((rows, width), BF16), row_block(256))] * 3
            + [(sds((width, rows), BF16), col_block(256))] * 3
            + [kept((8, width), F32)],
            0,
            34e6,
            name="norm",
        )

    attn_pieces, normed, tables, seg_row, seg_col = sync(attn_pieces, normed, tables, seg_row, seg_col)
    attn_in, mlp_in, dy, attn_t, mlp_t, dy_t, dy_sum = normed
    with jax.named_scope("gather"):
        attn_pieces = gather_third(attn_pieces)
        own_mlp_b, attn_pieces[0] = sync(own_mlp[1], attn_pieces[0])
        weights_b = lax.all_gather(own_mlp_b, "zero", axis=0, tiled=False)
        weights_q = lax.all_gather(sync(own_q, weights_b)[0], "zero", axis=0, tiled=False)

    def table_blocks(count):
        return [(t, row_block(count, 128)) for t in tables]

    def heads(value):
        return value, row_block(512, 256)

    def attention(group, projected):
        with jax.named_scope("attention"):
            head_block = spec((T, 128), lambda h, m: (h, m))
            return block_call(
                attn_body,
                (2, 2),
                [(value, head_block) for value in projected]
                + [(seg_col, spec((T, 1), lambda h, m: (h, 0)))]
                + [(seg_row, spec((1, 1, T), lambda h, m: (h, 0, 0)))]
                + [(t, spec((T, 128), lambda h, m: (h, 0))) for t in tables],
                [
                    (sds((rows, 256), BF16), head_block),
                    (sds((3, rows, 256), BF16), spec((3, T, 128), lambda h, m: (0, h, m))),
                ],
                30e9,
                10e6,
                scratch=[pltpu.VMEM((T, 128), F32)] * 3,
                name="attention",
            )

    def blocks_of(shape):
        return [kept((n,) + shape, BF16) for n in (4, 2, 2)]

    with jax.named_scope("qkv"):
        *projected, wq_a, full_out = block_call(
            qkv_first_body,
            (rows // 512,),
            [(ids, scalars())]
            + [const(piece) for piece in attn_pieces]
            + [(attn_in, row_block(512)), (dy, row_block(512)), const(bias_qkv)]
            + table_blocks(512),
            [(sds((rows, 256), BF16), row_block(512, 256))] * 4
            + [kept((1024, 768), BF16), kept((512, 1024), BF16)],
            2 * rows * 1024 * 1024,
            20e6,
            name="qkv",
        )
    projected, mlp_pieces = sync(projected, mlp_pieces)
    with jax.named_scope("gather"):
        mlp_pieces = gather_second(mlp_pieces)
    att_a, grad_a = attention(0, projected)
    att_a, grad_a, mlp_pieces, attn_t = sync(att_a, grad_a, mlp_pieces, attn_t)
    with jax.named_scope("gather"):
        mlp_pieces = gather_third(mlp_pieces)

    with jax.named_scope("attn_weights"):
        grad_block = spec((1, rows, 256), lambda n: (jnp.minimum(n, 2), 0, 0))
        *blocks, bias_sum_a = block_call(
            functools.partial(attn_weights_body, False),
            (3,),
            [(ids, scalars()), const(attn_t), (grad_a, grad_block)],
            blocks_of((128, 768)) + [kept((8, 768), F32)],
            2 * rows * 1024 * 768,
            12e6,
            scratch=[pltpu.VMEM((1024, 256), BF16)],
            name="attn_weights",
        )
    blocks, mlp_pieces, mlp_in = sync(blocks, mlp_pieces, mlp_in)
    reduce_q = reduce_first(*blocks)

    def mlp(part, weights, rows_in):
        with jax.named_scope("mlp"):
            *results, hid, gp, bias_up, w_up_full, w_down_full = block_call(
                functools.partial(mlp_body, part, steps),
                (steps,),
                [(ids, scalars())]
                + [const(w) for w in weights]
                + [const(vec), (rows_in, row_block(256)), (dy, row_block(256)), const(mlp_t), const(dy_t)],
                blocks_of((256, 1024))
                + [(sds((rows, width), BF16), row_block(256))] * 2
                + [kept((8, 1024), F32)]
                + [kept((1024, 1024), BF16)] * 2,
                2 * rows * 1024 * 1024 * 4,
                40e6,
                scratch=[pltpu.VMEM((rows, 1024), BF16)] * 2
                + [pltpu.VMEM((8, 1024), F32), pltpu.VMEM((1024, 512), BF16), pltpu.VMEM((1024, 1024), BF16)],
                name="mlp",
            )
            return results, hid, gp, bias_up[0], w_up_full, w_down_full

    mlp_a = mlp(0, mlp_pieces, mlp_in)
    mlp_a, reduce_q = sync(mlp_a, reduce_q)
    reduce_q = reduce_second(reduce_q)
    reduce_a = reduce_first(*mlp_a[0])
    mlp_in, *ready = sync(mlp_in, *reduce_q[3:5])
    mlp_b = mlp(1, [weights_b], mlp_in)
    mlp_b, reduce_q, reduce_a, attn_in = sync(mlp_b, reduce_q, reduce_a, attn_in)
    reduce_q = reduce_third(reduce_q)
    reduce_a = reduce_second(reduce_a)
    reduce_b = reduce_first(*mlp_b[0])
    attn_in, *ready = sync(attn_in, reduce_q[1], *reduce_a[3:5])

    with jax.named_scope("qkv"):
        wq_b = weights_q.reshape(1024, 768)
        projected = block_call(
            qkv_second_body,
            (rows // 512,),
            [(attn_in, row_block(512)), (dy, row_block(512)), const(wq_b), const(full_out), const(bias_qkv)]
            + table_blocks(512),
            [(sds((rows, 256), BF16), row_block(512, 256))] * 4,
            2 * rows * 1024 * 1024,
            20e6,
            name="qkv",
        )
    att_b, grad_b = attention(1, projected)
    att_b, grad_b, reduce_q, reduce_a, reduce_b = sync(att_b, grad_b, reduce_q, reduce_a, reduce_b)
    reduce_q = reduce_fourth(reduce_q)
    reduce_a = reduce_third(reduce_a)
    reduce_b = reduce_second(reduce_b)
    grad_b, *ready = sync(grad_b, reduce_a[1], *reduce_b[3:5])
    with jax.named_scope("attn_weights"):
        *blocks, bias_sum_b = block_call(
            functools.partial(attn_weights_body, True),
            (4,),
            [(ids, scalars()), const(attn_t), (grad_b, grad_block), const(dy_t), const(att_a), const(att_b)],
            blocks_of((128, 1280)) + [kept((8, 768), F32)],
            2 * rows * 1024 * 1280,
            20e6,
            scratch=[pltpu.VMEM((1024, 256), BF16), pltpu.VMEM((512, 1024), BF16)],
            name="attn_weights",
        )
    blocks, grad_b = sync(blocks, grad_b)
    reduce_o = reduce_first(*blocks)

    _, hid_a, gp_a, bias_up_a, up_a, down_a = mlp_a
    _, hid_b, gp_b, bias_up_b, up_b, down_b = mlp_b

    def back(own, grad, rows_tok, extra, outs):
        first = 0 if own else T // 256
        block = lambda c=width: spec((256, c), lambda i: (i + first, 0))
        lead = spec((3, 256, 256), lambda i: (0, i + first, 0))
        with jax.named_scope("back"):
            return block_call(
                functools.partial(back_body, own),
                (T // 256,),
                [(grad_a, lead), (grad, lead), (att_a, block(256)), (att_b, block(256))]
                + [(value, block()) for value in (hid_a, hid_b, gp_a, gp_b)]
                + [const(w) for w in (wq_a, wq_b, full_out, up_a, up_b, down_a, down_b)]
                + [(rows_tok, row_block(256)), const(vec)]
                + [(value, row_block(256)) for value in extra],
                [(sds((T, width), t), row_block(256)) for t in outs] + [kept((8, width), F32)],
                2 * T * 1024 * 6144,
                40e6,
                name="back",
            )

    out_part, scaled_part, sums_other = back(False, grad_b, tok_other, [], (BF16, BF16))
    out_part, scaled_part, sums_other, grad_b, reduce_q, reduce_a, reduce_b, reduce_o = sync(
        out_part, scaled_part, sums_other, grad_b, reduce_q, reduce_a, reduce_b, reduce_o
    )
    out_got, scaled_got = swap(out_part, 1, 0), swap(scaled_part, 1, 0)
    reduce_a = reduce_fourth(reduce_a)
    reduce_b = reduce_third(reduce_b)
    reduce_o = reduce_second(reduce_o)
    grad_b, *ready = sync(grad_b, reduce_a[0], reduce_b[1], *reduce_o[3:5])
    layer_out, tokens_grad, sums_own = back(
        True, grad_b, tokens, [cotangent, out_got, scaled_got], (BF16, F32)
    )
    sums_own, reduce_a, reduce_b, reduce_o = sync(sums_own, reduce_a, reduce_b, reduce_o)
    reduce_b = reduce_fourth(reduce_b)
    reduce_o = reduce_third(reduce_o)

    with jax.named_scope("vectors"):
        is_core = jnp.arange(2) == core
        grad_bias = jnp.where(core == 0, dy_sum[0:1], 0.0)
        bias_sum = jnp.concatenate([bias_sum_a[0].reshape(3, 256), bias_sum_b[0].reshape(3, 256)], axis=1)
        grad_bias_qkv = jnp.where(
            is_core[None, None, :, None], bias_sum.reshape(3, 8, 1, 64), 0.0
        ).reshape(3, width)
        grad_bias_up = jnp.where(
            is_core[None, None, :, None],
            jnp.swapaxes(jnp.stack([bias_up_a, bias_up_b]).reshape(2, 8, 128), 0, 1)[:, :, None],
            0.0,
        ).reshape(4, width)
        total = jnp.concatenate(
            [
                sums_own[0:4] + sums_other[0:4],
                grad_bias_qkv,
                grad_bias,
                grad_bias_up,
                grad_bias,
                jnp.zeros((3, width), F32),
            ],
            axis=0,
        )
        bits = [(0, b) for b in (1, 2, 4)]
        bit = 1
        while bit < copies:
            bits.append((bit, 0))
            bit *= 2
        for pair in bits:
            total = total + swap(total, *pair)
        share = lax.dynamic_slice_in_dim(total[0:13], me * 128, 128, 1)
        first_vectors, second_vectors, new_vectors = adam_math(
            vectors, m_vectors, v_vectors, share, RATE_VECTOR, 0.0
        )

    with jax.named_scope("adam"):

        def adam_mlp(part, totals, previous):
            wide = [spec((128, 256), lambda n: (0, 2 * n + part))] * 3
            wide += [spec((256, 128), lambda n: (part, n))] * 3
            return pl.pallas_call(
                adam_mlp_body,
                grid=(8,),
                in_specs=[scalars()]
                + [whole((256, 1024))] * 2
                + wide
                + [pl.BlockSpec(memory_space=pl.ANY)] * len(previous),
                out_specs=wide,
                out_shape=[sds((128, 4096), F32)] * 3 + [sds((512, 1024), F32)] * 3,
                input_output_aliases={9 + n: n for n in range(len(previous))},
                cost_estimate=pl.CostEstimate(flops=0, bytes_accessed=14000000, transcendentals=0),
                compiler_params=pltpu.CompilerParams(
                    vmem_limit_bytes=VMEM_LIMIT, dimension_semantics=("arbitrary",)
                ),
                name="adam_mlp",
            )(ids, *totals, w_up, m_up, v_up, w_down, m_down, v_down, *previous)

        updated_mlp = adam_mlp(0, reduce_a, [])
        updated_mlp, reduce_o, reduce_b = sync(updated_mlp, reduce_o, reduce_b)
        reduce_o = reduce_fourth(reduce_o)
        reduce_b, *ready = sync(reduce_b, reduce_o[0])
        updated_mlp = adam_mlp(1, reduce_b, updated_mlp)
        (own_b, other_b) = reduce_o
        (own_a, other_a) = reduce_q
        part_block = lambda n: (0, n)
        out_block = spec((128, 512), lambda n: (0, 0))
        wide = [spec((128, 1024), part_block)] * 3 + [whole((128, 1024))] * 3
        updated_attn = kernel_call(
            adam_attn_body,
            (3,),
            [scalars()] + [spec((128, 256), part_block)] * 4 + [whole((128, 512))] * 2 + wide,
            wide,
            [sds((128, 3072), F32)] * 3 + [sds((128, 1024), F32)] * 3,
            0,
            13e6,
            name="adam_attn",
        )(
            ids,
            own_a,
            other_a,
            own_b,
            other_b,
            own_b[:, 768:],
            other_b[:, 768:],
            w_qkv,
            m_qkv,
            v_qkv,
            w_out,
            m_out,
            v_out,
        )
    first_qkv, second_qkv, new_qkv, first_out, second_out, new_out = updated_attn
    first_up, second_up, new_up, first_down, second_down, new_down = updated_mlp
    return (
        layer_out,
        tokens_grad,
        first_qkv,
        first_out,
        first_up,
        first_down,
        first_vectors,
        second_qkv,
        second_out,
        second_up,
        second_down,
        second_vectors,
        new_qkv,
        new_out,
        new_up,
        new_down,
        new_vectors,
    )


def solution(mesh):
    rows, owned, spread = P(AXES, None), P("zero", None), P(None, "zero")
    state = (owned, owned, owned, owned, spread)
    return jax.shard_map(
        functools.partial(on_device, (mesh.shape["dp"], mesh.shape["zero"])),
        mesh=mesh,
        in_specs=(rows, P(AXES), rows) + state * 3,
        out_specs=(rows, rows) + state * 3,
        check_vma=False,
    )
```

```python
import functools

import jax
import jax.numpy as jnp
from jax import lax
from jax.experimental import pallas as pl
from jax.experimental.pallas import tpu as pltpu
from jax.sharding import PartitionSpec as P

HEAD_DIM = 64
ROT_DIM = 16
STEP = 10
EPS_NORM = 1e-05
BETA_ONE = 0.9
BETA_TWO = 0.999
ADAM_EPS = 1e-08
RATE_MATRIX = 0.05
RATE_VECTOR = 0.2
DECAY_MATRIX = 0.1
ROPE_BASE = 10000.0
INV_ROOT_TWO = 0.7071067811865476
INV_ROOT_TAU = 0.3989422804014327
MASKED = -1e30
LANES = 128
AXES = ("dp", "zero")
F32 = jnp.float32
BF16 = jnp.bfloat16
VMEM_LIMIT = 58 * 1024 * 1024


def spec(block, index, single=False):
    if single:
        return pl.BlockSpec(block, index, pipeline_mode=pl.Buffered(1))
    return pl.BlockSpec(block, index)


def whole(shape):
    return spec(shape, lambda *_: (0,) * len(shape), single=True)


def scalars():
    return pl.BlockSpec(memory_space=pltpu.SMEM)


def kernel_call(body, grid, in_specs, out_specs, out_shape, flops, moved, scratch=(), name=None):
    return pl.pallas_call(
        body,
        grid=grid,
        in_specs=in_specs,
        out_specs=out_specs,
        out_shape=out_shape,
        scratch_shapes=list(scratch),
        cost_estimate=pl.CostEstimate(flops=int(flops), bytes_accessed=int(moved), transcendentals=0),
        compiler_params=pltpu.CompilerParams(
            vmem_limit_bytes=VMEM_LIMIT, dimension_semantics=("arbitrary",) * len(grid)
        ),
        name=name,
    )


def nn(left, right):
    return lax.dot_general(left, right, (((1,), (0,)), ((), ())), preferred_element_type=F32)


def nt(left, right):
    return lax.dot_general(left, right, (((1,), (1,)), ((), ())), preferred_element_type=F32)


def tn(left, right):
    return lax.dot_general(left, right, (((0,), (0,)), ((), ())), preferred_element_type=F32)


def piece_owner(ids, place):
    step = place % 4
    if step > 1:
        step = 2 + ids[2] if step == 2 else 3 - ids[2]
    return jnp.bitwise_xor(ids[0], 2 * step + place // 4)


SLOTS = ((0, 0), (1, 0), (2, 0), (2, 1), (0, 1), (1, 1), (3, 0), (3, 1))


def slot_owner(ids, slot):
    step, side = SLOTS[slot]
    if step > 1:
        step = 2 + ids[2] if step == 2 else 3 - ids[2]
    return jnp.bitwise_xor(ids[0], 2 * step + side)


def slot_ref(outs, slot):
    return (outs[0], slot) if slot < 4 else (outs[1], slot - 4) if slot < 6 else (outs[2], slot - 6)


def low_lanes():
    return lax.broadcasted_iota(jnp.int32, (1, LANES), 1) < HEAD_DIM


def pick_parity(core, tile_a, tile_b):
    low = low_lanes()
    even = jnp.where(low, tile_a, pltpu.roll(tile_b, HEAD_DIM, 1))
    odd = jnp.where(low, pltpu.roll(tile_a, HEAD_DIM, 1), tile_b)
    return jnp.where(core == 0, even, odd)


def prep_attn_body(ids, w_qkv, w_out, out):
    core = ids[1]
    for part in range(3):
        for tile in range(2):
            base = part * 1024 + tile * 256
            at = part * 256 + tile * 128
            out[:, at : at + 128] = pick_parity(
                core, w_qkv[:, base : base + 128], w_qkv[:, base + 128 : base + 256]
            ).astype(BF16)
    rows = w_out[pl.ds(pl.multiple_of(core * 64, 64), 64), :].astype(BF16)
    for panel in range(4):
        at = 768 + 256 * (panel // 2)
        base = (panel % 2) * 64
        out[base : base + 64, at : at + 256] = rows[:, 256 * panel : 256 * panel + 256]


def prep_mlp_body(ids, w_up, w_down, w_qkv, out_a, out_b):
    core = ids[1]
    for part, out in enumerate((out_a, out_b)):
        for owner in range(8):
            start = pl.multiple_of(owner * 512 + part * 256 + core * 128, 128)
            out[0:128, owner * 128 : (owner + 1) * 128] = w_up[:, pl.ds(start, 128)].astype(BF16)
        out[128:256, :] = w_down[pl.ds(pl.multiple_of(part * 256 + core * 128, 128), 128), :].astype(BF16)
    for part in range(3):
        for tile in range(2):
            base = part * 1024 + 512 + tile * 256
            value = pick_parity(core, w_qkv[:, base : base + 128], w_qkv[:, base + 128 : base + 256]).astype(BF16)
            for panel in range(4):
                at = panel * 256 + tile * 128
                out_b[256 + 32 * part : 288 + 32 * part, at : at + 128] = value[32 * panel : 32 * panel + 32]


def join_vec_body(ids, pieces, vec, bias):
    for step in range(8):
        owner = jnp.bitwise_xor(ids[0], 2 * (step & 3) + step // 4)
        vec[:, pl.ds(pl.multiple_of(owner * 128, 128), 128)] = pieces[step].astype(F32)
    for part in range(3):
        for tile in range(4):
            base = tile * 256
            row = slice(4 + part, 5 + part)
            at = (tile // 2) * 768 + part * 256 + (tile % 2) * 128
            bias[:, at : at + 128] = pick_parity(
                ids[1], vec[row, base : base + 128], vec[row, base + 128 : base + 256]
            )


def normalize(inputs):
    centred = inputs - jnp.mean(inputs, axis=-1, keepdims=True)
    variance = jnp.mean(centred * centred, axis=-1, keepdims=True)
    inv_std = lax.rsqrt(variance + EPS_NORM)
    return centred * inv_std, inv_std


def turned(x, cos, sin_lo, sin_hi, sign):
    return x * cos[...] + sign * (pltpu.roll(x, 8, 1) * sin_hi[...] + pltpu.roll(x, 120, 1) * sin_lo[...])


def project(group, rows, w_qkv, bias, tables, outs):
    for part, out in enumerate(outs):
        cols = slice(part * 256, (part + 1) * 256)
        at = group * 768 + part * 256
        acc = nn(rows, w_qkv[:, cols]) + bias[:, at : at + 256]
        if part == 2:
            out[...] = acc.astype(BF16)
            continue
        for tile in range(2):
            x = turned(acc[:, tile * 128 : (tile + 1) * 128], *tables, 1.0)
            if part == 0:
                x = x * HEAD_DIM ** (-0.5)
            out[:, tile * 128 : (tile + 1) * 128] = x.astype(BF16)


def qkv_first_body(steps, ids, *refs):
    pieces, refs = refs[:8], refs[8:]
    tok_own, tok_other, dy_own, dy_other, vec, bias, cos, sin_lo, sin_hi = refs[:9]
    q, k, v, d_att, attn_in, attn_t, mlp_in, w_qkv, w_out = refs[9:]
    step = pl.program_id(0)

    @pl.when(step == 0)
    def _():
        for place, piece in enumerate(pieces):
            owner = piece_owner(ids, place)
            w_qkv[pl.ds(pl.multiple_of(owner * 128, 128), 128), :] = piece[:, 0:768]
            for panel in range(4):
                at = 768 + 256 * (panel // 2)
                base = (panel % 2) * 64
                w_out[pl.ds(pl.multiple_of(owner * 64, 64), 64), 256 * panel : 256 * panel + 256] = piece[
                    base : base + 64, at : at + 256
                ]

    first = step < steps // 2
    d_att[...] = nt(jnp.where(first, dy_own[...], dy_other[...]), w_out[...]).astype(BF16)
    normed, _ = normalize(jnp.where(first, tok_own[...], tok_other[...]).astype(F32))
    rows = (normed * vec[0:1, :] + vec[1:2, :]).astype(BF16)
    mlp_in[...] = (normed * vec[2:3, :] + vec[3:4, :]).astype(BF16)
    attn_in[...] = rows
    attn_t[...] = rows.T
    project(0, rows, w_qkv, bias, (cos, sin_lo, sin_hi), (q, k, v))


def qkv_second_body(ids, *refs):
    pieces, (attn_in, bias, cos, sin_lo, sin_hi, q, k, v, w_qkv) = refs[:8], refs[8:]

    @pl.when(pl.program_id(0) == 0)
    def _():
        for place, piece in enumerate(pieces):
            owner = piece_owner(ids, place)
            for part in range(3):
                for panel in range(4):
                    at = pl.ds(pl.multiple_of(owner * 128 + 32 * panel, 32), 32)
                    w_qkv[at, part * 256 : part * 256 + 256] = piece[
                        256 + 32 * part : 288 + 32 * part, panel * 256 : panel * 256 + 256
                    ]

    project(1, attn_in[...], w_qkv, bias, (cos, sin_lo, sin_hi), (q, k, v))


ATTN_ROWS = 256


def cat(parts, axis=0):
    return jnp.concatenate(parts, axis=axis) if len(parts) > 1 else parts[0]


def attn_body(q, k, v, d_att, seg_col, seg_row, cos, sin_lo, sin_hi, att, grad):
    count = q.shape[0]
    size = ATTN_ROWS
    blocks = count // size
    span = [slice(j * size, (j + 1) * size) for j in range(blocks)]
    low = low_lanes()
    zero = jnp.zeros((), BF16)
    causal = lax.broadcasted_iota(jnp.int32, (size, size), 0) >= lax.broadcasted_iota(
        jnp.int32, (size, size), 1
    )
    q_t, da_t = q[...].T, d_att[...].T

    def row_total(parts, reduce, join):
        cols = [reduce(part, axis=-1, keepdims=True) for part in parts]
        return [
            functools.reduce(join, [cols[j][(i - j) * size : (i - j + 1) * size] for j in range(i + 1)])
            for i in range(blocks)
        ]

    def row_sum(parts):
        return cat(
            [
                functools.reduce(jnp.add, [parts[j][(i - j) * size : (i - j + 1) * size] for j in range(i + 1)])
                for i in range(blocks)
            ]
        )

    def products(half):
        lanes = low if half == 0 else jnp.logical_not(low)
        q_h = jnp.where(lanes, q[...], zero)
        da_h = jnp.where(lanes, d_att[...], zero)
        scores = [nt(q_h[j * size :], k[span[j], :]) for j in range(blocks)]
        return scores, [nt(da_h[j * size :], v[span[j], :]) for j in range(blocks)]

    def softmax_both(scores, grad_probs):
        masked = []
        for j in range(blocks):
            allowed = seg_col[j * size :, :] == seg_row[0, :, span[j]]
            allowed = cat([allowed[:size] & causal] + ([allowed[size:]] if j < blocks - 1 else []))
            masked.append(jnp.where(allowed, scores[j], MASKED))
        top = row_total(masked, jnp.max, jnp.maximum)
        raised = [jnp.exp(masked[j] - cat(top[j:])) for j in range(blocks)]
        inv = [1.0 / total for total in row_total(raised, jnp.sum, jnp.add)]
        probs = [raised[j] * cat(inv[j:]) for j in range(blocks)]
        delta = row_total([g * p for g, p in zip(grad_probs, probs)], jnp.sum, jnp.add)
        grad_scores = [
            (probs[j] * (grad_probs[j] - cat(delta[j:]))).astype(BF16) for j in range(blocks)
        ]
        return [p.astype(BF16) for p in probs], grad_scores

    def results(half, probs, grad_scores):
        rows = slice(half * HEAD_DIM, (half + 1) * HEAD_DIM)
        return (
            row_sum([nn(probs[j], v[span[j], :]) for j in range(blocks)]),
            row_sum([nn(grad_scores[j], k[span[j], :]) for j in range(blocks)]),
            cat([nn(q_t[rows, j * size :], grad_scores[j]) for j in range(blocks)], 1),
            cat([nn(da_t[rows, j * size :], probs[j]) for j in range(blocks)], 1),
        )

    first = softmax_both(*products(0))
    second = products(1)
    out_a, dq_a, dk_a, dv_a = results(0, *first)
    out_b, dq_b, dk_b, dv_b = results(1, *softmax_both(*second))
    tables = (cos, sin_lo, sin_hi)
    att[...] = jnp.where(low, out_a, out_b).astype(BF16)
    grad[0] = turned(jnp.where(low, dq_a, dq_b) * HEAD_DIM ** (-0.5), *tables, -1.0).astype(BF16)
    grad[1] = turned(jnp.concatenate([dk_a, dk_b], axis=0).T, *tables, -1.0).astype(BF16)
    grad[2] = jnp.concatenate([dv_a, dv_b], axis=0).T.astype(BF16)


def attn_weights_body(ids, attn_t, grad_a, grad_b, att_a, att_b, dy_own, dy_other, keep, send_x, send_y, bias, result):
    step = pl.program_id(0)
    outs = (keep, send_x, send_y)

    @pl.when(step < 6)
    def _():
        rhs = jnp.where(step < 3, grad_a[0], grad_b[0])
        result[...] = nn(attn_t[...], rhs).astype(BF16)
        cols = pl.ds(pl.multiple_of(step * 256, 256), 256)
        bias[0:1, cols] = jnp.sum(rhs.astype(F32), axis=0, keepdims=True)
        for slot in range(8):
            out, at = slot_ref(outs, slot)
            base = pl.multiple_of(slot_owner(ids, slot) * 128, 128)
            out[at, :, cols] = result[pl.ds(base, 128), :]

    @pl.when(step == 6)
    def _():
        count = dy_own.shape[0]
        for group, att in enumerate((att_a, att_b)):
            flipped = att[...].T
            for panel in range(4):
                cols = slice(panel * 256, panel * 256 + 256)
                term = nn(flipped[:, :count], dy_own[:, cols]) + nn(flipped[:, count:], dy_other[:, cols])
                result[group * 256 : group * 256 + 256, :] = term.astype(BF16)
                for slot in range(8):
                    out, at = slot_ref(outs, slot)
                    owner = slot_owner(ids, slot)
                    col = 1536 + 256 * (panel // 2)
                    base = (panel % 2) * 64

                    @pl.when(owner // 4 == group)
                    def _():
                        out[at, base : base + 64, col : col + 256] = result[
                            pl.ds(pl.multiple_of(owner * 64, 64), 64), :
                        ]


def mlp_body(part, steps, ids, *refs):
    pieces = refs[:8]
    vec, mlp_in, dy_own, dy_other, keep, send_x, send_y, hidden_out, grad_out, sums, w_up, w_down = refs[8:-6]
    mlp_t, hidden_t, grad_pre, dy, bias, result = refs[-6:]
    outs = (keep, send_x, send_y)
    core = ids[1]
    step = pl.program_id(0)

    @pl.when(step == 0)
    def _():
        for owner in range(8):
            start = pl.multiple_of((owner % 2) * 512 + part * 256 + core * 128, 128)
            row = 8 + owner // 2
            bias[0:1, owner * 128 : (owner + 1) * 128] = vec[row : row + 1, pl.ds(start, 128)]
        sums[...] = jnp.zeros_like(sums)
        for place, piece in enumerate(pieces):
            at = pl.ds(pl.multiple_of(piece_owner(ids, place) * 128, 128), 128)
            w_up[at, :] = piece[0:128, :]
            w_down[at, :] = piece[128:256, :]

    rows = mlp_in[...]
    grads = jnp.where(step < steps // 2, dy_own[...], dy_other[...])
    count = rows.shape[0]
    at = pl.ds(pl.multiple_of(step * count, count), count)
    mlp_t[:, at] = rows.T
    dy[at, :] = grads
    sums[1:2, :] += jnp.sum(grads.astype(F32), axis=0, keepdims=True)
    for col in range(0, 1024, 256):
        cols = slice(col, col + 256)
        pre = nn(rows, w_up[:, cols]) + bias[0:1, cols]
        grad_hidden = nt(grads, w_down[cols, :])
        cdf = 0.5 + 0.5 * lax.erf(pre * INV_ROOT_TWO)
        pdf = jnp.exp(-0.5 * pre * pre) * INV_ROOT_TAU
        act = (pre * cdf).astype(BF16)
        hidden_t[cols, at] = act.T
        hidden_out[:, cols] = act
        gp = (grad_hidden * (cdf + pre * pdf)).astype(BF16)
        grad_pre[at, cols] = gp
        grad_out[:, cols] = gp
        sums[0:1, cols] += jnp.sum(gp.astype(F32), axis=0, keepdims=True)

    @pl.when(step == steps - 1)
    def _():
        for base_row, left, right in ((0, mlp_t, grad_pre), (128, hidden_t, dy)):
            for col in range(0, 1024, 512):
                cols = slice(col, col + 512)
                result[...] = nn(left[...], right[:, cols]).astype(BF16)
                for slot in range(8):
                    out, place = slot_ref(outs, slot)
                    base = pl.multiple_of(slot_owner(ids, slot) * 128, 128)
                    out[place, base_row : base_row + 128, cols] = result[pl.ds(base, 128), :]


def back_body(own, grad_a, grad_b, att_a, att_b, hid_a, hid_b, gp_a, gp_b, wq_a, wq_b, w_out, up_a, up_b, down_a, down_b, tok, vec, *refs):
    if own:
        dy, out_other, scaled_other, out, result, sums = refs
    else:
        out, result, sums = refs
    inputs = tok[...].astype(F32)
    normed, inv_std = normalize(inputs)
    branch = nn(att_a[...], w_out[0:256, :]) + nn(att_b[...], w_out[256:512, :])
    back_mlp = None
    for hid, gp, up, down in ((hid_a, gp_a, up_a, down_a), (hid_b, gp_b, up_b, down_b)):
        branch = branch + nn(hid[...], down[...])
        term = nt(gp[...], up[...])
        back_mlp = term if back_mlp is None else back_mlp + term
    back_attn = None
    for grad, w in ((grad_a, wq_a), (grad_b, wq_b)):
        for part in range(3):
            term = nt(grad[part], w[:, part * 256 : part * 256 + 256])
            back_attn = term if back_attn is None else back_attn + term
    scaled = back_attn * vec[0:1, :] + back_mlp * vec[2:3, :]

    @pl.when(pl.program_id(0) == 0)
    def _():
        sums[...] = jnp.zeros_like(sums)

    for row, value in enumerate((back_attn * normed, back_attn, back_mlp * normed, back_mlp)):
        sums[row : row + 1, :] += jnp.sum(value, axis=0, keepdims=True)
    if not own:
        out[...] = branch.astype(BF16)
        result[...] = scaled.astype(BF16)
        return
    branch = branch + out_other[...].astype(F32)
    out[...] = (inputs + branch + (vec[7:8, :] + vec[12:13, :])).astype(BF16)
    scaled = scaled + scaled_other[...].astype(F32)
    result[...] = dy[...].astype(F32) + inv_std * (
        scaled
        - jnp.mean(scaled, axis=-1, keepdims=True)
        - normed * jnp.mean(scaled * normed, axis=-1, keepdims=True)
    )


def adam_math(weight, first, second, gradient, rate, decay):
    first_new = BETA_ONE * first + (1.0 - BETA_ONE) * gradient
    second_new = BETA_TWO * second + (1.0 - BETA_TWO) * gradient * gradient
    first_hat = first_new / (1.0 - BETA_ONE**STEP)
    second_hat = second_new / (1.0 - BETA_TWO**STEP)
    weight_new = weight - rate * (first_hat / (jnp.sqrt(second_hat) + ADAM_EPS) + decay * weight)
    return (first_new, second_new, weight_new)


def adam_store(refs, at, gradient):
    w, m, v, m_out, v_out, w_out = refs
    first, second, weight = adam_math(w[at], m[at], v[at], gradient, RATE_MATRIX, DECAY_MATRIX)
    m_out[at] = first
    v_out[at] = second
    w_out[at] = weight


def parities(core, own, other):
    return jnp.where(core == 0, own, other), jnp.where(core == 0, other, own)


def adam_attn_body(ids, own, other, *refs):
    core = ids[1]
    low = low_lanes()
    qkv_refs = refs[0:3] + refs[6:9]
    for tile in range(4):
        start = (tile // 2) * 768 + (tile % 2) * 128
        cols = pl.ds(pl.multiple_of(pl.program_id(0) * 256 + start, 128), 128)
        even, odd = parities(core, own[:, cols].astype(F32), other[:, cols].astype(F32))
        first = jnp.where(low, even, pltpu.roll(odd, HEAD_DIM, 1))
        second = jnp.where(low, pltpu.roll(even, HEAD_DIM, 1), odd)
        adam_store(qkv_refs, (slice(None), slice(tile * 256, tile * 256 + 128)), first)
        adam_store(qkv_refs, (slice(None), slice(tile * 256 + 128, tile * 256 + 256)), second)

    @pl.when(pl.program_id(0) == 0)
    def _():
        out_refs = refs[3:6] + refs[9:12]
        for panel in range(4):
            rows = slice((panel % 2) * 64, (panel % 2) * 64 + 64)
            cols = slice(1536 + 256 * (panel // 2), 1792 + 256 * (panel // 2))
            span = slice(panel * 256, panel * 256 + 256)
            even, odd = parities(core, own[rows, cols].astype(F32), other[rows, cols].astype(F32))
            adam_store(out_refs, (slice(0, 64), span), even)
            adam_store(out_refs, (slice(64, 128), span), odd)


def adam_mlp_body(ids, own, other, *refs):
    core = ids[1]
    up_refs = refs[0:3] + refs[-6:-3]
    down_refs = refs[3:6] + refs[-3:]
    cols = pl.ds(pl.multiple_of(pl.program_id(0) * 128, 128), 128)
    for base, refs_of in ((0, up_refs), (128, down_refs)):
        rows = slice(base, base + 128)
        for parity, grad in enumerate(
            parities(core, own[rows, cols].astype(F32), other[rows, cols].astype(F32))
        ):
            span = slice(parity * 128, (parity + 1) * 128)
            adam_store(refs_of, (slice(None), span) if base == 0 else (span, slice(None)), grad)


def rotary_tables(segments):
    row_count = segments.shape[0]
    row_index = jnp.arange(row_count, dtype=jnp.int32)
    earlier = jnp.concatenate([jnp.full((1,), -1, jnp.int32), segments[:-1]])
    starts = jnp.where(segments != earlier, row_index, 0)
    position = (row_index - lax.cummax(starts, axis=0)).astype(F32)
    half_dim = ROT_DIM // 2
    dims = jnp.arange(LANES, dtype=jnp.int32) % HEAD_DIM
    frequency = ROPE_BASE ** (-2.0 * (dims % half_dim).astype(F32) / ROT_DIM)
    turned = dims < ROT_DIM
    angles = position[:, None] * jnp.where(turned, frequency, 0.0)[None, :]
    cosine, sine = jnp.cos(angles), jnp.sin(angles)
    front = (dims < half_dim)[None, :]
    return cosine, jnp.where(front, -sine, 0.0), jnp.where(front, 0.0, sine)


def on_device(
    sizes,
    tokens,
    segments,
    cotangent,
    w_qkv,
    w_out,
    w_up,
    w_down,
    vectors,
    m_qkv,
    m_out,
    m_up,
    m_down,
    m_vectors,
    v_qkv,
    v_out,
    v_up,
    v_down,
    v_vectors,
):
    copies, owners = sizes
    me = lax.axis_index("zero")
    plane = lax.axis_index("dp")
    core = plane % 2
    ids = jnp.stack([me, core, (plane // 2) % 2]).astype(jnp.int32)

    def move(value, target):
        pairs = []
        for d in range(copies):
            for z in range(owners):
                to_d, to_z = target(d, z)
                pairs.append((d * owners + z, to_d * owners + to_z))
        return lax.ppermute(value, AXES, pairs)

    def swap(value, dp_bits, zero_bits):
        return move(value, lambda d, z: (d ^ dp_bits, z ^ zero_bits))

    def swap_far(value):
        return move(value, lambda d, z: (d, z ^ (6 if d & 2 else 4)))

    def sync(*values):
        return lax.optimization_barrier(values)

    def add(*terms):
        return functools.reduce(jnp.add, [t.astype(F32) for t in terms])

    def reduce_first(keep, send_x, send_y):
        return keep, swap(send_x, 0, 1), swap(send_y, 2, 0)

    def reduce_second(state):
        keep, got_x, got_y = state
        far = add(keep[3], got_y[1]).astype(BF16)
        near = add(keep[1], got_x[1]).astype(BF16)
        return keep, got_x, got_y, far, near, swap(far, 0, 1), swap(near, 0, 2)

    def reduce_third(state):
        keep, got_x, got_y, _, _, got_far, got_near = state
        far = add(keep[2], got_y[0], got_far).astype(BF16)
        return add(keep[0], got_x[0], got_near), far, swap_far(far)

    def reduce_fourth(state):
        total = (state[0] + state[2].astype(F32)).astype(BF16)
        return total, swap(total, 2, 0)

    def reduce_fifth(state):
        total = add(*state).astype(BF16)
        bit = 4
        while bit < copies:
            total = add(total, swap(total, bit, 0)).astype(BF16)
            bit *= 2
        return total, swap(total, 1, 0)

    T, width = tokens.shape
    rows = 2 * T
    sds = jax.ShapeDtypeStruct
    row_block = lambda n, c=width: spec((n, c), lambda i: (i, 0))
    col_block = lambda n: spec((width, n), lambda i: (0, i))

    def block_call(body, grid, ins, outs, flops, moved, scratch=(), name=None):
        return kernel_call(
            body,
            grid,
            [place for _, place in ins],
            [place for _, place in outs],
            [shape for shape, _ in outs],
            flops,
            moved,
            scratch=scratch,
            name=name,
        )(*[value for value, _ in ins])

    def const(value):
        return value, whole(value.shape)

    def kept(shape, dtype):
        return sds(shape, dtype), whole(shape)

    steps = rows // 256
    with jax.named_scope("prep"):
        own_a = block_call(
            prep_attn_body,
            (1,),
            [(ids, scalars()), const(w_qkv), const(w_out)],
            [kept((128, 1280), BF16)],
            0,
            3e6,
            name="prep_attn",
        )[0]
        own_b, own_c = block_call(
            prep_mlp_body,
            (1,),
            [(ids, scalars()), const(w_up), const(w_down), const(w_qkv)],
            [kept((256, 1024), BF16), kept((352, 1024), BF16)],
            0,
            6e6,
            name="prep_mlp",
        )

    def z_moves(own):
        return swap(own, 0, 2), swap_far(own)

    with jax.named_scope("gather"):
        next_a, far_a = z_moves(own_a)
        across_a = swap(own_a, 0, 1)
        seg_other = swap(segments, 1, 0)
        vec_pieces = jnp.pad(vectors, ((0, 3), (0, 0))).astype(BF16)[None]
        next_a, far_a, across_a, own_b, own_c, seg_other, vec_pieces = sync(
            next_a, far_a, across_a, own_b, own_c, seg_other, vec_pieces
        )
        next_across_a, far_across_a, rest_a = swap(next_a, 0, 1), swap(far_a, 0, 1), swap(far_a, 2, 0)
        next_b, far_b = z_moves(own_b)
        tok_other = swap(tokens, 1, 0)
        dy_other = swap(cotangent, 1, 0)
        for bits in (2, 4):
            vec_pieces = jnp.concatenate([vec_pieces, swap(vec_pieces, 0, bits)], axis=0)

    with jax.named_scope("rows"):
        tables = [
            jnp.concatenate(pair, axis=0)
            for pair in zip(rotary_tables(segments), rotary_tables(seg_other))
        ]
        seg_row = jnp.stack([segments, seg_other])[:, None, :]
        seg_col = jnp.concatenate([segments, seg_other])[:, None]

    (next_across_a, far_across_a, rest_a, next_b, far_b, own_c, tables, seg_row, seg_col, tok_other, dy_other) = sync(
        next_across_a, far_across_a, rest_a, next_b, far_b, own_c, tables, seg_row, seg_col, tok_other, dy_other
    )
    with jax.named_scope("gather"):
        vec_pieces = jnp.concatenate([vec_pieces, swap(vec_pieces, 0, 1)], axis=0)
        rest_across_a = swap(far_across_a, 2, 0)
        far_across_b, next_across_b, rest_b = swap(far_b, 0, 1), swap(next_b, 0, 1), swap(far_b, 2, 0)
        next_c, far_c = z_moves(own_c)
        vec, bias_qkv = block_call(
            join_vec_body,
            (1,),
            [(ids, scalars()), const(vec_pieces)],
            [kept((16, 1024), F32), kept((1, 1536), F32)],
            0,
            1e5,
            name="join_vec",
        )
    attn_pieces = [own_a, next_a, far_a, rest_a, across_a, next_across_a, far_across_a, rest_across_a]

    def table_blocks(count):
        return [(t, row_block(count, 128)) for t in tables]

    def halves(own, other, count):
        last = T // count - 1
        return [
            (own, spec((count, width), lambda i: (jnp.minimum(i, last), 0))),
            (other, spec((count, width), lambda i: (jnp.maximum(i - last - 1, 0), 0))),
        ]

    def attention(group, projected, d_att):
        with jax.named_scope("attention"):
            head_block = spec((T, 128), lambda h, m: (h, m))
            return block_call(
                attn_body,
                (2, 2),
                [(value, head_block) for value in projected]
                + [(d_att, spec((T, 128), lambda h, m: (h, m + 2 * group)))]
                + [(seg_col, spec((T, 1), lambda h, m: (h, 0)))]
                + [(seg_row, spec((1, 1, T), lambda h, m: (h, 0, 0)))]
                + [(t, spec((T, 128), lambda h, m: (h, 0))) for t in tables],
                [
                    (sds((rows, 256), BF16), head_block),
                    (sds((3, rows, 256), BF16), spec((3, T, 128), lambda h, m: (0, h, m))),
                ],
                30e9,
                10e6,
                name="attention",
            )

    def blocks_of(shape):
        return [kept((n,) + shape, BF16) for n in (4, 2, 2)]

    with jax.named_scope("qkv"):
        *projected, d_att, attn_in, attn_t, mlp_in, wq_a, full_out = block_call(
            functools.partial(qkv_first_body, rows // 256),
            (rows // 256,),
            [(ids, scalars())]
            + [const(piece) for piece in attn_pieces]
            + halves(tokens, tok_other, 256)
            + halves(cotangent, dy_other, 256)
            + [const(vec), const(bias_qkv)]
            + table_blocks(256),
            [(sds((rows, 256), BF16), row_block(256, 256))] * 3
            + [(sds((rows, 512), BF16), row_block(256, 512)), (sds((rows, width), BF16), row_block(256))]
            + [(sds((width, rows), BF16), col_block(256)), (sds((rows, width), BF16), row_block(256))]
            + [kept((1024, 768), BF16), kept((512, 1024), BF16)],
            2 * rows * 1024 * 1280,
            30e6,
            name="qkv",
        )
    projected, far_across_b, next_across_b, rest_b, own_b, next_c, far_c = sync(
        projected, far_across_b, next_across_b, rest_b, own_b, next_c, far_c
    )
    with jax.named_scope("gather"):
        rest_across_b, across_b = swap(far_across_b, 2, 0), swap(own_b, 0, 1)
        far_across_c, rest_c = swap(far_c, 0, 1), swap(far_c, 2, 0)
    att_a, grad_a = attention(0, projected, d_att)
    att_a, grad_a, rest_across_b, across_b, far_across_c, rest_c, own_c, next_c, attn_t, mlp_in = sync(
        att_a, grad_a, rest_across_b, across_b, far_across_c, rest_c, own_c, next_c, attn_t, mlp_in
    )
    with jax.named_scope("gather"):
        across_c, next_across_c, rest_across_c = swap(own_c, 0, 1), swap(next_c, 0, 1), swap(far_across_c, 2, 0)
    pieces_b = [own_b, next_b, far_b, rest_b, across_b, next_across_b, far_across_b, rest_across_b]

    def mlp(part, weights, rows_in):
        with jax.named_scope("mlp"):
            *results, hid, gp, sums, w_up_full, w_down_full = block_call(
                functools.partial(mlp_body, part, steps),
                (steps,),
                [(ids, scalars())]
                + [const(w) for w in weights]
                + [const(vec), (rows_in, row_block(256))]
                + halves(cotangent, dy_other, 256),
                blocks_of((256, 1024))
                + [(sds((rows, width), BF16), row_block(256))] * 2
                + [kept((8, 1024), F32)]
                + [kept((1024, 1024), BF16)] * 2,
                2 * rows * 1024 * 1024 * 4,
                40e6,
                scratch=[
                    pltpu.VMEM((1024, rows), BF16),
                    pltpu.VMEM((1024, rows), BF16),
                    pltpu.VMEM((rows, 1024), BF16),
                    pltpu.VMEM((rows, 1024), BF16),
                    pltpu.VMEM((8, 1024), F32),
                    pltpu.VMEM((1024, 512), BF16),
                ],
                name="mlp",
            )
            return results, hid, gp, sums, w_up_full, w_down_full

    mlp_a = mlp(0, pieces_b, mlp_in)
    mlp_a, mlp_in, across_c, next_across_c, rest_across_c = sync(
        mlp_a, mlp_in, across_c, next_across_c, rest_across_c
    )
    pieces_c = [own_c, next_c, far_c, rest_c, across_c, next_across_c, far_across_c, rest_across_c]
    reduce_a = reduce_first(*mlp_a[0])
    mlp_b = mlp(1, pieces_c, mlp_in)
    mlp_b, reduce_a, attn_in = sync(mlp_b, reduce_a, attn_in)
    reduce_a = reduce_second(reduce_a)
    reduce_b = reduce_first(*mlp_b[0])
    attn_in, *ready = sync(attn_in, *reduce_a[3:5])

    with jax.named_scope("qkv"):
        *projected, wq_b = block_call(
            qkv_second_body,
            (rows // 512,),
            [(ids, scalars())]
            + [const(piece) for piece in pieces_c]
            + [(attn_in, row_block(512)), const(bias_qkv)]
            + table_blocks(512),
            [(sds((rows, 256), BF16), row_block(512, 256))] * 3 + [kept((1024, 768), BF16)],
            2 * rows * 1024 * 768,
            12e6,
            name="qkv",
        )
    att_b, grad_b = attention(1, projected, d_att)
    att_b, grad_b, reduce_a, reduce_b = sync(att_b, grad_b, reduce_a, reduce_b)
    reduce_a = reduce_third(reduce_a)
    reduce_b = reduce_second(reduce_b)
    grad_b, *ready = sync(grad_b, reduce_a[1], *reduce_b[3:5])
    with jax.named_scope("attn_weights"):
        *blocks, bias_sum = block_call(
            attn_weights_body,
            (7,),
            [(ids, scalars()), const(attn_t)]
            + [(grad_a, spec((1, rows, 256), lambda n: (jnp.minimum(n, 2), 0, 0)))]
            + [(grad_b, spec((1, rows, 256), lambda n: (jnp.clip(n - 3, 0, 2), 0, 0)))]
            + [const(value) for value in (att_a, att_b, cotangent, dy_other)],
            blocks_of((128, 2048)) + [kept((8, 1536), F32)],
            2 * rows * 1024 * 2048,
            24e6,
            scratch=[pltpu.VMEM((1024, 256), BF16)],
            name="attn_weights",
        )
    blocks, grad_b = sync(blocks, grad_b)
    reduce_o = reduce_first(*blocks)

    _, hid_a, gp_a, sums_a, up_a, down_a = mlp_a
    _, hid_b, gp_b, sums_b, up_b, down_b = mlp_b

    def adam_mlp(part, totals, previous):
        wide = [spec((128, 256), lambda n: (0, 2 * n + part))] * 3
        wide += [spec((256, 128), lambda n: (part, n))] * 3
        return pl.pallas_call(
            adam_mlp_body,
            grid=(8,),
            in_specs=[scalars()]
            + [whole((256, 1024))] * 2
            + wide
            + [pl.BlockSpec(memory_space=pl.ANY)] * len(previous),
            out_specs=wide,
            out_shape=[sds((128, 4096), F32)] * 3 + [sds((512, 1024), F32)] * 3,
            input_output_aliases={9 + n: n for n in range(len(previous))},
            cost_estimate=pl.CostEstimate(flops=0, bytes_accessed=14000000, transcendentals=0),
            compiler_params=pltpu.CompilerParams(
                vmem_limit_bytes=VMEM_LIMIT, dimension_semantics=("arbitrary",)
            ),
            name="adam_mlp",
        )(ids, *totals, w_up, m_up, v_up, w_down, m_down, v_down, *previous)

    def back(own, grad, rows_tok, extra, outs):
        first = 0 if own else T // 256
        block = lambda c=width: spec((256, c), lambda i: (i + first, 0))
        lead = spec((3, 256, 256), lambda i: (0, i + first, 0))
        with jax.named_scope("back"):
            return block_call(
                functools.partial(back_body, own),
                (T // 256,),
                [(grad_a, lead), (grad, lead), (att_a, block(256)), (att_b, block(256))]
                + [(value, block()) for value in (hid_a, hid_b, gp_a, gp_b)]
                + [const(w) for w in (wq_a, wq_b, full_out, up_a, up_b, down_a, down_b)]
                + [(rows_tok, row_block(256)), const(vec)]
                + [(value, row_block(256)) for value in extra],
                [(sds((T, width), t), row_block(256)) for t in outs] + [kept((8, width), F32)],
                2 * T * 1024 * 6144,
                40e6,
                name="back",
            )

    reduce_a = reduce_fourth(reduce_a)
    reduce_b = reduce_third(reduce_b)
    out_part, scaled_part, sums_other = back(False, grad_b, tok_other, [], (BF16, BF16))
    out_part, scaled_part, sums_other, grad_b, reduce_a, reduce_b, reduce_o = sync(
        out_part, scaled_part, sums_other, grad_b, reduce_a, reduce_b, reduce_o
    )
    reduce_a = reduce_fifth(reduce_a)
    reduce_o = reduce_second(reduce_o)
    reduce_b = reduce_fourth(reduce_b)
    out_got, scaled_got = swap(out_part, 1, 0), swap(scaled_part, 1, 0)
    updated_mlp = adam_mlp(0, reduce_a, [])
    updated_mlp, grad_b, reduce_b, reduce_o, out_got, scaled_got = sync(
        updated_mlp, grad_b, reduce_b, reduce_o, out_got, scaled_got
    )
    reduce_o = reduce_third(reduce_o)
    reduce_b = reduce_fifth(reduce_b)
    grad_b, *ready = sync(grad_b, reduce_o[1], reduce_b[0])
    layer_out, tokens_grad, sums_own = back(
        True, grad_b, tokens, [cotangent, out_got, scaled_got], (BF16, F32)
    )
    sums_own, updated_mlp, reduce_b, reduce_o = sync(sums_own, updated_mlp, reduce_b, reduce_o)
    reduce_o = reduce_fourth(reduce_o)

    with jax.named_scope("vectors"):
        is_core = jnp.arange(2) == core
        grad_bias = jnp.where(core == 0, sums_a[1:2], 0.0)
        bias_sum = jnp.swapaxes(bias_sum[0].reshape(2, 3, 256), 0, 1)
        grad_bias_qkv = jnp.where(
            is_core[None, None, :, None], bias_sum.reshape(3, 8, 1, 64), 0.0
        ).reshape(3, width)
        grad_bias_up = jnp.where(
            is_core[None, None, :, None],
            jnp.swapaxes(jnp.stack([sums_a[0], sums_b[0]]).reshape(2, 8, 128), 0, 1)[:, :, None],
            0.0,
        ).reshape(4, width)
        total = jnp.concatenate(
            [
                sums_own[0:4] + sums_other[0:4],
                grad_bias_qkv,
                grad_bias,
                grad_bias_up,
                grad_bias,
                jnp.zeros((3, width), F32),
            ],
            axis=0,
        )
        for step in (2, 4):
            total = total + swap(total, 0, step)
        across, beside, both = swap(total, 0, 1), swap(total, 2, 0), swap(total, 2, 1)
        total = (total + across) + (beside + both)
        bit = 4
        while bit < copies:
            total = total + swap(total, bit, 0)
            bit *= 2
        total = total + swap(total, 1, 0)
        share = lax.dynamic_slice_in_dim(total[0:13], me * 128, 128, 1)
        first_vectors, second_vectors, new_vectors = adam_math(
            vectors, m_vectors, v_vectors, share, RATE_VECTOR, 0.0
        )

    updated_mlp = adam_mlp(1, reduce_b, updated_mlp)
    updated_mlp, reduce_o = sync(updated_mlp, reduce_o)
    reduce_o = reduce_fifth(reduce_o)
    with jax.named_scope("adam"):
        wide = [spec((128, 1024), lambda n: (0, n))] * 3 + [whole((128, 1024))] * 3
        updated_attn = kernel_call(
            adam_attn_body,
            (3,),
            [scalars()] + [whole((128, 2048))] * 2 + wide,
            wide,
            [sds((128, 3072), F32)] * 3 + [sds((128, 1024), F32)] * 3,
            0,
            13e6,
            name="adam_attn",
        )(ids, *reduce_o, w_qkv, m_qkv, v_qkv, w_out, m_out, v_out)
    first_qkv, second_qkv, new_qkv, first_out, second_out, new_out = updated_attn
    first_up, second_up, new_up, first_down, second_down, new_down = updated_mlp
    return (
        layer_out,
        tokens_grad,
        first_qkv,
        first_out,
        first_up,
        first_down,
        first_vectors,
        second_qkv,
        second_out,
        second_up,
        second_down,
        second_vectors,
        new_qkv,
        new_out,
        new_up,
        new_down,
        new_vectors,
    )


def solution(mesh):
    rows, owned, spread = P(AXES, None), P("zero", None), P(None, "zero")
    state = (owned, owned, owned, owned, spread)
    return jax.shard_map(
        functools.partial(on_device, (mesh.shape["dp"], mesh.shape["zero"])),
        mesh=mesh,
        in_specs=(rows, P(AXES), rows) + state * 3,
        out_specs=(rows, rows) + state * 3,
        check_vma=False,
    )
```

```python
import functools

import jax
import jax.numpy as jnp
from jax import lax
from jax.experimental import pallas as pl
from jax.experimental.pallas import tpu as pltpu
from jax.sharding import PartitionSpec as P

HEAD_DIM = 64
ROT_DIM = 16
STEP = 10
EPS_NORM = 1e-05
BETA_ONE = 0.9
BETA_TWO = 0.999
ADAM_EPS = 1e-08
RATE_MATRIX = 0.05
RATE_VECTOR = 0.2
DECAY_MATRIX = 0.1
ROPE_BASE = 10000.0
INV_ROOT_TWO = 0.7071067811865476
INV_ROOT_TAU = 0.3989422804014327
MASKED = -1e30
LANES = 128
AXES = ("dp", "zero")
F32 = jnp.float32
BF16 = jnp.bfloat16
MIB = 1024 * 1024
VMEM_NEED = 58


def spec(block, index, single=False):
    if single:
        return pl.BlockSpec(block, index, pipeline_mode=pl.Buffered(1))
    return pl.BlockSpec(block, index)


def whole(shape):
    return spec(shape, lambda *_: (0,) * len(shape), single=True)


def distant():
    return pl.BlockSpec(memory_space=pl.ANY)


def scalars():
    return pl.BlockSpec(memory_space=pltpu.SMEM)


def kernel_call(body, grid, in_specs, out_specs, out_shape, flops, moved, scratch=(), name=None):
    return pl.pallas_call(
        body,
        grid=grid,
        in_specs=in_specs,
        out_specs=out_specs,
        out_shape=out_shape,
        scratch_shapes=list(scratch),
        cost_estimate=pl.CostEstimate(flops=int(flops), bytes_accessed=int(moved), transcendentals=0),
        compiler_params=pltpu.CompilerParams(
            vmem_limit_bytes=VMEM_NEED * MIB, dimension_semantics=("arbitrary",) * len(grid)
        ),
        name=name,
    )


def nn(left, right):
    return lax.dot_general(left, right, (((1,), (0,)), ((), ())), preferred_element_type=F32)


def nt(left, right):
    return lax.dot_general(left, right, (((1,), (1,)), ((), ())), preferred_element_type=F32)


def tn(left, right):
    return lax.dot_general(left, right, (((0,), (0,)), ((), ())), preferred_element_type=F32)


def piece_owner(ids, place):
    step = place % 4
    if step > 1:
        step = 2 + ids[2] if step == 2 else 3 - ids[2]
    return jnp.bitwise_xor(ids[0], 2 * step + place // 4)


SLOTS = ((0, 0), (1, 0), (2, 0), (2, 1), (0, 1), (1, 1), (3, 0), (3, 1))


def slot_owner(ids, slot):
    step, side = SLOTS[slot]
    if step > 1:
        step = 2 + ids[2] if step == 2 else 3 - ids[2]
    return jnp.bitwise_xor(ids[0], 2 * step + side)


def slot_ref(outs, slot):
    return (outs[0], slot) if slot < 4 else (outs[1], slot - 4) if slot < 6 else (outs[2], slot - 6)


def low_lanes():
    return lax.broadcasted_iota(jnp.int32, (1, LANES), 1) < HEAD_DIM


def pick_parity(core, tile_a, tile_b):
    low = low_lanes()
    even = jnp.where(low, tile_a, pltpu.roll(tile_b, HEAD_DIM, 1))
    odd = jnp.where(low, pltpu.roll(tile_a, HEAD_DIM, 1), tile_b)
    return jnp.where(core == 0, even, odd)


def prep_attn_body(ids, w_qkv, w_out, vec, out):
    core = ids[1]
    for part in range(3):
        for tile in range(2):
            base = part * 1024 + tile * 256
            at = part * 256 + tile * 128
            out[0:128, at : at + 128] = pick_parity(
                core, w_qkv[:, base : base + 128], w_qkv[:, base + 128 : base + 256]
            ).astype(BF16)
    rows = w_out[pl.ds(pl.multiple_of(core * 64, 64), 64), :].astype(BF16)
    for panel in range(4):
        at = 768 + 256 * (panel // 2)
        base = (panel % 2) * 64
        out[base : base + 64, at : at + 256] = rows[:, 256 * panel : 256 * panel + 256]
    out[128:144, 0:128] = jnp.where(lax.broadcasted_iota(jnp.int32, (16, 128), 0) < 13, vec[...], 0.0).astype(BF16)
    out[128:144, 128:1280] = jnp.zeros((16, 1152), BF16)


def prep_mlp_body(ids, w_up, w_down, w_qkv, out_a, out_b):
    core = ids[1]
    for part, out in enumerate((out_a, out_b)):
        for owner in range(8):
            start = pl.multiple_of(owner * 512 + part * 256 + core * 128, 128)
            out[0:128, owner * 128 : (owner + 1) * 128] = w_up[:, pl.ds(start, 128)].astype(BF16)
        out[128:256, :] = w_down[pl.ds(pl.multiple_of(part * 256 + core * 128, 128), 128), :].astype(BF16)
    for part in range(3):
        for tile in range(2):
            base = part * 1024 + 512 + tile * 256
            value = pick_parity(core, w_qkv[:, base : base + 128], w_qkv[:, base + 128 : base + 256]).astype(BF16)
            for panel in range(4):
                at = panel * 256 + tile * 128
                out_b[256 + 32 * part : 288 + 32 * part, at : at + 128] = value[32 * panel : 32 * panel + 32]


def normalize(inputs):
    centred = inputs - jnp.mean(inputs, axis=-1, keepdims=True)
    variance = jnp.mean(centred * centred, axis=-1, keepdims=True)
    inv_std = lax.rsqrt(variance + EPS_NORM)
    return centred * inv_std, inv_std


def turned(x, cos, sin_lo, sin_hi, sign):
    return x * cos[...] + sign * (pltpu.roll(x, 8, 1) * sin_hi[...] + pltpu.roll(x, 120, 1) * sin_lo[...])


def project(group, rows, w_qkv, bias, tables, outs):
    for part, out in enumerate(outs):
        cols = slice(part * 256, (part + 1) * 256)
        at = group * 768 + part * 256
        acc = nn(rows, w_qkv[:, cols]) + bias[:, at : at + 256]
        if part == 2:
            out[...] = acc.astype(BF16)
            continue
        for tile in range(2):
            x = turned(acc[:, tile * 128 : (tile + 1) * 128], *tables, 1.0)
            if part == 0:
                x = x * HEAD_DIM ** (-0.5)
            out[:, tile * 128 : (tile + 1) * 128] = x.astype(BF16)


def qkv_first_body(steps, ids, *refs):
    pieces, refs = refs[:8], refs[8:]
    tok_own, tok_other, dy_own, dy_other, cos, sin_lo, sin_hi = refs[:7]
    q, k, v, d_att, attn_in, attn_t, mlp_in, w_qkv, w_out, vec, bias = refs[7:]
    step = pl.program_id(0)

    @pl.when(step == 0)
    def _():
        for place, piece in enumerate(pieces):
            owner = piece_owner(ids, place)
            at_owner = pl.ds(pl.multiple_of(owner * 128, 128), 128)
            w_qkv[at_owner, :] = piece[0:128, 0:768]
            vec[:, at_owner] = piece[128:144, 0:128].astype(F32)
            for panel in range(4):
                at = 768 + 256 * (panel // 2)
                base = (panel % 2) * 64
                w_out[pl.ds(pl.multiple_of(owner * 64, 64), 64), 256 * panel : 256 * panel + 256] = piece[
                    base : base + 64, at : at + 256
                ]
        for part in range(3):
            for tile in range(4):
                base = tile * 256
                row = slice(4 + part, 5 + part)
                at = (tile // 2) * 768 + part * 256 + (tile % 2) * 128
                bias[:, at : at + 128] = pick_parity(
                    ids[1], vec[row, base : base + 128], vec[row, base + 128 : base + 256]
                )

    first = step < steps // 2
    d_att[...] = nt(jnp.where(first, dy_own[...], dy_other[...]), w_out[...]).astype(BF16)
    normed, _ = normalize(jnp.where(first, tok_own[...], tok_other[...]).astype(F32))
    rows = (normed * vec[0:1, :] + vec[1:2, :]).astype(BF16)
    mlp_in[...] = (normed * vec[2:3, :] + vec[3:4, :]).astype(BF16)
    attn_in[...] = rows
    attn_t[...] = rows.T
    project(0, rows, w_qkv, bias, (cos, sin_lo, sin_hi), (q, k, v))


def qkv_second_body(ids, *refs):
    pieces, (attn_in, bias, cos, sin_lo, sin_hi, q, k, v, w_qkv) = refs[:8], refs[8:]

    @pl.when(pl.program_id(0) == 0)
    def _():
        for place, piece in enumerate(pieces):
            owner = piece_owner(ids, place)
            for part in range(3):
                for panel in range(4):
                    at = pl.ds(pl.multiple_of(owner * 128 + 32 * panel, 32), 32)
                    w_qkv[at, part * 256 : part * 256 + 256] = piece[
                        256 + 32 * part : 288 + 32 * part, panel * 256 : panel * 256 + 256
                    ]

    project(1, attn_in[...], w_qkv, bias, (cos, sin_lo, sin_hi), (q, k, v))


ATTN_ROWS = 256


def cat(parts, axis=0):
    return jnp.concatenate(parts, axis=axis) if len(parts) > 1 else parts[0]


def attn_body(q, k, v, d_att, seg_col, seg_row, cos, sin_lo, sin_hi, att, grad):
    count = q.shape[0]
    size = ATTN_ROWS
    blocks = count // size
    span = [slice(j * size, (j + 1) * size) for j in range(blocks)]
    low = low_lanes()
    zero = jnp.zeros((), BF16)
    causal = lax.broadcasted_iota(jnp.int32, (size, size), 0) >= lax.broadcasted_iota(
        jnp.int32, (size, size), 1
    )
    q_t, da_t = q[...].T, d_att[...].T

    def row_total(parts, reduce, join):
        cols = [reduce(part, axis=-1, keepdims=True) for part in parts]
        return [
            functools.reduce(join, [cols[j][(i - j) * size : (i - j + 1) * size] for j in range(i + 1)])
            for i in range(blocks)
        ]

    def row_sum(parts):
        return cat(
            [
                functools.reduce(jnp.add, [parts[j][(i - j) * size : (i - j + 1) * size] for j in range(i + 1)])
                for i in range(blocks)
            ]
        )

    def products(half):
        lanes = low if half == 0 else jnp.logical_not(low)
        q_h = jnp.where(lanes, q[...], zero)
        da_h = jnp.where(lanes, d_att[...], zero)
        scores = [nt(q_h[j * size :], k[span[j], :]) for j in range(blocks)]
        return scores, [nt(da_h[j * size :], v[span[j], :]) for j in range(blocks)]

    def softmax_both(scores, grad_probs):
        masked = []
        for j in range(blocks):
            allowed = seg_col[j * size :, :] == seg_row[0, :, span[j]]
            allowed = cat([allowed[:size] & causal] + ([allowed[size:]] if j < blocks - 1 else []))
            masked.append(jnp.where(allowed, scores[j], MASKED))
        top = row_total(masked, jnp.max, jnp.maximum)
        raised = [jnp.exp(masked[j] - cat(top[j:])) for j in range(blocks)]
        inv = [1.0 / total for total in row_total(raised, jnp.sum, jnp.add)]
        probs = [raised[j] * cat(inv[j:]) for j in range(blocks)]
        delta = row_total([g * p for g, p in zip(grad_probs, probs)], jnp.sum, jnp.add)
        grad_scores = [
            (probs[j] * (grad_probs[j] - cat(delta[j:]))).astype(BF16) for j in range(blocks)
        ]
        return [p.astype(BF16) for p in probs], grad_scores

    def results(half, probs, grad_scores):
        rows = slice(half * HEAD_DIM, (half + 1) * HEAD_DIM)
        return (
            row_sum([nn(probs[j], v[span[j], :]) for j in range(blocks)]),
            row_sum([nn(grad_scores[j], k[span[j], :]) for j in range(blocks)]),
            cat([nn(q_t[rows, j * size :], grad_scores[j]) for j in range(blocks)], 1),
            cat([nn(da_t[rows, j * size :], probs[j]) for j in range(blocks)], 1),
        )

    first = softmax_both(*products(0))
    second = products(1)
    out_a, dq_a, dk_a, dv_a = results(0, *first)
    out_b, dq_b, dk_b, dv_b = results(1, *softmax_both(*second))
    tables = (cos, sin_lo, sin_hi)
    att[...] = jnp.where(low, out_a, out_b).astype(BF16)
    grad[0] = turned(jnp.where(low, dq_a, dq_b) * HEAD_DIM ** (-0.5), *tables, -1.0).astype(BF16)
    grad[1] = turned(jnp.concatenate([dk_a, dk_b], axis=0).T, *tables, -1.0).astype(BF16)
    grad[2] = jnp.concatenate([dv_a, dv_b], axis=0).T.astype(BF16)


def attn_weights_body(ids, attn_t, grad_a, grad_b, far_att_a, far_att_b, far_own, far_other, *refs):
    keep, send_x, send_y, bias, result, att_a, att_b, dy_own, dy_other, sems = refs
    copies = [
        pltpu.make_async_copy(source, target, sems.at[n])
        for n, (source, target) in enumerate(
            ((far_att_a, att_a), (far_att_b, att_b), (far_own, dy_own), (far_other, dy_other))
        )
    ]

    @pl.when(pl.program_id(0) == 0)
    def _():
        for copy in copies:
            copy.start()

    step = pl.program_id(0)
    outs = (keep, send_x, send_y)

    @pl.when(step < 6)
    def _():
        rhs = jnp.where(step < 3, grad_a[0], grad_b[0])
        result[...] = nn(attn_t[...], rhs).astype(BF16)
        cols = pl.ds(pl.multiple_of(step * 256, 256), 256)
        bias[0:1, cols] = jnp.sum(rhs.astype(F32), axis=0, keepdims=True)
        for slot in range(8):
            out, at = slot_ref(outs, slot)
            base = pl.multiple_of(slot_owner(ids, slot) * 128, 128)
            out[at, :, cols] = result[pl.ds(base, 128), :]

    @pl.when(step == 6)
    def _():
        for copy in copies:
            copy.wait()
        count = dy_own.shape[0]
        for group, att in enumerate((att_a, att_b)):
            flipped = att[...].T
            for panel in range(4):
                cols = slice(panel * 256, panel * 256 + 256)
                term = nn(flipped[:, :count], dy_own[:, cols]) + nn(flipped[:, count:], dy_other[:, cols])
                result[group * 256 : group * 256 + 256, :] = term.astype(BF16)
                for slot in range(8):
                    out, at = slot_ref(outs, slot)
                    owner = slot_owner(ids, slot)
                    col = 1536 + 256 * (panel // 2)
                    base = (panel % 2) * 64

                    @pl.when(owner // 4 == group)
                    def _():
                        out[at, base : base + 64, col : col + 256] = result[
                            pl.ds(pl.multiple_of(owner * 64, 64), 64), :
                        ]


def mlp_body(part, steps, ids, *refs):
    pieces, (vec, mlp_in, dy_own, dy_other) = refs[:8], refs[8:12]
    far_outs, (hidden_out, grad_out, sums, far_up, far_down) = refs[12:15], refs[15:20]
    mlp_t, hidden_t, grad_pre, dy, bias, result, keep, send_x, send_y, w_up, w_down, sems = refs[20:]
    outs = (keep, send_x, send_y)
    weight_copies = [
        pltpu.make_async_copy(w_up, far_up, sems.at[0]),
        pltpu.make_async_copy(w_down, far_down, sems.at[1]),
    ]
    core = ids[1]
    step = pl.program_id(0)

    @pl.when(step == 0)
    def _():
        for owner in range(8):
            start = pl.multiple_of((owner % 2) * 512 + part * 256 + core * 128, 128)
            row = 8 + owner // 2
            bias[0:1, owner * 128 : (owner + 1) * 128] = vec[row : row + 1, pl.ds(start, 128)]
        sums[...] = jnp.zeros_like(sums)
        for place, piece in enumerate(pieces):
            at = pl.ds(pl.multiple_of(piece_owner(ids, place) * 128, 128), 128)
            w_up[at, :] = piece[0:128, :]
            w_down[at, :] = piece[128:256, :]
        for copy in weight_copies:
            copy.start()

    rows = mlp_in[...]
    grads = jnp.where(step < steps // 2, dy_own[...], dy_other[...])
    count = rows.shape[0]
    at = pl.ds(pl.multiple_of(step * count, count), count)
    mlp_t[:, at] = rows.T
    dy[at, :] = grads
    sums[1:2, :] += jnp.sum(grads.astype(F32), axis=0, keepdims=True)
    for col in range(0, 1024, 512):
        cols = slice(col, col + 512)
        pre = nn(rows, w_up[:, cols]) + bias[0:1, cols]
        grad_hidden = nt(grads, w_down[cols, :])
        cdf = 0.5 + 0.5 * lax.erf(pre * INV_ROOT_TWO)
        pdf = jnp.exp(-0.5 * pre * pre) * INV_ROOT_TAU
        act = (pre * cdf).astype(BF16)
        hidden_t[cols, at] = act.T
        hidden_out[:, cols] = act
        gp = (grad_hidden * (cdf + pre * pdf)).astype(BF16)
        grad_pre[at, cols] = gp
        grad_out[:, cols] = gp
        sums[0:1, cols] += jnp.sum(gp.astype(F32), axis=0, keepdims=True)

    @pl.when(step == steps - 1)
    def _():
        copies = list(weight_copies)
        for base_row, left, right in ((0, mlp_t, grad_pre), (128, hidden_t, dy)):
            for col in range(0, 1024, 512):
                cols = slice(col, col + 512)
                result[...] = nn(left[...], right[:, cols]).astype(BF16)
                for slot in range(8):
                    out, place = slot_ref(outs, slot)
                    base = pl.multiple_of(slot_owner(ids, slot) * 128, 128)
                    out[place, base_row : base_row + 128, cols] = result[pl.ds(base, 128), :]
            span = pl.ds(base_row, 128)
            for out, far_out in zip(outs, far_outs):
                copy = pltpu.make_async_copy(out.at[:, span, :], far_out.at[:, span, :], sems.at[len(copies)])
                copy.start()
                copies.append(copy)
        for copy in copies:
            copy.wait()


def back_body(own, grad_a, grad_b, att_a, att_b, hid_a, hid_b, gp_a, gp_b, *refs):
    w_out, down_a, down_b, up_a, up_b, wq_a, wq_b, tok, vec = refs[:9]
    if own:
        dy, other, out, result, sums = refs[9:]
    else:
        out, sums = refs[9:]
    inputs = tok[...].astype(F32)
    normed, inv_std = normalize(inputs)
    branch = nn(att_a[...], w_out[0:256, :]) + nn(att_b[...], w_out[256:512, :])
    branch = branch + nn(hid_a[...], down_a[...]) + nn(hid_b[...], down_b[...])
    back_mlp = nt(gp_a[...], up_a[...]) + nt(gp_b[...], up_b[...])
    back_attn = None
    for grad, w in ((grad_a, wq_a), (grad_b, wq_b)):
        for part in range(3):
            term = nt(grad[part], w[:, part * 256 : part * 256 + 256])
            back_attn = term if back_attn is None else back_attn + term
    scaled = back_attn * vec[0:1, :] + back_mlp * vec[2:3, :]

    @pl.when(pl.program_id(0) == 0)
    def _():
        sums[...] = jnp.zeros_like(sums)

    for row, value in enumerate((back_attn * normed, back_attn, back_mlp * normed, back_mlp)):
        sums[row : row + 1, :] += jnp.sum(value, axis=0, keepdims=True)
    if not own:
        out[0] = branch.astype(BF16)
        out[1] = scaled.astype(BF16)
        return
    branch = branch + other[0].astype(F32)
    out[...] = (inputs + branch + (vec[7:8, :] + vec[12:13, :])).astype(BF16)
    scaled = scaled + other[1].astype(F32)
    result[...] = dy[...].astype(F32) + inv_std * (
        scaled
        - jnp.mean(scaled, axis=-1, keepdims=True)
        - normed * jnp.mean(scaled * normed, axis=-1, keepdims=True)
    )


def adam_math(weight, first, second, gradient, rate, decay):
    first_new = BETA_ONE * first + (1.0 - BETA_ONE) * gradient
    second_new = BETA_TWO * second + (1.0 - BETA_TWO) * gradient * gradient
    first_hat = first_new / (1.0 - BETA_ONE**STEP)
    second_hat = second_new / (1.0 - BETA_TWO**STEP)
    weight_new = weight - rate * (first_hat / (jnp.sqrt(second_hat) + ADAM_EPS) + decay * weight)
    return (first_new, second_new, weight_new)


def adam_store(refs, at, gradient):
    w, m, v, m_out, v_out, w_out = refs
    first, second, weight = adam_math(w[at], m[at], v[at], gradient, RATE_MATRIX, DECAY_MATRIX)
    m_out[at] = first
    v_out[at] = second
    w_out[at] = weight


def parities(core, own, other):
    return jnp.where(core == 0, own, other), jnp.where(core == 0, other, own)


def adam_attn_body(ids, own, other, *refs):
    core = ids[1]
    low = low_lanes()
    qkv_refs = refs[0:3] + refs[6:9]
    for tile in range(4):
        start = (tile // 2) * 768 + (tile % 2) * 128
        cols = pl.ds(pl.multiple_of(pl.program_id(0) * 256 + start, 128), 128)
        even, odd = parities(core, own[:, cols].astype(F32), other[:, cols].astype(F32))
        first = jnp.where(low, even, pltpu.roll(odd, HEAD_DIM, 1))
        second = jnp.where(low, pltpu.roll(even, HEAD_DIM, 1), odd)
        adam_store(qkv_refs, (slice(None), slice(tile * 256, tile * 256 + 128)), first)
        adam_store(qkv_refs, (slice(None), slice(tile * 256 + 128, tile * 256 + 256)), second)

    @pl.when(pl.program_id(0) == 0)
    def _():
        out_refs = refs[3:6] + refs[9:12]
        for panel in range(4):
            rows = slice((panel % 2) * 64, (panel % 2) * 64 + 64)
            cols = slice(1536 + 256 * (panel // 2), 1792 + 256 * (panel // 2))
            span = slice(panel * 256, panel * 256 + 256)
            even, odd = parities(core, own[rows, cols].astype(F32), other[rows, cols].astype(F32))
            adam_store(out_refs, (slice(0, 64), span), even)
            adam_store(out_refs, (slice(64, 128), span), odd)


def adam_mlp_body(ids, own, other, *refs):
    core = ids[1]
    up_refs = refs[0:3] + refs[-6:-3]
    down_refs = refs[3:6] + refs[-3:]
    cols = pl.ds(pl.multiple_of(pl.program_id(0) * 128, 128), 128)
    for base, refs_of in ((0, up_refs), (128, down_refs)):
        rows = slice(base, base + 128)
        for parity, grad in enumerate(
            parities(core, own[rows, cols].astype(F32), other[rows, cols].astype(F32))
        ):
            span = slice(parity * 128, (parity + 1) * 128)
            adam_store(refs_of, (slice(None), span) if base == 0 else (span, slice(None)), grad)


def rotary_tables(segments):
    row_count = segments.shape[0]
    row_index = jnp.arange(row_count, dtype=jnp.int32)
    earlier = jnp.concatenate([jnp.full((1,), -1, jnp.int32), segments[:-1]])
    starts = jnp.where(segments != earlier, row_index, 0)
    position = (row_index - lax.cummax(starts, axis=0)).astype(F32)
    half_dim = ROT_DIM // 2
    dims = jnp.arange(LANES, dtype=jnp.int32) % HEAD_DIM
    frequency = ROPE_BASE ** (-2.0 * (dims % half_dim).astype(F32) / ROT_DIM)
    turned = dims < ROT_DIM
    angles = position[:, None] * jnp.where(turned, frequency, 0.0)[None, :]
    cosine, sine = jnp.cos(angles), jnp.sin(angles)
    front = (dims < half_dim)[None, :]
    return cosine, jnp.where(front, -sine, 0.0), jnp.where(front, 0.0, sine)


def on_device(
    sizes,
    tokens,
    segments,
    cotangent,
    w_qkv,
    w_out,
    w_up,
    w_down,
    vectors,
    m_qkv,
    m_out,
    m_up,
    m_down,
    m_vectors,
    v_qkv,
    v_out,
    v_up,
    v_down,
    v_vectors,
):
    copies, owners = sizes
    me = lax.axis_index("zero")
    plane = lax.axis_index("dp")
    core = plane % 2
    ids = jnp.stack([me, core, (plane // 2) % 2]).astype(jnp.int32)

    def move(value, target):
        pairs = []
        for d in range(copies):
            for z in range(owners):
                to_d, to_z = target(d, z)
                pairs.append((d * owners + z, to_d * owners + to_z))
        return lax.ppermute(value, AXES, pairs)

    def swap(value, dp_bits, zero_bits):
        return move(value, lambda d, z: (d ^ dp_bits, z ^ zero_bits))

    def swap_far(value):
        return move(value, lambda d, z: (d, z ^ (6 if d & 2 else 4)))

    def sync(*values):
        return lax.optimization_barrier(values)

    def add(*terms):
        return functools.reduce(jnp.add, [t.astype(F32) for t in terms])

    def reduce_first(keep, send_x, send_y):
        return keep, swap(send_x, 0, 1), swap(send_y, 2, 0)

    def reduce_second(state):
        keep, got_x, got_y = state
        far = add(keep[3], got_y[1]).astype(BF16)
        near = add(keep[1], got_x[1]).astype(BF16)
        return keep, got_x, got_y, far, near, swap(far, 0, 1), swap(near, 0, 2)

    def reduce_third(state):
        keep, got_x, got_y, _, _, got_far, got_near = state
        far = add(keep[2], got_y[0], got_far).astype(BF16)
        return add(keep[0], got_x[0], got_near), far, swap_far(far)

    def reduce_fourth(state):
        total = (state[0] + state[2].astype(F32)).astype(BF16)
        return total, swap(total, 2, 0)

    def reduce_fifth(state):
        total = add(*state).astype(BF16)
        bit = 4
        while bit < copies:
            total = add(total, swap(total, bit, 0)).astype(BF16)
            bit *= 2
        return total, swap(total, 1, 0)

    T, width = tokens.shape
    rows = 2 * T
    sds = jax.ShapeDtypeStruct
    row_block = lambda n, c=width: spec((n, c), lambda i: (i, 0))
    col_block = lambda n: spec((width, n), lambda i: (0, i))

    def block_call(body, grid, ins, outs, flops, moved, scratch=(), name=None):
        return kernel_call(
            body,
            grid,
            [place for _, place in ins],
            [place for _, place in outs],
            [shape for shape, _ in outs],
            flops,
            moved,
            scratch=scratch,
            name=name,
        )(*[value for value, _ in ins])

    def const(value):
        return value, whole(value.shape)

    def kept(shape, dtype):
        return sds(shape, dtype), whole(shape)

    steps = rows // 256
    with jax.named_scope("prep"):
        own_a = block_call(
            prep_attn_body,
            (1,),
            [(ids, scalars()), const(w_qkv), const(w_out), (vectors, whole((16, 128)))],
            [kept((144, 1280), BF16)],
            0,
            3e6,
            name="prep_attn",
        )[0]
        own_b, own_c = block_call(
            prep_mlp_body,
            (1,),
            [(ids, scalars()), const(w_up), const(w_down), const(w_qkv)],
            [kept((256, 1024), BF16), kept((352, 1024), BF16)],
            0,
            6e6,
            name="prep_mlp",
        )

    def z_moves(own):
        return swap(own, 0, 2), swap_far(own)

    with jax.named_scope("gather"):
        next_a, far_a = z_moves(own_a)
        across_a = swap(own_a, 0, 1)
        seg_other = swap(segments, 1, 0)
        tables = [
            jnp.concatenate(pair, axis=0)
            for pair in zip(rotary_tables(segments), rotary_tables(seg_other))
        ]
        seg_row = jnp.stack([segments, seg_other])[:, None, :]
        seg_col = jnp.concatenate([segments, seg_other])[:, None]
        next_a, far_a, across_a, own_b, own_c, tables, seg_row, seg_col = sync(
            next_a, far_a, across_a, own_b, own_c, tables, seg_row, seg_col
        )
        next_across_a, far_across_a, rest_a = swap(next_a, 0, 1), swap(far_a, 0, 1), swap(far_a, 2, 0)
        rest_across_a = swap(far_a, 2, 1)
        next_b, far_b = z_moves(own_b)
        tok_other = swap(tokens, 1, 0)
        dy_other = swap(cotangent, 1, 0)

    (next_across_a, far_across_a, rest_a, rest_across_a, next_b, far_b, own_c, tok_other, dy_other) = sync(
        next_across_a, far_across_a, rest_a, rest_across_a, next_b, far_b, own_c, tok_other, dy_other
    )
    with jax.named_scope("gather"):
        far_across_b, next_across_b, rest_b = swap(far_b, 0, 1), swap(next_b, 0, 1), swap(far_b, 2, 0)
        next_c, far_c = z_moves(own_c)
    attn_pieces = [own_a, next_a, far_a, rest_a, across_a, next_across_a, far_across_a, rest_across_a]

    def table_blocks(count):
        return [(t, row_block(count, 128)) for t in tables]

    def halves(own, other, count):
        last = T // count - 1
        return [
            (own, spec((count, width), lambda i: (jnp.minimum(i, last), 0))),
            (other, spec((count, width), lambda i: (jnp.maximum(i - last - 1, 0), 0))),
        ]

    def attention(group, projected, d_att):
        with jax.named_scope("attention"):
            head_block = spec((T, 128), lambda h, m: (h, m))
            return block_call(
                attn_body,
                (2, 2),
                [(value, head_block) for value in projected]
                + [(d_att, spec((T, 128), lambda h, m: (h, m + 2 * group)))]
                + [(seg_col, spec((T, 1), lambda h, m: (h, 0)))]
                + [(seg_row, spec((1, 1, T), lambda h, m: (h, 0, 0)))]
                + [(t, spec((T, 128), lambda h, m: (h, 0))) for t in tables],
                [
                    (sds((rows, 256), BF16), head_block),
                    (sds((3, rows, 256), BF16), spec((3, T, 128), lambda h, m: (0, h, m))),
                ],
                30e9,
                10e6,
                name="attention",
            )

    def blocks_of(shape):
        return [kept((n,) + shape, BF16) for n in (4, 2, 2)]

    with jax.named_scope("qkv"):
        *projected, d_att, attn_in, attn_t, mlp_in, wq_a, full_out, vec, bias_qkv = block_call(
            functools.partial(qkv_first_body, rows // 256),
            (rows // 256,),
            [(ids, scalars())]
            + [const(piece) for piece in attn_pieces]
            + halves(tokens, tok_other, 256)
            + halves(cotangent, dy_other, 256)
            + table_blocks(256),
            [(sds((rows, 256), BF16), row_block(256, 256))] * 3
            + [(sds((rows, 512), BF16), row_block(256, 512)), (sds((rows, width), BF16), row_block(256))]
            + [(sds((width, rows), BF16), col_block(256)), (sds((rows, width), BF16), row_block(256))]
            + [kept((1024, 768), BF16), kept((512, 1024), BF16), kept((16, 1024), F32), kept((1, 1536), F32)],
            2 * rows * 1024 * 1280,
            30e6,
            name="qkv",
        )
    projected, far_across_b, next_across_b, rest_b, own_b, next_c, far_c = sync(
        projected, far_across_b, next_across_b, rest_b, own_b, next_c, far_c
    )
    with jax.named_scope("gather"):
        rest_across_b, across_b = swap(far_across_b, 2, 0), swap(own_b, 0, 1)
        far_across_c, rest_c = swap(far_c, 0, 1), swap(far_c, 2, 0)
    att_a, grad_a = attention(0, projected, d_att)
    att_a, grad_a, rest_across_b, across_b, far_across_c, rest_c, own_c, next_c, attn_t, mlp_in = sync(
        att_a, grad_a, rest_across_b, across_b, far_across_c, rest_c, own_c, next_c, attn_t, mlp_in
    )
    with jax.named_scope("gather"):
        across_c, next_across_c, rest_across_c = swap(own_c, 0, 1), swap(next_c, 0, 1), swap(far_across_c, 2, 0)
    pieces_b = [own_b, next_b, far_b, rest_b, across_b, next_across_b, far_across_b, rest_across_b]

    def mlp(part, weights, rows_in):
        with jax.named_scope("mlp"):
            *results, hid, gp, sums, w_up_full, w_down_full = block_call(
                functools.partial(mlp_body, part, steps),
                (steps,),
                [(ids, scalars())]
                + [const(w) for w in weights]
                + [const(vec), (rows_in, row_block(256))]
                + halves(cotangent, dy_other, 256),
                [(sds((n, 256, 1024), BF16), distant()) for n in (4, 2, 2)]
                + [(sds((rows, width), BF16), row_block(256))] * 2
                + [kept((8, 1024), F32)]
                + [(sds((1024, 1024), BF16), distant())] * 2,
                2 * rows * 1024 * 1024 * 4,
                40e6,
                scratch=[
                    pltpu.VMEM((1024, rows), BF16),
                    pltpu.VMEM((1024, rows), BF16),
                    pltpu.VMEM((rows, 1024), BF16),
                    pltpu.VMEM((rows, 1024), BF16),
                    pltpu.VMEM((8, 1024), F32),
                    pltpu.VMEM((1024, 512), BF16),
                ]
                + [pltpu.VMEM((n, 256, 1024), BF16) for n in (4, 2, 2)]
                + [pltpu.VMEM((1024, 1024), BF16)] * 2
                + [pltpu.SemaphoreType.DMA((8,))],
                name="mlp",
            )
            return results, hid, gp, sums, w_up_full, w_down_full

    mlp_a = mlp(0, pieces_b, mlp_in)
    mlp_a, mlp_in, across_c, next_across_c, rest_across_c = sync(
        mlp_a, mlp_in, across_c, next_across_c, rest_across_c
    )
    pieces_c = [own_c, next_c, far_c, rest_c, across_c, next_across_c, far_across_c, rest_across_c]
    reduce_a = reduce_first(*mlp_a[0])
    mlp_b = mlp(1, pieces_c, mlp_in)
    mlp_b, reduce_a, attn_in = sync(mlp_b, reduce_a, attn_in)
    reduce_a = reduce_second(reduce_a)
    reduce_b = reduce_first(*mlp_b[0])
    attn_in, *ready = sync(attn_in, *reduce_a[3:5])

    with jax.named_scope("qkv"):
        *projected, wq_b = block_call(
            qkv_second_body,
            (rows // 512,),
            [(ids, scalars())]
            + [const(piece) for piece in pieces_c]
            + [(attn_in, row_block(512)), const(bias_qkv)]
            + table_blocks(512),
            [(sds((rows, 256), BF16), row_block(512, 256))] * 3 + [kept((1024, 768), BF16)],
            2 * rows * 1024 * 768,
            12e6,
            name="qkv",
        )
    att_b, grad_b = attention(1, projected, d_att)
    att_b, grad_b, reduce_a, reduce_b = sync(att_b, grad_b, reduce_a, reduce_b)
    reduce_a = reduce_third(reduce_a)
    reduce_b = reduce_second(reduce_b)
    grad_b, *ready = sync(grad_b, reduce_a[1], *reduce_b[3:5])
    with jax.named_scope("attn_weights"):
        *blocks, bias_sum = block_call(
            attn_weights_body,
            (7,),
            [(ids, scalars()), const(attn_t)]
            + [(grad_a, spec((1, rows, 256), lambda n: (jnp.minimum(n, 2), 0, 0)))]
            + [(grad_b, spec((1, rows, 256), lambda n: (jnp.clip(n - 3, 0, 2), 0, 0)))]
            + [(value, distant()) for value in (att_a, att_b, cotangent, dy_other)],
            blocks_of((128, 2048)) + [kept((8, 1536), F32)],
            2 * rows * 1024 * 2048,
            24e6,
            scratch=[pltpu.VMEM((1024, 256), BF16)]
            + [pltpu.VMEM((rows, 256), BF16)] * 2
            + [pltpu.VMEM((T, width), BF16)] * 2
            + [pltpu.SemaphoreType.DMA((4,))],
            name="attn_weights",
        )
    blocks, grad_b = sync(blocks, grad_b)
    reduce_o = reduce_first(*blocks)

    _, hid_a, gp_a, sums_a, up_a, down_a = mlp_a
    _, hid_b, gp_b, sums_b, up_b, down_b = mlp_b

    def adam_mlp(part, totals, previous):
        wide = [spec((128, 256), lambda n: (0, 2 * n + part))] * 3
        wide += [spec((256, 128), lambda n: (part, n))] * 3
        return pl.pallas_call(
            adam_mlp_body,
            grid=(8,),
            in_specs=[scalars()]
            + [whole((256, 1024))] * 2
            + wide
            + [pl.BlockSpec(memory_space=pl.ANY)] * len(previous),
            out_specs=wide,
            out_shape=[sds((128, 4096), F32)] * 3 + [sds((512, 1024), F32)] * 3,
            input_output_aliases={9 + n: n for n in range(len(previous))},
            cost_estimate=pl.CostEstimate(flops=0, bytes_accessed=14000000, transcendentals=0),
            compiler_params=pltpu.CompilerParams(
                vmem_limit_bytes=VMEM_NEED * MIB, dimension_semantics=("arbitrary",)
            ),
            name="adam_mlp",
        )(ids, *totals, w_up, m_up, v_up, w_down, m_down, v_down, *previous)

    def back(own, grad, rows_tok, extra, outs):
        first = 0 if own else T // 256
        block = lambda c=width: spec((256, c), lambda i: (i + first, 0))
        lead = spec((3, 256, 256), lambda i: (0, i + first, 0))
        with jax.named_scope("back"):
            return block_call(
                functools.partial(back_body, own),
                (T // 256,),
                [(grad_a, lead), (grad, lead), (att_a, block(256)), (att_b, block(256))]
                + [(value, block()) for value in (hid_a, hid_b, gp_a, gp_b)]
                + [const(w) for w in (full_out, down_a, down_b, up_a, up_b, wq_a, wq_b)]
                + [(rows_tok, row_block(256)), const(vec)]
                + extra,
                outs + [kept((8, width), F32)],
                2 * T * 1024 * 6144,
                40e6,
                name="back",
            )

    reduce_a = reduce_fourth(reduce_a)
    reduce_b = reduce_third(reduce_b)
    pair_block = spec((2, 256, width), lambda i: (0, i, 0))
    part_other, sums_other = back(False, grad_b, tok_other, [], [(sds((2, T, width), BF16), pair_block)])
    part_other, sums_other, grad_b, reduce_a, reduce_b, reduce_o = sync(
        part_other, sums_other, grad_b, reduce_a, reduce_b, reduce_o
    )
    reduce_o = reduce_second(reduce_o)
    part_other, reduce_a, reduce_b, *ready = sync(part_other, reduce_a, reduce_b, *reduce_o[3:5])
    reduce_a = reduce_fifth(reduce_a)
    reduce_b = reduce_fourth(reduce_b)
    part_got = swap(part_other, 1, 0)
    updated_mlp = adam_mlp(0, reduce_a, [])
    updated_mlp, grad_b, reduce_b, reduce_o, part_got = sync(
        updated_mlp, grad_b, reduce_b, reduce_o, part_got
    )
    reduce_o = reduce_third(reduce_o)
    reduce_b = reduce_fifth(reduce_b)
    grad_b, *ready = sync(grad_b, reduce_o[1], reduce_b[0])
    layer_out, tokens_grad, sums_own = back(
        True,
        grad_b,
        tokens,
        [(cotangent, row_block(256)), (part_got, pair_block)],
        [(sds((T, width), BF16), row_block(256)), (sds((T, width), F32), row_block(256))],
    )
    sums_own, updated_mlp, reduce_b, reduce_o = sync(sums_own, updated_mlp, reduce_b, reduce_o)
    reduce_o = reduce_fourth(reduce_o)

    with jax.named_scope("vectors"):
        is_core = jnp.arange(2) == core
        grad_bias = jnp.where(core == 0, sums_a[1:2], 0.0)
        bias_sum = jnp.swapaxes(bias_sum[0].reshape(2, 3, 256), 0, 1)
        grad_bias_qkv = jnp.where(
            is_core[None, None, :, None], bias_sum.reshape(3, 8, 1, 64), 0.0
        ).reshape(3, width)
        grad_bias_up = jnp.where(
            is_core[None, None, :, None],
            jnp.swapaxes(jnp.stack([sums_a[0], sums_b[0]]).reshape(2, 8, 128), 0, 1)[:, :, None],
            0.0,
        ).reshape(4, width)
        total = jnp.concatenate(
            [
                sums_own[0:4] + sums_other[0:4],
                grad_bias_qkv,
                grad_bias,
                grad_bias_up,
                grad_bias,
                jnp.zeros((3, width), F32),
            ],
            axis=0,
        )
        moved = [swap(total, 0, step) for step in (2, 4, 6)]
        updated_mlp = adam_mlp(1, reduce_b, updated_mlp)
        updated_mlp, reduce_o, total, moved = sync(updated_mlp, reduce_o, total, moved)
        reduce_o = reduce_fifth(reduce_o)
        total = functools.reduce(jnp.add, moved, total)
        across, beside, both = swap(total, 0, 1), swap(total, 2, 0), swap(total, 2, 1)
        total = (total + across) + (beside + both)
        bit = 4
        while bit < copies:
            total = total + swap(total, bit, 0)
            bit *= 2
        total = total + swap(total, 1, 0)
        share = lax.dynamic_slice_in_dim(total[0:13], me * 128, 128, 1)
        first_vectors, second_vectors, new_vectors = adam_math(
            vectors, m_vectors, v_vectors, share, RATE_VECTOR, 0.0
        )

    with jax.named_scope("adam"):
        wide = [spec((128, 1024), lambda n: (0, n))] * 3 + [whole((128, 1024))] * 3
        updated_attn = kernel_call(
            adam_attn_body,
            (3,),
            [scalars()] + [whole((128, 2048))] * 2 + wide,
            wide,
            [sds((128, 3072), F32)] * 3 + [sds((128, 1024), F32)] * 3,
            0,
            13e6,
            name="adam",
        )(ids, *reduce_o, w_qkv, m_qkv, v_qkv, w_out, m_out, v_out)
    first_qkv, second_qkv, new_qkv, first_out, second_out, new_out = updated_attn
    first_up, second_up, new_up, first_down, second_down, new_down = updated_mlp
    return (
        layer_out,
        tokens_grad,
        first_qkv,
        first_out,
        first_up,
        first_down,
        first_vectors,
        second_qkv,
        second_out,
        second_up,
        second_down,
        second_vectors,
        new_qkv,
        new_out,
        new_up,
        new_down,
        new_vectors,
    )


def solution(mesh):
    rows, owned, spread = P(AXES, None), P("zero", None), P(None, "zero")
    state = (owned, owned, owned, owned, spread)
    return jax.shard_map(
        functools.partial(on_device, (mesh.shape["dp"], mesh.shape["zero"])),
        mesh=mesh,
        in_specs=(rows, P(AXES), rows) + state * 3,
        out_specs=(rows, rows) + state * 3,
        check_vma=False,
    )
```

```python
import functools

import jax
import jax.numpy as jnp
from jax import lax
from jax.experimental import pallas as pl
from jax.experimental.pallas import tpu as pltpu
from jax.sharding import PartitionSpec as P

HEAD_DIM = 64
ROT_DIM = 16
STEP = 10
EPS_NORM = 1e-05
BETA_ONE = 0.9
BETA_TWO = 0.999
ADAM_EPS = 1e-08
RATE_MATRIX = 0.05
RATE_VECTOR = 0.2
DECAY_MATRIX = 0.1
ROPE_BASE = 10000.0
INV_ROOT_TWO = 0.7071067811865476
INV_ROOT_TAU = 0.3989422804014327
MASKED = -1e30
LANES = 128
AXES = ("dp", "zero")
F32 = jnp.float32
BF16 = jnp.bfloat16
MIB = 1024 * 1024
VMEM_NEED = 58


def spec(block, index, single=False):
    if single:
        return pl.BlockSpec(block, index, pipeline_mode=pl.Buffered(1))
    return pl.BlockSpec(block, index)


def whole(shape):
    return spec(shape, lambda *_: (0,) * len(shape), single=True)


def distant():
    return pl.BlockSpec(memory_space=pl.ANY)


def scalars():
    return pl.BlockSpec(memory_space=pltpu.SMEM)


def kernel_call(body, grid, in_specs, out_specs, out_shape, flops, moved, scratch=(), name=None):
    return pl.pallas_call(
        body,
        grid=grid,
        in_specs=in_specs,
        out_specs=out_specs,
        out_shape=out_shape,
        scratch_shapes=list(scratch),
        cost_estimate=pl.CostEstimate(flops=int(flops), bytes_accessed=int(moved), transcendentals=0),
        compiler_params=pltpu.CompilerParams(
            vmem_limit_bytes=VMEM_NEED * MIB, dimension_semantics=("arbitrary",) * len(grid)
        ),
        name=name,
    )


def nn(left, right):
    return lax.dot_general(left, right, (((1,), (0,)), ((), ())), preferred_element_type=F32)


def nt(left, right):
    return lax.dot_general(left, right, (((1,), (1,)), ((), ())), preferred_element_type=F32)


def tn(left, right):
    return lax.dot_general(left, right, (((0,), (0,)), ((), ())), preferred_element_type=F32)


def piece_owner(ids, place):
    step = place % 4
    if step > 1:
        step = 2 + ids[2] if step == 2 else 3 - ids[2]
    return jnp.bitwise_xor(ids[0], 2 * step + place // 4)


SLOTS = ((0, 0), (1, 0), (2, 0), (2, 1), (0, 1), (1, 1), (3, 0), (3, 1))


def slot_owner(ids, slot):
    step, side = SLOTS[slot]
    if step > 1:
        step = 2 + ids[2] if step == 2 else 3 - ids[2]
    return jnp.bitwise_xor(ids[0], 2 * step + side)


def slot_ref(outs, slot):
    return (outs[0], slot) if slot < 4 else (outs[1], slot - 4) if slot < 6 else (outs[2], slot - 6)


def low_lanes():
    return lax.broadcasted_iota(jnp.int32, (1, LANES), 1) < HEAD_DIM


def pick_parity(core, tile_a, tile_b):
    low = low_lanes()
    even = jnp.where(low, tile_a, pltpu.roll(tile_b, HEAD_DIM, 1))
    odd = jnp.where(low, pltpu.roll(tile_a, HEAD_DIM, 1), tile_b)
    return jnp.where(core == 0, even, odd)


def prep_attn_body(ids, w_qkv, w_out, vec, out):
    core = ids[1]
    for part in range(3):
        for tile in range(2):
            base = part * 1024 + tile * 256
            at = part * 256 + tile * 128
            out[0:128, at : at + 128] = pick_parity(
                core, w_qkv[:, base : base + 128], w_qkv[:, base + 128 : base + 256]
            ).astype(BF16)
    rows = w_out[pl.ds(pl.multiple_of(core * 64, 64), 64), :].astype(BF16)
    for panel in range(4):
        at = 768 + 256 * (panel // 2)
        base = (panel % 2) * 64
        out[base : base + 64, at : at + 256] = rows[:, 256 * panel : 256 * panel + 256]
    out[128:144, 0:128] = jnp.where(lax.broadcasted_iota(jnp.int32, (16, 128), 0) < 13, vec[...], 0.0).astype(BF16)
    out[128:144, 128:1280] = jnp.zeros((16, 1152), BF16)


def prep_mlp_body(part, ids, w_up, w_down, *refs):
    out = refs[-1]
    core = ids[1]
    top = 96 * part
    for owner in range(8):
        start = pl.multiple_of(owner * 512 + part * 256 + core * 128, 128)
        out[top : top + 128, owner * 128 : (owner + 1) * 128] = w_up[:, pl.ds(start, 128)].astype(BF16)
    out[top + 128 : top + 256, :] = w_down[pl.ds(pl.multiple_of(core * 128, 128), 128), :].astype(BF16)
    if not part:
        return
    w_qkv = refs[0]
    for third in range(3):
        for tile in range(2):
            base = third * 1024 + 512 + tile * 256
            value = pick_parity(core, w_qkv[:, base : base + 128], w_qkv[:, base + 128 : base + 256]).astype(BF16)
            for panel in range(4):
                at = panel * 256 + tile * 128
                out[32 * third : 32 * third + 32, at : at + 128] = value[32 * panel : 32 * panel + 32]


def normalize(inputs):
    centred = inputs - jnp.mean(inputs, axis=-1, keepdims=True)
    variance = jnp.mean(centred * centred, axis=-1, keepdims=True)
    inv_std = lax.rsqrt(variance + EPS_NORM)
    return centred * inv_std, inv_std


def turned(x, cos, sin_lo, sin_hi, sign):
    return x * cos[...] + sign * (pltpu.roll(x, 8, 1) * sin_hi[...] + pltpu.roll(x, 120, 1) * sin_lo[...])


def project(group, rows, w_qkv, bias, tables, outs):
    for part, out in enumerate(outs):
        cols = slice(part * 256, (part + 1) * 256)
        at = group * 768 + part * 256
        acc = nn(rows, w_qkv[:, cols]) + bias[:, at : at + 256]
        if part == 2:
            out[...] = acc.astype(BF16)
            continue
        for tile in range(2):
            x = turned(acc[:, tile * 128 : (tile + 1) * 128], *tables, 1.0)
            if part == 0:
                x = x * HEAD_DIM ** (-0.5)
            out[:, tile * 128 : (tile + 1) * 128] = x.astype(BF16)


def qkv_first_body(steps, ids, *refs):
    pieces, refs = refs[:8], refs[8:]
    tok_own, tok_other, dy_own, dy_other, cos, sin_lo, sin_hi = refs[:7]
    q, k, v, d_att, attn_in, attn_t, mlp_in, w_qkv, w_out, vec, bias = refs[7:]
    step = pl.program_id(0)

    @pl.when(step == 0)
    def _():
        for place, piece in enumerate(pieces):
            owner = piece_owner(ids, place)
            at_owner = pl.ds(pl.multiple_of(owner * 128, 128), 128)
            w_qkv[at_owner, :] = piece[0:128, 0:768]
            vec[:, at_owner] = piece[128:144, 0:128].astype(F32)
            for panel in range(4):
                at = 768 + 256 * (panel // 2)
                base = (panel % 2) * 64
                w_out[pl.ds(pl.multiple_of(owner * 64, 64), 64), 256 * panel : 256 * panel + 256] = piece[
                    base : base + 64, at : at + 256
                ]
        for part in range(3):
            for tile in range(4):
                base = tile * 256
                row = slice(4 + part, 5 + part)
                at = (tile // 2) * 768 + part * 256 + (tile % 2) * 128
                bias[:, at : at + 128] = pick_parity(
                    ids[1], vec[row, base : base + 128], vec[row, base + 128 : base + 256]
                )

    first = step < steps // 2
    d_att[...] = nt(jnp.where(first, dy_own[...], dy_other[...]), w_out[...]).astype(BF16)
    normed, _ = normalize(jnp.where(first, tok_own[...], tok_other[...]).astype(F32))
    rows = (normed * vec[0:1, :] + vec[1:2, :]).astype(BF16)
    mlp_in[...] = (normed * vec[2:3, :] + vec[3:4, :]).astype(BF16)
    attn_in[...] = rows
    attn_t[...] = rows.T
    project(0, rows, w_qkv, bias, (cos, sin_lo, sin_hi), (q, k, v))


def qkv_second_body(ids, *refs):
    pieces, (attn_in, bias, cos, sin_lo, sin_hi, q, k, v, w_qkv) = refs[:8], refs[8:]

    @pl.when(pl.program_id(0) == 0)
    def _():
        for place, piece in enumerate(pieces):
            owner = piece_owner(ids, place)
            for part in range(3):
                for panel in range(4):
                    at = pl.ds(pl.multiple_of(owner * 128 + 32 * panel, 32), 32)
                    w_qkv[at, part * 256 : part * 256 + 256] = piece[
                        32 * part : 32 * part + 32, panel * 256 : panel * 256 + 256
                    ]

    project(1, attn_in[...], w_qkv, bias, (cos, sin_lo, sin_hi), (q, k, v))


ATTN_ROWS = 256


def cat(parts, axis=0):
    return jnp.concatenate(parts, axis=axis) if len(parts) > 1 else parts[0]


def attn_body(q, k, v, d_att, seg_col, seg_row, cos, sin_lo, sin_hi, *refs):
    att, grad = refs[-2:]
    count = q.shape[0]
    size = ATTN_ROWS
    blocks = count // size
    span = [slice(j * size, (j + 1) * size) for j in range(blocks)]
    low = low_lanes()
    zero = jnp.zeros((), BF16)
    causal = lax.broadcasted_iota(jnp.int32, (size, size), 0) >= lax.broadcasted_iota(
        jnp.int32, (size, size), 1
    )
    q_t, da_t = q[...].T, d_att[...].T

    def row_total(parts, reduce, join):
        cols = [reduce(part, axis=-1, keepdims=True) for part in parts]
        return [
            functools.reduce(join, [cols[j][(i - j) * size : (i - j + 1) * size] for j in range(i + 1)])
            for i in range(blocks)
        ]

    def row_sum(parts):
        return cat(
            [
                functools.reduce(jnp.add, [parts[j][(i - j) * size : (i - j + 1) * size] for j in range(i + 1)])
                for i in range(blocks)
            ]
        )

    def products(half):
        lanes = low if half == 0 else jnp.logical_not(low)
        q_h = jnp.where(lanes, q[...], zero)
        da_h = jnp.where(lanes, d_att[...], zero)
        scores = [nt(q_h[j * size :], k[span[j], :]) for j in range(blocks)]
        return scores, [nt(da_h[j * size :], v[span[j], :]) for j in range(blocks)]

    def softmax_both(scores, grad_probs):
        masked = []
        for j in range(blocks):
            allowed = seg_col[j * size :, 0:1] == seg_row[0, :, span[j]]
            allowed = cat([allowed[:size] & causal] + ([allowed[size:]] if j < blocks - 1 else []))
            masked.append(jnp.where(allowed, scores[j], MASKED))
        top = row_total(masked, jnp.max, jnp.maximum)
        raised = [jnp.exp(masked[j] - cat(top[j:])) for j in range(blocks)]
        inv = [1.0 / total for total in row_total(raised, jnp.sum, jnp.add)]
        probs = [raised[j] * cat(inv[j:]) for j in range(blocks)]
        delta = row_total([g * p for g, p in zip(grad_probs, probs)], jnp.sum, jnp.add)
        grad_scores = [
            (probs[j] * (grad_probs[j] - cat(delta[j:]))).astype(BF16) for j in range(blocks)
        ]
        return [p.astype(BF16) for p in probs], grad_scores

    def results(half, probs, grad_scores):
        rows = slice(half * HEAD_DIM, (half + 1) * HEAD_DIM)
        return (
            row_sum([nn(probs[j], v[span[j], :]) for j in range(blocks)]),
            row_sum([nn(grad_scores[j], k[span[j], :]) for j in range(blocks)]),
            cat([nn(q_t[rows, j * size :], grad_scores[j]) for j in range(blocks)], 1),
            cat([nn(da_t[rows, j * size :], probs[j]) for j in range(blocks)], 1),
        )

    first = softmax_both(*products(0))
    second = products(1)
    out_a, dq_a, dk_a, dv_a = results(0, *first)
    out_b, dq_b, dk_b, dv_b = results(1, *softmax_both(*second))
    tables = (cos, sin_lo, sin_hi)
    att[...] = jnp.where(low, out_a, out_b).astype(BF16)
    grad[0] = turned(jnp.where(low, dq_a, dq_b) * HEAD_DIM ** (-0.5), *tables, -1.0).astype(BF16)
    grad[1] = turned(jnp.concatenate([dk_a, dk_b], axis=0).T, *tables, -1.0).astype(BF16)
    grad[2] = jnp.concatenate([dv_a, dv_b], axis=0).T.astype(BF16)


def attn_weights_body(ids, attn_t, grad_a, grad_b, far_att_a, far_att_b, far_own, far_other, *refs):
    keep, send_x, send_y, bias, result, att_a, att_b, dy_own, dy_other, sems = refs
    copies = [
        pltpu.make_async_copy(source, target, sems.at[n])
        for n, (source, target) in enumerate(
            ((far_att_a, att_a), (far_att_b, att_b), (far_own, dy_own), (far_other, dy_other))
        )
    ]

    @pl.when(pl.program_id(0) == 0)
    def _():
        for copy in copies:
            copy.start()

    step = pl.program_id(0)
    outs = (keep, send_x, send_y)

    @pl.when(step < 6)
    def _():
        rhs = jnp.where(step < 3, grad_a[0], grad_b[0])
        result[...] = nn(attn_t[...], rhs).astype(BF16)
        cols = pl.ds(pl.multiple_of(step * 256, 256), 256)
        bias[0:1, cols] = jnp.sum(rhs.astype(F32), axis=0, keepdims=True)
        for slot in range(8):
            out, at = slot_ref(outs, slot)
            base = pl.multiple_of(slot_owner(ids, slot) * 128, 128)
            out[at, :, cols] = result[pl.ds(base, 128), :]

    @pl.when(step == 6)
    def _():
        for copy in copies:
            copy.wait()
        count = dy_own.shape[0]
        for group, att in enumerate((att_a, att_b)):
            flipped = att[...].T
            for panel in range(4):
                cols = slice(panel * 256, panel * 256 + 256)
                term = nn(flipped[:, :count], dy_own[:, cols]) + nn(flipped[:, count:], dy_other[:, cols])
                result[group * 256 : group * 256 + 256, :] = term.astype(BF16)
                for slot in range(8):
                    out, at = slot_ref(outs, slot)
                    owner = slot_owner(ids, slot)
                    col = 1536 + 256 * (panel // 2)
                    base = (panel % 2) * 64

                    @pl.when(owner // 4 == group)
                    def _():
                        out[at, base : base + 64, col : col + 256] = result[
                            pl.ds(pl.multiple_of(owner * 64, 64), 64), :
                        ]


def mlp_body(part, steps, ids, *refs):
    pieces, (vec, mlp_in, dy_own, dy_other) = refs[:8], refs[8:12]
    far_outs, (hidden_out, grad_out, sums, far_up, far_down) = refs[12:15], refs[15:20]
    mlp_t, hidden_t, grad_pre, dy, bias, result, keep, send_x, send_y, w_up, w_down, sems = refs[20:]
    outs = (keep, send_x, send_y)
    weight_copies = [
        pltpu.make_async_copy(w_up, far_up, sems.at[0]),
        pltpu.make_async_copy(w_down, far_down, sems.at[1]),
    ]
    core = ids[1]
    step = pl.program_id(0)

    @pl.when(step == 0)
    def _():
        for owner in range(8):
            start = pl.multiple_of((owner % 2) * 512 + part * 256 + core * 128, 128)
            row = 8 + owner // 2
            bias[0:1, owner * 128 : (owner + 1) * 128] = vec[row : row + 1, pl.ds(start, 128)]
        sums[...] = jnp.zeros_like(sums)
        for place, piece in enumerate(pieces):
            at = pl.ds(pl.multiple_of(piece_owner(ids, place) * 128, 128), 128)
            top = 96 * part
            w_up[at, :] = piece[top : top + 128, :]
            w_down[at, :] = piece[top + 128 : top + 256, :]
        for copy in weight_copies:
            copy.start()

    rows = mlp_in[...]
    grads = jnp.where(step < steps // 2, dy_own[...], dy_other[...])
    count = rows.shape[0]
    at = pl.ds(pl.multiple_of(step * count, count), count)
    mlp_t[:, at] = rows.T
    dy[at, :] = grads
    sums[1:2, :] += jnp.sum(grads.astype(F32), axis=0, keepdims=True)
    for col in range(0, 1024, 512):
        cols = slice(col, col + 512)
        pre = nn(rows, w_up[:, cols]) + bias[0:1, cols]
        grad_hidden = nt(grads, w_down[cols, :])
        cdf = 0.5 + 0.5 * lax.erf(pre * INV_ROOT_TWO)
        pdf = jnp.exp(-0.5 * pre * pre) * INV_ROOT_TAU
        act = (pre * cdf).astype(BF16)
        hidden_t[cols, at] = act.T
        hidden_out[:, cols] = act
        gp = (grad_hidden * (cdf + pre * pdf)).astype(BF16)
        grad_pre[at, cols] = gp
        grad_out[:, cols] = gp
        sums[0:1, cols] += jnp.sum(gp.astype(F32), axis=0, keepdims=True)

    @pl.when(step == steps - 1)
    def _():
        copies = list(weight_copies)
        for base_row, left, right in ((0, mlp_t, grad_pre), (128, hidden_t, dy)):
            for col in range(0, 1024, 512):
                cols = slice(col, col + 512)
                result[...] = nn(left[...], right[:, cols]).astype(BF16)
                for slot in range(8):
                    out, place = slot_ref(outs, slot)
                    base = pl.multiple_of(slot_owner(ids, slot) * 128, 128)
                    out[place, base_row : base_row + 128, cols] = result[pl.ds(base, 128), :]
            span = pl.ds(base_row, 128)
            for out, far_out in zip(outs, far_outs):
                copy = pltpu.make_async_copy(out.at[:, span, :], far_out.at[:, span, :], sems.at[len(copies)])
                copy.start()
                copies.append(copy)
        for copy in copies:
            copy.wait()


def back_body(own, grad_a, grad_b, att_a, att_b, hid_a, hid_b, gp_a, gp_b, *refs):
    w_out, down_a, down_b, up_a, up_b, wq_a, wq_b, tok, vec = refs[:9]
    if own:
        dy, other, out, result, sums = refs[9:]
    else:
        out, sums = refs[9:]
    inputs = tok[...].astype(F32)
    normed, inv_std = normalize(inputs)
    branch = nn(att_a[...], w_out[0:256, :]) + nn(att_b[...], w_out[256:512, :])
    branch = branch + nn(hid_a[...], down_a[...]) + nn(hid_b[...], down_b[...])
    back_mlp = nt(gp_a[...], up_a[...]) + nt(gp_b[...], up_b[...])
    back_attn = None
    for grad, w in ((grad_a, wq_a), (grad_b, wq_b)):
        for part in range(3):
            term = nt(grad[part], w[:, part * 256 : part * 256 + 256])
            back_attn = term if back_attn is None else back_attn + term
    scaled = back_attn * vec[0:1, :] + back_mlp * vec[2:3, :]

    @pl.when(pl.program_id(0) == 0)
    def _():
        sums[...] = jnp.zeros_like(sums)

    for row, value in enumerate((back_attn * normed, back_attn, back_mlp * normed, back_mlp)):
        sums[row : row + 1, :] += jnp.sum(value, axis=0, keepdims=True)
    if not own:
        out[0] = branch.astype(BF16)
        out[1] = scaled.astype(BF16)
        return
    branch = branch + other[0].astype(F32)
    out[...] = (inputs + branch + (vec[7:8, :] + vec[12:13, :])).astype(BF16)
    scaled = scaled + other[1].astype(F32)
    result[...] = dy[...].astype(F32) + inv_std * (
        scaled
        - jnp.mean(scaled, axis=-1, keepdims=True)
        - normed * jnp.mean(scaled * normed, axis=-1, keepdims=True)
    )


def adam_math(weight, first, second, gradient, rate, decay):
    first_new = BETA_ONE * first + (1.0 - BETA_ONE) * gradient
    second_new = BETA_TWO * second + (1.0 - BETA_TWO) * gradient * gradient
    first_hat = first_new / (1.0 - BETA_ONE**STEP)
    second_hat = second_new / (1.0 - BETA_TWO**STEP)
    weight_new = weight - rate * (first_hat / (jnp.sqrt(second_hat) + ADAM_EPS) + decay * weight)
    return (first_new, second_new, weight_new)


def adam_store(refs, at, gradient):
    w, m, v, m_out, v_out, w_out = refs
    first, second, weight = adam_math(w[at], m[at], v[at], gradient, RATE_MATRIX, DECAY_MATRIX)
    m_out[at] = first
    v_out[at] = second
    w_out[at] = weight


def parities(core, own, other):
    return jnp.where(core == 0, own, other), jnp.where(core == 0, other, own)


def adam_attn_body(ids, own, other, *refs):
    core = ids[1]
    low = low_lanes()
    qkv_refs = refs[0:3] + refs[6:9]
    for tile in range(4):
        start = (tile // 2) * 768 + (tile % 2) * 128
        cols = pl.ds(pl.multiple_of(pl.program_id(0) * 256 + start, 128), 128)
        even, odd = parities(core, own[:, cols].astype(F32), other[:, cols].astype(F32))
        first = jnp.where(low, even, pltpu.roll(odd, HEAD_DIM, 1))
        second = jnp.where(low, pltpu.roll(even, HEAD_DIM, 1), odd)
        adam_store(qkv_refs, (slice(None), slice(tile * 256, tile * 256 + 128)), first)
        adam_store(qkv_refs, (slice(None), slice(tile * 256 + 128, tile * 256 + 256)), second)

    @pl.when(pl.program_id(0) == 0)
    def _():
        out_refs = refs[3:6] + refs[9:12]
        for panel in range(4):
            rows = slice((panel % 2) * 64, (panel % 2) * 64 + 64)
            cols = slice(1536 + 256 * (panel // 2), 1792 + 256 * (panel // 2))
            span = slice(panel * 256, panel * 256 + 256)
            even, odd = parities(core, own[rows, cols].astype(F32), other[rows, cols].astype(F32))
            adam_store(out_refs, (slice(0, 64), span), even)
            adam_store(out_refs, (slice(64, 128), span), odd)


def adam_mlp_body(ids, own, other, *refs):
    core = ids[1]
    up_refs = refs[0:3] + refs[-6:-3]
    down_refs = refs[3:6] + refs[-3:]
    cols = pl.ds(pl.multiple_of(pl.program_id(0) * 128, 128), 128)
    for base, refs_of in ((0, up_refs), (128, down_refs)):
        rows = slice(base, base + 128)
        for parity, grad in enumerate(
            parities(core, own[rows, cols].astype(F32), other[rows, cols].astype(F32))
        ):
            span = slice(parity * 128, (parity + 1) * 128)
            adam_store(refs_of, (slice(None), span) if base == 0 else (span, slice(None)), grad)


def rotary_tables(segments):
    row_count = segments.shape[0]
    row_index = jnp.arange(row_count, dtype=jnp.int32)
    earlier = jnp.concatenate([jnp.full((1,), -1, jnp.int32), segments[:-1]])
    starts = jnp.where(segments != earlier, row_index, 0)
    position = (row_index - lax.cummax(starts, axis=0)).astype(F32)
    half_dim = ROT_DIM // 2
    dims = jnp.arange(LANES, dtype=jnp.int32) % HEAD_DIM
    frequency = ROPE_BASE ** (-2.0 * (dims % half_dim).astype(F32) / ROT_DIM)
    turned = dims < ROT_DIM
    angles = position[:, None] * jnp.where(turned, frequency, 0.0)[None, :]
    cosine, sine = jnp.cos(angles), jnp.sin(angles)
    front = (dims < half_dim)[None, :]
    return cosine, jnp.where(front, -sine, 0.0), jnp.where(front, 0.0, sine)


def on_device(
    sizes,
    tokens,
    segments,
    cotangent,
    w_qkv,
    w_out,
    w_up,
    w_down,
    vectors,
    m_qkv,
    m_out,
    m_up,
    m_down,
    m_vectors,
    v_qkv,
    v_out,
    v_up,
    v_down,
    v_vectors,
):
    copies, owners = sizes
    me = lax.axis_index("zero")
    plane = lax.axis_index("dp")
    core = plane % 2
    ids = jnp.stack([me, core, (plane // 2) % 2]).astype(jnp.int32)

    def move(value, target):
        pairs = []
        for d in range(copies):
            for z in range(owners):
                to_d, to_z = target(d, z)
                pairs.append((d * owners + z, to_d * owners + to_z))
        return lax.ppermute(value, AXES, pairs)

    def swap(value, dp_bits, zero_bits):
        return move(value, lambda d, z: (d ^ dp_bits, z ^ zero_bits))

    def swap_far(value):
        return move(value, lambda d, z: (d, z ^ (6 if d & 2 else 4)))

    def sync(*values):
        return lax.optimization_barrier(values)

    def add(*terms):
        return functools.reduce(jnp.add, [t.astype(F32) for t in terms])

    def reduce_first(keep, send_x, send_y):
        return keep, swap(send_x, 0, 1), swap(send_y, 2, 0)

    def reduce_second(state):
        keep, got_x, got_y = state
        far = add(keep[3], got_y[1]).astype(BF16)
        near = add(keep[1], got_x[1]).astype(BF16)
        return keep, got_x, got_y, far, near, swap(far, 0, 1), swap(near, 0, 2)

    def reduce_third(state):
        keep, got_x, got_y, _, _, got_far, got_near = state
        far = add(keep[2], got_y[0], got_far).astype(BF16)
        return add(keep[0], got_x[0], got_near), far, swap_far(far)

    def reduce_fourth(state):
        total = (state[0] + state[2].astype(F32)).astype(BF16)
        return total, swap(total, 2, 0)

    def reduce_fifth(state):
        total = add(*state).astype(BF16)
        bit = 4
        while bit < copies:
            total = add(total, swap(total, bit, 0)).astype(BF16)
            bit *= 2
        return total, swap(total, 1, 0)

    T, width = tokens.shape
    rows = 2 * T
    sds = jax.ShapeDtypeStruct
    row_block = lambda n, c=width: spec((n, c), lambda i: (i, 0))
    col_block = lambda n: spec((width, n), lambda i: (0, i))

    def block_call(body, grid, ins, outs, flops, moved, scratch=(), name=None):
        return kernel_call(
            body,
            grid,
            [place for _, place in ins],
            [place for _, place in outs],
            [shape for shape, _ in outs],
            flops,
            moved,
            scratch=scratch,
            name=name,
        )(*[value for value, _ in ins])

    def const(value):
        return value, whole(value.shape)

    def kept(shape, dtype):
        return sds(shape, dtype), whole(shape)

    steps = rows // 256
    with jax.named_scope("prep"):
        own_a = block_call(
            prep_attn_body,
            (1,),
            [(ids, scalars()), const(w_qkv), const(w_out), (vectors, whole((16, 128)))],
            [kept((144, 1280), BF16)],
            0,
            3e6,
            name="prep_attn",
        )[0]

    def prep_mlp(part, shape, ins, beside):
        with jax.named_scope("prep"):
            return block_call(
                functools.partial(prep_mlp_body, part),
                (1,),
                [(ids, scalars()), const(ins[0]), (ins[1], spec((256, width), lambda i: (part, 0), single=True))]
                + [const(value) for value in ins[2:]],
                [kept(shape, BF16)],
                0,
                beside * 3e6,
                name="prep_mlp",
            )[0]

    def z_moves(own):
        return swap(own, 0, 2), swap_far(own)

    with jax.named_scope("gather"):
        seg_other = swap(segments, 1, 0)
        tok_other = swap(tokens, 1, 0)
        dy_other = swap(cotangent, 1, 0)
        own_a, w_up_in = sync(own_a, w_up)
        next_a, far_a = z_moves(own_a)
        across_a = swap(own_a, 0, 1)
        own_b = prep_mlp(0, (256, 1024), (w_up_in, w_down), 20)
        tables = [
            jnp.concatenate(pair, axis=0)
            for pair in zip(rotary_tables(segments), rotary_tables(seg_other))
        ]
        seg_row = jnp.stack([segments, seg_other]).astype(F32)[:, None, :]
        seg_ids = jnp.concatenate([segments, seg_other]).astype(F32)
        next_a, far_a, across_a, own_b, w_up_in, tables, seg_row, seg_ids, tok_other, dy_other = sync(
            next_a, far_a, across_a, own_b, w_up_in, tables, seg_row, seg_ids, tok_other, dy_other
        )
        next_across_a, far_across_a, rest_across_a = swap(next_a, 0, 1), swap(far_a, 0, 1), swap(far_a, 2, 1)
        rest_a = swap(far_a, 2, 0)
        far_b = swap_far(own_b)
        seg_col = jnp.broadcast_to(seg_ids[:, None], (rows, LANES))
        own_c = prep_mlp(1, (352, 1024), (w_up_in, w_down, w_qkv), 25)
        next_across_a, far_across_a, rest_a, rest_across_a, far_b, own_b, own_c, seg_col = sync(
            next_across_a, far_across_a, rest_a, rest_across_a, far_b, own_b, own_c, seg_col
        )
        far_across_b, across_b, rest_b = swap(far_b, 0, 1), swap(own_b, 0, 1), swap(far_b, 2, 0)
        next_b = swap(own_b, 0, 2)
        far_c = swap_far(own_c)
    attn_pieces = [own_a, next_a, far_a, rest_a, across_a, next_across_a, far_across_a, rest_across_a]

    def table_blocks(count):
        return [(t, row_block(count, 128)) for t in tables]

    def halves(own, other, count):
        last = T // count - 1
        return [
            (own, spec((count, width), lambda i: (jnp.minimum(i, last), 0))),
            (other, spec((count, width), lambda i: (jnp.maximum(i - last - 1, 0), 0))),
        ]

    def attention(group, pairs, projected, d_att, previous):
        with jax.named_scope("attention"):
            first = pairs[0]
            head_block = spec((T, 128), lambda h, m: (h, m + first))
            outs = [
                (sds((rows, 256), BF16), head_block),
                (sds((3, rows, 256), BF16), spec((3, T, 128), lambda h, m: (0, h, m + first))),
            ]
            ins = (
                [(value, head_block) for value in projected]
                + [(d_att, spec((T, 128), lambda h, m: (h, m + first + 2 * group)))]
                + [(seg_col, spec((T, LANES), lambda h, m: (h, 0)))]
                + [(seg_row, spec((1, 1, T), lambda h, m: (h, 0, 0)))]
                + [(t, spec((T, 128), lambda h, m: (h, 0))) for t in tables]
            )
            aliases = {len(ins) + n: n for n in range(len(previous))}
            return pl.pallas_call(
                attn_body,
                grid=(2, len(pairs)),
                in_specs=[place for _, place in ins] + [distant()] * len(previous),
                out_specs=[place for _, place in outs],
                out_shape=[shape for shape, _ in outs],
                input_output_aliases=aliases,
                cost_estimate=pl.CostEstimate(
                    flops=len(pairs) * 15000000000, bytes_accessed=len(pairs) * 5000000, transcendentals=0
                ),
                compiler_params=pltpu.CompilerParams(
                    vmem_limit_bytes=VMEM_NEED * MIB, dimension_semantics=("arbitrary",) * 2
                ),
                name="attention",
            )(*[value for value, _ in ins], *previous)

    def blocks_of(shape):
        return [kept((n,) + shape, BF16) for n in (4, 2, 2)]

    with jax.named_scope("qkv"):
        *projected, d_att, attn_in, attn_t, mlp_in, wq_a, full_out, vec, bias_qkv = block_call(
            functools.partial(qkv_first_body, rows // 256),
            (rows // 256,),
            [(ids, scalars())]
            + [const(piece) for piece in attn_pieces]
            + halves(tokens, tok_other, 256)
            + halves(cotangent, dy_other, 256)
            + table_blocks(256),
            [(sds((rows, 256), BF16), row_block(256, 256))] * 3
            + [(sds((rows, 512), BF16), row_block(256, 512)), (sds((rows, width), BF16), row_block(256))]
            + [(sds((width, rows), BF16), col_block(256)), (sds((rows, width), BF16), row_block(256))]
            + [kept((1024, 768), BF16), kept((512, 1024), BF16), kept((16, 1024), F32), kept((1, 1536), F32)],
            2 * rows * 1024 * 1280,
            30e6,
            name="qkv",
        )
    projected, far_across_b, across_b, rest_b, next_b = sync(
        projected, far_across_b, across_b, rest_b, next_b
    )
    with jax.named_scope("gather"):
        rest_across_b, next_across_b = swap(far_across_b, 2, 0), swap(next_b, 0, 1)
    half_a = attention(0, (0,), projected, d_att, [])
    half_a, projected, far_c, own_c = sync(half_a, projected, far_c, own_c)
    with jax.named_scope("gather"):
        far_across_c, rest_c, next_c = swap(far_c, 0, 1), swap(far_c, 2, 0), swap(own_c, 0, 2)
    att_a, grad_a = attention(0, (1,), projected, d_att, half_a)
    att_a, grad_a, rest_across_b, next_across_b, far_across_c, rest_c, own_c, next_c, attn_t, mlp_in = sync(
        att_a, grad_a, rest_across_b, next_across_b, far_across_c, rest_c, own_c, next_c, attn_t, mlp_in
    )
    with jax.named_scope("gather"):
        across_c, next_across_c, rest_across_c = swap(own_c, 0, 1), swap(next_c, 0, 1), swap(far_across_c, 2, 0)
    pieces_b = [own_b, next_b, far_b, rest_b, across_b, next_across_b, far_across_b, rest_across_b]

    def mlp(part, weights, rows_in):
        with jax.named_scope("mlp"):
            *results, hid, gp, sums, w_up_full, w_down_full = block_call(
                functools.partial(mlp_body, part, steps),
                (steps,),
                [(ids, scalars())]
                + [const(w) for w in weights]
                + [const(vec), (rows_in, row_block(256))]
                + halves(cotangent, dy_other, 256),
                [(sds((n, 256, 1024), BF16), distant()) for n in (4, 2, 2)]
                + [(sds((rows, width), BF16), row_block(256))] * 2
                + [kept((8, 1024), F32)]
                + [(sds((1024, 1024), BF16), distant())] * 2,
                2 * rows * 1024 * 1024 * 4,
                40e6,
                scratch=[
                    pltpu.VMEM((1024, rows), BF16),
                    pltpu.VMEM((1024, rows), BF16),
                    pltpu.VMEM((rows, 1024), BF16),
                    pltpu.VMEM((rows, 1024), BF16),
                    pltpu.VMEM((8, 1024), F32),
                    pltpu.VMEM((1024, 512), BF16),
                ]
                + [pltpu.VMEM((n, 256, 1024), BF16) for n in (4, 2, 2)]
                + [pltpu.VMEM((1024, 1024), BF16)] * 2
                + [pltpu.SemaphoreType.DMA((8,))],
                name="mlp",
            )
            return results, hid, gp, sums, w_up_full, w_down_full

    mlp_a = mlp(0, pieces_b, mlp_in)
    mlp_a, mlp_in, across_c, next_across_c, rest_across_c = sync(
        mlp_a, mlp_in, across_c, next_across_c, rest_across_c
    )
    pieces_c = [own_c, next_c, far_c, rest_c, across_c, next_across_c, far_across_c, rest_across_c]
    reduce_a = reduce_first(*mlp_a[0])
    mlp_b = mlp(1, pieces_c, mlp_in)
    mlp_b, reduce_a, attn_in = sync(mlp_b, reduce_a, attn_in)
    reduce_a = reduce_second(reduce_a)
    reduce_b = reduce_first(*mlp_b[0])
    attn_in, *ready = sync(attn_in, *reduce_a[3:5])

    with jax.named_scope("qkv"):
        *projected, wq_b = block_call(
            qkv_second_body,
            (rows // 512,),
            [(ids, scalars())]
            + [(piece, whole((96, width))) for piece in pieces_c]
            + [(attn_in, row_block(512)), const(bias_qkv)]
            + table_blocks(512),
            [(sds((rows, 256), BF16), row_block(512, 256))] * 3 + [kept((1024, 768), BF16)],
            2 * rows * 1024 * 768,
            12e6,
            name="qkv",
        )
    att_b, grad_b = attention(1, (0, 1), projected, d_att, [])
    att_b, grad_b, reduce_a, reduce_b = sync(att_b, grad_b, reduce_a, reduce_b)
    reduce_a = reduce_third(reduce_a)
    reduce_b = reduce_second(reduce_b)
    grad_b, *ready = sync(grad_b, reduce_a[1], *reduce_b[3:5])
    with jax.named_scope("attn_weights"):
        *blocks, bias_sum = block_call(
            attn_weights_body,
            (7,),
            [(ids, scalars()), const(attn_t)]
            + [(grad_a, spec((1, rows, 256), lambda n: (jnp.minimum(n, 2), 0, 0)))]
            + [(grad_b, spec((1, rows, 256), lambda n: (jnp.clip(n - 3, 0, 2), 0, 0)))]
            + [(value, distant()) for value in (att_a, att_b, cotangent, dy_other)],
            blocks_of((128, 2048)) + [kept((8, 1536), F32)],
            2 * rows * 1024 * 2048,
            24e6,
            scratch=[pltpu.VMEM((1024, 256), BF16)]
            + [pltpu.VMEM((rows, 256), BF16)] * 2
            + [pltpu.VMEM((T, width), BF16)] * 2
            + [pltpu.SemaphoreType.DMA((4,))],
            name="attn_weights",
        )
    blocks, grad_b = sync(blocks, grad_b)
    reduce_o = reduce_first(*blocks)

    _, hid_a, gp_a, sums_a, up_a, down_a = mlp_a
    _, hid_b, gp_b, sums_b, up_b, down_b = mlp_b

    def adam_mlp(part, totals, previous):
        wide = [spec((128, 256), lambda n: (0, 2 * n + part))] * 3
        wide += [spec((256, 128), lambda n: (part, n))] * 3
        return pl.pallas_call(
            adam_mlp_body,
            grid=(8,),
            in_specs=[scalars()]
            + [whole((256, 1024))] * 2
            + wide
            + [pl.BlockSpec(memory_space=pl.ANY)] * len(previous),
            out_specs=wide,
            out_shape=[sds((128, 4096), F32)] * 3 + [sds((512, 1024), F32)] * 3,
            input_output_aliases={9 + n: n for n in range(len(previous))},
            cost_estimate=pl.CostEstimate(flops=0, bytes_accessed=14000000, transcendentals=0),
            compiler_params=pltpu.CompilerParams(
                vmem_limit_bytes=VMEM_NEED * MIB, dimension_semantics=("arbitrary",)
            ),
            name="adam_mlp",
        )(ids, *totals, w_up, m_up, v_up, w_down, m_down, v_down, *previous)

    def back(own, grad, rows_tok, extra, outs):
        first = 0 if own else T // 256
        block = lambda c=width: spec((256, c), lambda i: (i + first, 0))
        lead = spec((3, 256, 256), lambda i: (0, i + first, 0))
        with jax.named_scope("back"):
            return block_call(
                functools.partial(back_body, own),
                (T // 256,),
                [(grad_a, lead), (grad, lead), (att_a, block(256)), (att_b, block(256))]
                + [(value, block()) for value in (hid_a, hid_b, gp_a, gp_b)]
                + [const(w) for w in (full_out, down_a, down_b, up_a, up_b, wq_a, wq_b)]
                + [(rows_tok, row_block(256)), const(vec)]
                + extra,
                outs + [kept((8, width), F32)],
                2 * T * 1024 * 6144,
                40e6,
                name="back",
            )

    reduce_a = reduce_fourth(reduce_a)
    reduce_b = reduce_third(reduce_b)
    pair_block = spec((2, 256, width), lambda i: (0, i, 0))
    part_other, sums_other = back(False, grad_b, tok_other, [], [(sds((2, T, width), BF16), pair_block)])
    part_other, sums_other, grad_b, reduce_a, reduce_b, reduce_o = sync(
        part_other, sums_other, grad_b, reduce_a, reduce_b, reduce_o
    )
    reduce_o = reduce_second(reduce_o)
    part_other, reduce_a, reduce_b, *ready = sync(part_other, reduce_a, reduce_b, *reduce_o[3:5])
    reduce_a = reduce_fifth(reduce_a)
    reduce_b = reduce_fourth(reduce_b)
    part_got = swap(part_other, 1, 0)
    updated_mlp = adam_mlp(0, reduce_a, [])
    updated_mlp, grad_b, reduce_b, reduce_o, part_got = sync(
        updated_mlp, grad_b, reduce_b, reduce_o, part_got
    )
    reduce_o = reduce_third(reduce_o)
    reduce_b = reduce_fifth(reduce_b)
    grad_b, *ready = sync(grad_b, reduce_o[1], reduce_b[0])
    layer_out, tokens_grad, sums_own = back(
        True,
        grad_b,
        tokens,
        [(cotangent, row_block(256)), (part_got, pair_block)],
        [(sds((T, width), BF16), row_block(256)), (sds((T, width), F32), row_block(256))],
    )
    sums_own, updated_mlp, reduce_b, reduce_o = sync(sums_own, updated_mlp, reduce_b, reduce_o)
    reduce_o = reduce_fourth(reduce_o)

    with jax.named_scope("vectors"):
        is_core = jnp.arange(2) == core
        grad_bias = jnp.where(core == 0, sums_a[1:2], 0.0)
        bias_sum = jnp.swapaxes(bias_sum[0].reshape(2, 3, 256), 0, 1)
        grad_bias_qkv = jnp.where(
            is_core[None, None, :, None], bias_sum.reshape(3, 8, 1, 64), 0.0
        ).reshape(3, width)
        grad_bias_up = jnp.where(
            is_core[None, None, :, None],
            jnp.swapaxes(jnp.stack([sums_a[0], sums_b[0]]).reshape(2, 8, 128), 0, 1)[:, :, None],
            0.0,
        ).reshape(4, width)
        total = jnp.concatenate(
            [
                sums_own[0:4] + sums_other[0:4],
                grad_bias_qkv,
                grad_bias,
                grad_bias_up,
                grad_bias,
                jnp.zeros((3, width), F32),
            ],
            axis=0,
        )
        moved = [swap(total, 0, step) for step in (2, 4, 6)]
        updated_mlp = adam_mlp(1, reduce_b, updated_mlp)
        updated_mlp, reduce_o, total, moved = sync(updated_mlp, reduce_o, total, moved)
        reduce_o = reduce_fifth(reduce_o)
        total = functools.reduce(jnp.add, moved, total)
        across, beside, both = swap(total, 0, 1), swap(total, 2, 0), swap(total, 2, 1)
        total = (total + across) + (beside + both)
        bit = 4
        while bit < copies:
            total = total + swap(total, bit, 0)
            bit *= 2
        total = total + swap(total, 1, 0)
        share = lax.dynamic_slice_in_dim(total[0:13], me * 128, 128, 1)
        first_vectors, second_vectors, new_vectors = adam_math(
            vectors, m_vectors, v_vectors, share, RATE_VECTOR, 0.0
        )

    with jax.named_scope("adam"):
        wide = [spec((128, 1024), lambda n: (0, n))] * 3 + [whole((128, 1024))] * 3
        updated_attn = kernel_call(
            adam_attn_body,
            (3,),
            [scalars()] + [whole((128, 2048))] * 2 + wide,
            wide,
            [sds((128, 3072), F32)] * 3 + [sds((128, 1024), F32)] * 3,
            0,
            13e6,
            name="adam",
        )(ids, *reduce_o, w_qkv, m_qkv, v_qkv, w_out, m_out, v_out)
    first_qkv, second_qkv, new_qkv, first_out, second_out, new_out = updated_attn
    first_up, second_up, new_up, first_down, second_down, new_down = updated_mlp
    return (
        layer_out,
        tokens_grad,
        first_qkv,
        first_out,
        first_up,
        first_down,
        first_vectors,
        second_qkv,
        second_out,
        second_up,
        second_down,
        second_vectors,
        new_qkv,
        new_out,
        new_up,
        new_down,
        new_vectors,
    )


def solution(mesh):
    rows, owned, spread = P(AXES, None), P("zero", None), P(None, "zero")
    state = (owned, owned, owned, owned, spread)
    return jax.shard_map(
        functools.partial(on_device, (mesh.shape["dp"], mesh.shape["zero"])),
        mesh=mesh,
        in_specs=(rows, P(AXES), rows) + state * 3,
        out_specs=(rows, rows) + state * 3,
        check_vma=False,
    )
```

```python
import functools

import jax
import jax.numpy as jnp
from jax import lax
from jax.experimental import pallas as pl
from jax.experimental.pallas import tpu as pltpu
from jax.sharding import PartitionSpec as P

HEAD_DIM = 64
ROT_DIM = 16
STEP = 10
EPS_NORM = 1e-05
BETA_ONE = 0.9
BETA_TWO = 0.999
ADAM_EPS = 1e-08
RATE_MATRIX = 0.05
RATE_VECTOR = 0.2
DECAY_MATRIX = 0.1
ROPE_BASE = 10000.0
INV_ROOT_TWO = 0.7071067811865476
INV_ROOT_TAU = 0.3989422804014327
MASKED = -1e30
LANES = 128
AXES = ("dp", "zero")
F32 = jnp.float32
BF16 = jnp.bfloat16
MIB = 1024 * 1024
VMEM_NEED = 58


def spec(block, index, single=False):
    if single:
        return pl.BlockSpec(block, index, pipeline_mode=pl.Buffered(1))
    return pl.BlockSpec(block, index)


def whole(shape):
    return spec(shape, lambda *_: (0,) * len(shape), single=True)


def distant():
    return pl.BlockSpec(memory_space=pl.ANY)


def scalars():
    return pl.BlockSpec(memory_space=pltpu.SMEM)


def kernel_call(body, grid, in_specs, out_specs, out_shape, flops, moved, scratch=(), name=None):
    return pl.pallas_call(
        body,
        grid=grid,
        in_specs=in_specs,
        out_specs=out_specs,
        out_shape=out_shape,
        scratch_shapes=list(scratch),
        cost_estimate=pl.CostEstimate(flops=int(flops), bytes_accessed=int(moved), transcendentals=0),
        compiler_params=pltpu.CompilerParams(
            vmem_limit_bytes=VMEM_NEED * MIB, dimension_semantics=("arbitrary",) * len(grid)
        ),
        name=name,
    )


def nn(left, right):
    return lax.dot_general(left, right, (((1,), (0,)), ((), ())), preferred_element_type=F32)


def nt(left, right):
    return lax.dot_general(left, right, (((1,), (1,)), ((), ())), preferred_element_type=F32)


def tn(left, right):
    return lax.dot_general(left, right, (((0,), (0,)), ((), ())), preferred_element_type=F32)


def piece_owner(ids, place):
    step = place % 4
    if step > 1:
        step = 2 + ids[2] if step == 2 else 3 - ids[2]
    return jnp.bitwise_xor(ids[0], 2 * step + place // 4)


SLOTS = ((0, 0), (1, 0), (2, 0), (2, 1), (0, 1), (1, 1), (3, 0), (3, 1))


def slot_owner(ids, slot):
    step, side = SLOTS[slot]
    if step > 1:
        step = 2 + ids[2] if step == 2 else 3 - ids[2]
    return jnp.bitwise_xor(ids[0], 2 * step + side)


def slot_ref(outs, slot):
    return (outs[0], slot) if slot < 4 else (outs[1], slot - 4) if slot < 6 else (outs[2], slot - 6)


def low_lanes():
    return lax.broadcasted_iota(jnp.int32, (1, LANES), 1) < HEAD_DIM


def pick_parity(core, tile_a, tile_b):
    low = low_lanes()
    even = jnp.where(low, tile_a, pltpu.roll(tile_b, HEAD_DIM, 1))
    odd = jnp.where(low, pltpu.roll(tile_a, HEAD_DIM, 1), tile_b)
    return jnp.where(core == 0, even, odd)


def prep_attn_body(ids, w_qkv, w_out, vec, out):
    core = ids[1]
    for part in range(3):
        for tile in range(2):
            base = part * 1024 + tile * 256
            at = part * 256 + tile * 128
            out[0:128, at : at + 128] = pick_parity(
                core, w_qkv[:, base : base + 128], w_qkv[:, base + 128 : base + 256]
            ).astype(BF16)
    rows = w_out[pl.ds(pl.multiple_of(core * 64, 64), 64), :].astype(BF16)
    for panel in range(4):
        at = 768 + 256 * (panel // 2)
        base = (panel % 2) * 64
        out[base : base + 64, at : at + 256] = rows[:, 256 * panel : 256 * panel + 256]
    out[128:144, 0:128] = jnp.where(lax.broadcasted_iota(jnp.int32, (16, 128), 0) < 13, vec[...], 0.0).astype(BF16)
    out[128:144, 128:1280] = jnp.zeros((16, 1152), BF16)


def prep_mlp_body(part, ids, w_up, w_down, *refs):
    out = refs[-1]
    core = ids[1]
    top = 96 * part
    for owner in range(8):
        start = pl.multiple_of(owner * 512 + part * 256 + core * 128, 128)
        out[top : top + 128, owner * 128 : (owner + 1) * 128] = w_up[:, pl.ds(start, 128)].astype(BF16)
    out[top + 128 : top + 256, :] = w_down[pl.ds(pl.multiple_of(core * 128, 128), 128), :].astype(BF16)
    if not part:
        return
    w_qkv = refs[0]
    for third in range(3):
        for tile in range(2):
            base = third * 1024 + 512 + tile * 256
            value = pick_parity(core, w_qkv[:, base : base + 128], w_qkv[:, base + 128 : base + 256]).astype(BF16)
            for panel in range(4):
                at = panel * 256 + tile * 128
                out[32 * third : 32 * third + 32, at : at + 128] = value[32 * panel : 32 * panel + 32]


def normalize(inputs):
    centred = inputs - jnp.mean(inputs, axis=-1, keepdims=True)
    variance = jnp.mean(centred * centred, axis=-1, keepdims=True)
    inv_std = lax.rsqrt(variance + EPS_NORM)
    return centred * inv_std, inv_std


def turned(x, cos, sin_lo, sin_hi, sign):
    return x * cos[...] + sign * (pltpu.roll(x, 8, 1) * sin_hi[...] + pltpu.roll(x, 120, 1) * sin_lo[...])


def project(group, rows, w_qkv, bias, tables, outs):
    for part, out in enumerate(outs):
        cols = slice(part * 256, (part + 1) * 256)
        at = group * 768 + part * 256
        acc = nn(rows, w_qkv[:, cols]) + bias[:, at : at + 256]
        if part == 2:
            out[...] = acc.astype(BF16)
            continue
        for tile in range(2):
            x = turned(acc[:, tile * 128 : (tile + 1) * 128], *tables, 1.0)
            if part == 0:
                x = x * HEAD_DIM ** (-0.5)
            out[:, tile * 128 : (tile + 1) * 128] = x.astype(BF16)


def qkv_first_body(steps, ids, *refs):
    pieces, refs = refs[:8], refs[8:]
    tok_own, tok_other, dy_own, dy_other, cos, sin_lo, sin_hi = refs[:7]
    q, k, v, d_att, attn_in, attn_t, mlp_in, w_qkv, w_out, vec, bias = refs[7:]
    step = pl.program_id(0)

    @pl.when(step == 0)
    def _():
        for place, piece in enumerate(pieces):
            owner = piece_owner(ids, place)
            at_owner = pl.ds(pl.multiple_of(owner * 128, 128), 128)
            w_qkv[at_owner, :] = piece[0:128, 0:768]
            vec[:, at_owner] = piece[128:144, 0:128].astype(F32)
            for panel in range(4):
                at = 768 + 256 * (panel // 2)
                base = (panel % 2) * 64
                w_out[pl.ds(pl.multiple_of(owner * 64, 64), 64), 256 * panel : 256 * panel + 256] = piece[
                    base : base + 64, at : at + 256
                ]
        for part in range(3):
            for tile in range(4):
                base = tile * 256
                row = slice(4 + part, 5 + part)
                at = (tile // 2) * 768 + part * 256 + (tile % 2) * 128
                bias[:, at : at + 128] = pick_parity(
                    ids[1], vec[row, base : base + 128], vec[row, base + 128 : base + 256]
                )

    first = step < steps // 2
    d_att[...] = nt(jnp.where(first, dy_own[...], dy_other[...]), w_out[...]).astype(BF16)
    normed, _ = normalize(jnp.where(first, tok_own[...], tok_other[...]).astype(F32))
    rows = (normed * vec[0:1, :] + vec[1:2, :]).astype(BF16)
    mlp_in[...] = (normed * vec[2:3, :] + vec[3:4, :]).astype(BF16)
    attn_in[...] = rows
    attn_t[...] = rows.T
    project(0, rows, w_qkv, bias, (cos, sin_lo, sin_hi), (q, k, v))


ATTN_ROWS = 256


def cat(parts, axis=0):
    return jnp.concatenate(parts, axis=axis) if len(parts) > 1 else parts[0]


def attn_body(q, k, v, d_att, seg_col, seg_row, cos, sin_lo, sin_hi, *refs):
    att, grad = refs[-2:]
    count = q.shape[0]
    size = ATTN_ROWS
    blocks = count // size
    span = [slice(j * size, (j + 1) * size) for j in range(blocks)]
    low = low_lanes()
    zero = jnp.zeros((), BF16)
    causal = lax.broadcasted_iota(jnp.int32, (size, size), 0) >= lax.broadcasted_iota(
        jnp.int32, (size, size), 1
    )
    q_t, da_t = q[...].T, d_att[...].T

    def row_total(parts, reduce, join):
        cols = [reduce(part, axis=-1, keepdims=True) for part in parts]
        return [
            functools.reduce(join, [cols[j][(i - j) * size : (i - j + 1) * size] for j in range(i + 1)])
            for i in range(blocks)
        ]

    def row_sum(parts):
        return cat(
            [
                functools.reduce(jnp.add, [parts[j][(i - j) * size : (i - j + 1) * size] for j in range(i + 1)])
                for i in range(blocks)
            ]
        )

    def products(half):
        lanes = low if half == 0 else jnp.logical_not(low)
        q_h = jnp.where(lanes, q[...], zero)
        da_h = jnp.where(lanes, d_att[...], zero)
        scores = [nt(q_h[j * size :], k[span[j], :]) for j in range(blocks)]
        return scores, [nt(da_h[j * size :], v[span[j], :]) for j in range(blocks)]

    def softmax_both(scores, grad_probs):
        masked = []
        for j in range(blocks):
            allowed = seg_col[j * size :, 0:1] == seg_row[0, :, span[j]]
            allowed = cat([allowed[:size] & causal] + ([allowed[size:]] if j < blocks - 1 else []))
            masked.append(jnp.where(allowed, scores[j], MASKED))
        top = row_total(masked, jnp.max, jnp.maximum)
        raised = [jnp.exp(masked[j] - cat(top[j:])) for j in range(blocks)]
        inv = [1.0 / total for total in row_total(raised, jnp.sum, jnp.add)]
        probs = [raised[j] * cat(inv[j:]) for j in range(blocks)]
        delta = row_total([g * p for g, p in zip(grad_probs, probs)], jnp.sum, jnp.add)
        grad_scores = [
            (probs[j] * (grad_probs[j] - cat(delta[j:]))).astype(BF16) for j in range(blocks)
        ]
        return [p.astype(BF16) for p in probs], grad_scores

    def results(half, probs, grad_scores):
        rows = slice(half * HEAD_DIM, (half + 1) * HEAD_DIM)
        return (
            row_sum([nn(probs[j], v[span[j], :]) for j in range(blocks)]),
            row_sum([nn(grad_scores[j], k[span[j], :]) for j in range(blocks)]),
            cat([nn(q_t[rows, j * size :], grad_scores[j]) for j in range(blocks)], 1),
            cat([nn(da_t[rows, j * size :], probs[j]) for j in range(blocks)], 1),
        )

    first = softmax_both(*products(0))
    second = products(1)
    out_a, dq_a, dk_a, dv_a = results(0, *first)
    out_b, dq_b, dk_b, dv_b = results(1, *softmax_both(*second))
    tables = (cos, sin_lo, sin_hi)
    att[...] = jnp.where(low, out_a, out_b).astype(BF16)
    grad[0] = turned(jnp.where(low, dq_a, dq_b) * HEAD_DIM ** (-0.5), *tables, -1.0).astype(BF16)
    grad[1] = turned(jnp.concatenate([dk_a, dk_b], axis=0).T, *tables, -1.0).astype(BF16)
    grad[2] = jnp.concatenate([dv_a, dv_b], axis=0).T.astype(BF16)


def project_attn_body(ids, *refs):
    pieces, (attn_in, bias, d_att, seg_col, seg_row, *tables) = refs[:8], refs[8:16]
    att, grad, w_qkv, *projected = refs[16:]
    half, pair = pl.program_id(0), pl.program_id(1)

    @pl.when((half == 0) & (pair == 0))
    def _():
        for place, piece in enumerate(pieces):
            owner = piece_owner(ids, place)
            for part in range(3):
                for panel in range(4):
                    at = pl.ds(pl.multiple_of(owner * 128 + 32 * panel, 32), 32)
                    w_qkv[at, part * 256 : part * 256 + 256] = piece[
                        32 * part : 32 * part + 32, panel * 256 : panel * 256 + 256
                    ]

    @pl.when(pair == 0)
    def _():
        project(1, attn_in[...], w_qkv, bias, tables, projected)

    lanes = pl.ds(pl.multiple_of(pair * LANES, LANES), LANES)
    attn_body(*[value.at[:, lanes] for value in projected], d_att, seg_col, seg_row, *tables, att, grad)


def attn_weights_body(ids, attn_t, grad_a, grad_b, far_att_a, far_att_b, far_own, far_other, *refs):
    keep, send_x, send_y, bias, result, att_a, att_b, dy_own, dy_other, sems = refs
    copies = [
        pltpu.make_async_copy(source, target, sems.at[n])
        for n, (source, target) in enumerate(
            ((far_att_a, att_a), (far_att_b, att_b), (far_own, dy_own), (far_other, dy_other))
        )
    ]

    @pl.when(pl.program_id(0) == 0)
    def _():
        for copy in copies:
            copy.start()

    step = pl.program_id(0)
    outs = (keep, send_x, send_y)

    @pl.when(step < 6)
    def _():
        rhs = jnp.where(step < 3, grad_a[0], grad_b[0])
        result[...] = nn(attn_t[...], rhs).astype(BF16)
        cols = pl.ds(pl.multiple_of(step * 256, 256), 256)
        bias[0:1, cols] = jnp.sum(rhs.astype(F32), axis=0, keepdims=True)
        for slot in range(8):
            out, at = slot_ref(outs, slot)
            base = pl.multiple_of(slot_owner(ids, slot) * 128, 128)
            out[at, :, cols] = result[pl.ds(base, 128), :]

    @pl.when(step == 6)
    def _():
        for copy in copies:
            copy.wait()
        count = dy_own.shape[0]
        for group, att in enumerate((att_a, att_b)):
            flipped = att[...].T
            for panel in range(4):
                cols = slice(panel * 256, panel * 256 + 256)
                term = nn(flipped[:, :count], dy_own[:, cols]) + nn(flipped[:, count:], dy_other[:, cols])
                result[group * 256 : group * 256 + 256, :] = term.astype(BF16)
                for slot in range(8):
                    out, at = slot_ref(outs, slot)
                    owner = slot_owner(ids, slot)
                    col = 1536 + 256 * (panel // 2)
                    base = (panel % 2) * 64

                    @pl.when(owner // 4 == group)
                    def _():
                        out[at, base : base + 64, col : col + 256] = result[
                            pl.ds(pl.multiple_of(owner * 64, 64), 64), :
                        ]


def mlp_body(part, steps, ids, *refs):
    pieces, (vec, mlp_in, dy_own, dy_other) = refs[:8], refs[8:12]
    far_outs, (hidden_out, grad_out, sums, far_up, far_down) = refs[12:15], refs[15:20]
    mlp_t, hidden_t, grad_pre, dy, bias, result, keep, send_x, send_y, w_up, w_down, sems = refs[20:]
    outs = (keep, send_x, send_y)
    weight_copies = [
        pltpu.make_async_copy(w_up, far_up, sems.at[0]),
        pltpu.make_async_copy(w_down, far_down, sems.at[1]),
    ]
    core = ids[1]
    step = pl.program_id(0)

    @pl.when(step == 0)
    def _():
        for owner in range(8):
            start = pl.multiple_of((owner % 2) * 512 + part * 256 + core * 128, 128)
            row = 8 + owner // 2
            bias[0:1, owner * 128 : (owner + 1) * 128] = vec[row : row + 1, pl.ds(start, 128)]
        sums[...] = jnp.zeros_like(sums)
        for place, piece in enumerate(pieces):
            at = pl.ds(pl.multiple_of(piece_owner(ids, place) * 128, 128), 128)
            top = 96 * part
            w_up[at, :] = piece[top : top + 128, :]
            w_down[at, :] = piece[top + 128 : top + 256, :]
        for copy in weight_copies:
            copy.start()

    rows = mlp_in[...]
    grads = jnp.where(step < steps // 2, dy_own[...], dy_other[...])
    count = rows.shape[0]
    at = pl.ds(pl.multiple_of(step * count, count), count)
    mlp_t[:, at] = rows.T
    dy[at, :] = grads
    sums[1:2, :] += jnp.sum(grads.astype(F32), axis=0, keepdims=True)
    for col in range(0, 1024, 512):
        cols = slice(col, col + 512)
        pre = nn(rows, w_up[:, cols]) + bias[0:1, cols]
        grad_hidden = nt(grads, w_down[cols, :])
        cdf = 0.5 + 0.5 * lax.erf(pre * INV_ROOT_TWO)
        pdf = jnp.exp(-0.5 * pre * pre) * INV_ROOT_TAU
        act = (pre * cdf).astype(BF16)
        hidden_t[cols, at] = act.T
        hidden_out[:, cols] = act
        gp = (grad_hidden * (cdf + pre * pdf)).astype(BF16)
        grad_pre[at, cols] = gp
        grad_out[:, cols] = gp
        sums[0:1, cols] += jnp.sum(gp.astype(F32), axis=0, keepdims=True)

    @pl.when(step == steps - 1)
    def _():
        copies = list(weight_copies)
        for base_row, left, right in ((0, mlp_t, grad_pre), (128, hidden_t, dy)):
            for col in range(0, 1024, 512):
                cols = slice(col, col + 512)
                result[...] = nn(left[...], right[:, cols]).astype(BF16)
                for slot in range(8):
                    out, place = slot_ref(outs, slot)
                    base = pl.multiple_of(slot_owner(ids, slot) * 128, 128)
                    out[place, base_row : base_row + 128, cols] = result[pl.ds(base, 128), :]
            span = pl.ds(base_row, 128)
            for out, far_out in zip(outs, far_outs):
                copy = pltpu.make_async_copy(out.at[:, span, :], far_out.at[:, span, :], sems.at[len(copies)])
                copy.start()
                copies.append(copy)
        for copy in copies:
            copy.wait()


def back_body(own, grad_a, grad_b, att_a, att_b, hid_a, hid_b, gp_a, gp_b, *refs):
    w_out, down_a, down_b, up_a, up_b, wq_a, wq_b, tok, vec = refs[:9]
    if own:
        dy, other, out, result, sums = refs[9:]
    else:
        out, sums = refs[9:]
    inputs = tok[...].astype(F32)
    normed, inv_std = normalize(inputs)
    branch = nn(att_a[...], w_out[0:256, :]) + nn(att_b[...], w_out[256:512, :])
    branch = branch + nn(hid_a[...], down_a[...]) + nn(hid_b[...], down_b[...])
    back_mlp = nt(gp_a[...], up_a[...]) + nt(gp_b[...], up_b[...])
    back_attn = None
    for grad, w in ((grad_a, wq_a), (grad_b, wq_b)):
        for part in range(3):
            term = nt(grad[part], w[:, part * 256 : part * 256 + 256])
            back_attn = term if back_attn is None else back_attn + term
    scaled = back_attn * vec[0:1, :] + back_mlp * vec[2:3, :]

    @pl.when(pl.program_id(0) == 0)
    def _():
        sums[...] = jnp.zeros_like(sums)

    for row, value in enumerate((back_attn * normed, back_attn, back_mlp * normed, back_mlp)):
        sums[row : row + 1, :] += jnp.sum(value, axis=0, keepdims=True)
    if not own:
        out[0] = branch.astype(BF16)
        out[1] = scaled.astype(BF16)
        return
    branch = branch + other[0].astype(F32)
    out[...] = (inputs + branch + (vec[7:8, :] + vec[12:13, :])).astype(BF16)
    scaled = scaled + other[1].astype(F32)
    result[...] = dy[...].astype(F32) + inv_std * (
        scaled
        - jnp.mean(scaled, axis=-1, keepdims=True)
        - normed * jnp.mean(scaled * normed, axis=-1, keepdims=True)
    )


def adam_math(weight, first, second, gradient, rate, decay):
    first_new = BETA_ONE * first + (1.0 - BETA_ONE) * gradient
    second_new = BETA_TWO * second + (1.0 - BETA_TWO) * gradient * gradient
    first_hat = first_new / (1.0 - BETA_ONE**STEP)
    second_hat = second_new / (1.0 - BETA_TWO**STEP)
    weight_new = weight - rate * (first_hat / (jnp.sqrt(second_hat) + ADAM_EPS) + decay * weight)
    return (first_new, second_new, weight_new)


def adam_store(refs, at, gradient):
    w, m, v, m_out, v_out, w_out = refs
    first, second, weight = adam_math(w[at], m[at], v[at], gradient, RATE_MATRIX, DECAY_MATRIX)
    m_out[at] = first
    v_out[at] = second
    w_out[at] = weight


def parities(core, own, other):
    return jnp.where(core == 0, own, other), jnp.where(core == 0, other, own)


def adam_attn_body(ids, own, other, *refs):
    core = ids[1]
    low = low_lanes()
    qkv_refs = refs[0:3] + refs[6:9]
    for tile in range(4):
        start = (tile // 2) * 768 + (tile % 2) * 128
        cols = pl.ds(pl.multiple_of(pl.program_id(0) * 256 + start, 128), 128)
        even, odd = parities(core, own[:, cols].astype(F32), other[:, cols].astype(F32))
        first = jnp.where(low, even, pltpu.roll(odd, HEAD_DIM, 1))
        second = jnp.where(low, pltpu.roll(even, HEAD_DIM, 1), odd)
        adam_store(qkv_refs, (slice(None), slice(tile * 256, tile * 256 + 128)), first)
        adam_store(qkv_refs, (slice(None), slice(tile * 256 + 128, tile * 256 + 256)), second)

    @pl.when(pl.program_id(0) == 0)
    def _():
        out_refs = refs[3:6] + refs[9:12]
        for panel in range(4):
            rows = slice((panel % 2) * 64, (panel % 2) * 64 + 64)
            cols = slice(1536 + 256 * (panel // 2), 1792 + 256 * (panel // 2))
            span = slice(panel * 256, panel * 256 + 256)
            even, odd = parities(core, own[rows, cols].astype(F32), other[rows, cols].astype(F32))
            adam_store(out_refs, (slice(0, 64), span), even)
            adam_store(out_refs, (slice(64, 128), span), odd)


def adam_down_body(ids, own, other, *refs):
    core, parity = ids[1], pl.program_id(0)
    grad = jnp.where(core == parity, own[128:256, :], other[128:256, :]).astype(F32)
    adam_store(refs, (slice(None), slice(None)), grad)


def adam_mlp_body(ids, own_a, other_a, own_b, other_b, *refs):
    core, step = ids[1], pl.program_id(0)
    up_refs = refs[0:3] + refs[-6:-3]
    down_refs = refs[3:6] + refs[-3:]
    for owner in range(2):
        cols = pl.ds(pl.multiple_of(step * 256 + owner * 128, 128), 128)
        for part, (own, other) in enumerate(((own_a, other_a), (own_b, other_b))):
            halves = parities(core, own[0:128, cols].astype(F32), other[0:128, cols].astype(F32))
            for parity, grad in enumerate(halves):
                base = owner * 512 + part * 256 + parity * 128
                adam_store(up_refs, (slice(None), slice(base, base + 128)), grad)
    rows = pl.ds(pl.multiple_of(128 + (step % 2) * 64, 64), 64)
    grad = jnp.where(core == step // 2, own_b[rows, :], other_b[rows, :]).astype(F32)
    adam_store(down_refs, (slice(None), slice(None)), grad)


def rotary_tables(segments):
    row_count = segments.shape[0]
    row_index = jnp.arange(row_count, dtype=jnp.int32)
    earlier = jnp.concatenate([jnp.full((1,), -1, jnp.int32), segments[:-1]])
    starts = jnp.where(segments != earlier, row_index, 0)
    position = (row_index - lax.cummax(starts, axis=0)).astype(F32)
    half_dim = ROT_DIM // 2
    dims = jnp.arange(LANES, dtype=jnp.int32) % HEAD_DIM
    frequency = ROPE_BASE ** (-2.0 * (dims % half_dim).astype(F32) / ROT_DIM)
    turned = dims < ROT_DIM
    angles = position[:, None] * jnp.where(turned, frequency, 0.0)[None, :]
    cosine, sine = jnp.cos(angles), jnp.sin(angles)
    front = (dims < half_dim)[None, :]
    return cosine, jnp.where(front, -sine, 0.0), jnp.where(front, 0.0, sine)


def on_device(
    sizes,
    tokens,
    segments,
    cotangent,
    w_qkv,
    w_out,
    w_up,
    w_down,
    vectors,
    m_qkv,
    m_out,
    m_up,
    m_down,
    m_vectors,
    v_qkv,
    v_out,
    v_up,
    v_down,
    v_vectors,
):
    copies, owners = sizes
    me = lax.axis_index("zero")
    plane = lax.axis_index("dp")
    core = plane % 2
    ids = jnp.stack([me, core, (plane // 2) % 2]).astype(jnp.int32)

    def move(value, target):
        pairs = []
        for d in range(copies):
            for z in range(owners):
                to_d, to_z = target(d, z)
                pairs.append((d * owners + z, to_d * owners + to_z))
        return lax.ppermute(value, AXES, pairs)

    def swap(value, dp_bits, zero_bits):
        return move(value, lambda d, z: (d ^ dp_bits, z ^ zero_bits))

    def swap_far(value):
        return move(value, lambda d, z: (d, z ^ (6 if d & 2 else 4)))

    def sync(*values):
        return lax.optimization_barrier(values)

    def add(*terms):
        return functools.reduce(jnp.add, [t.astype(F32) for t in terms])

    def reduce_first(keep, send_x, send_y):
        return keep, swap(send_x, 0, 1), swap(send_y, 2, 0)

    def reduce_first_part(keep, send_x, send_y):
        return keep, [send_x[0], swap(send_x[1], 0, 1)], swap(send_y, 2, 0)

    def reduce_second(state):
        keep, got_x, got_y = state
        far = add(keep[3], got_y[1]).astype(BF16)
        near = add(keep[1], got_x[1]).astype(BF16)
        return keep, got_x, got_y, far, near, swap(far, 0, 1), swap(near, 0, 2)

    def reduce_third(state):
        keep, got_x, got_y, _, _, got_far, got_near = state
        far = add(keep[2], got_y[0], got_far).astype(BF16)
        return (keep, got_x, got_near), far, swap_far(far)

    def reduce_fourth(state):
        (keep, got_x, got_near), _, got = state
        total = add(keep[0], got_x[0], got_near, got).astype(BF16)
        return total, swap(total, 2, 0)

    def reduce_fifth(state):
        total = add(*state).astype(BF16)
        bit = 4
        while bit < copies:
            total = add(total, swap(total, bit, 0)).astype(BF16)
            bit *= 2
        return total, swap(total, 1, 0)

    T, width = tokens.shape
    rows = 2 * T
    sds = jax.ShapeDtypeStruct
    row_block = lambda n, c=width: spec((n, c), lambda i: (i, 0))
    col_block = lambda n: spec((width, n), lambda i: (0, i))

    def block_call(body, grid, ins, outs, flops, moved, scratch=(), name=None):
        return kernel_call(
            body,
            grid,
            [place for _, place in ins],
            [place for _, place in outs],
            [shape for shape, _ in outs],
            flops,
            moved,
            scratch=scratch,
            name=name,
        )(*[value for value, _ in ins])

    def const(value):
        return value, whole(value.shape)

    def kept(shape, dtype):
        return sds(shape, dtype), whole(shape)

    steps = rows // 256
    with jax.named_scope("prep"):
        own_a = block_call(
            prep_attn_body,
            (1,),
            [(ids, scalars()), const(w_qkv), const(w_out), (vectors, whole((16, 128)))],
            [kept((144, 1280), BF16)],
            0,
            3e6,
            name="prep_attn",
        )[0]

    def prep_mlp(part, shape, ins, beside):
        with jax.named_scope("prep"):
            return block_call(
                functools.partial(prep_mlp_body, part),
                (1,),
                [(ids, scalars()), const(ins[0]), (ins[1], spec((256, width), lambda i: (part, 0), single=True))]
                + [const(value) for value in ins[2:]],
                [kept(shape, BF16)],
                0,
                beside * 3e6,
                name="prep_mlp",
            )[0]

    def z_moves(own):
        return swap(own, 0, 2), swap_far(own)

    with jax.named_scope("gather"):
        seg_other = swap(segments, 1, 0)
        tok_other = swap(tokens, 1, 0)
        dy_other = swap(cotangent, 1, 0)
        own_a, w_up_in = sync(own_a, w_up)
        next_a, far_a = z_moves(own_a)
        across_a = swap(own_a, 0, 1)
        own_b = prep_mlp(0, (256, 1024), (w_up_in, w_down), 20)
        tables = [
            jnp.concatenate(pair, axis=0)
            for pair in zip(rotary_tables(segments), rotary_tables(seg_other))
        ]
        seg_row = jnp.stack([segments, seg_other]).astype(F32)[:, None, :]
        seg_ids = jnp.concatenate([segments, seg_other]).astype(F32)
        next_a, far_a, across_a, own_b, w_up_in, tables, seg_row, seg_ids, tok_other, dy_other = sync(
            next_a, far_a, across_a, own_b, w_up_in, tables, seg_row, seg_ids, tok_other, dy_other
        )
        next_across_a, far_across_a, rest_across_a = swap(next_a, 0, 1), swap(far_a, 0, 1), swap(far_a, 2, 1)
        rest_a = swap(far_a, 2, 0)
        far_b = swap_far(own_b)
        seg_col = jnp.broadcast_to(seg_ids[:, None], (rows, LANES))
        own_c = prep_mlp(1, (352, 1024), (w_up_in, w_down, w_qkv), 25)
        next_across_a, far_across_a, rest_a, rest_across_a, far_b, own_b, own_c, seg_col = sync(
            next_across_a, far_across_a, rest_a, rest_across_a, far_b, own_b, own_c, seg_col
        )
        far_across_b, across_b, rest_b = swap(far_b, 0, 1), swap(own_b, 0, 1), swap(far_b, 2, 0)
        next_b = swap(own_b, 0, 2)
        far_c = swap_far(own_c)
    attn_pieces = [own_a, next_a, far_a, rest_a, across_a, next_across_a, far_across_a, rest_across_a]

    def table_blocks(count):
        return [(t, row_block(count, 128)) for t in tables]

    def halves(own, other, count):
        last = T // count - 1
        return [
            (own, spec((count, width), lambda i: (jnp.minimum(i, last), 0))),
            (other, spec((count, width), lambda i: (jnp.maximum(i - last - 1, 0), 0))),
        ]

    def attention(group, pairs, projected, d_att, previous):
        with jax.named_scope("attention"):
            first = pairs[0]
            head_block = spec((T, 128), lambda h, m: (h, m + first))
            outs = [
                (sds((rows, 256), BF16), head_block),
                (sds((3, rows, 256), BF16), spec((3, T, 128), lambda h, m: (0, h, m + first))),
            ]
            ins = (
                [(value, head_block) for value in projected]
                + [(d_att, spec((T, 128), lambda h, m: (h, m + first + 2 * group)))]
                + [(seg_col, spec((T, LANES), lambda h, m: (h, 0)))]
                + [(seg_row, spec((1, 1, T), lambda h, m: (h, 0, 0)))]
                + [(t, spec((T, 128), lambda h, m: (h, 0))) for t in tables]
            )
            aliases = {len(ins) + n: n for n in range(len(previous))}
            return pl.pallas_call(
                attn_body,
                grid=(2, len(pairs)),
                in_specs=[place for _, place in ins] + [distant()] * len(previous),
                out_specs=[place for _, place in outs],
                out_shape=[shape for shape, _ in outs],
                input_output_aliases=aliases,
                cost_estimate=pl.CostEstimate(
                    flops=len(pairs) * 15000000000, bytes_accessed=len(pairs) * 5000000, transcendentals=0
                ),
                compiler_params=pltpu.CompilerParams(
                    vmem_limit_bytes=VMEM_NEED * MIB, dimension_semantics=("arbitrary",) * 2
                ),
                name="attention",
            )(*[value for value, _ in ins], *previous)

    def blocks_of(shape):
        return [kept((n,) + shape, BF16) for n in (4, 2, 2)]

    with jax.named_scope("qkv"):
        *projected, d_att, attn_in, attn_t, mlp_in, wq_a, full_out, vec, bias_qkv = block_call(
            functools.partial(qkv_first_body, rows // 256),
            (rows // 256,),
            [(ids, scalars())]
            + [const(piece) for piece in attn_pieces]
            + halves(tokens, tok_other, 256)
            + halves(cotangent, dy_other, 256)
            + table_blocks(256),
            [(sds((rows, 256), BF16), row_block(256, 256))] * 3
            + [(sds((rows, 512), BF16), row_block(256, 512)), (sds((rows, width), BF16), row_block(256))]
            + [(sds((width, rows), BF16), col_block(256)), (sds((rows, width), BF16), row_block(256))]
            + [kept((1024, 768), BF16), kept((512, 1024), BF16), kept((16, 1024), F32), kept((1, 1536), F32)],
            2 * rows * 1024 * 1280,
            30e6,
            name="qkv",
        )
    projected, far_across_b, across_b, rest_b, own_b = sync(
        projected, far_across_b, across_b, rest_b, own_b
    )
    with jax.named_scope("gather"):
        rest_across_b, next_across_b = swap(far_across_b, 2, 0), swap(own_b, 0, 3)
    half_a = attention(0, (0,), projected, d_att, [])
    half_a, projected, far_c, own_c, next_b = sync(half_a, projected, far_c, own_c, next_b)
    with jax.named_scope("gather"):
        far_across_c, rest_c, next_c = swap(far_c, 0, 1), swap(far_c, 2, 0), swap(own_c, 0, 2)
    att_a, grad_a = attention(0, (1,), projected, d_att, half_a)
    att_a, grad_a, rest_across_b, next_across_b, far_across_c, rest_c, own_c, next_c, attn_t, mlp_in = sync(
        att_a, grad_a, rest_across_b, next_across_b, far_across_c, rest_c, own_c, next_c, attn_t, mlp_in
    )
    with jax.named_scope("gather"):
        across_c, next_across_c, rest_across_c = swap(own_c, 0, 1), swap(next_c, 0, 1), swap(far_across_c, 2, 0)
    pieces_b = [own_b, next_b, far_b, rest_b, across_b, next_across_b, far_across_b, rest_across_b]

    def mlp(part, weights, rows_in):
        with jax.named_scope("mlp"):
            *results, hid, gp, sums, w_up_full, w_down_full = block_call(
                functools.partial(mlp_body, part, steps),
                (steps,),
                [(ids, scalars())]
                + [const(w) for w in weights]
                + [const(vec), (rows_in, row_block(256))]
                + halves(cotangent, dy_other, 256),
                [(sds((n, 256, 1024), BF16), distant()) for n in (4, 2, 2)]
                + [(sds((rows, width), BF16), row_block(256))] * 2
                + [kept((8, 1024), F32)]
                + [(sds((1024, 1024), BF16), distant())] * 2,
                2 * rows * 1024 * 1024 * 4,
                40e6,
                scratch=[
                    pltpu.VMEM((1024, rows), BF16),
                    pltpu.VMEM((1024, rows), BF16),
                    pltpu.VMEM((rows, 1024), BF16),
                    pltpu.VMEM((rows, 1024), BF16),
                    pltpu.VMEM((8, 1024), F32),
                    pltpu.VMEM((1024, 512), BF16),
                ]
                + [pltpu.VMEM((n, 256, 1024), BF16) for n in (4, 2, 2)]
                + [pltpu.VMEM((1024, 1024), BF16)] * 2
                + [pltpu.SemaphoreType.DMA((8,))],
                name="mlp",
            )
            return results, hid, gp, sums, w_up_full, w_down_full

    mlp_a = mlp(0, pieces_b, mlp_in)
    mlp_a, mlp_in, across_c, next_across_c, rest_across_c = sync(
        mlp_a, mlp_in, across_c, next_across_c, rest_across_c
    )
    pieces_c = [own_c, next_c, far_c, rest_c, across_c, next_across_c, far_across_c, rest_across_c]
    reduce_a = reduce_first(*mlp_a[0])
    mlp_b = mlp(1, pieces_c, mlp_in)
    mlp_b, reduce_a, attn_in = sync(mlp_b, reduce_a, attn_in)
    reduce_a = reduce_second(reduce_a)
    reduce_b = reduce_first_part(*mlp_b[0])
    attn_in, *ready = sync(attn_in, *reduce_a[3:5])

    with jax.named_scope("attention"):
        head_block = spec((T, 128), lambda h, m: (h, m))
        att_b, grad_b, wq_b = block_call(
            project_attn_body,
            (2, 2),
            [(ids, scalars())]
            + [(piece, whole((96, width))) for piece in pieces_c]
            + [(attn_in, spec((T, width), lambda h, m: (h, 0))), const(bias_qkv)]
            + [(d_att, spec((T, 128), lambda h, m: (h, m + 2)))]
            + [(seg_col, spec((T, LANES), lambda h, m: (h, 0)))]
            + [(seg_row, spec((1, 1, T), lambda h, m: (h, 0, 0)))]
            + [(t, spec((T, 128), lambda h, m: (h, 0))) for t in tables],
            [
                (sds((rows, 256), BF16), head_block),
                (sds((3, rows, 256), BF16), spec((3, T, 128), lambda h, m: (0, h, m))),
                kept((1024, 768), BF16),
            ],
            38e9,
            20e6,
            scratch=[pltpu.VMEM((T, 256), BF16)] * 3,
            name="attention",
        )
    att_b, grad_b, reduce_a, reduce_b = sync(att_b, grad_b, reduce_a, reduce_b)
    reduce_a = reduce_third(reduce_a)
    reduce_b[1][0] = swap(reduce_b[1][0], 0, 1)
    reduce_b = reduce_second(reduce_b)
    grad_b, *ready = sync(grad_b, reduce_a[1], *reduce_b[3:5])
    with jax.named_scope("attn_weights"):
        *blocks, bias_sum = block_call(
            attn_weights_body,
            (7,),
            [(ids, scalars()), const(attn_t)]
            + [(grad_a, spec((1, rows, 256), lambda n: (jnp.minimum(n, 2), 0, 0)))]
            + [(grad_b, spec((1, rows, 256), lambda n: (jnp.clip(n - 3, 0, 2), 0, 0)))]
            + [(value, distant()) for value in (att_a, att_b, cotangent, dy_other)],
            blocks_of((128, 2048)) + [kept((8, 1536), F32)],
            2 * rows * 1024 * 2048,
            24e6,
            scratch=[pltpu.VMEM((1024, 256), BF16)]
            + [pltpu.VMEM((rows, 256), BF16)] * 2
            + [pltpu.VMEM((T, width), BF16)] * 2
            + [pltpu.SemaphoreType.DMA((4,))],
            name="attn_weights",
        )
    blocks, grad_b, reduce_a, reduce_b = sync(blocks, grad_b, reduce_a, reduce_b)
    reduce_o = reduce_first(*blocks)

    _, hid_a, gp_a, sums_a, up_a, down_a = mlp_a
    _, hid_b, gp_b, sums_b, up_b, down_b = mlp_b

    def adam_down(totals):
        wide = [spec((128, width), lambda n: (n, 0))] * 3
        return kernel_call(
            adam_down_body,
            (2,),
            [scalars()] + [whole((256, 1024))] * 2 + wide,
            wide,
            [sds((512, 1024), F32)] * 3,
            0,
            7e6,
            name="adam_down",
        )(ids, *totals, w_down, m_down, v_down)

    def adam_mlp(totals_a, totals_b, previous):
        wide = [spec((128, 1024), lambda n: (0, n))] * 3 + [spec((64, width), lambda n: (4 + n, 0))] * 3
        return pl.pallas_call(
            adam_mlp_body,
            grid=(4,),
            in_specs=[scalars()] + [whole((256, 1024))] * 4 + wide + [distant()] * 3,
            out_specs=wide,
            out_shape=[sds((128, 4096), F32)] * 3 + [sds((512, 1024), F32)] * 3,
            input_output_aliases={11 + n: 3 + n for n in range(3)},
            cost_estimate=pl.CostEstimate(flops=0, bytes_accessed=21000000, transcendentals=0),
            compiler_params=pltpu.CompilerParams(
                vmem_limit_bytes=VMEM_NEED * MIB, dimension_semantics=("arbitrary",)
            ),
            name="adam_mlp",
        )(ids, *totals_a, *totals_b, w_up, m_up, v_up, w_down, m_down, v_down, *previous)

    def back(own, grad, rows_tok, extra, outs):
        first = 0 if own else T // 256
        block = lambda c=width: spec((256, c), lambda i: (i + first, 0))
        lead = spec((3, 256, 256), lambda i: (0, i + first, 0))
        with jax.named_scope("back"):
            return block_call(
                functools.partial(back_body, own),
                (T // 256,),
                [(grad_a, lead), (grad, lead), (att_a, block(256)), (att_b, block(256))]
                + [(value, block()) for value in (hid_a, hid_b, gp_a, gp_b)]
                + [const(w) for w in (full_out, down_a, down_b, up_a, up_b, wq_a, wq_b)]
                + [(rows_tok, row_block(256)), const(vec)]
                + extra,
                outs + [kept((8, width), F32)],
                2 * T * 1024 * 6144,
                40e6,
                name="back",
            )

    reduce_a = reduce_fourth(reduce_a)
    reduce_b = reduce_third(reduce_b)
    pair_block = spec((2, 256, width), lambda i: (0, i, 0))
    part_other, sums_other = back(False, grad_b, tok_other, [], [(sds((2, T, width), BF16), pair_block)])
    part_other, sums_other, grad_b, reduce_a, reduce_b, reduce_o = sync(
        part_other, sums_other, grad_b, reduce_a, reduce_b, reduce_o
    )
    reduce_o = reduce_second(reduce_o)
    part_other, reduce_a, reduce_b, *ready = sync(part_other, reduce_a, reduce_b, *reduce_o[3:5])
    reduce_a = reduce_fifth(reduce_a)
    reduce_b = reduce_fourth(reduce_b)
    part_got = swap(part_other, 1, 0)
    updated_mlp = adam_down(reduce_a)
    updated_mlp, grad_b, reduce_b, reduce_o, part_got = sync(
        updated_mlp, grad_b, reduce_b, reduce_o, part_got
    )
    reduce_o = reduce_third(reduce_o)
    reduce_b = reduce_fifth(reduce_b)
    grad_b, *ready = sync(grad_b, reduce_o[1], reduce_b[0])
    layer_out, tokens_grad, sums_own = back(
        True,
        grad_b,
        tokens,
        [(cotangent, row_block(256)), (part_got, pair_block)],
        [(sds((T, width), BF16), row_block(256)), (sds((T, width), F32), row_block(256))],
    )
    sums_own, updated_mlp, reduce_b, reduce_o = sync(sums_own, updated_mlp, reduce_b, reduce_o)
    reduce_o = reduce_fourth(reduce_o)

    with jax.named_scope("vectors"):
        is_core = jnp.arange(2) == core
        grad_bias = jnp.where(core == 0, sums_a[1:2], 0.0)
        bias_sum = jnp.swapaxes(bias_sum[0].reshape(2, 3, 256), 0, 1)
        grad_bias_qkv = jnp.where(
            is_core[None, None, :, None], bias_sum.reshape(3, 8, 1, 64), 0.0
        ).reshape(3, width)
        grad_bias_up = jnp.where(
            is_core[None, None, :, None],
            jnp.swapaxes(jnp.stack([sums_a[0], sums_b[0]]).reshape(2, 8, 128), 0, 1)[:, :, None],
            0.0,
        ).reshape(4, width)
        total = jnp.concatenate(
            [
                sums_own[0:4] + sums_other[0:4],
                grad_bias_qkv,
                grad_bias,
                grad_bias_up,
                grad_bias,
                jnp.zeros((3, width), F32),
            ],
            axis=0,
        )
        moved = [swap(total, 0, step) for step in (2, 4, 6)]
        updated_mlp = adam_mlp(reduce_a, reduce_b, updated_mlp)
        updated_mlp, reduce_o, total, moved = sync(updated_mlp, reduce_o, total, moved)
        reduce_o = reduce_fifth(reduce_o)
        total = functools.reduce(jnp.add, moved, total)
        others = swap(total, 0, 1), swap(total, 2, 0), swap(total, 2, 1)

    with jax.named_scope("adam"):
        wide = [spec((128, 1024), lambda n: (0, n))] * 3 + [whole((128, 1024))] * 3
        updated_attn = kernel_call(
            adam_attn_body,
            (3,),
            [scalars()] + [whole((128, 2048))] * 2 + wide,
            wide,
            [sds((128, 3072), F32)] * 3 + [sds((128, 1024), F32)] * 3,
            0,
            13e6,
            name="adam",
        )(ids, *reduce_o, w_qkv, m_qkv, v_qkv, w_out, m_out, v_out)

    with jax.named_scope("vectors"):
        updated_attn, total, (across, beside, both) = sync(updated_attn, total, others)
        total = (total + across) + (beside + both)
        bit = 4
        while bit < copies:
            total = total + swap(total, bit, 0)
            bit *= 2
        total = total + swap(total, 1, 0)
        share = lax.dynamic_slice_in_dim(total[0:13], me * 128, 128, 1)
        first_vectors, second_vectors, new_vectors = adam_math(
            vectors, m_vectors, v_vectors, share, RATE_VECTOR, 0.0
        )
    first_qkv, second_qkv, new_qkv, first_out, second_out, new_out = updated_attn
    first_up, second_up, new_up, first_down, second_down, new_down = updated_mlp
    return (
        layer_out,
        tokens_grad,
        first_qkv,
        first_out,
        first_up,
        first_down,
        first_vectors,
        second_qkv,
        second_out,
        second_up,
        second_down,
        second_vectors,
        new_qkv,
        new_out,
        new_up,
        new_down,
        new_vectors,
    )


def solution(mesh):
    rows, owned, spread = P(AXES, None), P("zero", None), P(None, "zero")
    state = (owned, owned, owned, owned, spread)
    return jax.shard_map(
        functools.partial(on_device, (mesh.shape["dp"], mesh.shape["zero"])),
        mesh=mesh,
        in_specs=(rows, P(AXES), rows) + state * 3,
        out_specs=(rows, rows) + state * 3,
        check_vma=False,
    )
```

```python
import functools

import jax
import jax.numpy as jnp
from jax import lax
from jax.experimental import pallas as pl
from jax.experimental.pallas import tpu as pltpu
from jax.sharding import PartitionSpec as P

HEAD_DIM = 64
ROT_DIM = 16
STEP = 10
EPS_NORM = 1e-05
BETA_ONE = 0.9
BETA_TWO = 0.999
ADAM_EPS = 1e-08
RATE_MATRIX = 0.05
RATE_VECTOR = 0.2
DECAY_MATRIX = 0.1
ROPE_BASE = 10000.0
INV_ROOT_TWO = 0.7071067811865476
INV_ROOT_TAU = 0.3989422804014327
MASKED = -1e30
LANES = 128
AXES = ("dp", "zero")
F32 = jnp.float32
BF16 = jnp.bfloat16
MIB = 1024 * 1024
VMEM_NEED = 58


def spec(block, index, single=False):
    if single:
        return pl.BlockSpec(block, index, pipeline_mode=pl.Buffered(1))
    return pl.BlockSpec(block, index)


def whole(shape):
    return spec(shape, lambda *_: (0,) * len(shape), single=True)


def distant():
    return pl.BlockSpec(memory_space=pl.ANY)


def scalars():
    return pl.BlockSpec(memory_space=pltpu.SMEM)


def kernel_call(body, grid, in_specs, out_specs, out_shape, flops, moved, scratch=(), name=None):
    return pl.pallas_call(
        body,
        grid=grid,
        in_specs=in_specs,
        out_specs=out_specs,
        out_shape=out_shape,
        scratch_shapes=list(scratch),
        cost_estimate=pl.CostEstimate(flops=int(flops), bytes_accessed=int(moved), transcendentals=0),
        compiler_params=pltpu.CompilerParams(
            vmem_limit_bytes=VMEM_NEED * MIB, dimension_semantics=("arbitrary",) * len(grid)
        ),
        name=name,
    )


def nn(left, right):
    return lax.dot_general(left, right, (((1,), (0,)), ((), ())), preferred_element_type=F32)


def nt(left, right):
    return lax.dot_general(left, right, (((1,), (1,)), ((), ())), preferred_element_type=F32)


def tn(left, right):
    return lax.dot_general(left, right, (((0,), (0,)), ((), ())), preferred_element_type=F32)


def piece_owner(ids, place):
    step = place % 4
    if step > 1:
        step = 2 + ids[2] if step == 2 else 3 - ids[2]
    return jnp.bitwise_xor(ids[0], 2 * step + place // 4)


SLOTS = ((0, 0), (1, 0), (2, 0), (2, 1), (0, 1), (1, 1), (3, 0), (3, 1))


def slot_owner(ids, slot):
    step, side = SLOTS[slot]
    if step > 1:
        step = 2 + ids[2] if step == 2 else 3 - ids[2]
    return jnp.bitwise_xor(ids[0], 2 * step + side)


def slot_ref(outs, slot):
    return (outs[0], slot) if slot < 4 else (outs[1], slot - 4) if slot < 6 else (outs[2], slot - 6)


def low_lanes():
    return lax.broadcasted_iota(jnp.int32, (1, LANES), 1) < HEAD_DIM


def pick_parity(core, tile_a, tile_b):
    low = low_lanes()
    even = jnp.where(low, tile_a, pltpu.roll(tile_b, HEAD_DIM, 1))
    odd = jnp.where(low, pltpu.roll(tile_a, HEAD_DIM, 1), tile_b)
    return jnp.where(core == 0, even, odd)


def prep_attn_body(ids, w_q, w_k, w_v, w_out, vec, out):
    core = ids[1]
    for part, w in enumerate((w_q, w_k, w_v)):
        for tile in range(2):
            base = tile * 256
            at = part * 256 + tile * 128
            out[0:128, at : at + 128] = pick_parity(
                core, w[:, base : base + 128], w[:, base + 128 : base + 256]
            ).astype(BF16)
    rows = w_out[pl.ds(pl.multiple_of(core * 64, 64), 64), :].astype(BF16)
    for panel in range(4):
        at = 768 + 256 * (panel // 2)
        base = (panel % 2) * 64
        out[base : base + 64, at : at + 256] = rows[:, 256 * panel : 256 * panel + 256]
    out[128:144, 0:128] = jnp.where(lax.broadcasted_iota(jnp.int32, (16, 128), 0) < 13, vec[...], 0.0).astype(BF16)
    out[128:144, 128:1280] = jnp.zeros((16, 1152), BF16)


def prep_mlp_body(part, ids, w_up, w_down, *refs):
    out = refs[-1]
    core = ids[1]
    top = 96 * part
    for owner in range(8):
        start = pl.multiple_of(owner * 512 + part * 256 + core * 128, 128)
        out[top : top + 128, owner * 128 : (owner + 1) * 128] = w_up[:, pl.ds(start, 128)].astype(BF16)
    out[top + 128 : top + 256, :] = w_down[pl.ds(pl.multiple_of(core * 128, 128), 128), :].astype(BF16)
    if not part:
        return
    w_qkv = refs[0]
    for third in range(3):
        for tile in range(2):
            base = third * 1024 + 512 + tile * 256
            value = pick_parity(core, w_qkv[:, base : base + 128], w_qkv[:, base + 128 : base + 256]).astype(BF16)
            for panel in range(4):
                at = panel * 256 + tile * 128
                out[32 * third : 32 * third + 32, at : at + 128] = value[32 * panel : 32 * panel + 32]


def normalize(inputs):
    centred = inputs - jnp.mean(inputs, axis=-1, keepdims=True)
    variance = jnp.mean(centred * centred, axis=-1, keepdims=True)
    inv_std = lax.rsqrt(variance + EPS_NORM)
    return centred * inv_std, inv_std


def turned(x, cos, sin_lo, sin_hi, sign):
    return x * cos[...] + sign * (pltpu.roll(x, 8, 1) * sin_hi[...] + pltpu.roll(x, 120, 1) * sin_lo[...])


def project(group, rows, w_qkv, bias, tables, outs):
    for part, out in enumerate(outs):
        cols = slice(part * 256, (part + 1) * 256)
        at = group * 768 + part * 256
        acc = nn(rows, w_qkv[:, cols]) + bias[:, at : at + 256]
        if part == 2:
            out[...] = acc.astype(BF16)
            continue
        for tile in range(2):
            x = turned(acc[:, tile * 128 : (tile + 1) * 128], *tables, 1.0)
            if part == 0:
                x = x * HEAD_DIM ** (-0.5)
            out[:, tile * 128 : (tile + 1) * 128] = x.astype(BF16)


def qkv_first_body(steps, ids, *refs):
    pieces, refs = refs[:8], refs[8:]
    tok_own, tok_other, dy_own, dy_other, cos, sin_lo, sin_hi = refs[:7]
    q, k, v, d_att, attn_in, attn_t, mlp_in, w_qkv, w_out, vec, bias = refs[7:]
    step = pl.program_id(0)

    @pl.when(step == 0)
    def _():
        for place, piece in enumerate(pieces):
            owner = piece_owner(ids, place)
            at_owner = pl.ds(pl.multiple_of(owner * 128, 128), 128)
            w_qkv[at_owner, :] = piece[0:128, 0:768]
            vec[:, at_owner] = piece[128:144, 0:128].astype(F32)
            for panel in range(4):
                at = 768 + 256 * (panel // 2)
                base = (panel % 2) * 64
                w_out[pl.ds(pl.multiple_of(owner * 64, 64), 64), 256 * panel : 256 * panel + 256] = piece[
                    base : base + 64, at : at + 256
                ]
        for part in range(3):
            for tile in range(4):
                base = tile * 256
                row = slice(4 + part, 5 + part)
                at = (tile // 2) * 768 + part * 256 + (tile % 2) * 128
                bias[:, at : at + 128] = pick_parity(
                    ids[1], vec[row, base : base + 128], vec[row, base + 128 : base + 256]
                )

    first = step < steps // 2
    d_att[...] = nt(jnp.where(first, dy_own[...], dy_other[...]), w_out[...]).astype(BF16)
    normed, _ = normalize(jnp.where(first, tok_own[...], tok_other[...]).astype(F32))
    rows = (normed * vec[0:1, :] + vec[1:2, :]).astype(BF16)
    mlp_in[...] = (normed * vec[2:3, :] + vec[3:4, :]).astype(BF16)
    attn_in[...] = rows
    attn_t[...] = rows.T
    project(0, rows, w_qkv, bias, (cos, sin_lo, sin_hi), (q, k, v))


ATTN_ROWS = 256


def cat(parts, axis=0):
    return jnp.concatenate(parts, axis=axis) if len(parts) > 1 else parts[0]


def attn_body(q, k, v, d_att, seg_col, seg_row, cos, sin_lo, sin_hi, *refs):
    att, grad = refs[-2:]
    count = q.shape[0]
    size = ATTN_ROWS
    blocks = count // size
    span = [slice(j * size, (j + 1) * size) for j in range(blocks)]
    low = low_lanes()
    zero = jnp.zeros((), BF16)
    causal = lax.broadcasted_iota(jnp.int32, (size, size), 0) >= lax.broadcasted_iota(
        jnp.int32, (size, size), 1
    )
    q_t, da_t = q[...].T, d_att[...].T

    def row_total(parts, reduce, join):
        cols = [reduce(part, axis=-1, keepdims=True) for part in parts]
        return [
            functools.reduce(join, [cols[j][(i - j) * size : (i - j + 1) * size] for j in range(i + 1)])
            for i in range(blocks)
        ]

    def row_sum(parts):
        return cat(
            [
                functools.reduce(jnp.add, [parts[j][(i - j) * size : (i - j + 1) * size] for j in range(i + 1)])
                for i in range(blocks)
            ]
        )

    def products(half):
        lanes = low if half == 0 else jnp.logical_not(low)
        q_h = jnp.where(lanes, q[...], zero)
        da_h = jnp.where(lanes, d_att[...], zero)
        scores = [nt(q_h[j * size :], k[span[j], :]) for j in range(blocks)]
        return scores, [nt(da_h[j * size :], v[span[j], :]) for j in range(blocks)]

    def softmax_both(scores, grad_probs):
        masked = []
        for j in range(blocks):
            allowed = seg_col[j * size :, 0:1] == seg_row[0, :, span[j]]
            allowed = cat([allowed[:size] & causal] + ([allowed[size:]] if j < blocks - 1 else []))
            masked.append(jnp.where(allowed, scores[j], MASKED))
        top = row_total(masked, jnp.max, jnp.maximum)
        raised = [jnp.exp(masked[j] - cat(top[j:])) for j in range(blocks)]
        inv = [1.0 / total for total in row_total(raised, jnp.sum, jnp.add)]
        probs = [raised[j] * cat(inv[j:]) for j in range(blocks)]
        delta = row_total([g * p for g, p in zip(grad_probs, probs)], jnp.sum, jnp.add)
        grad_scores = [
            (probs[j] * (grad_probs[j] - cat(delta[j:]))).astype(BF16) for j in range(blocks)
        ]
        return [p.astype(BF16) for p in probs], grad_scores

    def results(half, probs, grad_scores):
        rows = slice(half * HEAD_DIM, (half + 1) * HEAD_DIM)
        return (
            row_sum([nn(probs[j], v[span[j], :]) for j in range(blocks)]),
            row_sum([nn(grad_scores[j], k[span[j], :]) for j in range(blocks)]),
            cat([nn(q_t[rows, j * size :], grad_scores[j]) for j in range(blocks)], 1),
            cat([nn(da_t[rows, j * size :], probs[j]) for j in range(blocks)], 1),
        )

    first = softmax_both(*products(0))
    second = products(1)
    out_a, dq_a, dk_a, dv_a = results(0, *first)
    out_b, dq_b, dk_b, dv_b = results(1, *softmax_both(*second))
    tables = (cos, sin_lo, sin_hi)
    att[...] = jnp.where(low, out_a, out_b).astype(BF16)
    grad[0] = turned(jnp.where(low, dq_a, dq_b) * HEAD_DIM ** (-0.5), *tables, -1.0).astype(BF16)
    grad[1] = turned(jnp.concatenate([dk_a, dk_b], axis=0).T, *tables, -1.0).astype(BF16)
    grad[2] = jnp.concatenate([dv_a, dv_b], axis=0).T.astype(BF16)


def project_attn_body(ids, *refs):
    pieces, (attn_in, bias, d_att, seg_col, seg_row, *tables) = refs[:8], refs[8:16]
    att, grad, w_qkv, *projected = refs[16:]
    half, pair = pl.program_id(0), pl.program_id(1)

    @pl.when((half == 0) & (pair == 0))
    def _():
        for place, piece in enumerate(pieces):
            owner = piece_owner(ids, place)
            for part in range(3):
                for panel in range(4):
                    at = pl.ds(pl.multiple_of(owner * 128 + 32 * panel, 32), 32)
                    w_qkv[at, part * 256 : part * 256 + 256] = piece[
                        32 * part : 32 * part + 32, panel * 256 : panel * 256 + 256
                    ]

    @pl.when(pair == 0)
    def _():
        project(1, attn_in[...], w_qkv, bias, tables, projected)

    lanes = pl.ds(pl.multiple_of(pair * LANES, LANES), LANES)
    attn_body(*[value.at[:, lanes] for value in projected], d_att, seg_col, seg_row, *tables, att, grad)


def attn_weights_body(ids, attn_t, grad_a, grad_b, far_att_a, far_att_b, far_own, far_other, *refs):
    keep, send_x, send_y, bias, result, att_a, att_b, dy_own, dy_other, sems = refs
    copies = [
        pltpu.make_async_copy(source, target, sems.at[n])
        for n, (source, target) in enumerate(
            ((far_att_a, att_a), (far_att_b, att_b), (far_own, dy_own), (far_other, dy_other))
        )
    ]

    @pl.when(pl.program_id(0) == 0)
    def _():
        for copy in copies:
            copy.start()

    step = pl.program_id(0)
    outs = (keep, send_x, send_y)

    @pl.when(step < 6)
    def _():
        rhs = jnp.where(step < 3, grad_a[0], grad_b[0])
        result[...] = nn(attn_t[...], rhs).astype(BF16)
        cols = pl.ds(pl.multiple_of(step * 256, 256), 256)
        bias[0:1, cols] = jnp.sum(rhs.astype(F32), axis=0, keepdims=True)
        for slot in range(8):
            out, at = slot_ref(outs, slot)
            base = pl.multiple_of(slot_owner(ids, slot) * 128, 128)
            out[at, :, cols] = result[pl.ds(base, 128), :]

    @pl.when(step == 6)
    def _():
        for copy in copies:
            copy.wait()
        count = dy_own.shape[0]
        for group, att in enumerate((att_a, att_b)):
            flipped = att[...].T
            for panel in range(4):
                cols = slice(panel * 256, panel * 256 + 256)
                term = nn(flipped[:, :count], dy_own[:, cols]) + nn(flipped[:, count:], dy_other[:, cols])
                result[group * 256 : group * 256 + 256, :] = term.astype(BF16)
                for slot in range(8):
                    out, at = slot_ref(outs, slot)
                    owner = slot_owner(ids, slot)
                    col = 1536 + 256 * (panel // 2)
                    base = (panel % 2) * 64

                    @pl.when(owner // 4 == group)
                    def _():
                        out[at, base : base + 64, col : col + 256] = result[
                            pl.ds(pl.multiple_of(owner * 64, 64), 64), :
                        ]


def mlp_body(part, steps, ids, *refs):
    pieces, (vec, mlp_in, dy_own, dy_other) = refs[:8], refs[8:12]
    far_outs, (hidden_out, grad_out, sums, far_up, far_down) = refs[12:15], refs[15:20]
    mlp_t, hidden_t, grad_pre, dy, bias, result, keep, send_x, send_y, w_up, w_down, sems = refs[20:]
    outs = (keep, send_x, send_y)
    weight_copies = [
        pltpu.make_async_copy(w_up, far_up, sems.at[0]),
        pltpu.make_async_copy(w_down, far_down, sems.at[1]),
    ]
    core = ids[1]
    step = pl.program_id(0)

    @pl.when(step == 0)
    def _():
        for owner in range(8):
            start = pl.multiple_of((owner % 2) * 512 + part * 256 + core * 128, 128)
            row = 8 + owner // 2
            bias[0:1, owner * 128 : (owner + 1) * 128] = vec[row : row + 1, pl.ds(start, 128)]
        sums[...] = jnp.zeros_like(sums)
        for place, piece in enumerate(pieces):
            at = pl.ds(pl.multiple_of(piece_owner(ids, place) * 128, 128), 128)
            top = 96 * part
            w_up[at, :] = piece[top : top + 128, :]
            w_down[at, :] = piece[top + 128 : top + 256, :]
        for copy in weight_copies:
            copy.start()

    rows = mlp_in[...]
    grads = jnp.where(step < steps // 2, dy_own[...], dy_other[...])
    count = rows.shape[0]
    at = pl.ds(pl.multiple_of(step * count, count), count)
    mlp_t[:, at] = rows.T
    dy[at, :] = grads
    sums[1:2, :] += jnp.sum(grads.astype(F32), axis=0, keepdims=True)
    for col in range(0, 1024, 512):
        cols = slice(col, col + 512)
        pre = nn(rows, w_up[:, cols]) + bias[0:1, cols]
        grad_hidden = nt(grads, w_down[cols, :])
        cdf = 0.5 + 0.5 * lax.erf(pre * INV_ROOT_TWO)
        pdf = jnp.exp(-0.5 * pre * pre) * INV_ROOT_TAU
        act = (pre * cdf).astype(BF16)
        hidden_t[cols, at] = act.T
        hidden_out[:, cols] = act
        gp = (grad_hidden * (cdf + pre * pdf)).astype(BF16)
        grad_pre[at, cols] = gp
        grad_out[:, cols] = gp
        sums[0:1, cols] += jnp.sum(gp.astype(F32), axis=0, keepdims=True)

    @pl.when(step == steps - 1)
    def _():
        copies = list(weight_copies)
        for base_row, left, right in ((0, mlp_t, grad_pre), (128, hidden_t, dy)):
            for col in range(0, 1024, 512):
                cols = slice(col, col + 512)
                result[...] = nn(left[...], right[:, cols]).astype(BF16)
                for slot in range(8):
                    out, place = slot_ref(outs, slot)
                    base = pl.multiple_of(slot_owner(ids, slot) * 128, 128)
                    out[place, base_row : base_row + 128, cols] = result[pl.ds(base, 128), :]
            span = pl.ds(base_row, 128)
            for out, far_out in zip(outs, far_outs):
                copy = pltpu.make_async_copy(out.at[:, span, :], far_out.at[:, span, :], sems.at[len(copies)])
                copy.start()
                copies.append(copy)
        for copy in copies:
            copy.wait()


def back_body(own, grad_a, grad_b, att_a, att_b, hid_a, hid_b, gp_a, gp_b, *refs):
    w_out, down_a, down_b, up_a, up_b, wq_a, wq_b, tok, vec = refs[:9]
    if own:
        dy, other, out, result, sums = refs[9:]
    else:
        out, sums = refs[9:]
    inputs = tok[...].astype(F32)
    normed, inv_std = normalize(inputs)
    branch = nn(att_a[...], w_out[0:256, :]) + nn(att_b[...], w_out[256:512, :])
    branch = branch + nn(hid_a[...], down_a[...]) + nn(hid_b[...], down_b[...])
    back_mlp = nt(gp_a[...], up_a[...]) + nt(gp_b[...], up_b[...])
    back_attn = None
    for grad, w in ((grad_a, wq_a), (grad_b, wq_b)):
        for part in range(3):
            term = nt(grad[part], w[:, part * 256 : part * 256 + 256])
            back_attn = term if back_attn is None else back_attn + term
    scaled = back_attn * vec[0:1, :] + back_mlp * vec[2:3, :]

    @pl.when(pl.program_id(0) == 0)
    def _():
        sums[...] = jnp.zeros_like(sums)

    for row, value in enumerate((back_attn * normed, back_attn, back_mlp * normed, back_mlp)):
        sums[row : row + 1, :] += jnp.sum(value, axis=0, keepdims=True)
    if not own:
        out[0] = branch.astype(BF16)
        out[1] = scaled.astype(BF16)
        return
    branch = branch + other[0].astype(F32)
    out[...] = (inputs + branch + (vec[7:8, :] + vec[12:13, :])).astype(BF16)
    scaled = scaled + other[1].astype(F32)
    result[...] = dy[...].astype(F32) + inv_std * (
        scaled
        - jnp.mean(scaled, axis=-1, keepdims=True)
        - normed * jnp.mean(scaled * normed, axis=-1, keepdims=True)
    )


def adam_math(weight, first, second, gradient, rate, decay):
    first_new = BETA_ONE * first + (1.0 - BETA_ONE) * gradient
    second_new = BETA_TWO * second + (1.0 - BETA_TWO) * gradient * gradient
    first_hat = first_new / (1.0 - BETA_ONE**STEP)
    second_hat = second_new / (1.0 - BETA_TWO**STEP)
    weight_new = weight - rate * (first_hat / (jnp.sqrt(second_hat) + ADAM_EPS) + decay * weight)
    return (first_new, second_new, weight_new)


def adam_store(refs, at, gradient):
    w, m, v, m_out, v_out, w_out = refs
    first, second, weight = adam_math(w[at], m[at], v[at], gradient, RATE_MATRIX, DECAY_MATRIX)
    m_out[at] = first
    v_out[at] = second
    w_out[at] = weight


def parities(core, own, other):
    return jnp.where(core == 0, own, other), jnp.where(core == 0, other, own)


def adam_attn_body(ids, own, other, *refs):
    core = ids[1]
    low = low_lanes()
    qkv_refs = refs[0:3] + refs[6:9]
    for tile in range(6):
        count = pl.program_id(0) * 6 + tile
        part, place = count // 4, count % 4
        start = (place // 2) * 768 + part * 256 + (place % 2) * 128
        cols = pl.ds(pl.multiple_of(start, 128), 128)
        even, odd = parities(core, own[:, cols].astype(F32), other[:, cols].astype(F32))
        first = jnp.where(low, even, pltpu.roll(odd, HEAD_DIM, 1))
        second = jnp.where(low, pltpu.roll(even, HEAD_DIM, 1), odd)
        adam_store(qkv_refs, (slice(None), slice(tile * 256, tile * 256 + 128)), first)
        adam_store(qkv_refs, (slice(None), slice(tile * 256 + 128, tile * 256 + 256)), second)

    @pl.when(pl.program_id(0) == 0)
    def _():
        out_refs = refs[3:6] + refs[9:12]
        for panel in range(4):
            rows = slice((panel % 2) * 64, (panel % 2) * 64 + 64)
            cols = slice(1536 + 256 * (panel // 2), 1792 + 256 * (panel // 2))
            span = slice(panel * 256, panel * 256 + 256)
            even, odd = parities(core, own[rows, cols].astype(F32), other[rows, cols].astype(F32))
            adam_store(out_refs, (slice(0, 64), span), even)
            adam_store(out_refs, (slice(64, 128), span), odd)


def adam_down_body(ids, own, other, *refs):
    core, parity = ids[1], pl.program_id(0)
    grad = jnp.where(core == parity, own[128:256, :], other[128:256, :]).astype(F32)
    adam_store(refs, (slice(None), slice(None)), grad)


def adam_mlp_body(ids, own_a, other_a, own_b, other_b, *refs):
    core, step = ids[1], pl.program_id(0)
    up_refs = refs[0:3] + refs[-6:-3]
    down_refs = refs[3:6] + refs[-3:]
    for owner in range(2):
        cols = pl.ds(pl.multiple_of(step * 256 + owner * 128, 128), 128)
        for part, (own, other) in enumerate(((own_a, other_a), (own_b, other_b))):
            halves = parities(core, own[0:128, cols].astype(F32), other[0:128, cols].astype(F32))
            for parity, grad in enumerate(halves):
                base = owner * 512 + part * 256 + parity * 128
                adam_store(up_refs, (slice(None), slice(base, base + 128)), grad)
    rows = pl.ds(pl.multiple_of(128 + (step % 2) * 64, 64), 64)
    grad = jnp.where(core == step // 2, own_b[rows, :], other_b[rows, :]).astype(F32)
    adam_store(down_refs, (slice(None), slice(None)), grad)


def rotary_tables(segments):
    row_count = segments.shape[0]
    row_index = jnp.arange(row_count, dtype=jnp.int32)
    earlier = jnp.concatenate([jnp.full((1,), -1, jnp.int32), segments[:-1]])
    starts = jnp.where(segments != earlier, row_index, 0)
    position = (row_index - lax.cummax(starts, axis=0)).astype(F32)
    half_dim = ROT_DIM // 2
    dims = jnp.arange(LANES, dtype=jnp.int32) % HEAD_DIM
    frequency = ROPE_BASE ** (-2.0 * (dims % half_dim).astype(F32) / ROT_DIM)
    turned = dims < ROT_DIM
    angles = position[:, None] * jnp.where(turned, frequency, 0.0)[None, :]
    cosine, sine = jnp.cos(angles), jnp.sin(angles)
    front = (dims < half_dim)[None, :]
    return cosine, jnp.where(front, -sine, 0.0), jnp.where(front, 0.0, sine)


def on_device(
    sizes,
    tokens,
    segments,
    cotangent,
    w_qkv,
    w_out,
    w_up,
    w_down,
    vectors,
    m_qkv,
    m_out,
    m_up,
    m_down,
    m_vectors,
    v_qkv,
    v_out,
    v_up,
    v_down,
    v_vectors,
):
    copies, owners = sizes
    me = lax.axis_index("zero")
    plane = lax.axis_index("dp")
    core = plane % 2
    ids = jnp.stack([me, core, (plane // 2) % 2]).astype(jnp.int32)

    def move(value, target):
        pairs = []
        for d in range(copies):
            for z in range(owners):
                to_d, to_z = target(d, z)
                pairs.append((d * owners + z, to_d * owners + to_z))
        return lax.ppermute(value, AXES, pairs)

    def swap(value, dp_bits, zero_bits):
        return move(value, lambda d, z: (d ^ dp_bits, z ^ zero_bits))

    def swap_far(value):
        return move(value, lambda d, z: (d, z ^ (6 if d & 2 else 4)))

    def sync(*values):
        return lax.optimization_barrier(values)

    def add(*terms):
        return functools.reduce(jnp.add, [t.astype(F32) for t in terms])

    def reduce_first(keep, send_x, send_y):
        return keep, swap(send_x, 0, 1), swap(send_y, 2, 0)

    def reduce_first_part(keep, send_x, send_y):
        return keep, [send_x[0], swap(send_x[1], 0, 1)], swap(send_y, 2, 0)

    def reduce_second(state):
        keep, got_x, got_y = state
        far = add(keep[3], got_y[1]).astype(BF16)
        near = add(keep[1], got_x[1]).astype(BF16)
        return keep, got_x, got_y, far, near, swap(far, 0, 1), swap(near, 0, 2)

    def reduce_third(state):
        keep, got_x, got_y, _, _, got_far, got_near = state
        far = add(keep[2], got_y[0], got_far).astype(BF16)
        return (keep, got_x, got_near), far, swap_far(far)

    def reduce_fourth(state):
        (keep, got_x, got_near), _, got = state
        total = add(keep[0], got_x[0], got_near, got).astype(BF16)
        return total, swap(total, 2, 0)

    def reduce_fifth(state):
        total = add(*state).astype(BF16)
        bit = 4
        while bit < copies:
            total = add(total, swap(total, bit, 0)).astype(BF16)
            bit *= 2
        return total, swap(total, 1, 0)

    T, width = tokens.shape
    rows = 2 * T
    sds = jax.ShapeDtypeStruct
    row_block = lambda n, c=width: spec((n, c), lambda i: (i, 0))
    col_block = lambda n: spec((width, n), lambda i: (0, i))

    def block_call(body, grid, ins, outs, flops, moved, scratch=(), name=None):
        return kernel_call(
            body,
            grid,
            [place for _, place in ins],
            [place for _, place in outs],
            [shape for shape, _ in outs],
            flops,
            moved,
            scratch=scratch,
            name=name,
        )(*[value for value, _ in ins])

    def const(value):
        return value, whole(value.shape)

    def kept(shape, dtype):
        return sds(shape, dtype), whole(shape)

    steps = rows // 256
    with jax.named_scope("prep"):
        own_a = block_call(
            prep_attn_body,
            (1,),
            [(ids, scalars())]
            + [(w_qkv, spec((128, 512), lambda i, n=part: (0, 2 * n), single=True)) for part in range(3)]
            + [const(w_out), (vectors, whole((16, 128)))],
            [kept((144, 1280), BF16)],
            0,
            3e6,
            name="prep_attn",
        )[0]

    def prep_mlp(part, shape, ins, beside):
        with jax.named_scope("prep"):
            return block_call(
                functools.partial(prep_mlp_body, part),
                (1,),
                [(ids, scalars()), const(ins[0]), (ins[1], spec((256, width), lambda i: (part, 0), single=True))]
                + [const(value) for value in ins[2:]],
                [kept(shape, BF16)],
                0,
                beside * 3e6,
                name="prep_mlp",
            )[0]

    def z_moves(own):
        return swap(own, 0, 2), swap_far(own)

    with jax.named_scope("gather"):
        seg_other = swap(segments, 1, 0)
        tok_other = swap(tokens, 1, 0)
        dy_other = swap(cotangent, 1, 0)
        own_a, w_up_in = sync(own_a, w_up)
        next_a, far_a = z_moves(own_a)
        across_a = swap(own_a, 0, 1)
        own_b = prep_mlp(0, (256, 1024), (w_up_in, w_down), 20)
        tables = [
            jnp.concatenate(pair, axis=0)
            for pair in zip(rotary_tables(segments), rotary_tables(seg_other))
        ]
        seg_row = jnp.stack([segments, seg_other]).astype(F32)[:, None, :]
        seg_ids = jnp.concatenate([segments, seg_other]).astype(F32)
        next_a, far_a, across_a, own_b, w_up_in, tables, seg_row, seg_ids, tok_other, dy_other = sync(
            next_a, far_a, across_a, own_b, w_up_in, tables, seg_row, seg_ids, tok_other, dy_other
        )
        next_across_a, far_across_a, rest_across_a = swap(next_a, 0, 1), swap(far_a, 0, 1), swap(far_a, 2, 1)
        rest_a = swap(far_a, 2, 0)
        far_b = swap_far(own_b)
        seg_col = jnp.broadcast_to(seg_ids[:, None], (rows, LANES))
        w_up_in, seg_col = sync(w_up_in, seg_col)
        own_c = prep_mlp(1, (352, 1024), (w_up_in, w_down, w_qkv), 25)
        next_across_a, far_across_a, rest_a, rest_across_a, far_b, own_b, own_c = sync(
            next_across_a, far_across_a, rest_a, rest_across_a, far_b, own_b, own_c
        )
        far_across_b, across_b, rest_b = swap(far_b, 0, 1), swap(own_b, 0, 1), swap(far_b, 2, 0)
        next_b = swap(own_b, 0, 2)
        far_c = swap_far(own_c)
    attn_pieces = [own_a, next_a, far_a, rest_a, across_a, next_across_a, far_across_a, rest_across_a]

    def table_blocks(count):
        return [(t, row_block(count, 128)) for t in tables]

    def halves(own, other, count):
        last = T // count - 1
        return [
            (own, spec((count, width), lambda i: (jnp.minimum(i, last), 0))),
            (other, spec((count, width), lambda i: (jnp.maximum(i - last - 1, 0), 0))),
        ]

    def attention(group, pairs, projected, d_att, previous):
        with jax.named_scope("attention"):
            first = pairs[0]
            head_block = spec((T, 128), lambda h, m: (h, m + first))
            outs = [
                (sds((rows, 256), BF16), head_block),
                (sds((3, rows, 256), BF16), spec((3, T, 128), lambda h, m: (0, h, m + first))),
            ]
            ins = (
                [(value, head_block) for value in projected]
                + [(d_att, spec((T, 128), lambda h, m: (h, m + first + 2 * group)))]
                + [(seg_col, spec((T, LANES), lambda h, m: (h, 0)))]
                + [(seg_row, spec((1, 1, T), lambda h, m: (h, 0, 0)))]
                + [(t, spec((T, 128), lambda h, m: (h, 0))) for t in tables]
            )
            aliases = {len(ins) + n: n for n in range(len(previous))}
            return pl.pallas_call(
                attn_body,
                grid=(2, len(pairs)),
                in_specs=[place for _, place in ins] + [distant()] * len(previous),
                out_specs=[place for _, place in outs],
                out_shape=[shape for shape, _ in outs],
                input_output_aliases=aliases,
                cost_estimate=pl.CostEstimate(
                    flops=len(pairs) * 15000000000, bytes_accessed=len(pairs) * 5000000, transcendentals=0
                ),
                compiler_params=pltpu.CompilerParams(
                    vmem_limit_bytes=VMEM_NEED * MIB, dimension_semantics=("arbitrary",) * 2
                ),
                name="attention",
            )(*[value for value, _ in ins], *previous)

    def blocks_of(shape):
        return [kept((n,) + shape, BF16) for n in (4, 2, 2)]

    with jax.named_scope("qkv"):
        *projected, d_att, attn_in, attn_t, mlp_in, wq_a, full_out, vec, bias_qkv = block_call(
            functools.partial(qkv_first_body, rows // 256),
            (rows // 256,),
            [(ids, scalars())]
            + [const(piece) for piece in attn_pieces]
            + halves(tokens, tok_other, 256)
            + halves(cotangent, dy_other, 256)
            + table_blocks(256),
            [(sds((rows, 256), BF16), row_block(256, 256))] * 3
            + [(sds((rows, 512), BF16), row_block(256, 512)), (sds((rows, width), BF16), row_block(256))]
            + [(sds((width, rows), BF16), col_block(256)), (sds((rows, width), BF16), row_block(256))]
            + [kept((1024, 768), BF16), kept((512, 1024), BF16), kept((16, 1024), F32), kept((1, 1536), F32)],
            2 * rows * 1024 * 1280,
            30e6,
            name="qkv",
        )
    projected, far_across_b, across_b, rest_b, own_b = sync(
        projected, far_across_b, across_b, rest_b, own_b
    )
    with jax.named_scope("gather"):
        rest_across_b, next_across_b = swap(far_across_b, 2, 0), swap(own_b, 0, 3)
    half_a = attention(0, (0,), projected, d_att, [])
    half_a, projected, far_c, own_c, next_b = sync(half_a, projected, far_c, own_c, next_b)
    with jax.named_scope("gather"):
        far_across_c, rest_c, next_c = swap(far_c, 0, 1), swap(far_c, 2, 0), swap(own_c, 0, 2)
    att_a, grad_a = attention(0, (1,), projected, d_att, half_a)
    att_a, grad_a, rest_across_b, next_across_b, far_across_c, rest_c, own_c, next_c, attn_t, mlp_in = sync(
        att_a, grad_a, rest_across_b, next_across_b, far_across_c, rest_c, own_c, next_c, attn_t, mlp_in
    )
    with jax.named_scope("gather"):
        across_c, next_across_c, rest_across_c = swap(own_c, 0, 1), swap(next_c, 0, 1), swap(far_across_c, 2, 0)
    pieces_b = [own_b, next_b, far_b, rest_b, across_b, next_across_b, far_across_b, rest_across_b]

    def mlp(part, weights, rows_in):
        with jax.named_scope("mlp"):
            *results, hid, gp, sums, w_up_full, w_down_full = block_call(
                functools.partial(mlp_body, part, steps),
                (steps,),
                [(ids, scalars())]
                + [const(w) for w in weights]
                + [const(vec), (rows_in, row_block(256))]
                + halves(cotangent, dy_other, 256),
                [(sds((n, 256, 1024), BF16), distant()) for n in (4, 2, 2)]
                + [(sds((rows, width), BF16), row_block(256))] * 2
                + [kept((8, 1024), F32)]
                + [(sds((1024, 1024), BF16), distant())] * 2,
                2 * rows * 1024 * 1024 * 4,
                40e6,
                scratch=[
                    pltpu.VMEM((1024, rows), BF16),
                    pltpu.VMEM((1024, rows), BF16),
                    pltpu.VMEM((rows, 1024), BF16),
                    pltpu.VMEM((rows, 1024), BF16),
                    pltpu.VMEM((8, 1024), F32),
                    pltpu.VMEM((1024, 512), BF16),
                ]
                + [pltpu.VMEM((n, 256, 1024), BF16) for n in (4, 2, 2)]
                + [pltpu.VMEM((1024, 1024), BF16)] * 2
                + [pltpu.SemaphoreType.DMA((8,))],
                name="mlp",
            )
            return results, hid, gp, sums, w_up_full, w_down_full

    mlp_a = mlp(0, pieces_b, mlp_in)
    mlp_a, mlp_in, across_c, next_across_c, rest_across_c = sync(
        mlp_a, mlp_in, across_c, next_across_c, rest_across_c
    )
    pieces_c = [own_c, next_c, far_c, rest_c, across_c, next_across_c, far_across_c, rest_across_c]
    reduce_a = reduce_first(*mlp_a[0])
    mlp_b = mlp(1, pieces_c, mlp_in)
    mlp_b, reduce_a, attn_in = sync(mlp_b, reduce_a, attn_in)
    reduce_a = reduce_second(reduce_a)
    reduce_b = reduce_first_part(*mlp_b[0])
    attn_in, *ready = sync(attn_in, *reduce_a[3:5])

    with jax.named_scope("attention"):
        head_block = spec((T, 128), lambda h, m: (h, m))
        att_b, grad_b, wq_b = block_call(
            project_attn_body,
            (2, 2),
            [(ids, scalars())]
            + [(piece, whole((96, width))) for piece in pieces_c]
            + [(attn_in, spec((T, width), lambda h, m: (h, 0))), const(bias_qkv)]
            + [(d_att, spec((T, 128), lambda h, m: (h, m + 2)))]
            + [(seg_col, spec((T, LANES), lambda h, m: (h, 0)))]
            + [(seg_row, spec((1, 1, T), lambda h, m: (h, 0, 0)))]
            + [(t, spec((T, 128), lambda h, m: (h, 0))) for t in tables],
            [
                (sds((rows, 256), BF16), head_block),
                (sds((3, rows, 256), BF16), spec((3, T, 128), lambda h, m: (0, h, m))),
                kept((1024, 768), BF16),
            ],
            38e9,
            20e6,
            scratch=[pltpu.VMEM((T, 256), BF16)] * 3,
            name="attention",
        )
    att_b, grad_b, reduce_a, reduce_b = sync(att_b, grad_b, reduce_a, reduce_b)
    reduce_a = reduce_third(reduce_a)
    reduce_b[1][0] = swap(reduce_b[1][0], 0, 1)
    reduce_b = reduce_second(reduce_b)
    grad_b, *ready = sync(grad_b, reduce_a[1], *reduce_b[3:5])
    with jax.named_scope("attn_weights"):
        *blocks, bias_sum = block_call(
            attn_weights_body,
            (7,),
            [(ids, scalars()), const(attn_t)]
            + [(grad_a, spec((1, rows, 256), lambda n: (jnp.minimum(n, 2), 0, 0)))]
            + [(grad_b, spec((1, rows, 256), lambda n: (jnp.clip(n - 3, 0, 2), 0, 0)))]
            + [(value, distant()) for value in (att_a, att_b, cotangent, dy_other)],
            blocks_of((128, 2048)) + [kept((8, 1536), F32)],
            2 * rows * 1024 * 2048,
            24e6,
            scratch=[pltpu.VMEM((1024, 256), BF16)]
            + [pltpu.VMEM((rows, 256), BF16)] * 2
            + [pltpu.VMEM((T, width), BF16)] * 2
            + [pltpu.SemaphoreType.DMA((4,))],
            name="attn_weights",
        )
    blocks, grad_b, reduce_a, reduce_b = sync(blocks, grad_b, reduce_a, reduce_b)
    reduce_o = reduce_first(*blocks)

    _, hid_a, gp_a, sums_a, up_a, down_a = mlp_a
    _, hid_b, gp_b, sums_b, up_b, down_b = mlp_b

    def adam_down(totals):
        wide = [spec((128, width), lambda n: (n, 0))] * 3
        return kernel_call(
            adam_down_body,
            (2,),
            [scalars()] + [whole((256, 1024))] * 2 + wide,
            wide,
            [sds((512, 1024), F32)] * 3,
            0,
            7e6,
            name="adam_down",
        )(ids, *totals, w_down, m_down, v_down)

    def adam_mlp(totals_a, totals_b, previous):
        wide = [spec((128, 1024), lambda n: (0, n))] * 3 + [spec((64, width), lambda n: (4 + n, 0))] * 3
        return pl.pallas_call(
            adam_mlp_body,
            grid=(4,),
            in_specs=[scalars()] + [whole((256, 1024))] * 4 + wide + [distant()] * 3,
            out_specs=wide,
            out_shape=[sds((128, 4096), F32)] * 3 + [sds((512, 1024), F32)] * 3,
            input_output_aliases={11 + n: 3 + n for n in range(3)},
            cost_estimate=pl.CostEstimate(flops=0, bytes_accessed=21000000, transcendentals=0),
            compiler_params=pltpu.CompilerParams(
                vmem_limit_bytes=VMEM_NEED * MIB, dimension_semantics=("arbitrary",)
            ),
            name="adam_mlp",
        )(ids, *totals_a, *totals_b, w_up, m_up, v_up, w_down, m_down, v_down, *previous)

    def back(own, grad, rows_tok, extra, outs):
        first = 0 if own else T // 256
        block = lambda c=width: spec((256, c), lambda i: (i + first, 0))
        lead = spec((3, 256, 256), lambda i: (0, i + first, 0))
        with jax.named_scope("back"):
            return block_call(
                functools.partial(back_body, own),
                (T // 256,),
                [(grad_a, lead), (grad, lead), (att_a, block(256)), (att_b, block(256))]
                + [(value, block()) for value in (hid_a, hid_b, gp_a, gp_b)]
                + [const(w) for w in (full_out, down_a, down_b, up_a, up_b, wq_a, wq_b)]
                + [(rows_tok, row_block(256)), const(vec)]
                + extra,
                outs + [kept((8, width), F32)],
                2 * T * 1024 * 6144,
                40e6,
                name="back",
            )

    reduce_a = reduce_fourth(reduce_a)
    reduce_b = reduce_third(reduce_b)
    pair_block = spec((2, 256, width), lambda i: (0, i, 0))
    part_other, sums_other = back(False, grad_b, tok_other, [], [(sds((2, T, width), BF16), pair_block)])
    part_other, sums_other, grad_b, reduce_a, reduce_b, reduce_o = sync(
        part_other, sums_other, grad_b, reduce_a, reduce_b, reduce_o
    )
    reduce_o = reduce_second(reduce_o)
    part_other, reduce_a, reduce_b, *ready = sync(part_other, reduce_a, reduce_b, *reduce_o[3:5])
    reduce_a = reduce_fifth(reduce_a)
    reduce_b = reduce_fourth(reduce_b)
    part_got = swap(part_other, 1, 0)
    updated_mlp = adam_down(reduce_a)
    updated_mlp, grad_b, reduce_b, reduce_o, part_got = sync(
        updated_mlp, grad_b, reduce_b, reduce_o, part_got
    )
    reduce_o = reduce_third(reduce_o)
    reduce_b = reduce_fifth(reduce_b)
    grad_b, *ready = sync(grad_b, reduce_o[1], reduce_b[0])
    layer_out, tokens_grad, sums_own = back(
        True,
        grad_b,
        tokens,
        [(cotangent, row_block(256)), (part_got, pair_block)],
        [(sds((T, width), BF16), row_block(256)), (sds((T, width), F32), row_block(256))],
    )
    sums_own, updated_mlp, reduce_b, reduce_o = sync(sums_own, updated_mlp, reduce_b, reduce_o)
    reduce_o = reduce_fourth(reduce_o)

    with jax.named_scope("vectors"):
        is_core = jnp.arange(2) == core
        grad_bias = jnp.where(core == 0, sums_a[1:2], 0.0)
        bias_sum = jnp.swapaxes(bias_sum[0].reshape(2, 3, 256), 0, 1)
        grad_bias_qkv = jnp.where(
            is_core[None, None, :, None], bias_sum.reshape(3, 8, 1, 64), 0.0
        ).reshape(3, width)
        grad_bias_up = jnp.where(
            is_core[None, None, :, None],
            jnp.swapaxes(jnp.stack([sums_a[0], sums_b[0]]).reshape(2, 8, 128), 0, 1)[:, :, None],
            0.0,
        ).reshape(4, width)
        total = jnp.concatenate(
            [
                sums_own[0:4] + sums_other[0:4],
                grad_bias_qkv,
                grad_bias,
                grad_bias_up,
                grad_bias,
                jnp.zeros((3, width), F32),
            ],
            axis=0,
        )
        moved = [swap(total, 0, step) for step in (2, 4, 6)]
        updated_mlp = adam_mlp(reduce_a, reduce_b, updated_mlp)
        updated_mlp, reduce_o, total, moved = sync(updated_mlp, reduce_o, total, moved)
        reduce_o = reduce_fifth(reduce_o)
        total = functools.reduce(jnp.add, moved, total)
        others = swap(total, 0, 1), swap(total, 2, 0), swap(total, 2, 1)

    with jax.named_scope("adam"):
        wide = [spec((128, 1536), lambda n: (0, n))] * 3 + [whole((128, 1024))] * 3
        updated_attn = kernel_call(
            adam_attn_body,
            (2,),
            [scalars()] + [whole((128, 2048))] * 2 + wide,
            wide,
            [sds((128, 3072), F32)] * 3 + [sds((128, 1024), F32)] * 3,
            0,
            13e6,
            name="adam",
        )(ids, *reduce_o, w_qkv, m_qkv, v_qkv, w_out, m_out, v_out)

    with jax.named_scope("vectors"):
        updated_attn, total, (across, beside, both) = sync(updated_attn, total, others)
        total = (total + across) + (beside + both)
        bit = 4
        while bit < copies:
            total = total + swap(total, bit, 0)
            bit *= 2
        total = total + swap(total, 1, 0)
        share = lax.dynamic_slice_in_dim(total[0:13], me * 128, 128, 1)
        first_vectors, second_vectors, new_vectors = adam_math(
            vectors, m_vectors, v_vectors, share, RATE_VECTOR, 0.0
        )
    first_qkv, second_qkv, new_qkv, first_out, second_out, new_out = updated_attn
    first_up, second_up, new_up, first_down, second_down, new_down = updated_mlp
    return (
        layer_out,
        tokens_grad,
        first_qkv,
        first_out,
        first_up,
        first_down,
        first_vectors,
        second_qkv,
        second_out,
        second_up,
        second_down,
        second_vectors,
        new_qkv,
        new_out,
        new_up,
        new_down,
        new_vectors,
    )


def solution(mesh):
    rows, owned, spread = P(AXES, None), P("zero", None), P(None, "zero")
    state = (owned, owned, owned, owned, spread)
    return jax.shard_map(
        functools.partial(on_device, (mesh.shape["dp"], mesh.shape["zero"])),
        mesh=mesh,
        in_specs=(rows, P(AXES), rows) + state * 3,
        out_specs=(rows, rows) + state * 3,
        check_vma=False,
    )
```

```python
import functools

import jax
import jax.numpy as jnp
from jax import lax
from jax.experimental import pallas as pl
from jax.experimental.pallas import tpu as pltpu
from jax.sharding import PartitionSpec as P

HEAD_DIM = 64
ROT_DIM = 16
STEP = 10
EPS_NORM = 1e-05
BETA_ONE = 0.9
BETA_TWO = 0.999
ADAM_EPS = 1e-08
RATE_MATRIX = 0.05
RATE_VECTOR = 0.2
DECAY_MATRIX = 0.1
ROPE_BASE = 10000.0
INV_ROOT_TWO = 0.7071067811865476
INV_ROOT_TAU = 0.3989422804014327
MASKED = -1e30
LANES = 128
AXES = ("dp", "zero")
F32 = jnp.float32
BF16 = jnp.bfloat16
MIB = 1024 * 1024
VMEM_NEED = 58


def spec(block, index, single=False):
    if single:
        return pl.BlockSpec(block, index, pipeline_mode=pl.Buffered(1))
    return pl.BlockSpec(block, index)


def whole(shape):
    return spec(shape, lambda *_: (0,) * len(shape), single=True)


def distant():
    return pl.BlockSpec(memory_space=pl.ANY)


def scalars():
    return pl.BlockSpec(memory_space=pltpu.SMEM)


def kernel_call(body, grid, in_specs, out_specs, out_shape, flops, moved, scratch=(), name=None):
    return pl.pallas_call(
        body,
        grid=grid,
        in_specs=in_specs,
        out_specs=out_specs,
        out_shape=out_shape,
        scratch_shapes=list(scratch),
        cost_estimate=pl.CostEstimate(flops=int(flops), bytes_accessed=int(moved), transcendentals=0),
        compiler_params=pltpu.CompilerParams(
            vmem_limit_bytes=VMEM_NEED * MIB, dimension_semantics=("arbitrary",) * len(grid)
        ),
        name=name,
    )


def nn(left, right):
    return lax.dot_general(left, right, (((1,), (0,)), ((), ())), preferred_element_type=F32)


def nt(left, right):
    return lax.dot_general(left, right, (((1,), (1,)), ((), ())), preferred_element_type=F32)


def tn(left, right):
    return lax.dot_general(left, right, (((0,), (0,)), ((), ())), preferred_element_type=F32)


def piece_owner(ids, place):
    step = place % 4
    if step > 1:
        step = 2 + ids[2] if step == 2 else 3 - ids[2]
    return jnp.bitwise_xor(ids[0], 2 * step + place // 4)


SLOTS = ((0, 0), (1, 0), (2, 0), (2, 1), (0, 1), (1, 1), (3, 0), (3, 1))


def slot_owner(ids, slot):
    step, side = SLOTS[slot]
    if step > 1:
        step = 2 + ids[2] if step == 2 else 3 - ids[2]
    return jnp.bitwise_xor(ids[0], 2 * step + side)


def slot_ref(outs, slot):
    return (outs[0], slot) if slot < 4 else (outs[1], slot - 4) if slot < 6 else (outs[2], slot - 6)


def low_lanes():
    return lax.broadcasted_iota(jnp.int32, (1, LANES), 1) < HEAD_DIM


def pick_parity(core, tile_a, tile_b):
    low = low_lanes()
    even = jnp.where(low, tile_a, pltpu.roll(tile_b, HEAD_DIM, 1))
    odd = jnp.where(low, pltpu.roll(tile_a, HEAD_DIM, 1), tile_b)
    return jnp.where(core == 0, even, odd)


def prep_attn_body(ids, w_q, w_k, w_v, w_out, vec, out, padded):
    core = ids[1]
    for part, w in enumerate((w_q, w_k, w_v)):
        for tile in range(2):
            base = tile * 256
            at = part * 256 + tile * 128
            out[0:128, at : at + 128] = pick_parity(
                core, w[:, base : base + 128], w[:, base + 128 : base + 256]
            ).astype(BF16)
    rows = w_out[pl.ds(pl.multiple_of(core * 64, 64), 64), :].astype(BF16)
    for panel in range(4):
        at = 768 + 256 * (panel // 2)
        base = (panel % 2) * 64
        out[base : base + 64, at : at + 256] = rows[:, 256 * panel : 256 * panel + 256]
    padded[...] = jnp.zeros_like(padded)
    padded[0:13, :] = vec[...]
    out[128:144, 0:128] = padded[...].astype(BF16)
    out[128:144, 128:1280] = jnp.zeros((16, 1152), BF16)


def prep_mlp_body(part, ids, w_up, w_down, *refs):
    out = refs[-1]
    core = ids[1]
    top = 96 * part
    for owner in range(8):
        start = pl.multiple_of(owner * 512 + part * 256 + core * 128, 128)
        out[top : top + 128, owner * 128 : (owner + 1) * 128] = w_up[:, pl.ds(start, 128)].astype(BF16)
    out[top + 128 : top + 256, :] = w_down[pl.ds(pl.multiple_of(core * 128, 128), 128), :].astype(BF16)
    if not part:
        return
    w_qkv = refs[0]
    for third in range(3):
        for tile in range(2):
            base = third * 1024 + 512 + tile * 256
            value = pick_parity(core, w_qkv[:, base : base + 128], w_qkv[:, base + 128 : base + 256]).astype(BF16)
            for panel in range(4):
                at = panel * 256 + tile * 128
                out[32 * third : 32 * third + 32, at : at + 128] = value[32 * panel : 32 * panel + 32]


def normalize(inputs):
    centred = inputs - jnp.mean(inputs, axis=-1, keepdims=True)
    variance = jnp.mean(centred * centred, axis=-1, keepdims=True)
    inv_std = lax.rsqrt(variance + EPS_NORM)
    return centred * inv_std, inv_std


def turned(x, cos, sin_lo, sin_hi, sign):
    return x * cos[...] + sign * (pltpu.roll(x, 8, 1) * sin_hi[...] + pltpu.roll(x, 120, 1) * sin_lo[...])


def project(group, rows, w_qkv, bias, tables, outs):
    for part, out in enumerate(outs):
        cols = slice(part * 256, (part + 1) * 256)
        at = group * 768 + part * 256
        acc = nn(rows, w_qkv[:, cols]) + bias[:, at : at + 256]
        if part == 2:
            out[...] = acc.astype(BF16)
            continue
        for tile in range(2):
            x = turned(acc[:, tile * 128 : (tile + 1) * 128], *tables, 1.0)
            if part == 0:
                x = x * HEAD_DIM ** (-0.5)
            out[:, tile * 128 : (tile + 1) * 128] = x.astype(BF16)


def qkv_first_body(steps, ids, *refs):
    pieces, refs = refs[:8], refs[8:]
    tok_own, tok_other, dy_own, dy_other, cos, sin_lo, sin_hi = refs[:7]
    q, k, v, d_att, attn_in, attn_t, mlp_in, w_qkv, w_out, vec, bias = refs[7:]
    step = pl.program_id(0)

    @pl.when(step == 0)
    def _():
        for place, piece in enumerate(pieces):
            owner = piece_owner(ids, place)
            at_owner = pl.ds(pl.multiple_of(owner * 128, 128), 128)
            w_qkv[at_owner, :] = piece[0:128, 0:768]
            vec[:, at_owner] = piece[128:144, 0:128].astype(F32)
            for panel in range(4):
                at = 768 + 256 * (panel // 2)
                base = (panel % 2) * 64
                w_out[pl.ds(pl.multiple_of(owner * 64, 64), 64), 256 * panel : 256 * panel + 256] = piece[
                    base : base + 64, at : at + 256
                ]
        for part in range(3):
            for tile in range(4):
                base = tile * 256
                row = slice(4 + part, 5 + part)
                at = (tile // 2) * 768 + part * 256 + (tile % 2) * 128
                bias[:, at : at + 128] = pick_parity(
                    ids[1], vec[row, base : base + 128], vec[row, base + 128 : base + 256]
                )

    first = step < steps // 2
    d_att[...] = nt(jnp.where(first, dy_own[...], dy_other[...]), w_out[...]).astype(BF16)
    normed, _ = normalize(jnp.where(first, tok_own[...], tok_other[...]).astype(F32))
    rows = (normed * vec[0:1, :] + vec[1:2, :]).astype(BF16)
    mlp_in[...] = (normed * vec[2:3, :] + vec[3:4, :]).astype(BF16)
    attn_in[...] = rows
    attn_t[...] = rows.T
    project(0, rows, w_qkv, bias, (cos, sin_lo, sin_hi), (q, k, v))


ATTN_ROWS = 256


def cat(parts, axis=0):
    return jnp.concatenate(parts, axis=axis) if len(parts) > 1 else parts[0]


def attn_body(q, k, v, d_att, seg_col, seg_row, cos, sin_lo, sin_hi, *refs):
    att, grad = refs[-2:]
    count = q.shape[0]
    size = ATTN_ROWS
    blocks = count // size
    span = [slice(j * size, (j + 1) * size) for j in range(blocks)]
    low = low_lanes()
    zero = jnp.zeros((), BF16)
    causal = lax.broadcasted_iota(jnp.int32, (size, size), 0) >= lax.broadcasted_iota(
        jnp.int32, (size, size), 1
    )
    q_t, da_t = q[...].T, d_att[...].T

    def row_total(parts, reduce, join):
        cols = [reduce(part, axis=-1, keepdims=True) for part in parts]
        return [
            functools.reduce(join, [cols[j][(i - j) * size : (i - j + 1) * size] for j in range(i + 1)])
            for i in range(blocks)
        ]

    def row_sum(parts):
        return cat(
            [
                functools.reduce(jnp.add, [parts[j][(i - j) * size : (i - j + 1) * size] for j in range(i + 1)])
                for i in range(blocks)
            ]
        )

    def products(half):
        lanes = low if half == 0 else jnp.logical_not(low)
        q_h = jnp.where(lanes, q[...], zero)
        da_h = jnp.where(lanes, d_att[...], zero)
        scores = [nt(q_h[j * size :], k[span[j], :]) for j in range(blocks)]
        return scores, [nt(da_h[j * size :], v[span[j], :]) for j in range(blocks)]

    def softmax_both(scores, grad_probs):
        masked = []
        for j in range(blocks):
            allowed = seg_col[j * size :, 0:1] == seg_row[0, :, span[j]]
            allowed = cat([allowed[:size] & causal] + ([allowed[size:]] if j < blocks - 1 else []))
            masked.append(jnp.where(allowed, scores[j], MASKED))
        top = row_total(masked, jnp.max, jnp.maximum)
        raised = [jnp.exp(masked[j] - cat(top[j:])) for j in range(blocks)]
        inv = [1.0 / total for total in row_total(raised, jnp.sum, jnp.add)]
        probs = [raised[j] * cat(inv[j:]) for j in range(blocks)]
        delta = row_total([g * p for g, p in zip(grad_probs, probs)], jnp.sum, jnp.add)
        grad_scores = [
            (probs[j] * (grad_probs[j] - cat(delta[j:]))).astype(BF16) for j in range(blocks)
        ]
        return [p.astype(BF16) for p in probs], grad_scores

    def results(half, probs, grad_scores):
        rows = slice(half * HEAD_DIM, (half + 1) * HEAD_DIM)
        return (
            row_sum([nn(probs[j], v[span[j], :]) for j in range(blocks)]),
            row_sum([nn(grad_scores[j], k[span[j], :]) for j in range(blocks)]),
            cat([nn(q_t[rows, j * size :], grad_scores[j]) for j in range(blocks)], 1),
            cat([nn(da_t[rows, j * size :], probs[j]) for j in range(blocks)], 1),
        )

    first = softmax_both(*products(0))
    second = products(1)
    out_a, dq_a, dk_a, dv_a = results(0, *first)
    out_b, dq_b, dk_b, dv_b = results(1, *softmax_both(*second))
    tables = (cos, sin_lo, sin_hi)
    att[...] = jnp.where(low, out_a, out_b).astype(BF16)
    grad[0] = turned(jnp.where(low, dq_a, dq_b) * HEAD_DIM ** (-0.5), *tables, -1.0).astype(BF16)
    grad[1] = turned(jnp.concatenate([dk_a, dk_b], axis=0).T, *tables, -1.0).astype(BF16)
    grad[2] = jnp.concatenate([dv_a, dv_b], axis=0).T.astype(BF16)


def project_attn_body(ids, *refs):
    pieces, (attn_in, bias, d_att, seg_col, seg_row, *tables) = refs[:8], refs[8:16]
    att, grad, w_qkv, *projected = refs[16:]
    half, pair = pl.program_id(0), pl.program_id(1)

    @pl.when((half == 0) & (pair == 0))
    def _():
        for place, piece in enumerate(pieces):
            owner = piece_owner(ids, place)
            for part in range(3):
                for panel in range(4):
                    at = pl.ds(pl.multiple_of(owner * 128 + 32 * panel, 32), 32)
                    w_qkv[at, part * 256 : part * 256 + 256] = piece[
                        32 * part : 32 * part + 32, panel * 256 : panel * 256 + 256
                    ]

    @pl.when(pair == 0)
    def _():
        project(1, attn_in[...], w_qkv, bias, tables, projected)

    lanes = pl.ds(pl.multiple_of(pair * LANES, LANES), LANES)
    attn_body(*[value.at[:, lanes] for value in projected], d_att, seg_col, seg_row, *tables, att, grad)


def attn_weights_body(ids, attn_t, grad_a, grad_b, far_att_a, far_att_b, far_own, far_other, *refs):
    keep, send_x, send_y, bias, result, att_a, att_b, dy_own, dy_other, sems = refs
    copies = [
        pltpu.make_async_copy(source, target, sems.at[n])
        for n, (source, target) in enumerate(
            ((far_att_a, att_a), (far_att_b, att_b), (far_own, dy_own), (far_other, dy_other))
        )
    ]

    @pl.when(pl.program_id(0) == 0)
    def _():
        for copy in copies:
            copy.start()

    step = pl.program_id(0)
    outs = (keep, send_x, send_y)

    @pl.when(step < 6)
    def _():
        rhs = jnp.where(step < 3, grad_a[0], grad_b[0])
        result[...] = nn(attn_t[...], rhs).astype(BF16)
        cols = pl.ds(pl.multiple_of(step * 256, 256), 256)
        bias[0:1, cols] = jnp.sum(rhs.astype(F32), axis=0, keepdims=True)
        for slot in range(8):
            out, at = slot_ref(outs, slot)
            base = pl.multiple_of(slot_owner(ids, slot) * 128, 128)
            out[at, :, cols] = result[pl.ds(base, 128), :]

    @pl.when(step == 6)
    def _():
        for copy in copies:
            copy.wait()
        count = dy_own.shape[0]
        for group, att in enumerate((att_a, att_b)):
            flipped = att[...].T
            for panel in range(4):
                cols = slice(panel * 256, panel * 256 + 256)
                term = nn(flipped[:, :count], dy_own[:, cols]) + nn(flipped[:, count:], dy_other[:, cols])
                result[group * 256 : group * 256 + 256, :] = term.astype(BF16)
                for slot in range(8):
                    out, at = slot_ref(outs, slot)
                    owner = slot_owner(ids, slot)
                    col = 1536 + 256 * (panel // 2)
                    base = (panel % 2) * 64

                    @pl.when(owner // 4 == group)
                    def _():
                        out[at, base : base + 64, col : col + 256] = result[
                            pl.ds(pl.multiple_of(owner * 64, 64), 64), :
                        ]


def mlp_body(part, steps, ids, *refs):
    pieces, (vec, mlp_in, dy_own, dy_other) = refs[:8], refs[8:12]
    far_outs, (hidden_out, grad_out, sums, far_up, far_down) = refs[12:15], refs[15:20]
    mlp_t, hidden_t, grad_pre, dy, bias, result, keep, send_x, send_y, w_up, w_down, sems = refs[20:]
    outs = (keep, send_x, send_y)
    weight_copies = [
        pltpu.make_async_copy(w_up, far_up, sems.at[0]),
        pltpu.make_async_copy(w_down, far_down, sems.at[1]),
    ]
    core = ids[1]
    step = pl.program_id(0)

    @pl.when(step == 0)
    def _():
        for owner in range(8):
            start = pl.multiple_of((owner % 2) * 512 + part * 256 + core * 128, 128)
            row = 8 + owner // 2
            bias[0:1, owner * 128 : (owner + 1) * 128] = vec[row : row + 1, pl.ds(start, 128)]
        sums[...] = jnp.zeros_like(sums)
        for place, piece in enumerate(pieces):
            at = pl.ds(pl.multiple_of(piece_owner(ids, place) * 128, 128), 128)
            top = 96 * part
            w_up[at, :] = piece[top : top + 128, :]
            w_down[at, :] = piece[top + 128 : top + 256, :]
        for copy in weight_copies:
            copy.start()

    rows = mlp_in[...]
    grads = jnp.where(step < steps // 2, dy_own[...], dy_other[...])
    count = rows.shape[0]
    at = pl.ds(pl.multiple_of(step * count, count), count)
    mlp_t[:, at] = rows.T
    dy[at, :] = grads
    sums[1:2, :] += jnp.sum(grads.astype(F32), axis=0, keepdims=True)
    for col in range(0, 1024, 512):
        cols = slice(col, col + 512)
        pre = nn(rows, w_up[:, cols]) + bias[0:1, cols]
        grad_hidden = nt(grads, w_down[cols, :])
        cdf = 0.5 + 0.5 * lax.erf(pre * INV_ROOT_TWO)
        pdf = jnp.exp(-0.5 * pre * pre) * INV_ROOT_TAU
        act = (pre * cdf).astype(BF16)
        hidden_t[cols, at] = act.T
        hidden_out[:, cols] = act
        gp = (grad_hidden * (cdf + pre * pdf)).astype(BF16)
        grad_pre[at, cols] = gp
        grad_out[:, cols] = gp
        sums[0:1, cols] += jnp.sum(gp.astype(F32), axis=0, keepdims=True)

    @pl.when(step == steps - 1)
    def _():
        copies = list(weight_copies)
        for base_row, left, right in ((0, mlp_t, grad_pre), (128, hidden_t, dy)):
            for col in range(0, 1024, 512):
                cols = slice(col, col + 512)
                result[...] = nn(left[...], right[:, cols]).astype(BF16)
                for slot in range(8):
                    out, place = slot_ref(outs, slot)
                    base = pl.multiple_of(slot_owner(ids, slot) * 128, 128)
                    out[place, base_row : base_row + 128, cols] = result[pl.ds(base, 128), :]
            span = pl.ds(base_row, 128)
            for out, far_out in zip(outs, far_outs):
                copy = pltpu.make_async_copy(out.at[:, span, :], far_out.at[:, span, :], sems.at[len(copies)])
                copy.start()
                copies.append(copy)
        for copy in copies:
            copy.wait()


def back_body(own, grad_a, grad_b, att_a, att_b, hid_a, hid_b, gp_a, gp_b, *refs):
    w_out, down_a, down_b, up_a, up_b, wq_a, wq_b, tok, vec = refs[:9]
    if own:
        dy, other, out, result, sums = refs[9:]
    else:
        out, sums = refs[9:]
    inputs = tok[...].astype(F32)
    normed, inv_std = normalize(inputs)
    branch = nn(att_a[...], w_out[0:256, :]) + nn(att_b[...], w_out[256:512, :])
    branch = branch + nn(hid_a[...], down_a[...]) + nn(hid_b[...], down_b[...])
    back_mlp = nt(gp_a[...], up_a[...]) + nt(gp_b[...], up_b[...])
    back_attn = None
    for grad, w in ((grad_a, wq_a), (grad_b, wq_b)):
        for part in range(3):
            term = nt(grad[part], w[:, part * 256 : part * 256 + 256])
            back_attn = term if back_attn is None else back_attn + term
    scaled = back_attn * vec[0:1, :] + back_mlp * vec[2:3, :]

    @pl.when(pl.program_id(0) == 0)
    def _():
        sums[...] = jnp.zeros_like(sums)

    for row, value in enumerate((back_attn * normed, back_attn, back_mlp * normed, back_mlp)):
        sums[row : row + 1, :] += jnp.sum(value, axis=0, keepdims=True)
    if not own:
        out[0] = branch.astype(BF16)
        out[1] = scaled.astype(BF16)
        return
    branch = branch + other[0].astype(F32)
    out[...] = (inputs + branch + (vec[7:8, :] + vec[12:13, :])).astype(BF16)
    scaled = scaled + other[1].astype(F32)
    result[...] = dy[...].astype(F32) + inv_std * (
        scaled
        - jnp.mean(scaled, axis=-1, keepdims=True)
        - normed * jnp.mean(scaled * normed, axis=-1, keepdims=True)
    )


def adam_math(weight, first, second, gradient, rate, decay):
    first_new = BETA_ONE * first + (1.0 - BETA_ONE) * gradient
    second_new = BETA_TWO * second + (1.0 - BETA_TWO) * gradient * gradient
    first_hat = first_new / (1.0 - BETA_ONE**STEP)
    second_hat = second_new / (1.0 - BETA_TWO**STEP)
    weight_new = weight - rate * (first_hat / (jnp.sqrt(second_hat) + ADAM_EPS) + decay * weight)
    return (first_new, second_new, weight_new)


def adam_store(refs, at, gradient):
    w, m, v, m_out, v_out, w_out = refs
    first, second, weight = adam_math(w[at], m[at], v[at], gradient, RATE_MATRIX, DECAY_MATRIX)
    m_out[at] = first
    v_out[at] = second
    w_out[at] = weight


def parities(core, own, other):
    return jnp.where(core == 0, own, other), jnp.where(core == 0, other, own)


def adam_attn_body(ids, own, other, *refs):
    core = ids[1]
    low = low_lanes()
    qkv_refs = refs[0:3] + refs[6:9]
    for tile in range(6):
        count = pl.program_id(0) * 6 + tile
        part, place = count // 4, count % 4
        start = (place // 2) * 768 + part * 256 + (place % 2) * 128
        cols = pl.ds(pl.multiple_of(start, 128), 128)
        even, odd = parities(core, own[:, cols].astype(F32), other[:, cols].astype(F32))
        first = jnp.where(low, even, pltpu.roll(odd, HEAD_DIM, 1))
        second = jnp.where(low, pltpu.roll(even, HEAD_DIM, 1), odd)
        adam_store(qkv_refs, (slice(None), slice(tile * 256, tile * 256 + 128)), first)
        adam_store(qkv_refs, (slice(None), slice(tile * 256 + 128, tile * 256 + 256)), second)

    @pl.when(pl.program_id(0) == 0)
    def _():
        out_refs = refs[3:6] + refs[9:12]
        for panel in range(4):
            rows = slice((panel % 2) * 64, (panel % 2) * 64 + 64)
            cols = slice(1536 + 256 * (panel // 2), 1792 + 256 * (panel // 2))
            span = slice(panel * 256, panel * 256 + 256)
            even, odd = parities(core, own[rows, cols].astype(F32), other[rows, cols].astype(F32))
            adam_store(out_refs, (slice(0, 64), span), even)
            adam_store(out_refs, (slice(64, 128), span), odd)


def adam_down_body(ids, own, other, *refs):
    core, parity = ids[1], pl.program_id(0)
    grad = jnp.where(core == parity, own[128:256, :], other[128:256, :]).astype(F32)
    adam_store(refs, (slice(None), slice(None)), grad)


def adam_mlp_body(ids, own_a, other_a, own_b, other_b, *refs):
    core, step = ids[1], pl.program_id(0)
    up_refs = refs[0:3] + refs[-6:-3]
    down_refs = refs[3:6] + refs[-3:]
    for owner in range(2):
        cols = pl.ds(pl.multiple_of(step * 256 + owner * 128, 128), 128)
        for part, (own, other) in enumerate(((own_a, other_a), (own_b, other_b))):
            halves = parities(core, own[0:128, cols].astype(F32), other[0:128, cols].astype(F32))
            for parity, grad in enumerate(halves):
                base = owner * 512 + part * 256 + parity * 128
                adam_store(up_refs, (slice(None), slice(base, base + 128)), grad)
    rows = pl.ds(pl.multiple_of(128 + (step % 2) * 64, 64), 64)
    grad = jnp.where(core == step // 2, own_b[rows, :], other_b[rows, :]).astype(F32)
    adam_store(down_refs, (slice(None), slice(None)), grad)


def rotary_tables(segments):
    row_count = segments.shape[0]
    row_index = jnp.arange(row_count, dtype=jnp.int32)
    earlier = jnp.concatenate([jnp.full((1,), -1, jnp.int32), segments[:-1]])
    starts = jnp.where(segments != earlier, row_index, 0)
    position = (row_index - lax.cummax(starts, axis=0)).astype(F32)
    half_dim = ROT_DIM // 2
    dims = jnp.arange(LANES, dtype=jnp.int32) % HEAD_DIM
    frequency = ROPE_BASE ** (-2.0 * (dims % half_dim).astype(F32) / ROT_DIM)
    turned = dims < ROT_DIM
    angles = position[:, None] * jnp.where(turned, frequency, 0.0)[None, :]
    cosine, sine = jnp.cos(angles), jnp.sin(angles)
    front = (dims < half_dim)[None, :]
    return cosine, jnp.where(front, -sine, 0.0), jnp.where(front, 0.0, sine)


def on_device(
    sizes,
    tokens,
    segments,
    cotangent,
    w_qkv,
    w_out,
    w_up,
    w_down,
    vectors,
    m_qkv,
    m_out,
    m_up,
    m_down,
    m_vectors,
    v_qkv,
    v_out,
    v_up,
    v_down,
    v_vectors,
):
    copies, owners = sizes
    me = lax.axis_index("zero")
    plane = lax.axis_index("dp")
    core = plane % 2
    ids = jnp.stack([me, core, (plane // 2) % 2]).astype(jnp.int32)

    def move(value, target):
        pairs = []
        for d in range(copies):
            for z in range(owners):
                to_d, to_z = target(d, z)
                pairs.append((d * owners + z, to_d * owners + to_z))
        return lax.ppermute(value, AXES, pairs)

    def swap(value, dp_bits, zero_bits):
        return move(value, lambda d, z: (d ^ dp_bits, z ^ zero_bits))

    def swap_far(value):
        return move(value, lambda d, z: (d, z ^ (6 if d & 2 else 4)))

    def sync(*values):
        return lax.optimization_barrier(values)

    def add(*terms):
        return functools.reduce(jnp.add, [t.astype(F32) for t in terms])

    def reduce_first(keep, send_x, send_y):
        return keep, swap(send_x, 0, 1), swap(send_y, 2, 0)

    def reduce_first_part(keep, send_x, send_y):
        return keep, [send_x[0], swap(send_x[1], 0, 1)], swap(send_y, 2, 0)

    def reduce_second(state):
        keep, got_x, got_y = state
        far = add(keep[3], got_y[1]).astype(BF16)
        near = add(keep[1], got_x[1]).astype(BF16)
        return keep, got_x, got_y, far, near, swap(far, 0, 1), swap(near, 0, 2)

    def reduce_third(state):
        keep, got_x, got_y, _, _, got_far, got_near = state
        far = add(keep[2], got_y[0], got_far).astype(BF16)
        return (keep, got_x, got_near), far, swap_far(far)

    def reduce_fourth(state):
        (keep, got_x, got_near), _, got = state
        total = add(keep[0], got_x[0], got_near, got).astype(BF16)
        return total, swap(total, 2, 0)

    def reduce_fifth(state):
        total = add(*state).astype(BF16)
        bit = 4
        while bit < copies:
            total = add(total, swap(total, bit, 0)).astype(BF16)
            bit *= 2
        return total, swap(total, 1, 0)

    T, width = tokens.shape
    rows = 2 * T
    sds = jax.ShapeDtypeStruct
    row_block = lambda n, c=width: spec((n, c), lambda i: (i, 0))
    col_block = lambda n: spec((width, n), lambda i: (0, i))

    def block_call(body, grid, ins, outs, flops, moved, scratch=(), name=None):
        return kernel_call(
            body,
            grid,
            [place for _, place in ins],
            [place for _, place in outs],
            [shape for shape, _ in outs],
            flops,
            moved,
            scratch=scratch,
            name=name,
        )(*[value for value, _ in ins])

    def const(value):
        return value, whole(value.shape)

    def kept(shape, dtype):
        return sds(shape, dtype), whole(shape)

    steps = rows // 256
    with jax.named_scope("prep"):
        own_a = block_call(
            prep_attn_body,
            (1,),
            [(ids, scalars())]
            + [(w_qkv, spec((128, 512), lambda i, n=part: (0, 2 * n), single=True)) for part in range(3)]
            + [const(w_out), (vectors, whole((13, 128)))],
            [kept((144, 1280), BF16)],
            0,
            3e6,
            scratch=[pltpu.VMEM((16, 128), F32)],
            name="prep_attn",
        )[0]

    def prep_mlp(part, shape, ins, beside):
        with jax.named_scope("prep"):
            return block_call(
                functools.partial(prep_mlp_body, part),
                (1,),
                [(ids, scalars()), const(ins[0]), (ins[1], spec((256, width), lambda i: (part, 0), single=True))]
                + [const(value) for value in ins[2:]],
                [kept(shape, BF16)],
                0,
                beside * 3e6,
                name="prep_mlp",
            )[0]

    def z_moves(own):
        return swap(own, 0, 2), swap_far(own)

    with jax.named_scope("gather"):
        seg_other = swap(segments, 1, 0)
        tok_other = swap(tokens, 1, 0)
        dy_other = swap(cotangent, 1, 0)
        own_a, w_up_in = sync(own_a, w_up)
        next_a, far_a = z_moves(own_a)
        across_a = swap(own_a, 0, 1)
        own_b = prep_mlp(0, (256, 1024), (w_up_in, w_down), 20)
        tables = [
            jnp.concatenate(pair, axis=0)
            for pair in zip(rotary_tables(segments), rotary_tables(seg_other))
        ]
        seg_row = jnp.stack([segments, seg_other]).astype(F32)[:, None, :]
        seg_ids = jnp.concatenate([segments, seg_other]).astype(F32)
        next_a, far_a, across_a, own_b, w_up_in, tables, seg_row, seg_ids, tok_other, dy_other = sync(
            next_a, far_a, across_a, own_b, w_up_in, tables, seg_row, seg_ids, tok_other, dy_other
        )
        next_across_a, far_across_a, rest_across_a = swap(next_a, 0, 1), swap(far_a, 0, 1), swap(far_a, 2, 1)
        rest_a = swap(far_a, 2, 0)
        far_b = swap_far(own_b)
        seg_col = jnp.broadcast_to(seg_ids[:, None], (rows, LANES))
        w_up_in, seg_col = sync(w_up_in, seg_col)
        own_c = prep_mlp(1, (352, 1024), (w_up_in, w_down, w_qkv), 25)
        next_across_a, far_across_a, rest_a, rest_across_a, far_b, own_b, own_c = sync(
            next_across_a, far_across_a, rest_a, rest_across_a, far_b, own_b, own_c
        )
        far_across_b, across_b, rest_b = swap(far_b, 0, 1), swap(own_b, 0, 1), swap(far_b, 2, 0)
        next_b = swap(own_b, 0, 2)
        far_c = swap_far(own_c)
    attn_pieces = [own_a, next_a, far_a, rest_a, across_a, next_across_a, far_across_a, rest_across_a]

    def table_blocks(count):
        return [(t, row_block(count, 128)) for t in tables]

    def halves(own, other, count):
        last = T // count - 1
        return [
            (own, spec((count, width), lambda i: (jnp.minimum(i, last), 0))),
            (other, spec((count, width), lambda i: (jnp.maximum(i - last - 1, 0), 0))),
        ]

    def attention(group, pairs, projected, d_att, previous):
        with jax.named_scope("attention"):
            first = pairs[0]
            head_block = spec((T, 128), lambda h, m: (h, m + first))
            outs = [
                (sds((rows, 256), BF16), head_block),
                (sds((3, rows, 256), BF16), spec((3, T, 128), lambda h, m: (0, h, m + first))),
            ]
            ins = (
                [(value, head_block) for value in projected]
                + [(d_att, spec((T, 128), lambda h, m: (h, m + first + 2 * group)))]
                + [(seg_col, spec((T, LANES), lambda h, m: (h, 0)))]
                + [(seg_row, spec((1, 1, T), lambda h, m: (h, 0, 0)))]
                + [(t, spec((T, 128), lambda h, m: (h, 0))) for t in tables]
            )
            aliases = {len(ins) + n: n for n in range(len(previous))}
            return pl.pallas_call(
                attn_body,
                grid=(2, len(pairs)),
                in_specs=[place for _, place in ins] + [distant()] * len(previous),
                out_specs=[place for _, place in outs],
                out_shape=[shape for shape, _ in outs],
                input_output_aliases=aliases,
                cost_estimate=pl.CostEstimate(
                    flops=len(pairs) * 15000000000, bytes_accessed=len(pairs) * 5000000, transcendentals=0
                ),
                compiler_params=pltpu.CompilerParams(
                    vmem_limit_bytes=VMEM_NEED * MIB, dimension_semantics=("arbitrary",) * 2
                ),
                name="attention",
            )(*[value for value, _ in ins], *previous)

    def blocks_of(shape):
        return [kept((n,) + shape, BF16) for n in (4, 2, 2)]

    with jax.named_scope("qkv"):
        *projected, d_att, attn_in, attn_t, mlp_in, wq_a, full_out, vec, bias_qkv = block_call(
            functools.partial(qkv_first_body, rows // 512),
            (rows // 512,),
            [(ids, scalars())]
            + [const(piece) for piece in attn_pieces]
            + halves(tokens, tok_other, 512)
            + halves(cotangent, dy_other, 512)
            + table_blocks(512),
            [(sds((rows, 256), BF16), row_block(512, 256))] * 3
            + [(sds((rows, 512), BF16), row_block(512, 512)), (sds((rows, width), BF16), row_block(512))]
            + [(sds((width, rows), BF16), col_block(512)), (sds((rows, width), BF16), row_block(512))]
            + [kept((1024, 768), BF16), kept((512, 1024), BF16), kept((16, 1024), F32), kept((1, 1536), F32)],
            2 * rows * 1024 * 1280,
            30e6,
            name="qkv",
        )
    projected, far_across_b, across_b, rest_b, own_b = sync(
        projected, far_across_b, across_b, rest_b, own_b
    )
    with jax.named_scope("gather"):
        rest_across_b, next_across_b = swap(far_across_b, 2, 0), swap(own_b, 0, 3)
    half_a = attention(0, (0,), projected, d_att, [])
    half_a, projected, far_c, own_c, next_b = sync(half_a, projected, far_c, own_c, next_b)
    with jax.named_scope("gather"):
        far_across_c, rest_c, next_c = swap(far_c, 0, 1), swap(far_c, 2, 0), swap(own_c, 0, 2)
    att_a, grad_a = attention(0, (1,), projected, d_att, half_a)
    att_a, grad_a, rest_across_b, next_across_b, far_across_c, rest_c, own_c, next_c, attn_t, mlp_in = sync(
        att_a, grad_a, rest_across_b, next_across_b, far_across_c, rest_c, own_c, next_c, attn_t, mlp_in
    )
    with jax.named_scope("gather"):
        across_c, next_across_c, rest_across_c = swap(own_c, 0, 1), swap(next_c, 0, 1), swap(far_across_c, 2, 0)
    pieces_b = [own_b, next_b, far_b, rest_b, across_b, next_across_b, far_across_b, rest_across_b]

    def mlp(part, weights, rows_in):
        with jax.named_scope("mlp"):
            *results, hid, gp, sums, w_up_full, w_down_full = block_call(
                functools.partial(mlp_body, part, steps),
                (steps,),
                [(ids, scalars())]
                + [const(w) for w in weights]
                + [const(vec), (rows_in, row_block(256))]
                + halves(cotangent, dy_other, 256),
                [(sds((n, 256, 1024), BF16), distant()) for n in (4, 2, 2)]
                + [(sds((rows, width), BF16), row_block(256))] * 2
                + [kept((8, 1024), F32)]
                + [(sds((1024, 1024), BF16), distant())] * 2,
                2 * rows * 1024 * 1024 * 4,
                40e6,
                scratch=[
                    pltpu.VMEM((1024, rows), BF16),
                    pltpu.VMEM((1024, rows), BF16),
                    pltpu.VMEM((rows, 1024), BF16),
                    pltpu.VMEM((rows, 1024), BF16),
                    pltpu.VMEM((8, 1024), F32),
                    pltpu.VMEM((1024, 512), BF16),
                ]
                + [pltpu.VMEM((n, 256, 1024), BF16) for n in (4, 2, 2)]
                + [pltpu.VMEM((1024, 1024), BF16)] * 2
                + [pltpu.SemaphoreType.DMA((8,))],
                name="mlp",
            )
            return results, hid, gp, sums, w_up_full, w_down_full

    mlp_a = mlp(0, pieces_b, mlp_in)
    mlp_a, mlp_in, across_c, next_across_c, rest_across_c = sync(
        mlp_a, mlp_in, across_c, next_across_c, rest_across_c
    )
    pieces_c = [own_c, next_c, far_c, rest_c, across_c, next_across_c, far_across_c, rest_across_c]
    reduce_a = reduce_first(*mlp_a[0])
    mlp_b = mlp(1, pieces_c, mlp_in)
    mlp_b, reduce_a, attn_in = sync(mlp_b, reduce_a, attn_in)
    reduce_a = reduce_second(reduce_a)
    reduce_b = reduce_first_part(*mlp_b[0])
    attn_in, *ready = sync(attn_in, *reduce_a[3:5])

    with jax.named_scope("attention"):
        head_block = spec((T, 128), lambda h, m: (h, m))
        att_b, grad_b, wq_b = block_call(
            project_attn_body,
            (2, 2),
            [(ids, scalars())]
            + [(piece, whole((96, width))) for piece in pieces_c]
            + [(attn_in, spec((T, width), lambda h, m: (h, 0))), const(bias_qkv)]
            + [(d_att, spec((T, 128), lambda h, m: (h, m + 2)))]
            + [(seg_col, spec((T, LANES), lambda h, m: (h, 0)))]
            + [(seg_row, spec((1, 1, T), lambda h, m: (h, 0, 0)))]
            + [(t, spec((T, 128), lambda h, m: (h, 0))) for t in tables],
            [
                (sds((rows, 256), BF16), head_block),
                (sds((3, rows, 256), BF16), spec((3, T, 128), lambda h, m: (0, h, m))),
                kept((1024, 768), BF16),
            ],
            38e9,
            20e6,
            scratch=[pltpu.VMEM((T, 256), BF16)] * 3,
            name="attention",
        )
    att_b, grad_b, reduce_a, reduce_b = sync(att_b, grad_b, reduce_a, reduce_b)
    reduce_a = reduce_third(reduce_a)
    reduce_b[1][0] = swap(reduce_b[1][0], 0, 1)
    reduce_b = reduce_second(reduce_b)
    grad_b, *ready = sync(grad_b, reduce_a[1], *reduce_b[3:5])
    with jax.named_scope("attn_weights"):
        *blocks, bias_sum = block_call(
            attn_weights_body,
            (7,),
            [(ids, scalars()), const(attn_t)]
            + [(grad_a, spec((1, rows, 256), lambda n: (jnp.minimum(n, 2), 0, 0)))]
            + [(grad_b, spec((1, rows, 256), lambda n: (jnp.clip(n - 3, 0, 2), 0, 0)))]
            + [(value, distant()) for value in (att_a, att_b, cotangent, dy_other)],
            blocks_of((128, 2048)) + [kept((8, 1536), F32)],
            2 * rows * 1024 * 2048,
            24e6,
            scratch=[pltpu.VMEM((1024, 256), BF16)]
            + [pltpu.VMEM((rows, 256), BF16)] * 2
            + [pltpu.VMEM((T, width), BF16)] * 2
            + [pltpu.SemaphoreType.DMA((4,))],
            name="attn_weights",
        )
    blocks, grad_b, reduce_a, reduce_b = sync(blocks, grad_b, reduce_a, reduce_b)
    reduce_o = reduce_first(*blocks)

    _, hid_a, gp_a, sums_a, up_a, down_a = mlp_a
    _, hid_b, gp_b, sums_b, up_b, down_b = mlp_b

    def adam_down(totals):
        wide = [spec((128, width), lambda n: (n, 0))] * 3
        return kernel_call(
            adam_down_body,
            (2,),
            [scalars()] + [whole((256, 1024))] * 2 + wide,
            wide,
            [sds((512, 1024), F32)] * 3,
            0,
            7e6,
            name="adam_down",
        )(ids, *totals, w_down, m_down, v_down)

    def adam_mlp(totals_a, totals_b, previous):
        wide = [spec((128, 1024), lambda n: (0, n))] * 3 + [spec((64, width), lambda n: (4 + n, 0))] * 3
        return pl.pallas_call(
            adam_mlp_body,
            grid=(4,),
            in_specs=[scalars()] + [whole((256, 1024))] * 4 + wide + [distant()] * 3,
            out_specs=wide,
            out_shape=[sds((128, 4096), F32)] * 3 + [sds((512, 1024), F32)] * 3,
            input_output_aliases={11 + n: 3 + n for n in range(3)},
            cost_estimate=pl.CostEstimate(flops=0, bytes_accessed=21000000, transcendentals=0),
            compiler_params=pltpu.CompilerParams(
                vmem_limit_bytes=VMEM_NEED * MIB, dimension_semantics=("arbitrary",)
            ),
            name="adam_mlp",
        )(ids, *totals_a, *totals_b, w_up, m_up, v_up, w_down, m_down, v_down, *previous)

    def back(own, grad, rows_tok, extra, outs):
        first = 0 if own else T // 256
        block = lambda c=width: spec((256, c), lambda i: (i + first, 0))
        lead = spec((3, 256, 256), lambda i: (0, i + first, 0))
        with jax.named_scope("back"):
            return block_call(
                functools.partial(back_body, own),
                (T // 256,),
                [(grad_a, lead), (grad, lead), (att_a, block(256)), (att_b, block(256))]
                + [(value, block()) for value in (hid_a, hid_b, gp_a, gp_b)]
                + [const(w) for w in (full_out, down_a, down_b, up_a, up_b, wq_a, wq_b)]
                + [(rows_tok, row_block(256)), const(vec)]
                + extra,
                outs + [kept((8, width), F32)],
                2 * T * 1024 * 6144,
                40e6,
                name="back",
            )

    reduce_a = reduce_fourth(reduce_a)
    reduce_b = reduce_third(reduce_b)
    pair_block = spec((2, 256, width), lambda i: (0, i, 0))
    part_other, sums_other = back(False, grad_b, tok_other, [], [(sds((2, T, width), BF16), pair_block)])
    part_other, sums_other, grad_b, reduce_a, reduce_b, reduce_o = sync(
        part_other, sums_other, grad_b, reduce_a, reduce_b, reduce_o
    )
    reduce_o = reduce_second(reduce_o)
    part_other, reduce_a, reduce_b, *ready = sync(part_other, reduce_a, reduce_b, *reduce_o[3:5])
    reduce_a = reduce_fifth(reduce_a)
    reduce_b = reduce_fourth(reduce_b)
    part_got = swap(part_other, 1, 0)
    updated_mlp = adam_down(reduce_a)
    updated_mlp, grad_b, reduce_b, reduce_o, part_got = sync(
        updated_mlp, grad_b, reduce_b, reduce_o, part_got
    )
    reduce_o = reduce_third(reduce_o)
    reduce_b = reduce_fifth(reduce_b)
    grad_b, *ready = sync(grad_b, reduce_o[1], reduce_b[0])
    layer_out, tokens_grad, sums_own = back(
        True,
        grad_b,
        tokens,
        [(cotangent, row_block(256)), (part_got, pair_block)],
        [(sds((T, width), BF16), row_block(256)), (sds((T, width), F32), row_block(256))],
    )
    sums_own, updated_mlp, reduce_b, reduce_o = sync(sums_own, updated_mlp, reduce_b, reduce_o)
    reduce_o = reduce_fourth(reduce_o)

    with jax.named_scope("vectors"):
        is_core = jnp.arange(2) == core
        grad_bias = jnp.where(core == 0, sums_a[1:2], 0.0)
        bias_sum = jnp.swapaxes(bias_sum[0].reshape(2, 3, 256), 0, 1)
        grad_bias_qkv = jnp.where(
            is_core[None, None, :, None], bias_sum.reshape(3, 8, 1, 64), 0.0
        ).reshape(3, width)
        grad_bias_up = jnp.where(
            is_core[None, None, :, None],
            jnp.swapaxes(jnp.stack([sums_a[0], sums_b[0]]).reshape(2, 8, 128), 0, 1)[:, :, None],
            0.0,
        ).reshape(4, width)
        total = jnp.concatenate(
            [
                sums_own[0:4] + sums_other[0:4],
                grad_bias_qkv,
                grad_bias,
                grad_bias_up,
                grad_bias,
                jnp.zeros((3, width), F32),
            ],
            axis=0,
        )
        moved = [swap(total, 0, step) for step in (2, 4, 6)]
        updated_mlp = adam_mlp(reduce_a, reduce_b, updated_mlp)
        updated_mlp, reduce_o, total, moved = sync(updated_mlp, reduce_o, total, moved)
        reduce_o = reduce_fifth(reduce_o)
        total = functools.reduce(jnp.add, moved, total)
        others = swap(total, 0, 1), swap(total, 2, 0), swap(total, 2, 1)

    with jax.named_scope("adam"):
        wide = [spec((128, 1536), lambda n: (0, n))] * 3 + [whole((128, 1024))] * 3
        updated_attn = kernel_call(
            adam_attn_body,
            (2,),
            [scalars()] + [whole((128, 2048))] * 2 + wide,
            wide,
            [sds((128, 3072), F32)] * 3 + [sds((128, 1024), F32)] * 3,
            0,
            13e6,
            name="adam",
        )(ids, *reduce_o, w_qkv, m_qkv, v_qkv, w_out, m_out, v_out)

    with jax.named_scope("vectors"):
        updated_attn, total, (across, beside, both) = sync(updated_attn, total, others)
        total = (total + across) + (beside + both)
        bit = 4
        while bit < copies:
            total = total + swap(total, bit, 0)
            bit *= 2
        total = total + swap(total, 1, 0)
        share = lax.dynamic_slice_in_dim(total[0:13], me * 128, 128, 1)
        first_vectors, second_vectors, new_vectors = adam_math(
            vectors, m_vectors, v_vectors, share, RATE_VECTOR, 0.0
        )
    first_qkv, second_qkv, new_qkv, first_out, second_out, new_out = updated_attn
    first_up, second_up, new_up, first_down, second_down, new_down = updated_mlp
    return (
        layer_out,
        tokens_grad,
        first_qkv,
        first_out,
        first_up,
        first_down,
        first_vectors,
        second_qkv,
        second_out,
        second_up,
        second_down,
        second_vectors,
        new_qkv,
        new_out,
        new_up,
        new_down,
        new_vectors,
    )


def solution(mesh):
    rows, owned, spread = P(AXES, None), P("zero", None), P(None, "zero")
    state = (owned, owned, owned, owned, spread)
    return jax.shard_map(
        functools.partial(on_device, (mesh.shape["dp"], mesh.shape["zero"])),
        mesh=mesh,
        in_specs=(rows, P(AXES), rows) + state * 3,
        out_specs=(rows, rows) + state * 3,
        check_vma=False,
    )
```

```python
import functools

import jax
import jax.numpy as jnp
from jax import lax
from jax.experimental import pallas as pl
from jax.experimental.pallas import tpu as pltpu
from jax.sharding import PartitionSpec as P

HEAD_DIM = 64
ROT_DIM = 16
STEP = 10
EPS_NORM = 1e-05
BETA_ONE = 0.9
BETA_TWO = 0.999
ADAM_EPS = 1e-08
RATE_MATRIX = 0.05
RATE_VECTOR = 0.2
DECAY_MATRIX = 0.1
ROPE_BASE = 10000.0
INV_ROOT_TWO = 0.7071067811865476
INV_ROOT_TAU = 0.3989422804014327
MASKED = -1e30
LANES = 128
AXES = ("dp", "zero")
F32 = jnp.float32
BF16 = jnp.bfloat16
MIB = 1024 * 1024
VMEM_NEED = 51


def spec(block, index, single=False):
    if single:
        return pl.BlockSpec(block, index, pipeline_mode=pl.Buffered(1))
    return pl.BlockSpec(block, index)


def whole(shape):
    return spec(shape, lambda *_: (0,) * len(shape), single=True)


def distant():
    return pl.BlockSpec(memory_space=pl.ANY)


def scalars():
    return pl.BlockSpec(memory_space=pltpu.SMEM)


def kernel_call(body, grid, in_specs, out_specs, out_shape, flops, moved, scratch=(), name=None):
    return pl.pallas_call(
        body,
        grid=grid,
        in_specs=in_specs,
        out_specs=out_specs,
        out_shape=out_shape,
        scratch_shapes=list(scratch),
        cost_estimate=pl.CostEstimate(flops=int(flops), bytes_accessed=int(moved), transcendentals=0),
        compiler_params=pltpu.CompilerParams(
            vmem_limit_bytes=VMEM_NEED * MIB, dimension_semantics=("arbitrary",) * len(grid)
        ),
        name=name,
    )


def nn(left, right):
    return lax.dot_general(left, right, (((1,), (0,)), ((), ())), preferred_element_type=F32)


def nt(left, right):
    return lax.dot_general(left, right, (((1,), (1,)), ((), ())), preferred_element_type=F32)


def tn(left, right):
    return lax.dot_general(left, right, (((0,), (0,)), ((), ())), preferred_element_type=F32)


def piece_owner(ids, place):
    step = place % 4
    if step > 1:
        step = 2 + ids[2] if step == 2 else 3 - ids[2]
    return jnp.bitwise_xor(ids[0], 2 * step + place // 4)


SLOTS = ((0, 0), (1, 0), (2, 0), (2, 1), (0, 1), (1, 1), (3, 0), (3, 1))


def slot_owner(ids, slot):
    step, side = SLOTS[slot]
    if step > 1:
        step = 2 + ids[2] if step == 2 else 3 - ids[2]
    return jnp.bitwise_xor(ids[0], 2 * step + side)


def slot_ref(outs, slot):
    return (outs[0], slot) if slot < 4 else (outs[1], slot - 4) if slot < 6 else (outs[2], slot - 6)


def low_lanes():
    return lax.broadcasted_iota(jnp.int32, (1, LANES), 1) < HEAD_DIM


def pick_parity(core, tile_a, tile_b):
    low = low_lanes()
    even = jnp.where(low, tile_a, pltpu.roll(tile_b, HEAD_DIM, 1))
    odd = jnp.where(low, pltpu.roll(tile_a, HEAD_DIM, 1), tile_b)
    return jnp.where(core == 0, even, odd)


def prep_attn_body(ids, w_q, w_k, w_v, w_out, vec, out, padded):
    core = ids[1]
    for part, w in enumerate((w_q, w_k, w_v)):
        for tile in range(2):
            base = tile * 256
            at = part * 256 + tile * 128
            out[0:128, at : at + 128] = pick_parity(
                core, w[:, base : base + 128], w[:, base + 128 : base + 256]
            ).astype(BF16)
    rows = w_out[pl.ds(pl.multiple_of(core * 64, 64), 64), :].astype(BF16)
    for panel in range(4):
        at = 768 + 256 * (panel // 2)
        base = (panel % 2) * 64
        out[base : base + 64, at : at + 256] = rows[:, 256 * panel : 256 * panel + 256]
    padded[...] = jnp.zeros_like(padded)
    padded[0:13, :] = vec[...]
    out[128:144, 0:128] = padded[...].astype(BF16)
    out[128:144, 128:1280] = jnp.zeros((16, 1152), BF16)


def prep_mlp_body(part, ids, w_up, w_down, *refs):
    out = refs[-1]
    core = ids[1]
    top = 96 * part
    for owner in range(8):
        start = pl.multiple_of(owner * 512 + part * 256 + core * 128, 128)
        out[top : top + 128, owner * 128 : (owner + 1) * 128] = w_up[:, pl.ds(start, 128)].astype(BF16)
    out[top + 128 : top + 256, :] = w_down[pl.ds(pl.multiple_of(core * 128, 128), 128), :].astype(BF16)
    if not part:
        return
    w_qkv = refs[0]
    for third in range(3):
        for tile in range(2):
            base = third * 1024 + 512 + tile * 256
            value = pick_parity(core, w_qkv[:, base : base + 128], w_qkv[:, base + 128 : base + 256]).astype(BF16)
            for panel in range(4):
                at = panel * 256 + tile * 128
                out[32 * third : 32 * third + 32, at : at + 128] = value[32 * panel : 32 * panel + 32]


def normalize(inputs):
    centred = inputs - jnp.mean(inputs, axis=-1, keepdims=True)
    variance = jnp.mean(centred * centred, axis=-1, keepdims=True)
    inv_std = lax.rsqrt(variance + EPS_NORM)
    return centred * inv_std, inv_std


def turned(x, cos, sin_lo, sin_hi, sign):
    return x * cos[...] + sign * (pltpu.roll(x, 8, 1) * sin_hi[...] + pltpu.roll(x, 120, 1) * sin_lo[...])


def project(group, rows, w_qkv, bias, tables, outs):
    for part, out in enumerate(outs):
        cols = slice(part * 256, (part + 1) * 256)
        at = group * 768 + part * 256
        acc = nn(rows, w_qkv[:, cols]) + bias[:, at : at + 256]
        if part == 2:
            out[...] = acc.astype(BF16)
            continue
        for tile in range(2):
            x = turned(acc[:, tile * 128 : (tile + 1) * 128], *tables, 1.0)
            if part == 0:
                x = x * HEAD_DIM ** (-0.5)
            out[:, tile * 128 : (tile + 1) * 128] = x.astype(BF16)


def qkv_first_body(steps, ids, *refs):
    pieces, refs = refs[:8], refs[8:]
    tok_own, tok_other, dy_own, dy_other, cos, sin_lo, sin_hi = refs[:7]
    q, k, v, d_att, attn_in, attn_t, mlp_in, w_qkv, w_out, vec, bias = refs[7:]
    step = pl.program_id(0)

    @pl.when(step == 0)
    def _():
        for place, piece in enumerate(pieces):
            owner = piece_owner(ids, place)
            at_owner = pl.ds(pl.multiple_of(owner * 128, 128), 128)
            w_qkv[at_owner, :] = piece[0:128, 0:768]
            vec[:, at_owner] = piece[128:144, 0:128].astype(F32)
            for panel in range(4):
                at = 768 + 256 * (panel // 2)
                base = (panel % 2) * 64
                w_out[pl.ds(pl.multiple_of(owner * 64, 64), 64), 256 * panel : 256 * panel + 256] = piece[
                    base : base + 64, at : at + 256
                ]
        for part in range(3):
            for tile in range(4):
                base = tile * 256
                row = slice(4 + part, 5 + part)
                at = (tile // 2) * 768 + part * 256 + (tile % 2) * 128
                bias[:, at : at + 128] = pick_parity(
                    ids[1], vec[row, base : base + 128], vec[row, base + 128 : base + 256]
                )

    first = step < steps // 2
    d_att[...] = nt(jnp.where(first, dy_own[...], dy_other[...]), w_out[...]).astype(BF16)
    normed, _ = normalize(jnp.where(first, tok_own[...], tok_other[...]).astype(F32))
    rows = (normed * vec[0:1, :] + vec[1:2, :]).astype(BF16)
    mlp_in[...] = (normed * vec[2:3, :] + vec[3:4, :]).astype(BF16)
    attn_in[...] = rows
    attn_t[...] = rows.T
    project(0, rows, w_qkv, bias, (cos, sin_lo, sin_hi), (q, k, v))


ATTN_ROWS = 256


def cat(parts, axis=0):
    return jnp.concatenate(parts, axis=axis) if len(parts) > 1 else parts[0]


def attn_body(q, k, v, d_att, seg_col, seg_row, cos, sin_lo, sin_hi, *refs):
    att, grad = refs[-2:]
    count = q.shape[0]
    size = ATTN_ROWS
    blocks = count // size
    span = [slice(j * size, (j + 1) * size) for j in range(blocks)]
    low = low_lanes()
    zero = jnp.zeros((), BF16)
    causal = lax.broadcasted_iota(jnp.int32, (size, size), 0) >= lax.broadcasted_iota(
        jnp.int32, (size, size), 1
    )
    q_t, da_t = q[...].T, d_att[...].T

    def row_total(parts, reduce, join):
        cols = [reduce(part, axis=-1, keepdims=True) for part in parts]
        return [
            functools.reduce(join, [cols[j][(i - j) * size : (i - j + 1) * size] for j in range(i + 1)])
            for i in range(blocks)
        ]

    def row_sum(parts):
        return cat(
            [
                functools.reduce(jnp.add, [parts[j][(i - j) * size : (i - j + 1) * size] for j in range(i + 1)])
                for i in range(blocks)
            ]
        )

    def products(half):
        lanes = low if half == 0 else jnp.logical_not(low)
        q_h = jnp.where(lanes, q[...], zero)
        da_h = jnp.where(lanes, d_att[...], zero)
        scores = [nt(q_h[j * size :], k[span[j], :]) for j in range(blocks)]
        return scores, [nt(da_h[j * size :], v[span[j], :]) for j in range(blocks)]

    def softmax_both(scores, grad_probs):
        masked = []
        for j in range(blocks):
            allowed = seg_col[j * size :, 0:1] == seg_row[0, :, span[j]]
            allowed = cat([allowed[:size] & causal] + ([allowed[size:]] if j < blocks - 1 else []))
            masked.append(jnp.where(allowed, scores[j], MASKED))
        top = row_total(masked, jnp.max, jnp.maximum)
        raised = [jnp.exp(masked[j] - cat(top[j:])) for j in range(blocks)]
        inv = [1.0 / total for total in row_total(raised, jnp.sum, jnp.add)]
        probs = [raised[j] * cat(inv[j:]) for j in range(blocks)]
        delta = row_total([g * p for g, p in zip(grad_probs, probs)], jnp.sum, jnp.add)
        grad_scores = [
            (probs[j] * (grad_probs[j] - cat(delta[j:]))).astype(BF16) for j in range(blocks)
        ]
        return [p.astype(BF16) for p in probs], grad_scores

    def results(half, probs, grad_scores):
        rows = slice(half * HEAD_DIM, (half + 1) * HEAD_DIM)
        return (
            row_sum([nn(probs[j], v[span[j], :]) for j in range(blocks)]),
            row_sum([nn(grad_scores[j], k[span[j], :]) for j in range(blocks)]),
            cat([nn(q_t[rows, j * size :], grad_scores[j]) for j in range(blocks)], 1),
            cat([nn(da_t[rows, j * size :], probs[j]) for j in range(blocks)], 1),
        )

    first = softmax_both(*products(0))
    second = products(1)
    out_a, dq_a, dk_a, dv_a = results(0, *first)
    out_b, dq_b, dk_b, dv_b = results(1, *softmax_both(*second))
    tables = (cos, sin_lo, sin_hi)
    att[...] = jnp.where(low, out_a, out_b).astype(BF16)
    grad[0] = turned(jnp.where(low, dq_a, dq_b) * HEAD_DIM ** (-0.5), *tables, -1.0).astype(BF16)
    grad[1] = turned(jnp.concatenate([dk_a, dk_b], axis=0).T, *tables, -1.0).astype(BF16)
    grad[2] = jnp.concatenate([dv_a, dv_b], axis=0).T.astype(BF16)


def project_attn_body(ids, *refs):
    pieces, (attn_in, bias, d_att, seg_col, seg_row, *tables) = refs[:8], refs[8:16]
    att, grad, w_qkv, *projected = refs[16:]
    half, pair = pl.program_id(0), pl.program_id(1)

    @pl.when((half == 0) & (pair == 0))
    def _():
        for place, piece in enumerate(pieces):
            owner = piece_owner(ids, place)
            for part in range(3):
                for panel in range(4):
                    at = pl.ds(pl.multiple_of(owner * 128 + 32 * panel, 32), 32)
                    w_qkv[at, part * 256 : part * 256 + 256] = piece[
                        32 * part : 32 * part + 32, panel * 256 : panel * 256 + 256
                    ]

    @pl.when(pair == 0)
    def _():
        project(1, attn_in[...], w_qkv, bias, tables, projected)

    lanes = pl.ds(pl.multiple_of(pair * LANES, LANES), LANES)
    attn_body(*[value.at[:, lanes] for value in projected], d_att, seg_col, seg_row, *tables, att, grad)


def attn_weights_body(ids, attn_t, grad_a, grad_b, far_att_a, far_att_b, far_own, far_other, *refs):
    keep, send_x, send_y, bias, result, att_a, att_b, dy_own, dy_other, sems = refs
    copies = [
        pltpu.make_async_copy(source, target, sems.at[n])
        for n, (source, target) in enumerate(
            ((far_att_a, att_a), (far_att_b, att_b), (far_own, dy_own), (far_other, dy_other))
        )
    ]

    @pl.when(pl.program_id(0) == 0)
    def _():
        for copy in copies:
            copy.start()

    step = pl.program_id(0)
    outs = (keep, send_x, send_y)

    @pl.when(step < 6)
    def _():
        rhs = jnp.where(step < 3, grad_a[0], grad_b[0])
        result[...] = nn(attn_t[...], rhs).astype(BF16)
        cols = pl.ds(pl.multiple_of(step * 256, 256), 256)
        bias[0:1, cols] = jnp.sum(rhs.astype(F32), axis=0, keepdims=True)
        for slot in range(8):
            out, at = slot_ref(outs, slot)
            base = pl.multiple_of(slot_owner(ids, slot) * 128, 128)
            out[at, :, cols] = result[pl.ds(base, 128), :]

    @pl.when(step == 6)
    def _():
        for copy in copies:
            copy.wait()
        count = dy_own.shape[0]
        for group, att in enumerate((att_a, att_b)):
            flipped = att[...].T
            for panel in range(4):
                cols = slice(panel * 256, panel * 256 + 256)
                term = nn(flipped[:, :count], dy_own[:, cols]) + nn(flipped[:, count:], dy_other[:, cols])
                result[group * 256 : group * 256 + 256, :] = term.astype(BF16)
                for slot in range(8):
                    out, at = slot_ref(outs, slot)
                    owner = slot_owner(ids, slot)
                    col = 1536 + 256 * (panel // 2)
                    base = (panel % 2) * 64

                    @pl.when(owner // 4 == group)
                    def _():
                        out[at, base : base + 64, col : col + 256] = result[
                            pl.ds(pl.multiple_of(owner * 64, 64), 64), :
                        ]


def mlp_body(part, steps, ids, *refs):
    pieces, (vec, mlp_in, dy_own, dy_other) = refs[:8], refs[8:12]
    far_outs, (hidden_out, grad_out, sums, far_up, far_down) = refs[12:15], refs[15:20]
    mlp_t, hidden_t, grad_pre, dy, bias, result, keep, send_x, send_y, w_up, w_down, sems = refs[20:]
    outs = (keep, send_x, send_y)
    weight_copies = [
        pltpu.make_async_copy(w_up, far_up, sems.at[0]),
        pltpu.make_async_copy(w_down, far_down, sems.at[1]),
    ]
    core = ids[1]
    step = pl.program_id(0)

    @pl.when(step == 0)
    def _():
        for owner in range(8):
            start = pl.multiple_of((owner % 2) * 512 + part * 256 + core * 128, 128)
            row = 8 + owner // 2
            bias[0:1, owner * 128 : (owner + 1) * 128] = vec[row : row + 1, pl.ds(start, 128)]
        sums[...] = jnp.zeros_like(sums)
        for place, piece in enumerate(pieces):
            at = pl.ds(pl.multiple_of(piece_owner(ids, place) * 128, 128), 128)
            top = 96 * part
            w_up[at, :] = piece[top : top + 128, :]
            w_down[at, :] = piece[top + 128 : top + 256, :]
        for copy in weight_copies:
            copy.start()

    rows = mlp_in[...]
    grads = jnp.where(step < steps // 2, dy_own[...], dy_other[...])
    count = rows.shape[0]
    at = pl.ds(pl.multiple_of(step * count, count), count)
    mlp_t[:, at] = rows.T
    dy[at, :] = grads
    sums[1:2, :] += jnp.sum(grads.astype(F32), axis=0, keepdims=True)
    for col in range(0, 1024, 512):
        cols = slice(col, col + 512)
        pre = nn(rows, w_up[:, cols]) + bias[0:1, cols]
        grad_hidden = nt(grads, w_down[cols, :])
        cdf = 0.5 + 0.5 * lax.erf(pre * INV_ROOT_TWO)
        pdf = jnp.exp(-0.5 * pre * pre) * INV_ROOT_TAU
        act = (pre * cdf).astype(BF16)
        hidden_t[cols, at] = act.T
        hidden_out[:, cols] = act
        gp = (grad_hidden * (cdf + pre * pdf)).astype(BF16)
        grad_pre[at, cols] = gp
        grad_out[:, cols] = gp
        sums[0:1, cols] += jnp.sum(gp.astype(F32), axis=0, keepdims=True)

    @pl.when(step == steps - 1)
    def _():
        copies = list(weight_copies)
        for base_row, left, right in ((0, mlp_t, grad_pre), (128, hidden_t, dy)):
            for col in range(0, 1024, 512):
                cols = slice(col, col + 512)
                result[...] = nn(left[...], right[:, cols]).astype(BF16)
                for slot in range(8):
                    out, place = slot_ref(outs, slot)
                    base = pl.multiple_of(slot_owner(ids, slot) * 128, 128)
                    out[place, base_row : base_row + 128, cols] = result[pl.ds(base, 128), :]
            span = pl.ds(base_row, 128)
            for out, far_out in zip(outs, far_outs):
                copy = pltpu.make_async_copy(out.at[:, span, :], far_out.at[:, span, :], sems.at[len(copies)])
                copy.start()
                copies.append(copy)
        for copy in copies:
            copy.wait()


def back_body(own, grad_a, grad_b, att_a, att_b, hid_a, hid_b, gp_a, gp_b, *refs):
    w_out, down_a, down_b, up_a, up_b, wq_a, wq_b, tok, vec = refs[:9]
    if own:
        dy, other, out, result, sums = refs[9:]
    else:
        out, sums = refs[9:]
    inputs = tok[...].astype(F32)
    normed, inv_std = normalize(inputs)
    branch = nn(att_a[...], w_out[0:256, :]) + nn(att_b[...], w_out[256:512, :])
    branch = branch + nn(hid_a[...], down_a[...]) + nn(hid_b[...], down_b[...])
    back_mlp = nt(gp_a[...], up_a[...]) + nt(gp_b[...], up_b[...])
    back_attn = None
    for grad, w in ((grad_a, wq_a), (grad_b, wq_b)):
        for part in range(3):
            term = nt(grad[part], w[:, part * 256 : part * 256 + 256])
            back_attn = term if back_attn is None else back_attn + term
    scaled = back_attn * vec[0:1, :] + back_mlp * vec[2:3, :]

    @pl.when(pl.program_id(0) == 0)
    def _():
        sums[...] = jnp.zeros_like(sums)

    for row, value in enumerate((back_attn * normed, back_attn, back_mlp * normed, back_mlp)):
        sums[row : row + 1, :] += jnp.sum(value, axis=0, keepdims=True)
    if not own:
        out[0] = branch.astype(BF16)
        out[1] = scaled.astype(BF16)
        return
    branch = branch + other[0].astype(F32)
    out[...] = (inputs + branch + (vec[7:8, :] + vec[12:13, :])).astype(BF16)
    scaled = scaled + other[1].astype(F32)
    result[...] = dy[...].astype(F32) + inv_std * (
        scaled
        - jnp.mean(scaled, axis=-1, keepdims=True)
        - normed * jnp.mean(scaled * normed, axis=-1, keepdims=True)
    )


def adam_math(weight, first, second, gradient, rate, decay):
    first_new = BETA_ONE * first + (1.0 - BETA_ONE) * gradient
    second_new = BETA_TWO * second + (1.0 - BETA_TWO) * gradient * gradient
    first_hat = first_new / (1.0 - BETA_ONE**STEP)
    second_hat = second_new / (1.0 - BETA_TWO**STEP)
    weight_new = weight - rate * (first_hat / (jnp.sqrt(second_hat) + ADAM_EPS) + decay * weight)
    return (first_new, second_new, weight_new)


def adam_store(refs, at, gradient):
    w, m, v, m_out, v_out, w_out = refs
    first, second, weight = adam_math(w[at], m[at], v[at], gradient, RATE_MATRIX, DECAY_MATRIX)
    m_out[at] = first
    v_out[at] = second
    w_out[at] = weight


def parities(core, own, other):
    return jnp.where(core == 0, own, other), jnp.where(core == 0, other, own)


def adam_attn_body(ids, own, other, *refs):
    core = ids[1]
    low = low_lanes()
    qkv_refs = refs[0:3] + refs[6:9]
    for tile in range(6):
        count = pl.program_id(0) * 6 + tile
        part, place = count // 4, count % 4
        start = (place // 2) * 768 + part * 256 + (place % 2) * 128
        cols = pl.ds(pl.multiple_of(start, 128), 128)
        even, odd = parities(core, own[:, cols].astype(F32), other[:, cols].astype(F32))
        first = jnp.where(low, even, pltpu.roll(odd, HEAD_DIM, 1))
        second = jnp.where(low, pltpu.roll(even, HEAD_DIM, 1), odd)
        adam_store(qkv_refs, (slice(None), slice(tile * 256, tile * 256 + 128)), first)
        adam_store(qkv_refs, (slice(None), slice(tile * 256 + 128, tile * 256 + 256)), second)

    @pl.when(pl.program_id(0) == 0)
    def _():
        out_refs = refs[3:6] + refs[9:12]
        for panel in range(4):
            rows = slice((panel % 2) * 64, (panel % 2) * 64 + 64)
            cols = slice(1536 + 256 * (panel // 2), 1792 + 256 * (panel // 2))
            span = slice(panel * 256, panel * 256 + 256)
            even, odd = parities(core, own[rows, cols].astype(F32), other[rows, cols].astype(F32))
            adam_store(out_refs, (slice(0, 64), span), even)
            adam_store(out_refs, (slice(64, 128), span), odd)


def adam_down_body(ids, own, other, *refs):
    core, parity = ids[1], pl.program_id(0)
    grad = jnp.where(core == parity, own[128:256, :], other[128:256, :]).astype(F32)
    adam_store(refs, (slice(None), slice(None)), grad)


def adam_mlp_body(ids, own_a, other_a, own_b, other_b, *refs):
    core, step = ids[1], pl.program_id(0)
    up_refs = refs[0:3] + refs[-6:-3]
    down_refs = refs[3:6] + refs[-3:]
    for owner in range(2):
        cols = pl.ds(pl.multiple_of(step * 256 + owner * 128, 128), 128)
        for part, (own, other) in enumerate(((own_a, other_a), (own_b, other_b))):
            halves = parities(core, own[0:128, cols].astype(F32), other[0:128, cols].astype(F32))
            for parity, grad in enumerate(halves):
                base = owner * 512 + part * 256 + parity * 128
                adam_store(up_refs, (slice(None), slice(base, base + 128)), grad)
    rows = pl.ds(pl.multiple_of(128 + (step % 2) * 64, 64), 64)
    grad = jnp.where(core == step // 2, own_b[rows, :], other_b[rows, :]).astype(F32)
    adam_store(down_refs, (slice(None), slice(None)), grad)


def rotary_tables(segments):
    row_count = segments.shape[0]
    row_index = jnp.arange(row_count, dtype=jnp.int32)
    earlier = jnp.concatenate([jnp.full((1,), -1, jnp.int32), segments[:-1]])
    starts = jnp.where(segments != earlier, row_index, 0)
    position = (row_index - lax.cummax(starts, axis=0)).astype(F32)
    half_dim = ROT_DIM // 2
    dims = jnp.arange(LANES, dtype=jnp.int32) % HEAD_DIM
    frequency = ROPE_BASE ** (-2.0 * (dims % half_dim).astype(F32) / ROT_DIM)
    turned = dims < ROT_DIM
    angles = position[:, None] * jnp.where(turned, frequency, 0.0)[None, :]
    cosine, sine = jnp.cos(angles), jnp.sin(angles)
    front = (dims < half_dim)[None, :]
    return cosine, jnp.where(front, -sine, 0.0), jnp.where(front, 0.0, sine)


def on_device(
    sizes,
    tokens,
    segments,
    cotangent,
    w_qkv,
    w_out,
    w_up,
    w_down,
    vectors,
    m_qkv,
    m_out,
    m_up,
    m_down,
    m_vectors,
    v_qkv,
    v_out,
    v_up,
    v_down,
    v_vectors,
):
    copies, owners = sizes
    me = lax.axis_index("zero")
    plane = lax.axis_index("dp")
    core = plane % 2
    ids = jnp.stack([me, core, (plane // 2) % 2]).astype(jnp.int32)

    def move(value, target):
        pairs = []
        for d in range(copies):
            for z in range(owners):
                to_d, to_z = target(d, z)
                pairs.append((d * owners + z, to_d * owners + to_z))
        return lax.ppermute(value, AXES, pairs)

    def swap(value, dp_bits, zero_bits):
        return move(value, lambda d, z: (d ^ dp_bits, z ^ zero_bits))

    def swap_far(value):
        return move(value, lambda d, z: (d, z ^ (6 if d & 2 else 4)))

    def sync(*values):
        return lax.optimization_barrier(values)

    def add(*terms):
        return functools.reduce(jnp.add, [t.astype(F32) for t in terms])

    def reduce_first(keep, send_x, send_y):
        return keep, swap(send_x, 0, 1), swap(send_y, 2, 0)

    def reduce_first_part(keep, send_x, send_y):
        return keep, [send_x[0], swap(send_x[1], 0, 1)], swap(send_y, 2, 0)

    def reduce_second(state):
        keep, got_x, got_y = state
        far = add(keep[3], got_y[1]).astype(BF16)
        near = add(keep[1], got_x[1]).astype(BF16)
        return keep, got_x, got_y, far, near, swap(far, 0, 1), swap(near, 0, 2)

    def reduce_third(state):
        keep, got_x, got_y, _, _, got_far, got_near = state
        far = add(keep[2], got_y[0], got_far).astype(BF16)
        return (keep, got_x, got_near), far, swap_far(far)

    def reduce_fourth(state):
        (keep, got_x, got_near), _, got = state
        total = add(keep[0], got_x[0], got_near, got).astype(BF16)
        return total, swap(total, 2, 0)

    def reduce_fifth(state):
        total = add(*state).astype(BF16)
        bit = 4
        while bit < copies:
            total = add(total, swap(total, bit, 0)).astype(BF16)
            bit *= 2
        return total, swap(total, 1, 0)

    T, width = tokens.shape
    rows = 2 * T
    sds = jax.ShapeDtypeStruct
    row_block = lambda n, c=width: spec((n, c), lambda i: (i, 0))
    col_block = lambda n: spec((width, n), lambda i: (0, i))

    def block_call(body, grid, ins, outs, flops, moved, scratch=(), name=None):
        return kernel_call(
            body,
            grid,
            [place for _, place in ins],
            [place for _, place in outs],
            [shape for shape, _ in outs],
            flops,
            moved,
            scratch=scratch,
            name=name,
        )(*[value for value, _ in ins])

    def const(value):
        return value, whole(value.shape)

    def kept(shape, dtype):
        return sds(shape, dtype), whole(shape)

    steps = rows // 256
    with jax.named_scope("prep"):
        own_a = block_call(
            prep_attn_body,
            (1,),
            [(ids, scalars())]
            + [(w_qkv, spec((128, 512), lambda i, n=part: (0, 2 * n), single=True)) for part in range(3)]
            + [const(w_out), (vectors, whole((13, 128)))],
            [kept((144, 1280), BF16)],
            0,
            3e6,
            scratch=[pltpu.VMEM((16, 128), F32)],
            name="prep_attn",
        )[0]

    def prep_mlp(part, shape, ins, beside):
        with jax.named_scope("prep"):
            return block_call(
                functools.partial(prep_mlp_body, part),
                (1,),
                [(ids, scalars()), const(ins[0]), (ins[1], spec((256, width), lambda i: (part, 0), single=True))]
                + [const(value) for value in ins[2:]],
                [kept(shape, BF16)],
                0,
                beside * 3e6,
                name="prep_mlp",
            )[0]

    def z_moves(own):
        return swap(own, 0, 2), swap_far(own)

    with jax.named_scope("gather"):
        seg_other = swap(segments, 1, 0)
        tok_other = swap(tokens, 1, 0)
        dy_other = swap(cotangent, 1, 0)
        own_a, w_up_in = sync(own_a, w_up)
        next_a, far_a = z_moves(own_a)
        across_a = swap(own_a, 0, 1)
        own_b = prep_mlp(0, (256, 1024), (w_up_in, w_down), 20)
        tables = [
            jnp.concatenate(pair, axis=0)
            for pair in zip(rotary_tables(segments), rotary_tables(seg_other))
        ]
        seg_row = jnp.stack([segments, seg_other]).astype(F32)[:, None, :]
        seg_ids = jnp.concatenate([segments, seg_other]).astype(F32)
        next_a, far_a, across_a, own_b, w_up_in, tables, seg_row, seg_ids, tok_other, dy_other = sync(
            next_a, far_a, across_a, own_b, w_up_in, tables, seg_row, seg_ids, tok_other, dy_other
        )
        next_across_a, far_across_a, rest_across_a = swap(next_a, 0, 1), swap(far_a, 0, 1), swap(far_a, 2, 1)
        rest_a = swap(far_a, 2, 0)
        far_b = swap_far(own_b)
        seg_col = jnp.broadcast_to(seg_ids[:, None], (rows, LANES))
        w_up_in, seg_col = sync(w_up_in, seg_col)
        own_c = prep_mlp(1, (352, 1024), (w_up_in, w_down, w_qkv), 25)
        next_across_a, far_across_a, rest_a, rest_across_a, far_b, own_b, own_c = sync(
            next_across_a, far_across_a, rest_a, rest_across_a, far_b, own_b, own_c
        )
        far_across_b, across_b, rest_b = swap(far_b, 0, 1), swap(own_b, 0, 1), swap(far_b, 2, 0)
        next_b = swap(own_b, 0, 2)
        far_c = swap_far(own_c)
    attn_pieces = [own_a, next_a, far_a, rest_a, across_a, next_across_a, far_across_a, rest_across_a]

    def table_blocks(count):
        return [(t, row_block(count, 128)) for t in tables]

    def halves(own, other, count):
        last = T // count - 1
        return [
            (own, spec((count, width), lambda i: (jnp.minimum(i, last), 0))),
            (other, spec((count, width), lambda i: (jnp.maximum(i - last - 1, 0), 0))),
        ]

    def attention(group, pairs, projected, d_att, previous):
        with jax.named_scope("attention"):
            first = pairs[0]
            head_block = spec((T, 128), lambda h, m: (h, m + first))
            outs = [
                (sds((rows, 256), BF16), head_block),
                (sds((3, rows, 256), BF16), spec((3, T, 128), lambda h, m: (0, h, m + first))),
            ]
            ins = (
                [(value, head_block) for value in projected]
                + [(d_att, spec((T, 128), lambda h, m: (h, m + first + 2 * group)))]
                + [(seg_col, spec((T, LANES), lambda h, m: (h, 0)))]
                + [(seg_row, spec((1, 1, T), lambda h, m: (h, 0, 0)))]
                + [(t, spec((T, 128), lambda h, m: (h, 0))) for t in tables]
            )
            aliases = {len(ins) + n: n for n in range(len(previous))}
            return pl.pallas_call(
                attn_body,
                grid=(2, len(pairs)),
                in_specs=[place for _, place in ins] + [distant()] * len(previous),
                out_specs=[place for _, place in outs],
                out_shape=[shape for shape, _ in outs],
                input_output_aliases=aliases,
                cost_estimate=pl.CostEstimate(
                    flops=len(pairs) * 15000000000, bytes_accessed=len(pairs) * 5000000, transcendentals=0
                ),
                compiler_params=pltpu.CompilerParams(
                    vmem_limit_bytes=VMEM_NEED * MIB, dimension_semantics=("arbitrary",) * 2
                ),
                name="attention",
            )(*[value for value, _ in ins], *previous)

    def blocks_of(shape):
        return [kept((n,) + shape, BF16) for n in (4, 2, 2)]

    with jax.named_scope("qkv"):
        *projected, d_att, attn_in, attn_t, mlp_in, wq_a, full_out, vec, bias_qkv = block_call(
            functools.partial(qkv_first_body, rows // 512),
            (rows // 512,),
            [(ids, scalars())]
            + [const(piece) for piece in attn_pieces]
            + halves(tokens, tok_other, 512)
            + halves(cotangent, dy_other, 512)
            + table_blocks(512),
            [(sds((rows, 256), BF16), row_block(512, 256))] * 3
            + [(sds((rows, 512), BF16), row_block(512, 512)), (sds((rows, width), BF16), row_block(512))]
            + [(sds((width, rows), BF16), col_block(512)), (sds((rows, width), BF16), row_block(512))]
            + [kept((1024, 768), BF16), kept((512, 1024), BF16), kept((16, 1024), F32), kept((1, 1536), F32)],
            2 * rows * 1024 * 1280,
            30e6,
            name="qkv",
        )
    projected, far_across_b, across_b, rest_b, own_b = sync(
        projected, far_across_b, across_b, rest_b, own_b
    )
    with jax.named_scope("gather"):
        rest_across_b, next_across_b = swap(far_across_b, 2, 0), swap(own_b, 0, 3)
    half_a = attention(0, (0,), projected, d_att, [])
    half_a, projected, far_c, own_c, next_b = sync(half_a, projected, far_c, own_c, next_b)
    with jax.named_scope("gather"):
        far_across_c, rest_c, next_c = swap(far_c, 0, 1), swap(far_c, 2, 0), swap(own_c, 0, 2)
    att_a, grad_a = attention(0, (1,), projected, d_att, half_a)
    att_a, grad_a, rest_across_b, next_across_b, far_across_c, rest_c, own_c, next_c, attn_t, mlp_in = sync(
        att_a, grad_a, rest_across_b, next_across_b, far_across_c, rest_c, own_c, next_c, attn_t, mlp_in
    )
    with jax.named_scope("gather"):
        across_c, next_across_c, rest_across_c = swap(own_c, 0, 1), swap(next_c, 0, 1), swap(far_across_c, 2, 0)
    pieces_b = [own_b, next_b, far_b, rest_b, across_b, next_across_b, far_across_b, rest_across_b]

    def mlp(part, weights, rows_in):
        with jax.named_scope("mlp"):
            *results, hid, gp, sums, w_up_full, w_down_full = block_call(
                functools.partial(mlp_body, part, steps),
                (steps,),
                [(ids, scalars())]
                + [const(w) for w in weights]
                + [const(vec), (rows_in, row_block(256))]
                + halves(cotangent, dy_other, 256),
                [(sds((n, 256, 1024), BF16), distant()) for n in (4, 2, 2)]
                + [(sds((rows, width), BF16), row_block(256))] * 2
                + [kept((8, 1024), F32)]
                + [(sds((1024, 1024), BF16), distant())] * 2,
                2 * rows * 1024 * 1024 * 4,
                40e6,
                scratch=[
                    pltpu.VMEM((1024, rows), BF16),
                    pltpu.VMEM((1024, rows), BF16),
                    pltpu.VMEM((rows, 1024), BF16),
                    pltpu.VMEM((rows, 1024), BF16),
                    pltpu.VMEM((8, 1024), F32),
                    pltpu.VMEM((1024, 512), BF16),
                ]
                + [pltpu.VMEM((n, 256, 1024), BF16) for n in (4, 2, 2)]
                + [pltpu.VMEM((1024, 1024), BF16)] * 2
                + [pltpu.SemaphoreType.DMA((8,))],
                name="mlp",
            )
            return results, hid, gp, sums, w_up_full, w_down_full

    mlp_a = mlp(0, pieces_b, mlp_in)
    mlp_a, mlp_in, across_c, next_across_c, rest_across_c = sync(
        mlp_a, mlp_in, across_c, next_across_c, rest_across_c
    )
    pieces_c = [own_c, next_c, far_c, rest_c, across_c, next_across_c, far_across_c, rest_across_c]
    reduce_a = reduce_first(*mlp_a[0])
    mlp_b = mlp(1, pieces_c, mlp_in)
    mlp_b, reduce_a, attn_in = sync(mlp_b, reduce_a, attn_in)
    reduce_a = reduce_second(reduce_a)
    reduce_b = reduce_first_part(*mlp_b[0])
    attn_in, *ready = sync(attn_in, *reduce_a[3:5])

    with jax.named_scope("attention"):
        head_block = spec((T, 128), lambda h, m: (h, m))
        att_b, grad_b, wq_b = block_call(
            project_attn_body,
            (2, 2),
            [(ids, scalars())]
            + [(piece, whole((96, width))) for piece in pieces_c]
            + [(attn_in, spec((T, width), lambda h, m: (h, 0))), const(bias_qkv)]
            + [(d_att, spec((T, 128), lambda h, m: (h, m + 2)))]
            + [(seg_col, spec((T, LANES), lambda h, m: (h, 0)))]
            + [(seg_row, spec((1, 1, T), lambda h, m: (h, 0, 0)))]
            + [(t, spec((T, 128), lambda h, m: (h, 0))) for t in tables],
            [
                (sds((rows, 256), BF16), head_block),
                (sds((3, rows, 256), BF16), spec((3, T, 128), lambda h, m: (0, h, m))),
                kept((1024, 768), BF16),
            ],
            38e9,
            20e6,
            scratch=[pltpu.VMEM((T, 256), BF16)] * 3,
            name="attention",
        )
    att_b, grad_b, reduce_a, reduce_b = sync(att_b, grad_b, reduce_a, reduce_b)
    reduce_a = reduce_third(reduce_a)
    reduce_b[1][0] = swap(reduce_b[1][0], 0, 1)
    reduce_b = reduce_second(reduce_b)
    grad_b, *ready = sync(grad_b, reduce_a[1], *reduce_b[3:5])
    with jax.named_scope("attn_weights"):
        *blocks, bias_sum = block_call(
            attn_weights_body,
            (7,),
            [(ids, scalars()), const(attn_t)]
            + [(grad_a, spec((1, rows, 256), lambda n: (jnp.minimum(n, 2), 0, 0)))]
            + [(grad_b, spec((1, rows, 256), lambda n: (jnp.clip(n - 3, 0, 2), 0, 0)))]
            + [(value, distant()) for value in (att_a, att_b, cotangent, dy_other)],
            blocks_of((128, 2048)) + [kept((8, 1536), F32)],
            2 * rows * 1024 * 2048,
            24e6,
            scratch=[pltpu.VMEM((1024, 256), BF16)]
            + [pltpu.VMEM((rows, 256), BF16)] * 2
            + [pltpu.VMEM((T, width), BF16)] * 2
            + [pltpu.SemaphoreType.DMA((4,))],
            name="attn_weights",
        )
    blocks, grad_b, reduce_a, reduce_b = sync(blocks, grad_b, reduce_a, reduce_b)
    reduce_o = reduce_first(*blocks)

    _, hid_a, gp_a, sums_a, up_a, down_a = mlp_a
    _, hid_b, gp_b, sums_b, up_b, down_b = mlp_b

    def adam_down(totals):
        wide = [spec((128, width), lambda n: (n, 0))] * 3
        return kernel_call(
            adam_down_body,
            (2,),
            [scalars()] + [whole((256, 1024))] * 2 + wide,
            wide,
            [sds((512, 1024), F32)] * 3,
            0,
            7e6,
            name="adam_down",
        )(ids, *totals, w_down, m_down, v_down)

    def adam_mlp(totals_a, totals_b, previous):
        wide = [spec((128, 1024), lambda n: (0, n))] * 3 + [spec((64, width), lambda n: (4 + n, 0))] * 3
        return pl.pallas_call(
            adam_mlp_body,
            grid=(4,),
            in_specs=[scalars()] + [whole((256, 1024))] * 4 + wide + [distant()] * 3,
            out_specs=wide,
            out_shape=[sds((128, 4096), F32)] * 3 + [sds((512, 1024), F32)] * 3,
            input_output_aliases={11 + n: 3 + n for n in range(3)},
            cost_estimate=pl.CostEstimate(flops=0, bytes_accessed=21000000, transcendentals=0),
            compiler_params=pltpu.CompilerParams(
                vmem_limit_bytes=VMEM_NEED * MIB, dimension_semantics=("arbitrary",)
            ),
            name="adam_mlp",
        )(ids, *totals_a, *totals_b, w_up, m_up, v_up, w_down, m_down, v_down, *previous)

    def back(own, grad, rows_tok, extra, outs):
        first = 0 if own else T // 256
        block = lambda c=width: spec((256, c), lambda i: (i + first, 0))
        lead = spec((3, 256, 256), lambda i: (0, i + first, 0))
        with jax.named_scope("back"):
            return block_call(
                functools.partial(back_body, own),
                (T // 256,),
                [(grad_a, lead), (grad, lead), (att_a, block(256)), (att_b, block(256))]
                + [(value, block()) for value in (hid_a, hid_b, gp_a, gp_b)]
                + [const(w) for w in (full_out, down_a, down_b, up_a, up_b, wq_a, wq_b)]
                + [(rows_tok, row_block(256)), const(vec)]
                + extra,
                outs + [kept((8, width), F32)],
                2 * T * 1024 * 6144,
                40e6,
                name="back",
            )

    reduce_a = reduce_fourth(reduce_a)
    reduce_b = reduce_third(reduce_b)
    pair_block = spec((2, 256, width), lambda i: (0, i, 0))
    part_other, sums_other = back(False, grad_b, tok_other, [], [(sds((2, T, width), BF16), pair_block)])
    part_other, sums_other, grad_b, reduce_a, reduce_b, reduce_o = sync(
        part_other, sums_other, grad_b, reduce_a, reduce_b, reduce_o
    )
    reduce_o = reduce_second(reduce_o)
    part_other, reduce_a, reduce_b, *ready = sync(part_other, reduce_a, reduce_b, *reduce_o[3:5])
    reduce_a = reduce_fifth(reduce_a)
    reduce_b = reduce_fourth(reduce_b)
    part_got = swap(part_other, 1, 0)
    updated_mlp = adam_down(reduce_a)
    updated_mlp, grad_b, reduce_b, reduce_o, part_got = sync(
        updated_mlp, grad_b, reduce_b, reduce_o, part_got
    )
    reduce_o = reduce_third(reduce_o)
    reduce_b = reduce_fifth(reduce_b)
    grad_b, *ready = sync(grad_b, reduce_o[1], reduce_b[0])
    layer_out, tokens_grad, sums_own = back(
        True,
        grad_b,
        tokens,
        [(cotangent, row_block(256)), (part_got, pair_block)],
        [(sds((T, width), BF16), row_block(256)), (sds((T, width), F32), row_block(256))],
    )
    sums_own, updated_mlp, reduce_b, reduce_o = sync(sums_own, updated_mlp, reduce_b, reduce_o)
    reduce_o = reduce_fourth(reduce_o)

    with jax.named_scope("vectors"):
        is_core = jnp.arange(2) == core
        grad_bias = jnp.where(core == 0, sums_a[1:2], 0.0)
        bias_sum = jnp.swapaxes(bias_sum[0].reshape(2, 3, 256), 0, 1)
        grad_bias_qkv = jnp.where(
            is_core[None, None, :, None], bias_sum.reshape(3, 8, 1, 64), 0.0
        ).reshape(3, width)
        grad_bias_up = jnp.where(
            is_core[None, None, :, None],
            jnp.swapaxes(jnp.stack([sums_a[0], sums_b[0]]).reshape(2, 8, 128), 0, 1)[:, :, None],
            0.0,
        ).reshape(4, width)
        total = jnp.concatenate(
            [
                sums_own[0:4] + sums_other[0:4],
                grad_bias_qkv,
                grad_bias,
                grad_bias_up,
                grad_bias,
                jnp.zeros((3, width), F32),
            ],
            axis=0,
        )
        moved = [swap(total, 0, step) for step in (2, 4, 6)]
        updated_mlp = adam_mlp(reduce_a, reduce_b, updated_mlp)
        updated_mlp, reduce_o, total, moved = sync(updated_mlp, reduce_o, total, moved)
        reduce_o = reduce_fifth(reduce_o)
        total = functools.reduce(jnp.add, moved, total)
        others = swap(total, 0, 1), swap(total, 2, 0), swap(total, 2, 1)

    with jax.named_scope("adam"):
        wide = [spec((128, 1536), lambda n: (0, n))] * 3 + [whole((128, 1024))] * 3
        updated_attn = kernel_call(
            adam_attn_body,
            (2,),
            [scalars()] + [whole((128, 2048))] * 2 + wide,
            wide,
            [sds((128, 3072), F32)] * 3 + [sds((128, 1024), F32)] * 3,
            0,
            13e6,
            name="adam",
        )(ids, *reduce_o, w_qkv, m_qkv, v_qkv, w_out, m_out, v_out)

    with jax.named_scope("vectors"):
        updated_attn, total, (across, beside, both) = sync(updated_attn, total, others)
        total = (total + across) + (beside + both)
        bit = 4
        while bit < copies:
            total = total + swap(total, bit, 0)
            bit *= 2
        total = total + swap(total, 1, 0)
        share = lax.dynamic_slice_in_dim(total[0:13], me * 128, 128, 1)
        first_vectors, second_vectors, new_vectors = adam_math(
            vectors, m_vectors, v_vectors, share, RATE_VECTOR, 0.0
        )
    first_qkv, second_qkv, new_qkv, first_out, second_out, new_out = updated_attn
    first_up, second_up, new_up, first_down, second_down, new_down = updated_mlp
    return (
        layer_out,
        tokens_grad,
        first_qkv,
        first_out,
        first_up,
        first_down,
        first_vectors,
        second_qkv,
        second_out,
        second_up,
        second_down,
        second_vectors,
        new_qkv,
        new_out,
        new_up,
        new_down,
        new_vectors,
    )


def solution(mesh):
    rows, owned, spread = P(AXES, None), P("zero", None), P(None, "zero")
    state = (owned, owned, owned, owned, spread)
    return jax.shard_map(
        functools.partial(on_device, (mesh.shape["dp"], mesh.shape["zero"])),
        mesh=mesh,
        in_specs=(rows, P(AXES), rows) + state * 3,
        out_specs=(rows, rows) + state * 3,
        check_vma=False,
    )
```
